32 devices in a mesh: px: 8 (over z, y), py: 4 (over x, core).
Axes of the slice: x: 2, y: 2, z: 4, core: 2. Of those that a mesh axis runs over, the one named last changes fastest.
Arguments:
- residual: float32 [32, 128, 512], P(None, 'px', 'py'), may hold values from -6 to 6
- factor_fine: bfloat16 [64, 4, 520, 256], P('px', 'py'), may hold values from -0.25 to 0.25
- factor_one: bfloat16 [32, 2, 520, 256], P('px'), may hold values from -0.25 to 0.25
- factor_two: bfloat16 [16, 1, 520, 256], P('px'), may hold values from -0.25 to 0.25
- factor_three: bfloat16 [8, 1, 264, 128], P('px'), may hold values from -0.375 to 0.375
- factor_four: bfloat16 [4, 1, 136, 64], replicated, may hold values from -0.5 to 0.5
- coarse_inverse: bfloat16 [64, 64], replicated, may hold values from -0.75 to 0.75
Outputs:
- preconditioned: float32 [32, 128, 512], P(None, 'px', 'py')
The draws below stay inside these ranges and needn't reach their ends.
All inputs are finite; a program needn't handle non-finite values.
Results may differ from the reference program's by a relative error of at most 0.0029.
Values sent between devices are 32-bit elements; how exact they have to be, the bound alone decides.
No kernel may reach another device: no remote copies, remote signals or barrier semaphores. Data moves between devices by JAX's collectives and lax.ppermute only.
A program may use at most 128 MiB of HBM per device.

```python
import math
import jax
import jax.numpy as jnp
from jax import lax

RHS = 32
CY = 128
NX = 128
NY = 512
NX1 = 64
NY1 = 256
NX2 = 32
NY2 = 128
NX3 = 16
NY3 = 64
NX4 = 8
NY4 = 32
NX5 = 4
NY5 = 16
TW1 = 128
TW2 = 128
TW3 = 64
TW4 = 32
N_PY = 4


def steps_of(own_key, dims, split, low, top_value):
    level, own = 1.0, jax.random.fold_in(own_key, 6)
    for axis_at, blocks in split:
        steps = jnp.exp(jax.random.uniform(jax.random.fold_in(own, axis_at), (blocks,), jnp.float32, low / len(split), top_value / len(split)))
        level = level * jnp.repeat(steps, dims[axis_at] // blocks).reshape([-1 if axis == axis_at else 1 for axis in range(len(dims))])
    return level


def centred(key, dims, scale, most, pieces=(), kind=jnp.bfloat16):
    drawn = jax.random.normal(key, dims, jnp.float32) * scale
    if len(pieces) > 0:
        drawn = steps_of(key, dims, pieces, -0.22, 0.18) * drawn
    return jnp.clip(drawn, min=-most, max=most).astype(kind)


def setup_inputs(seed: int = 0) -> dict:
    arg_keys = jax.random.split(jax.random.key(seed), 8)
    return {
        "residual": centred(arg_keys[0], (RHS, NX, NY), 1.0, 6.0, ((1, 8), (2, 4)), jnp.float32),
        "factor_fine": centred(arg_keys[1], (NX // 2, N_PY, 4 * (CY + 2), 2 * CY), (4 * (CY + 2)) ** -0.5, 0.25, ((0, 8), (1, 4))),
        "factor_one": centred(arg_keys[2], (NX1 // 2, NY1 // TW1, 4 * (TW1 + 2), 2 * TW1), (4 * (TW1 + 2)) ** -0.5, 0.25, ((0, 8),)),
        "factor_two": centred(arg_keys[3], (NX2 // 2, NY2 // TW2, 4 * (TW2 + 2), 2 * TW2), (4 * (TW2 + 2)) ** -0.5, 0.25, ((0, 8),)),
        "factor_three": centred(arg_keys[4], (NX3 // 2, NY3 // TW3, 4 * (TW3 + 2), 2 * TW3), (4 * (TW3 + 2)) ** -0.5, 0.375, ((0, 8),)),
        "factor_four": centred(arg_keys[5], (NX4 // 2, NY4 // TW4, 4 * (TW4 + 2), 2 * TW4), (4 * (TW4 + 2)) ** -0.5, 0.5),
        "coarse_inverse": centred(arg_keys[6], (NX5 * NY5, NX5 * NY5), (NX5 * NY5) ** -0.5, 0.75),
    }


tap_scale = 1.0 / math.sqrt(20.0)

def shrink(padded, dimension):
    length = padded.shape[dimension] - 2
    before = padded.shape[:dimension]
    after = padded.shape[dimension + 1:]
    lower = lax.slice_in_dim(padded, 0, length, axis=dimension).reshape(before + (length // 2, 2) + after)
    upper = lax.slice_in_dim(padded, 2, length + 2, axis=dimension).reshape(before + (length // 2, 2) + after)
    outer_low = lax.index_in_dim(lower, 0, dimension + 1, keepdims=False)
    inner_low = lax.index_in_dim(lower, 1, dimension + 1, keepdims=False)
    inner_high = lax.index_in_dim(upper, 0, dimension + 1, keepdims=False)
    outer_high = lax.index_in_dim(upper, 1, dimension + 1, keepdims=False)
    return tap_scale * (outer_low + 3.0 * inner_low + 3.0 * inner_high + outer_high)

def prolong(padded, dimension):
    length = padded.shape[dimension] - 2
    left = lax.slice_in_dim(padded, 0, length, axis=dimension)
    centre = lax.slice_in_dim(padded, 1, length + 1, axis=dimension)
    right = lax.slice_in_dim(padded, 2, length + 2, axis=dimension)
    even_cells = tap_scale * (3.0 * centre + left)
    odd_cells = tap_scale * (3.0 * centre + right)
    stacked = jnp.stack([even_cells, odd_cells], axis=dimension + 1)
    target = list(centre.shape)
    target[dimension] = 2 * length
    return stacked.reshape(tuple(target))

def pad_both(field):
    return jnp.pad(field, ((0, 0), (1, 1), (1, 1)))

def restrict_both(padded):
    return shrink(shrink(padded, 1), 2)

def prolong_both(padded):
    return prolong(prolong(padded, 1), 2)

def make_windows(padded, width):
    systems, height, breadth = padded.shape
    inner_rows = height - 2
    inner_cols = breadth - 2
    tiles = inner_cols // width
    pairs = inner_rows // 2
    top = padded[:, :inner_rows].reshape(systems, pairs, 2, breadth)
    bottom = padded[:, 2:].reshape(systems, pairs, 2, breadth)
    strips = jnp.concatenate([top, bottom], axis=2)
    main = strips[..., :inner_cols].reshape(systems, pairs, 4, tiles, width)
    extra = jnp.pad(strips[..., width:], ((0, 0), (0, 0), (0, 0), (0, width - 2)))
    extra = extra.reshape(systems, pairs, 4, tiles, width)[..., :2]
    windows = jnp.concatenate([main, extra], axis=4).transpose(0, 1, 3, 2, 4)
    return windows.reshape(systems, pairs, tiles, 4 * (width + 2)).astype(jnp.bfloat16)

def solve_blocks(padded, factor):
    width = factor.shape[3] // 2
    systems, height, breadth = padded.shape
    windows = make_windows(padded, width)
    pairs = windows.shape[1]
    tiles = windows.shape[2]
    solved = jnp.einsum('rbqe,bqeo->rbqo', windows.astype(jnp.float32), factor.astype(jnp.float32), precision=lax.Precision.HIGHEST)
    solved = solved.reshape(systems, pairs, tiles, 2, width).transpose(0, 1, 3, 2, 4)
    return solved.reshape(systems, height - 2, breadth - 2)

def reference(residual, factor_fine, factor_one, factor_two, factor_three, factor_four, coarse_inverse):
    factors = [factor_fine, factor_one, factor_two, factor_three, factor_four]
    parts = []
    level_now = residual
    for level in range(5):
        padded = pad_both(level_now)
        parts.append(solve_blocks(padded, factors[level]))
        level_now = restrict_both(padded)
    systems, rows_five, cols_five = level_now.shape
    flat = level_now.reshape(systems, rows_five * cols_five).astype(jnp.bfloat16)
    correction = jnp.dot(flat, coarse_inverse, preferred_element_type=jnp.float32).reshape(systems, rows_five, cols_five)
    for level in range(4, 0, -1):
        correction = parts[level] + prolong_both(pad_both(correction))
    return parts[0] + prolong_both(pad_both(correction))
```

```python
import functools

import jax
import jax.numpy as jnp
import numpy as np
from jax import lax
from jax.experimental import pallas as pl
from jax.experimental.pallas import tpu as pltpu
from jax.sharding import PartitionSpec as P

F32 = jnp.float32
BF16 = jnp.bfloat16
LANES = 128
SHRINK = 1.0 / 20.0
TAPS = (1, 3, 3, 1)
VMEM_BYTES = 24 * 1024 * 1024


def round_up(value, unit=LANES):
    return -(-value // unit) * unit


def local_shrink(fine, coarse, halo_in, first, last):
    out = np.zeros((fine + 2 * halo_in, coarse + 2))
    for i in range(-1, coarse + 1):
        if (i == -1 and first) or (i == coarse and last):
            continue
        for t, tap in enumerate(TAPS):
            j = 2 * i - 1 + t
            if -halo_in <= j < fine + halo_in:
                out[j + halo_in, i + 1] = tap
    return out


def global_prolong(coarse):
    out = np.zeros((coarse, 2 * coarse))
    for i in range(coarse):
        out[i, 2 * i] += 3
        out[i, 2 * i + 1] += 3
        if i > 0:
            out[i, 2 * i - 1] += 1
        if i + 1 < coarse:
            out[i, 2 * i + 2] += 1
    return out


def bf(array):
    return np.asarray(array, np.float32).astype(jnp.bfloat16)


class Plan:
    def __init__(self, mesh_shape, residual, factors):
        self.n, self.m = mesh_shape["px"], mesh_shape["py"]
        self.rhs, self.h0, self.w0 = residual
        self.h = [self.h0 >> l for l in range(5)]
        self.w = [self.w0 >> l for l in range(5)]
        self.ny = [self.w0 * self.m >> l for l in range(6)]
        self.nx = [self.h0 * self.n >> l for l in range(6)]
        self.tile = [f[3] // 2 for f in factors]
        self.tiles = [f[1] for f in factors]
        self.slots = self.h[1] + 2
        self.offset = [None, 0, self.w[1] + 2, self.w[1] + self.w[2] + 4]
        self.spare = self.w[1] + self.w[2] + self.w[3] + 6

    def scale(self):
        out = np.ones((1, LANES), np.float32)
        for l in (1, 2, 3):
            out[:, self.offset[l] : self.offset[l] + self.w[l] + 2] = SHRINK**l
        return out

    def shrink_columns(self):
        out = np.zeros((self.m, 3, self.w0, LANES))
        for c in range(self.m):
            ends = (c == 0, c == self.m - 1)
            now = local_shrink(self.w0, self.w[1], 0, *ends)
            for l in (1, 2, 3):
                if l > 1:
                    now = now @ local_shrink(self.w[l - 1], self.w[l], 1, *ends)
                o = self.offset[l]
                out[c, l - 1, :, o : o + self.w[l] + 2] = now
        return bf(out)

    def pick_sides(self):
        out = np.zeros((2, self.w0, LANES))
        for k in range(2):
            out[k, 0, self.spare + 2 * k] = 1
            out[k, self.w0 - 1, self.spare + 2 * k + 1] = 1
        return bf(out)

    def place(self, level, lead, width, at=0):
        out = np.zeros((self.m, LANES, width))
        for c in range(self.m):
            for k in range(self.w[level] + 2):
                column = self.w[level] * c - 1 + k
                if -lead <= column < self.ny[level]:
                    out[c, self.offset[level] + k, at + column + lead] = 1
        return out

    def halo_lanes(self):
        out = np.zeros((2, LANES, 2 * LANES))
        for k in range(2):
            for position in range(4):
                out[0, self.spare + 2 * k + 1, LANES * k + 2 * position] = 1
                out[1, self.spare + 2 * k, LANES * k + 2 * position + 1] = 1
        return bf(out)

    def lift_columns(self, level):
        out = np.eye(self.ny[level])
        for l in range(level, 0, -1):
            out = out @ global_prolong(self.ny[l])
        return out.reshape(self.ny[level], self.m, self.w0).transpose(1, 0, 2)

    def lift_rows_of(self, level):
        w, tiles = self.tile[level], self.tiles[level]
        full = self.lift_columns(level).reshape(self.m, tiles, w, self.w0)
        out = np.zeros((self.m, 2, tiles, 2 * w, self.w0))
        for j in range(2):
            out[:, j, :, j * w : (j + 1) * w] = full
        return out

    def coarse_shrink(self):
        ny3, ny4 = self.ny[3], self.ny[4]
        columns = global_prolong(ny4).T
        width = round_up(ny4 + 2)
        out = np.zeros((2, 2, ny3, width))
        for side, taps in enumerate(((1, 3), (3, 1))):
            for j in range(2):
                out[side, j, :, 1 : 1 + ny4] = taps[j] * columns
        return bf(out.reshape(2, 2 * ny3, width))

    def coarsest_shrink(self):
        nx5, ny5, ny4 = self.nx[5], self.ny[5], self.ny[4]
        columns = global_prolong(ny5).T
        width = round_up(ny4 + 2)
        out = np.zeros((nx5, width, nx5 * ny5))
        for i in range(nx5):
            out[i, 1 : 1 + ny4, i * ny5 : (i + 1) * ny5] = columns
        return bf(out.reshape(nx5 * width, nx5 * ny5))

    def coarsest_lift(self):
        rows, columns = global_prolong(self.nx[5]), global_prolong(self.ny[5])
        both = np.einsum("ia,jb->ijab", rows, columns)
        w, tiles = self.tile[4], self.tiles[4]
        both = both.reshape(self.nx[5] * self.ny[5], self.nx[4] // 2, 2, tiles, w)
        both = both.transpose(0, 1, 3, 2, 4)
        return bf(both.reshape(self.nx[5] * self.ny[5], self.nx[4] * self.ny[4]))

    def level_four_lift(self):
        pair = 2 * self.tile[4] * self.tiles[4]
        group = max(1, LANES // pair)
        width = group * pair
        rows = self.lift_rows_of(4).reshape(self.m, 2, pair, self.w0)
        out = np.zeros((self.m, group, 2, width, self.w0))
        for g in range(group):
            out[:, g, :, g * pair : (g + 1) * pair] = rows
        return bf(out), group


def split(value):
    high = value.astype(BF16)
    return high, (value - high.astype(F32)).astype(BF16)


def product(value, matrix):
    high, low = split(value)
    return jnp.dot(high, matrix, preferred_element_type=F32) + jnp.dot(
        low, matrix, preferred_element_type=F32
    )


def shrink_rows(rows, count, halo):
    out = []
    for i in range(-1, count // 2 + 1):
        total = None
        for t, tap in enumerate(TAPS):
            j = 2 * i - 1 + t
            if -halo <= j < count + halo:
                term = rows[j + halo] * float(tap) if tap > 1 else rows[j + halo]
                total = term if total is None else total + term
        out.append(total)
    return out


def lift_rows(rows, first, last):
    out = []
    for f in range(first, last):
        i = f // 2
        other = i - 1 if f % 2 == 0 else i + 1
        out.append((rows[i + 1] * 3.0 + rows[other + 1]) * SHRINK)
    return out


def lane_index(rows):
    return lax.broadcasted_iota(jnp.int32, (rows, LANES), 1)


def assemble(pieces, width):
    total = 4 * (width + 2)
    tiles = [[] for _ in range(-(-total // LANES))]
    lane = lane_index(pieces[0][0].shape[0])
    for k, piece in enumerate(pieces):
        for q, value in enumerate(piece):
            start = k * (width + 2) + LANES * q
            count = min(LANES, width + 2 - LANES * q)
            shift, at = start % LANES, start // LANES
            rolled = pltpu.roll(value, shift, 1) if shift else value
            tiles[at].append((min(LANES, shift + count), rolled))
            if shift + count > LANES:
                tiles[at + 1].append((shift + count - LANES, rolled))
    out = []
    for segments in tiles:
        segments = sorted(segments, key=lambda s: -s[0])
        end, value = segments[0]
        if end < LANES:
            value = jnp.where(lane < end, value, 0.0)
        for end, part in segments[1:]:
            value = jnp.where(lane < end, part, value)
        out.append(value)
    return jnp.concatenate(out, axis=1).astype(BF16)[:, :total]


def solve(lhs, factor):
    return jnp.dot(lhs, factor, preferred_element_type=F32)


def kernel_call(body, out_shape, scratch=()):
    return pl.pallas_call(
        body,
        out_shape=out_shape,
        scratch_shapes=list(scratch),
        compiler_params=pltpu.CompilerParams(vmem_limit_bytes=VMEM_BYTES),
    )


def shape(*dims):
    return jax.ShapeDtypeStruct(dims, F32)


def restrict_kernel(plan, x_ref, shrink_ref, sides_ref, scale_ref, own_ref, down_ref, up_ref):
    r, c = lax.axis_index("px"), lax.axis_index("py")
    rhs, slots, h = plan.rhs, plan.slots, plan.h
    above = jnp.where(r > 0, 1.0, 0.0).astype(F32)
    below = jnp.where(r < plan.n - 1, 1.0, 0.0).astype(F32)
    x = [x_ref[pl.ds(row, rhs, stride=h[0]), :] for row in range(h[0])]
    rows, total = x, None
    for level in (1, 2, 3):
        rows = shrink_rows(rows, h[level - 1], 0 if level == 1 else 1)
        rows[0] = rows[0] * above
        rows[-1] = rows[-1] * below
        part = product(jnp.concatenate(rows, axis=0), shrink_ref[c, level - 1])
        if total is None:
            total = part
        else:
            count = part.shape[0]
            total = jnp.concatenate([total[:count] + part, total[count:]], axis=0)
    sides = [jnp.zeros_like(x[0])] + x[: slots - 1]
    total = total + jnp.dot(
        jnp.concatenate(sides, axis=0).astype(BF16), sides_ref[0], preferred_element_type=F32
    )
    rest = jnp.concatenate(x[slots - 1 :], axis=0).astype(BF16)
    more = jnp.dot(rest, sides_ref[1], preferred_element_type=F32)
    count = more.shape[0]
    total = jnp.concatenate([total[:count] + more, total[count:]], axis=0)
    total = total * scale_ref[...]
    own = total.reshape(slots, rhs, LANES)
    own_ref[...] = own
    lane = lane_index(rhs)
    one, two = plan.offset[2], plan.offset[3]
    down_ref[0] = x[-1]
    up_ref[0] = x[0]
    for k in range(2):
        three_own = own[h[3] + k]
        down_ref[1 + k] = jnp.where(
            lane < one, own[h[1] + k], jnp.where(lane < two, own[h[2] + k], three_own)
        )
        up_ref[1 + k] = own[k]


def merge_kernel(plan, own_ref, down_ref, up_ref, sides_ref, out_ref):
    r = lax.axis_index("px")
    rhs, h = plan.rhs, plan.h
    above = jnp.where(r > 0, 1.0, 0.0).astype(F32)
    below = jnp.where(r < plan.n - 1, 1.0, 0.0).astype(F32)
    lane = lane_index(rhs)
    one, two, end = plan.offset[2], plan.offset[3], plan.spare
    out_ref[...] = own_ref[...]
    wrapped = jnp.logical_and(lane >= two, lane < end)
    in_band = lane < end
    for k in range(2):
        piece = down_ref[1 + k]
        piece = jnp.where(wrapped, piece, jnp.where(in_band, piece * above, 0.0))
        out_ref[k] = out_ref[k] + piece
        piece = up_ref[1 + k]
        piece = jnp.where(wrapped, piece, jnp.where(in_band, piece * below, 0.0))
        for level, low, high in ((1, 0, one), (2, one, two), (3, two, end)):
            row = h[level] + k
            chosen = jnp.logical_and(lane >= low, lane < high)
            out_ref[row] = out_ref[row] + jnp.where(chosen, piece, 0.0)
    top = (down_ref[0] * above).astype(BF16)
    out_ref[0] = out_ref[0] + jnp.dot(top, sides_ref[0], preferred_element_type=F32)
    bottom = (up_ref[0] * below).astype(BF16)
    at = h[0] + 1 - plan.slots
    out_ref[at] = out_ref[at] + jnp.dot(bottom, sides_ref[1], preferred_element_type=F32)


def gather_kernel(plan, place_ref, *refs):
    band_refs, out_ref = refs[:-1], refs[-1]
    c = lax.axis_index("py")
    rhs, width = plan.rhs, 2 * plan.ny[3]
    for half in range(2):
        total = jnp.zeros((rhs, width), F32)
        for k, band in enumerate(band_refs):
            owner = jnp.bitwise_xor(c, k)
            for j in range(2):
                total = total + product(band[2 * half + j], place_ref[owner, j])
        out_ref[half] = total


def level_rows(plan, level, band_refs, place_ref, c):
    rhs, count = plan.rhs, plan.h[level] + 2
    total = None
    for k, band in enumerate(band_refs):
        owner = jnp.bitwise_xor(c, k)
        value = band[:count].reshape(count * rhs, LANES)
        part = product(value, place_ref[owner])
        total = part if total is None else total + part
    return total


def coarse_kernel(plan, places, lifts, factors, *refs):
    bands, outs = refs[: plan.m], refs[plan.m :]
    r, c = lax.axis_index("px"), lax.axis_index("py")
    rhs = plan.rhs
    above = jnp.where(r > 0, 1.0, 0.0).astype(F32)
    below = jnp.where(r < plan.n - 1, 1.0, 0.0).astype(F32)
    down_ref, up_ref = outs[3], outs[4]
    for level in (1, 2, 3):
        w, tiles = plan.tile[level], plan.tiles[level]
        whole = level_rows(plan, level, bands, places[level - 1], c)
        count = plan.h[level] + 2
        rows = [whole[i * rhs : (i + 1) * rhs] for i in range(count)]
        if level == 3:
            rows[0] = rows[0] * above
            rows[-1] = rows[-1] * below
        lift_ref, factor_ref, out_ref = lifts[level - 1], factors[level - 1], outs[level - 1]
        solved = [[] for _ in range(tiles)]
        for b in range(plan.h[level] // 2):
            for t in range(tiles):
                pieces = []
                for k in range(4):
                    row = rows[2 * b + k]
                    lanes = range(t * w, t * w + w + 2, LANES)
                    pieces.append([row[:, lo : lo + LANES] for lo in lanes])
                solved[t].append(solve(assemble(pieces, w), factor_ref[b, t]))
        pairs = plan.h[level] // 2
        lifted = [None, None]
        for t in range(tiles):
            stacked = jnp.concatenate(solved[t], axis=0)
            for j in range(2):
                if w % LANES == 0:
                    part = product(
                        stacked[:, j * w : (j + 1) * w], lift_ref[c, t * w : (t + 1) * w]
                    )
                else:
                    part = product(stacked, lift_ref[c, j * tiles + t])
                lifted[j] = part if lifted[j] is None else lifted[j] + part
        for b in range(pairs):
            for j in range(2):
                out_ref[2 * b + j] = lifted[j][b * rhs : (b + 1) * rhs]
        down_ref[level - 1] = lifted[1][(pairs - 1) * rhs :]
        up_ref[level - 1] = lifted[0][:rhs]


def fine_kernel(plan, x_ref, down_ref, up_ref, halo_ref, factor_ref, *refs):
    bands, out_ref = refs[: plan.m], refs[plan.m]
    r, c = lax.axis_index("px"), lax.axis_index("py")
    rhs, h0, w0, slots = plan.rhs, plan.h0, plan.w0, plan.slots
    above = jnp.where(r > 0, 1.0, 0.0).astype(F32)
    below = jnp.where(r < plan.n - 1, 1.0, 0.0).astype(F32)
    halo = None
    for k, band in enumerate(bands):
        owner = jnp.bitwise_xor(c, k)
        from_left = jnp.where(owner == c - 1, 1.0, 0.0).astype(BF16)
        from_right = jnp.where(owner == c + 1, 1.0, 0.0).astype(BF16)
        matrix = halo_ref[0] * from_left + halo_ref[1] * from_right
        value = band[...].reshape(slots * rhs, LANES).astype(BF16)
        part = jnp.dot(value, matrix, preferred_element_type=F32)
        halo = part if halo is None else halo + part
    lane = lane_index(rhs)
    rows, sides = [], []
    for row in range(-1, h0 + 1):
        if row == -1:
            rows.append(down_ref[0] * above)
        elif row == h0:
            rows.append(up_ref[0] * below)
        else:
            rows.append(x_ref[pl.ds(row, rhs, stride=h0), :])
        part, slot = divmod(row + 1, slots)
        sides.append(halo[slot * rhs : (slot + 1) * rhs, part * LANES : (part + 1) * LANES])
    for b in range(h0 // 2):
        tiles, before = [], None
        for k in range(5):
            if k < 4:
                row, side = rows[2 * b + k], sides[2 * b + k]
                rolled = pltpu.roll(row, 2 * k + 1, 1)
                value = jnp.where(lane == 2 * k, side, rolled)
            else:
                value = jnp.zeros((rhs, LANES), F32)
            if before is not None:
                old, old_side = before
                value = jnp.where(lane == 2 * k - 1, old_side, value)
                value = jnp.where(lane < 2 * k - 1, old, value)
            tiles.append(value)
            before = (rolled, side)
        lhs = jnp.concatenate(tiles, axis=1).astype(BF16)[:, : 4 * (w0 + 2)]
        solved = solve(lhs, factor_ref[b, 0])
        for j in range(2):
            out_ref[2 * b + j] = solved[:, j * w0 : (j + 1) * w0]


def final_kernel(plan, group, fine_ref, one_ref, two_ref, three_ref, down_ref, up_ref, four_ref,
                 inverse_ref, shrink_ref, flat_ref, spread_ref, lift_ref, *refs):
    count = plan.n // 2
    gathered, out_ref, pair_ref, four_rows = refs[:count], refs[count], refs[-2], refs[-1]
    r, c = lax.axis_index("px"), lax.axis_index("py")
    rhs, n, ny3, ny4 = plan.rhs, plan.n, plan.ny[3], plan.ny[4]
    nx4, nx5 = plan.nx[4], plan.nx[5]
    above = jnp.where(r > 0, 1.0, 0.0).astype(F32)
    below = jnp.where(r < n - 1, 1.0, 0.0).astype(F32)
    for k, block in enumerate(gathered):
        for half in range(2):
            at = lax.rem(r + 2 * k + half, n)
            pair_ref[at] = block[half]
    lane = lax.broadcasted_iota(jnp.int32, (rhs, 2 * ny3), 1)
    ring = pair_ref[0]
    pair_ref[0] = jnp.where(lane < ny3, 0.0, ring)
    pair_ref[n] = jnp.where(lane < ny3, ring, 0.0)
    low = pair_ref[0:n].reshape(n * rhs, 2 * ny3)
    high = pair_ref[1 : n + 1].reshape(n * rhs, 2 * ny3)
    four = (product(low, shrink_ref[0]) + product(high, shrink_ref[1])) * SHRINK
    zero = jnp.zeros((rhs, four.shape[1]), F32)
    rows = [zero] + [four[i * rhs : (i + 1) * rhs] for i in range(nx4)] + [zero]
    five = shrink_rows(rows, nx4, 1)[1:-1]
    flat = product(jnp.concatenate(five, axis=1), flat_ref[...]) * SHRINK
    part_five = jnp.dot(flat.astype(BF16), inverse_ref[...], preferred_element_type=F32)
    lifted = product(part_five, spread_ref[...]) * SHRINK
    w, tiles = plan.tile[4], plan.tiles[4]
    parts = []
    for b in range(nx4 // 2):
        for t in range(tiles):
            pieces = []
            for k in range(4):
                lanes = range(t * w, t * w + w + 2, LANES)
                pieces.append([rows[2 * b + k][:, lo : lo + LANES] for lo in lanes])
            parts.append(solve(assemble(pieces, w), four_ref[b, t]))
    correction = jnp.concatenate(parts, axis=1) + lifted
    width = lift_ref.shape[3]
    bands = nx4 // 2 // group
    stacked = jnp.concatenate(
        [correction[:, i * width : (i + 1) * width] for i in range(bands)], axis=0
    )
    four_rows[0] = jnp.zeros((rhs, LANES), F32)
    four_rows[nx4 + 1] = jnp.zeros((rhs, LANES), F32)
    for g in range(group):
        for j in range(2):
            value = product(stacked, lift_ref[c, 2 * g + j])
            for i in range(bands):
                four_rows[1 + 2 * (i * group + g) + j] = value[i * rhs : (i + 1) * rhs]
    rows = [four_rows[r + k] for k in range(3)]
    for level, own_ref in ((3, three_ref), (2, two_ref), (1, one_ref)):
        height = plan.h[level]
        lifted = lift_rows(rows, -1, height + 1)
        rows = [(lifted[0] + down_ref[level - 1]) * above]
        rows += [lifted[i + 1] + own_ref[i] for i in range(height)]
        rows += [(lifted[-1] + up_ref[level - 1]) * below]
    lifted = lift_rows(rows, 0, plan.h0)
    for row in range(plan.h0):
        out_ref[pl.ds(row, rhs, stride=plan.h0), :] = lifted[row] + fine_ref[row]


def per_device(mesh_shape, residual, factor_fine, factor_one, factor_two, factor_three,
               factor_four, coarse_inverse):
    factors = [factor_fine, factor_one, factor_two, factor_three, factor_four]
    plan = Plan(mesh_shape, residual.shape, [f.shape for f in factors])
    n, m, rhs, h, h0 = plan.n, plan.m, plan.rhs, plan.h, plan.h0
    x = residual.reshape(rhs * h0, plan.w0)

    def shift(value, by):
        return lax.ppermute(value, "px", [(i, (i + by) % n) for i in range(n)])

    def swap(value, bits):
        return lax.ppermute(value, "py", [(i, i ^ bits) for i in range(m)])

    sides = jnp.asarray(plan.pick_sides())
    own, down, up = kernel_call(
        functools.partial(restrict_kernel, plan),
        (shape(plan.slots, rhs, LANES), shape(3, rhs, LANES), shape(3, rhs, LANES)),
    )(x, jnp.asarray(plan.shrink_columns()), sides, jnp.asarray(plan.scale()))
    from_above, from_below = shift(down, 1), shift(up, -1)
    band = kernel_call(functools.partial(merge_kernel, plan), shape(plan.slots, rhs, LANES))(
        own, from_above, from_below, sides
    )
    bands = {0: band}
    bit = m // 2
    while bit:
        bands.update({k ^ bit: swap(value, bit) for k, value in list(bands.items())})
        bit //= 2
    bands = [bands[k] for k in range(m)]

    width3 = 2 * plan.ny[3]
    place = np.stack([plan.place(3, 0, width3, j * plan.ny[3]) for j in range(2)], axis=1)
    pairs = kernel_call(functools.partial(gather_kernel, plan), shape(2, rhs, width3))(
        jnp.asarray(bf(place)), *bands
    )
    gathered = [pairs] + [shift(pairs, -2 * k) for k in range(1, n // 2)]

    places = [jnp.asarray(bf(plan.place(l, 1, round_up(plan.ny[l] + 2)))) for l in (1, 2, 3)]
    lifts = []
    for l in (1, 2, 3):
        if plan.tile[l] % LANES == 0:
            lifts.append(jnp.asarray(bf(plan.lift_columns(l))))
        else:
            rows = plan.lift_rows_of(l)
            lifts.append(jnp.asarray(bf(rows.reshape((m, -1) + rows.shape[3:]))))

    def coarse(*refs):
        coarse_kernel(plan, refs[0:3], refs[3:6], refs[6:9], *refs[9:])

    one, two, three, down, up = kernel_call(
        coarse,
        tuple(shape(h[l], rhs, LANES) for l in (1, 2, 3))
        + (shape(3, rhs, LANES), shape(3, rhs, LANES)),
    )(*places, *lifts, factor_one, factor_two, factor_three, *bands)
    down, up = shift(down, 1), shift(up, -1)

    fine = kernel_call(functools.partial(fine_kernel, plan), shape(h0, rhs, plan.w0))(
        x, from_above, from_below, jnp.asarray(plan.halo_lanes()), factor_fine, *bands
    )
    lift_four, group = plan.level_four_lift()
    lift_four = lift_four.reshape((m, -1) + lift_four.shape[3:])
    out = kernel_call(
        functools.partial(final_kernel, plan, group),
        shape(rhs * h0, plan.w0),
        scratch=(
            pltpu.VMEM((n + 1, rhs, width3), F32),
            pltpu.VMEM((plan.nx[4] + 2, rhs, LANES), F32),
        ),
    )(fine, one, two, three, down, up, factor_four, coarse_inverse,
      jnp.asarray(plan.coarse_shrink()), jnp.asarray(plan.coarsest_shrink()),
      jnp.asarray(plan.coarsest_lift()), jnp.asarray(lift_four), *gathered)
    return out.reshape(rhs, h0, plan.w0)


def solution(mesh):
    placed = (
        P(None, "px", "py"),
        P("px", "py", None, None),
        P("px", None, None, None),
        P("px", None, None, None),
        P("px", None, None, None),
        P(),
        P(),
    )
    return jax.shard_map(
        functools.partial(per_device, dict(mesh.shape)),
        mesh=mesh, in_specs=placed, out_specs=P(None, "px", "py"), check_vma=False,
    )
```

```python
import functools
import math

import jax
import jax.numpy as jnp
import numpy as np
from jax import lax
from jax.experimental import pallas as pl
from jax.experimental.pallas import tpu as pltpu
from jax.sharding import PartitionSpec as P

F32 = jnp.float32
BF16 = jnp.bfloat16
LANES = 128
SHRINK = 1.0 / 20.0
TAPS = (1, 3, 3, 1)
VMEM_BYTES = 24 * 1024 * 1024


def round_up(value, unit=LANES):
    return -(-value // unit) * unit


def global_prolong(coarse):
    out = np.zeros((coarse, 2 * coarse))
    for i in range(coarse):
        out[i, 2 * i] += 3
        out[i, 2 * i + 1] += 3
        if i > 0:
            out[i, 2 * i - 1] += 1
        if i + 1 < coarse:
            out[i, 2 * i + 2] += 1
    return out


def bf(array):
    return np.asarray(array, np.float32).astype(jnp.bfloat16)


class Plan:
    def __init__(self, mesh_shape, residual, factors):
        self.n, self.m = mesh_shape["px"], mesh_shape["py"]
        self.rhs, self.h0, self.w0 = residual
        self.h = [self.h0 >> l for l in range(5)]
        self.w = [self.w0 >> l for l in range(5)]
        self.ny = [self.w0 * self.m >> l for l in range(6)]
        self.nx = [self.h0 * self.n >> l for l in range(6)]
        self.tile = [f[3] // 2 for f in factors]
        self.tiles = [f[1] for f in factors]
        self.slots = self.h[1] + 2
        self.offset = [None, 0, self.w[1] + 2, self.w[1] + self.w[2] + 4]
        self.spare = self.w[1] + self.w[2] + self.w[3] + 6

    def place(self, level, lead, width, at=0):
        out = np.zeros((self.m, LANES, width))
        for c in range(self.m):
            for k in range(self.w[level] + 2):
                column = self.w[level] * c - 1 + k
                if -lead <= column < self.ny[level]:
                    out[c, self.offset[level] + k, at + column + lead] = 1
        return out

    def halo_lanes(self):
        out = np.zeros((2, LANES, 2 * LANES))
        for k in range(2):
            for position in range(4):
                out[0, self.spare + 2 * k + 1, LANES * k + 2 * position] = 1
                out[1, self.spare + 2 * k, LANES * k + 2 * position + 1] = 1
        return bf(out)

    def lift_columns(self, level):
        out = np.eye(self.ny[level])
        for l in range(level, 0, -1):
            out = out @ global_prolong(self.ny[l])
        return out.reshape(self.ny[level], self.m, self.w0).transpose(1, 0, 2)

    def lift_rows_of(self, level):
        w, tiles = self.tile[level], self.tiles[level]
        full = self.lift_columns(level).reshape(self.m, tiles, w, self.w0)
        out = np.zeros((self.m, 2, tiles, 2 * w, self.w0))
        for j in range(2):
            out[:, j, :, j * w : (j + 1) * w] = full
        return out

    def coarse_shrink(self):
        ny3, ny4 = self.ny[3], self.ny[4]
        columns = global_prolong(ny4).T
        width = round_up(ny4 + 2)
        out = np.zeros((2, 2, ny3, width))
        for side, taps in enumerate(((1, 3), (3, 1))):
            for j in range(2):
                out[side, j, :, 1 : 1 + ny4] = taps[j] * columns
        return bf(out.reshape(4 * ny3, width))

    def coarsest_shrink(self):
        nx5, ny5, ny4 = self.nx[5], self.ny[5], self.ny[4]
        columns = global_prolong(ny5).T
        width = round_up(ny4 + 2)
        out = np.zeros((nx5, width, nx5 * ny5))
        for i in range(nx5):
            out[i, 1 : 1 + ny4, i * ny5 : (i + 1) * ny5] = columns
        return bf(out.reshape(nx5 * width, nx5 * ny5))

    def coarsest_lift(self):
        rows, columns = global_prolong(self.nx[5]), global_prolong(self.ny[5])
        both = np.einsum("ia,jb->ijab", rows, columns)
        w, tiles = self.tile[4], self.tiles[4]
        both = both.reshape(self.nx[5] * self.ny[5], self.nx[4] // 2, 2, tiles, w)
        both = both.transpose(0, 1, 3, 2, 4)
        return bf(both.reshape(self.nx[5] * self.ny[5], self.nx[4] * self.ny[4]))

    def level_four_lift(self):
        pair = 2 * self.tile[4] * self.tiles[4]
        group = max(1, LANES // pair)
        width = group * pair
        rows = self.lift_rows_of(4).reshape(self.m, 2, pair, self.w0)
        out = np.zeros((self.m, group, 2, width, self.w0))
        for g in range(group):
            out[:, g, :, g * pair : (g + 1) * pair] = rows
        return bf(out), group


class Blocks:
    def __init__(self):
        self.parts, self.places, self.count = [], {}, 0

    def add(self, name, array):
        lead, (rows, columns) = array.shape[:-2], array.shape[-2:]
        high, wide = round_up(rows) // LANES, round_up(columns) // LANES
        out = np.zeros((math.prod(lead), high * LANES, wide * LANES), np.float32)
        out[:, :rows, :columns] = np.asarray(array, np.float32).reshape((-1, rows, columns))
        out = out.reshape(-1, high, LANES, wide, LANES).transpose(0, 1, 3, 2, 4)
        self.parts.append(out.reshape(-1, LANES, LANES))
        self.places[name] = (self.count, high, wide)
        self.count += len(self.parts[-1])

    def array(self):
        return jnp.asarray(bf(np.concatenate(self.parts, axis=0)))

    def get(self, ref, name, lead=0):
        base, high, wide = self.places[name]
        base = base + lead * (high * wide)
        rows = [
            jnp.concatenate([ref[base + i * wide + j] for j in range(wide)], axis=1)
            for i in range(high)
        ]
        return jnp.concatenate(rows, axis=0)


def split(value):
    high = value.astype(BF16)
    return high, (value - high.astype(F32)).astype(BF16)


def product(value, matrix):
    high, low = split(value)
    count = value.shape[0]
    both = jnp.dot(
        jnp.concatenate([high, low], axis=0), matrix, preferred_element_type=F32
    )
    return both[:count] + both[count:]


def shrink_rows(rows, count, halo):
    out = []
    for i in range(-1, count // 2 + 1):
        total = None
        for t, tap in enumerate(TAPS):
            j = 2 * i - 1 + t
            if -halo <= j < count + halo:
                term = rows[j + halo] * float(tap) if tap > 1 else rows[j + halo]
                total = term if total is None else total + term
        out.append(total)
    return out


def lift_rows(rows, first, last):
    out = []
    for f in range(first, last):
        i = f // 2
        other = i - 1 if f % 2 == 0 else i + 1
        out.append((rows[i + 1] * 3.0 + rows[other + 1]) * SHRINK)
    return out


def lane_index(rows):
    return lax.broadcasted_iota(jnp.int32, (rows, LANES), 1)


def assemble(pieces, width):
    total = 4 * (width + 2)
    tiles = [[] for _ in range(-(-total // LANES))]
    lane = lane_index(pieces[0][0].shape[0])
    for k, piece in enumerate(pieces):
        for q, value in enumerate(piece):
            start = k * (width + 2) + LANES * q
            count = min(LANES, width + 2 - LANES * q)
            shift, at = start % LANES, start // LANES
            rolled = pltpu.roll(value, shift, 1) if shift else value
            tiles[at].append((min(LANES, shift + count), rolled))
            if shift + count > LANES:
                tiles[at + 1].append((shift + count - LANES, rolled))
    out = []
    for segments in tiles:
        segments = sorted(segments, key=lambda s: -s[0])
        end, value = segments[0]
        if end < LANES:
            value = jnp.where(lane < end, value, 0.0)
        for end, part in segments[1:]:
            value = jnp.where(lane < end, part, value)
        out.append(value)
    return jnp.concatenate(out, axis=1).astype(BF16)[:, :total]


def solve(lhs, factor):
    return jnp.dot(lhs, factor, preferred_element_type=F32)


def kernel_call(body, out_shape, scratch=(), cost_us=1.0):
    whole = pl.BlockSpec(memory_space=pltpu.VMEM)

    def call(*operands):
        return pl.pallas_call(
            body,
            out_shape=out_shape,
            in_specs=[whole] * len(operands),
            out_specs=jax.tree.map(lambda _: whole, out_shape),
            scratch_shapes=list(scratch),
            compiler_params=pltpu.CompilerParams(vmem_limit_bytes=VMEM_BYTES),
            cost_estimate=pl.CostEstimate(
                flops=int(cost_us * 1e9), bytes_accessed=int(cost_us * 3e6), transcendentals=0
            ),
        )(*operands)

    return call


def shape(*dims):
    return jax.ShapeDtypeStruct(dims, F32)


def tap_matrix(row_lead, lane_lead, count, first, last):
    row = lax.broadcasted_iota(jnp.int32, (LANES, LANES), 0) - row_lead
    lane = lax.broadcasted_iota(jnp.int32, (LANES, LANES), 1) - lane_lead
    tap = row - 2 * lane + 3
    outer = jnp.logical_or(tap == 0, tap == 3)
    inner = jnp.logical_or(tap == 1, tap == 2)
    value = jnp.where(outer, 1.0, jnp.where(inner, 3.0, 0.0))
    value = jnp.where(jnp.logical_or(lane < first, lane > count + 1 - last), 0.0, value)
    return value.astype(BF16)


def side_matrix(plan, k):
    row = lax.broadcasted_iota(jnp.int32, (LANES, LANES), 0)
    lane = lax.broadcasted_iota(jnp.int32, (LANES, LANES), 1) - plan.spare - 2 * k
    left = jnp.logical_and(row == 0, lane == 0)
    right = jnp.logical_and(row == plan.w0 - 1, lane == 1)
    return jnp.where(jnp.logical_or(left, right), 1.0, 0.0).astype(BF16)


def restrict_kernel(plan, x_ref, own_ref, down_ref, up_ref, rows_ref):
    r, c = lax.axis_index("px"), lax.axis_index("py")
    rhs, slots, h = plan.rhs, plan.slots, plan.h
    first = jnp.where(c == 0, 1, 0)
    last = jnp.where(c == plan.m - 1, 1, 0)
    shrink = None
    matrices = []
    for level in (1, 2, 3):
        lead = 0 if level == 1 else plan.offset[level - 1] + 1
        step = tap_matrix(lead, plan.offset[level], plan.w[level], first, last)
        if shrink is None:
            shrink = step
        else:
            shrink = jnp.dot(shrink, step, preferred_element_type=F32).astype(BF16)
        matrices.append(shrink)
    above = jnp.where(r > 0, 1.0, 0.0).astype(F32)
    below = jnp.where(r < plan.n - 1, 1.0, 0.0).astype(F32)
    x = [x_ref[pl.ds(row, rhs, stride=h[0]), :] for row in range(h[0])]
    for i, row in enumerate(x):
        rows_ref[i] = row
    rows, total = x, None
    for level in (1, 2, 3):
        rows = shrink_rows(rows, h[level - 1], 0 if level == 1 else 1)
        rows[0] = rows[0] * above
        rows[-1] = rows[-1] * below
        part = product(jnp.concatenate(rows, axis=0), matrices[level - 1])
        if total is None:
            total = part
        else:
            count = part.shape[0]
            total = jnp.concatenate([total[:count] + part, total[count:]], axis=0)
    sides = [jnp.zeros_like(x[0])] + x[: slots - 1]
    total = total + jnp.dot(
        jnp.concatenate(sides, axis=0).astype(BF16), side_matrix(plan, 0),
        preferred_element_type=F32,
    )
    rest = jnp.concatenate(x[slots - 1 :], axis=0).astype(BF16)
    more = jnp.dot(rest, side_matrix(plan, 1), preferred_element_type=F32)
    count = more.shape[0]
    total = jnp.concatenate([total[:count] + more, total[count:]], axis=0)
    lane = lane_index(slots * rhs)
    one, two = plan.offset[2], plan.offset[3]
    scale = jnp.where(lane < two, SHRINK**2, jnp.where(lane < plan.spare, SHRINK**3, 1.0))
    total = total * jnp.where(lane < one, SHRINK, scale)
    own = total.reshape(slots, rhs, LANES)
    own_ref[...] = own
    lane = lane_index(rhs)
    down_ref[0] = x[-1]
    up_ref[0] = x[0]
    for k in range(2):
        three_own = own[h[3] + k]
        down_ref[1 + k] = jnp.where(
            lane < one, own[h[1] + k], jnp.where(lane < two, own[h[2] + k], three_own)
        )
        up_ref[1 + k] = own[k]


def merge_kernel(plan, own_ref, down_ref, up_ref, out_ref):
    r = lax.axis_index("px")
    rhs, h = plan.rhs, plan.h
    above = jnp.where(r > 0, 1.0, 0.0).astype(F32)
    below = jnp.where(r < plan.n - 1, 1.0, 0.0).astype(F32)
    lane = lane_index(rhs)
    one, two, end = plan.offset[2], plan.offset[3], plan.spare
    out_ref[...] = own_ref[...]
    wrapped = jnp.logical_and(lane >= two, lane < end)
    in_band = lane < end
    for k in range(2):
        piece = down_ref[1 + k]
        piece = jnp.where(wrapped, piece, jnp.where(in_band, piece * above, 0.0))
        out_ref[k] = out_ref[k] + piece
        piece = up_ref[1 + k]
        piece = jnp.where(wrapped, piece, jnp.where(in_band, piece * below, 0.0))
        for level, low, high in ((1, 0, one), (2, one, two), (3, two, end)):
            row = h[level] + k
            chosen = jnp.logical_and(lane >= low, lane < high)
            out_ref[row] = out_ref[row] + jnp.where(chosen, piece, 0.0)
    top = (down_ref[0] * above).astype(BF16)
    out_ref[0] = out_ref[0] + jnp.dot(top, side_matrix(plan, 0), preferred_element_type=F32)
    bottom = (up_ref[0] * below).astype(BF16)
    at = h[0] + 1 - plan.slots
    out_ref[at] = out_ref[at] + jnp.dot(bottom, side_matrix(plan, 1), preferred_element_type=F32)


def banded(bands, matrices):
    return product(jnp.concatenate(bands, axis=1), jnp.concatenate(matrices, axis=0))


def owners(plan):
    c = lax.axis_index("py")
    return [jnp.bitwise_xor(c, k) for k in range(plan.m)]


def gather_kernel(plan, blocks, block_ref, *refs):
    band_refs, out_ref = refs[:-1], refs[-1]
    rhs = plan.rhs
    values, matrices = [], []
    for band, owner in zip(band_refs, owners(plan)):
        for j in range(2):
            values.append(jnp.concatenate([band[j], band[2 + j]], axis=0))
            matrices.append(blocks.get(block_ref, "pairs", 2 * owner + j))
    total = banded(values, matrices)
    for half in range(2):
        out_ref[half] = total[half * rhs : (half + 1) * rhs]


def level_rows(plan, level, band_refs, blocks, block_ref):
    rhs, count = plan.rhs, plan.h[level] + 2
    values = [band[:count].reshape(count * rhs, LANES) for band in band_refs]
    matrices = [blocks.get(block_ref, f"place{level}", owner) for owner in owners(plan)]
    return banded(values, matrices)


def coarse_kernel(plan, blocks, block_ref, *refs):
    factors, bands, outs = refs[:3], refs[3 : 3 + plan.m], refs[3 + plan.m :]
    r, c = lax.axis_index("px"), lax.axis_index("py")
    rhs = plan.rhs
    above = jnp.where(r > 0, 1.0, 0.0).astype(F32)
    below = jnp.where(r < plan.n - 1, 1.0, 0.0).astype(F32)
    down_ref, up_ref = outs[3], outs[4]
    for level in (1, 2, 3):
        w, tiles = plan.tile[level], plan.tiles[level]
        whole = level_rows(plan, level, bands, blocks, block_ref)
        count = plan.h[level] + 2
        rows = [whole[i * rhs : (i + 1) * rhs] for i in range(count)]
        if level == 3:
            rows[0] = rows[0] * above
            rows[-1] = rows[-1] * below
        factor_ref, out_ref = factors[level - 1], outs[level - 1]
        solved = [[] for _ in range(tiles)]
        for b in range(plan.h[level] // 2):
            for t in range(tiles):
                pieces = []
                for k in range(4):
                    row = rows[2 * b + k]
                    lanes = range(t * w, t * w + w + 2, LANES)
                    pieces.append([row[:, lo : lo + LANES] for lo in lanes])
                solved[t].append(solve(assemble(pieces, w), factor_ref[b, t]))
        pairs = plan.h[level] // 2
        stacked = [jnp.concatenate(solved[t], axis=0) for t in range(tiles)]
        lifted = []
        name = f"lift{level}"
        for j in range(2):
            if w % LANES == 0:
                row = jnp.concatenate([v[:, j * w : (j + 1) * w] for v in stacked], axis=1)
                lifted.append(product(row, blocks.get(block_ref, name, c)))
            else:
                row = jnp.concatenate(stacked, axis=1)
                lifted.append(product(row, blocks.get(block_ref, name, 2 * c + j)))
        for b in range(pairs):
            for j in range(2):
                out_ref[2 * b + j] = lifted[j][b * rhs : (b + 1) * rhs]
        down_ref[level - 1] = lifted[1][(pairs - 1) * rhs :]
        up_ref[level - 1] = lifted[0][:rhs]


def fine_kernel(plan, blocks, block_ref, rows_ref, down_ref, up_ref, factor_ref, *refs):
    bands, out_ref = refs[: plan.m], refs[plan.m]
    r, c = lax.axis_index("px"), lax.axis_index("py")
    rhs, h0, w0, slots = plan.rhs, plan.h0, plan.w0, plan.slots
    above = jnp.where(r > 0, 1.0, 0.0).astype(F32)
    below = jnp.where(r < plan.n - 1, 1.0, 0.0).astype(F32)
    values, matrices = [], []
    left = blocks.get(block_ref, "halo", 0)
    right = blocks.get(block_ref, "halo", 1)
    for band, owner in zip(bands, owners(plan)):
        from_left = jnp.where(owner == c - 1, 1.0, 0.0).astype(BF16)
        from_right = jnp.where(owner == c + 1, 1.0, 0.0).astype(BF16)
        matrices.append(left * from_left + right * from_right)
        values.append(band[...].reshape(slots * rhs, LANES).astype(BF16))
    halo = jnp.dot(
        jnp.concatenate(values, axis=1), jnp.concatenate(matrices, axis=0),
        preferred_element_type=F32,
    )
    lane = lane_index(rhs)
    rows, sides = [], []
    for row in range(-1, h0 + 1):
        if row == -1:
            rows.append(down_ref[0] * above)
        elif row == h0:
            rows.append(up_ref[0] * below)
        else:
            rows.append(rows_ref[row])
        part, slot = divmod(row + 1, slots)
        sides.append(halo[slot * rhs : (slot + 1) * rhs, part * LANES : (part + 1) * LANES])
    for b in range(h0 // 2):
        tiles, before = [], None
        for k in range(5):
            if k < 4:
                row, side = rows[2 * b + k], sides[2 * b + k]
                rolled = pltpu.roll(row, 2 * k + 1, 1)
                value = jnp.where(lane == 2 * k, side, rolled)
            else:
                value = jnp.zeros((rhs, LANES), F32)
            if before is not None:
                old, old_side = before
                value = jnp.where(lane == 2 * k - 1, old_side, value)
                value = jnp.where(lane < 2 * k - 1, old, value)
            tiles.append(value)
            before = (rolled, side)
        lhs = jnp.concatenate(tiles, axis=1).astype(BF16)[:, : 4 * (w0 + 2)]
        solved = solve(lhs, factor_ref[b, 0])
        for j in range(2):
            out_ref[2 * b + j] = solved[:, j * w0 : (j + 1) * w0]


def whole_kernel(plan, group, blocks, block_ref, four_ref, inverse_ref, *refs):
    count = plan.n // 2
    gathered, out_ref, pair_ref, four_rows = refs[:count], refs[count], refs[-2], refs[-1]
    r, c = lax.axis_index("px"), lax.axis_index("py")
    rhs, n, ny3, ny4 = plan.rhs, plan.n, plan.ny[3], plan.ny[4]
    nx4, nx5 = plan.nx[4], plan.nx[5]
    for k, block in enumerate(gathered):
        for half in range(2):
            at = lax.rem(jnp.bitwise_xor(r, 2 * k) + half, n)
            pair_ref[at] = block[half]
    lane = lax.broadcasted_iota(jnp.int32, (rhs, 2 * ny3), 1)
    ring = pair_ref[0]
    pair_ref[0] = jnp.where(lane < ny3, 0.0, ring)
    pair_ref[n] = jnp.where(lane < ny3, ring, 0.0)
    low = pair_ref[0:n].reshape(n * rhs, 2 * ny3)
    high = pair_ref[1 : n + 1].reshape(n * rhs, 2 * ny3)
    both = jnp.concatenate([low, high], axis=1)
    four = product(both, blocks.get(block_ref, "shrink4")) * SHRINK
    zero = jnp.zeros((rhs, four.shape[1]), F32)
    rows = [zero] + [four[i * rhs : (i + 1) * rhs] for i in range(nx4)] + [zero]
    five = shrink_rows(rows, nx4, 1)[1:-1]
    flat = product(jnp.concatenate(five, axis=1), blocks.get(block_ref, "shrink5")) * SHRINK
    flat = flat[:, : inverse_ref.shape[0]]
    part_five = jnp.dot(flat.astype(BF16), inverse_ref[...], preferred_element_type=F32)
    spread = blocks.get(block_ref, "lift5")[: part_five.shape[1], : nx4 * ny4]
    lifted = product(part_five, spread) * SHRINK
    w, tiles = plan.tile[4], plan.tiles[4]
    parts = []
    for b in range(nx4 // 2):
        for t in range(tiles):
            pieces = []
            for k in range(4):
                lanes = range(t * w, t * w + w + 2, LANES)
                pieces.append([rows[2 * b + k][:, lo : lo + LANES] for lo in lanes])
            lhs = assemble(pieces, w)
            parts.append(
                lax.dot_general(
                    lhs, four_ref[b, t], (((1,), (1,)), ((), ())), preferred_element_type=F32
                )
            )
    correction = jnp.concatenate(parts, axis=1) + lifted
    width = group * 2 * w * tiles
    bands = nx4 // 2 // group
    stacked = jnp.concatenate(
        [correction[:, i * width : (i + 1) * width] for i in range(bands)], axis=0
    )
    four_rows[0] = jnp.zeros((rhs, LANES), F32)
    four_rows[nx4 + 1] = jnp.zeros((rhs, LANES), F32)
    for g in range(group):
        for j in range(2):
            value = product(stacked, blocks.get(block_ref, "lift4", (c * group + g) * 2 + j))
            for i in range(bands):
                four_rows[1 + 2 * (i * group + g) + j] = value[i * rhs : (i + 1) * rhs]
    for k in range(3):
        out_ref[k] = four_rows[r + k]


def final_kernel(plan, fine_ref, one_ref, two_ref, three_ref, four_ref, down_ref, up_ref, out_ref):
    r, rhs = lax.axis_index("px"), plan.rhs
    above = jnp.where(r > 0, 1.0, 0.0).astype(F32)
    below = jnp.where(r < plan.n - 1, 1.0, 0.0).astype(F32)
    rows = [four_ref[k] for k in range(3)]
    for level, own_ref in ((3, three_ref), (2, two_ref), (1, one_ref)):
        height = plan.h[level]
        lifted = lift_rows(rows, -1, height + 1)
        rows = [(lifted[0] + down_ref[level - 1]) * above]
        rows += [lifted[i + 1] + own_ref[i] for i in range(height)]
        rows += [(lifted[-1] + up_ref[level - 1]) * below]
    lifted = lift_rows(rows, 0, plan.h0)
    for row in range(plan.h0):
        out_ref[pl.ds(row, rhs, stride=plan.h0), :] = lifted[row] + fine_ref[row]


def per_device(mesh_shape, residual, factor_fine, factor_one, factor_two, factor_three,
               factor_four, coarse_inverse):
    factors = [factor_fine, factor_one, factor_two, factor_three, factor_four]
    plan = Plan(mesh_shape, residual.shape, [f.shape for f in factors])
    n, m, rhs, h, h0 = plan.n, plan.m, plan.rhs, plan.h, plan.h0
    x = residual.reshape(rhs * h0, plan.w0)

    def shift(value, by):
        return lax.ppermute(value, "px", [(i, (i + by) % n) for i in range(n)])

    def swap(value, bits):
        return lax.ppermute(value, "py", [(i, i ^ bits) for i in range(m)])

    width3 = 2 * plan.ny[3]
    blocks = Blocks()
    pairs = [plan.place(3, 0, width3, j * plan.ny[3]) for j in range(2)]
    blocks.add("pairs", np.stack(pairs, axis=1))
    for l in (1, 2, 3):
        blocks.add(f"place{l}", plan.place(l, 1, round_up(plan.ny[l] + 2)))
        if plan.tile[l] % LANES == 0:
            blocks.add(f"lift{l}", plan.lift_columns(l))
        else:
            lifted = plan.lift_rows_of(l)
            blocks.add(f"lift{l}", lifted.reshape(m, 2, -1, plan.w0))
    lifted, group = plan.level_four_lift()
    blocks.add("lift4", lifted)
    blocks.add("halo", plan.halo_lanes())
    blocks.add("shrink4", plan.coarse_shrink())
    blocks.add("shrink5", plan.coarsest_shrink())
    blocks.add("lift5", plan.coarsest_lift())
    matrices = blocks.array()

    own, down, up, rows = kernel_call(
        functools.partial(restrict_kernel, plan),
        (shape(plan.slots, rhs, LANES), shape(3, rhs, LANES), shape(3, rhs, LANES),
         shape(h0, rhs, plan.w0)),
    )(x)
    from_above, from_below = shift(down, 1), shift(up, -1)
    band = kernel_call(functools.partial(merge_kernel, plan), shape(plan.slots, rhs, LANES))(
        own, from_above, from_below
    )
    bands = {0: band}
    bit = m // 2
    while bit:
        bands.update({k ^ bit: swap(value, bit) for k, value in list(bands.items())})
        bit //= 2
    bands = [bands[k] for k in range(m)]

    pairs = kernel_call(
        functools.partial(gather_kernel, plan, blocks), shape(2, rhs, width3), cost_us=0.3
    )(matrices, *bands)
    gathered = {0: pairs}
    bit = 1
    while 2 * bit < n:
        for k, value in list(gathered.items()):
            gathered[k ^ bit] = lax.ppermute(value, "px", [(i, i ^ (2 * bit)) for i in range(n)])
        bit *= 2
    gathered = [gathered[k] for k in range(n // 2)]
    bands, pairs = lax.optimization_barrier((bands, pairs))

    one, two, three, down, up = kernel_call(
        functools.partial(coarse_kernel, plan, blocks),
        tuple(shape(h[l], rhs, LANES) for l in (1, 2, 3))
        + (shape(3, rhs, LANES), shape(3, rhs, LANES)),
        cost_us=2.5,
    )(matrices, factor_one, factor_two, factor_three, *bands)
    down, up = shift(down, 1), shift(up, -1)

    fine = kernel_call(
        functools.partial(fine_kernel, plan, blocks), shape(h0, rhs, plan.w0)
    )(matrices, rows, from_above, from_below, factor_fine, *bands)
    four = kernel_call(
        functools.partial(whole_kernel, plan, group, blocks),
        shape(3, rhs, LANES),
        scratch=(
            pltpu.VMEM((n + 1, rhs, width3), F32),
            pltpu.VMEM((plan.nx[4] + 2, rhs, LANES), F32),
        ),
    )(matrices, jnp.swapaxes(factor_four, 2, 3), coarse_inverse, *gathered)
    out = kernel_call(functools.partial(final_kernel, plan), shape(rhs * h0, plan.w0))(
        fine, one, two, three, four, down, up
    )
    return out.reshape(rhs, h0, plan.w0)


def solution(mesh):
    placed = (
        P(None, "px", "py"),
        P("px", "py", None, None),
        P("px", None, None, None),
        P("px", None, None, None),
        P("px", None, None, None),
        P(),
        P(),
    )
    return jax.shard_map(
        functools.partial(per_device, dict(mesh.shape)),
        mesh=mesh, in_specs=placed, out_specs=P(None, "px", "py"), check_vma=False,
    )
```

```python
import functools
import math

import jax
import jax.numpy as jnp
import numpy as np
from jax import lax
from jax.experimental import pallas as pl
from jax.experimental.pallas import tpu as pltpu
from jax.sharding import PartitionSpec as P

F32 = jnp.float32
BF16 = jnp.bfloat16
LANES = 128
SHRINK = 1.0 / 20.0
TAPS = (1, 3, 3, 1)
VMEM_BYTES = 24 * 1024 * 1024


def round_up(value, unit=LANES):
    return -(-value // unit) * unit


def global_prolong(coarse):
    out = np.zeros((coarse, 2 * coarse))
    for i in range(coarse):
        out[i, 2 * i] += 3
        out[i, 2 * i + 1] += 3
        if i > 0:
            out[i, 2 * i - 1] += 1
        if i + 1 < coarse:
            out[i, 2 * i + 2] += 1
    return out


def bf(array):
    return np.asarray(array, np.float32).astype(jnp.bfloat16)


class Plan:
    def __init__(self, mesh_shape, residual, factors):
        self.n, self.m = mesh_shape["px"], mesh_shape["py"]
        self.rhs, self.h0, self.w0 = residual
        self.h = [self.h0 >> l for l in range(5)]
        self.w = [self.w0 >> l for l in range(5)]
        self.ny = [self.w0 * self.m >> l for l in range(6)]
        self.nx = [self.h0 * self.n >> l for l in range(6)]
        self.tile = [f[3] // 2 for f in factors]
        self.tiles = [f[1] for f in factors]
        self.slots = self.h[1] + 2
        self.offset = [None, 0, self.w[1] + 2, self.w[1] + self.w[2] + 4]
        self.spare = self.w[1] + self.w[2] + self.w[3] + 6

    def place(self, level, lead, width, at=0):
        out = np.zeros((self.m, LANES, width))
        for c in range(self.m):
            for k in range(self.w[level] + 2):
                column = self.w[level] * c - 1 + k
                if -lead <= column < self.ny[level]:
                    out[c, self.offset[level] + k, at + column + lead] = 1
        return out

    def halo_lanes(self):
        out = np.zeros((2, LANES, 2 * LANES))
        for k in range(2):
            for position in range(4):
                out[0, self.spare + 2 * k + 1, LANES * k + 2 * position] = 1
                out[1, self.spare + 2 * k, LANES * k + 2 * position + 1] = 1
        return bf(out)

    def lift_columns(self, level):
        out = np.eye(self.ny[level])
        for l in range(level, 0, -1):
            out = out @ global_prolong(self.ny[l])
        return out.reshape(self.ny[level], self.m, self.w0).transpose(1, 0, 2)

    def lift_rows_of(self, level):
        w, tiles = self.tile[level], self.tiles[level]
        full = self.lift_columns(level).reshape(self.m, tiles, w, self.w0)
        out = np.zeros((self.m, 2, tiles, 2 * w, self.w0))
        for j in range(2):
            out[:, j, :, j * w : (j + 1) * w] = full
        return out

    def coarse_shrink(self):
        ny3, ny4 = self.ny[3], self.ny[4]
        columns = global_prolong(ny4).T
        width = round_up(ny4 + 2)
        out = np.zeros((2, 2, ny3, width))
        for side, taps in enumerate(((1, 3), (3, 1))):
            for j in range(2):
                out[side, j, :, 1 : 1 + ny4] = taps[j] * columns
        return bf(out.reshape(4 * ny3, width))

    def coarsest_shrink(self):
        nx5, ny5, ny4 = self.nx[5], self.ny[5], self.ny[4]
        columns = global_prolong(ny5).T
        width = round_up(ny4 + 2)
        out = np.zeros((nx5, width, nx5 * ny5))
        for i in range(nx5):
            out[i, 1 : 1 + ny4, i * ny5 : (i + 1) * ny5] = columns
        return bf(out.reshape(nx5 * width, nx5 * ny5))

    def coarsest_lift(self):
        rows, columns = global_prolong(self.nx[5]), global_prolong(self.ny[5])
        both = np.einsum("ia,jb->ijab", rows, columns)
        w, tiles = self.tile[4], self.tiles[4]
        both = both.reshape(self.nx[5] * self.ny[5], self.nx[4] // 2, 2, tiles, w)
        both = both.transpose(0, 1, 3, 2, 4)
        return bf(both.reshape(self.nx[5] * self.ny[5], self.nx[4] * self.ny[4]))

    def level_four_lift(self):
        pair = 2 * self.tile[4] * self.tiles[4]
        group = max(1, LANES // pair)
        width = group * pair
        rows = self.lift_rows_of(4).reshape(self.m, 2, pair, self.w0)
        out = np.zeros((self.m, group, 2, width, self.w0))
        for g in range(group):
            out[:, g, :, g * pair : (g + 1) * pair] = rows
        return bf(out), group


class Blocks:
    def __init__(self):
        self.parts, self.places, self.count = [], {}, 0

    def add(self, name, array):
        lead, (rows, columns) = array.shape[:-2], array.shape[-2:]
        high, wide = round_up(rows) // LANES, round_up(columns) // LANES
        out = np.zeros((math.prod(lead), high * LANES, wide * LANES), np.float32)
        out[:, :rows, :columns] = np.asarray(array, np.float32).reshape((-1, rows, columns))
        out = out.reshape(-1, high, LANES, wide, LANES).transpose(0, 1, 3, 2, 4)
        self.parts.append(out.reshape(-1, LANES, LANES))
        self.places[name] = (self.count, high, wide)
        self.count += len(self.parts[-1])

    def array(self):
        return jnp.asarray(bf(np.concatenate(self.parts, axis=0)))

    def get(self, ref, name, lead=0):
        base, high, wide = self.places[name]
        base = base + lead * (high * wide)
        rows = [
            jnp.concatenate([ref[base + i * wide + j] for j in range(wide)], axis=1)
            for i in range(high)
        ]
        return jnp.concatenate(rows, axis=0)


def split(value):
    high = value.astype(BF16)
    return high, (value - high.astype(F32)).astype(BF16)


def product(value, matrix):
    high, low = split(value)
    count = value.shape[0]
    both = jnp.dot(
        jnp.concatenate([high, low], axis=0), matrix, preferred_element_type=F32
    )
    return both[:count] + both[count:]


def shrink_rows(rows, count, halo):
    out = []
    for i in range(-1, count // 2 + 1):
        total = None
        for t, tap in enumerate(TAPS):
            j = 2 * i - 1 + t
            if -halo <= j < count + halo:
                term = rows[j + halo] * float(tap) if tap > 1 else rows[j + halo]
                total = term if total is None else total + term
        out.append(total)
    return out


def lift_rows(rows, first, last):
    out = []
    for f in range(first, last):
        i = f // 2
        other = i - 1 if f % 2 == 0 else i + 1
        out.append((rows[i + 1] * 3.0 + rows[other + 1]) * SHRINK)
    return out


def lane_index(rows):
    return lax.broadcasted_iota(jnp.int32, (rows, LANES), 1)


def assemble(pieces, width):
    total = 4 * (width + 2)
    tiles = [[] for _ in range(-(-total // LANES))]
    lane = lane_index(pieces[0][0].shape[0])
    for k, piece in enumerate(pieces):
        for q, value in enumerate(piece):
            start = k * (width + 2) + LANES * q
            count = min(LANES, width + 2 - LANES * q)
            shift, at = start % LANES, start // LANES
            rolled = pltpu.roll(value, shift, 1) if shift else value
            tiles[at].append((min(LANES, shift + count), rolled))
            if shift + count > LANES:
                tiles[at + 1].append((shift + count - LANES, rolled))
    out = []
    for segments in tiles:
        segments = sorted(segments, key=lambda s: -s[0])
        end, value = segments[0]
        if end < LANES:
            value = jnp.where(lane < end, value, 0.0)
        for end, part in segments[1:]:
            value = jnp.where(lane < end, part, value)
        out.append(value)
    return jnp.concatenate(out, axis=1).astype(BF16)[:, :total]


def solve(lhs, factor):
    return jnp.dot(lhs, factor, preferred_element_type=F32)


def kernel_call(body, out_shape, scratch=(), cost_us=1.0):
    whole = pl.BlockSpec(memory_space=pltpu.VMEM)

    def call(*operands):
        return pl.pallas_call(
            body,
            out_shape=out_shape,
            in_specs=[whole] * len(operands),
            out_specs=jax.tree.map(lambda _: whole, out_shape),
            scratch_shapes=list(scratch),
            compiler_params=pltpu.CompilerParams(vmem_limit_bytes=VMEM_BYTES),
            cost_estimate=pl.CostEstimate(
                flops=int(cost_us * 1e9), bytes_accessed=int(cost_us * 3e6), transcendentals=0
            ),
        )(*operands)

    return call


def shape(*dims):
    return jax.ShapeDtypeStruct(dims, F32)


def tap_matrix(row_lead, lane_lead, count, first, last):
    row = lax.broadcasted_iota(jnp.int32, (LANES, LANES), 0) - row_lead
    lane = lax.broadcasted_iota(jnp.int32, (LANES, LANES), 1) - lane_lead
    tap = row - 2 * lane + 3
    outer = jnp.logical_or(tap == 0, tap == 3)
    inner = jnp.logical_or(tap == 1, tap == 2)
    value = jnp.where(outer, 1.0, jnp.where(inner, 3.0, 0.0))
    value = jnp.where(jnp.logical_or(lane < first, lane > count + 1 - last), 0.0, value)
    return value.astype(BF16)


def side_matrix(plan, k):
    row = lax.broadcasted_iota(jnp.int32, (LANES, LANES), 0)
    lane = lax.broadcasted_iota(jnp.int32, (LANES, LANES), 1) - plan.spare - 2 * k
    left = jnp.logical_and(row == 0, lane == 0)
    right = jnp.logical_and(row == plan.w0 - 1, lane == 1)
    return jnp.where(jnp.logical_or(left, right), 1.0, 0.0).astype(BF16)


def restrict_kernel(plan, x_ref, own_ref, down_ref, up_ref, rows_ref):
    r, c = lax.axis_index("px"), lax.axis_index("py")
    rhs, slots, h = plan.rhs, plan.slots, plan.h
    first = jnp.where(c == 0, 1, 0)
    last = jnp.where(c == plan.m - 1, 1, 0)
    shrink = None
    matrices = []
    for level in (1, 2, 3):
        lead = 0 if level == 1 else plan.offset[level - 1] + 1
        step = tap_matrix(lead, plan.offset[level], plan.w[level], first, last)
        if shrink is None:
            shrink = step
        else:
            shrink = jnp.dot(shrink, step, preferred_element_type=F32).astype(BF16)
        matrices.append(shrink)
    above = jnp.where(r > 0, 1.0, 0.0).astype(F32)
    below = jnp.where(r < plan.n - 1, 1.0, 0.0).astype(F32)
    x = [x_ref[pl.ds(row, rhs, stride=h[0]), :] for row in range(h[0])]
    for i, row in enumerate(x):
        rows_ref[i] = row
    rows, total = x, None
    for level in (1, 2, 3):
        rows = shrink_rows(rows, h[level - 1], 0 if level == 1 else 1)
        rows[0] = rows[0] * above
        rows[-1] = rows[-1] * below
        part = product(jnp.concatenate(rows, axis=0), matrices[level - 1])
        if total is None:
            total = part
        else:
            count = part.shape[0]
            total = jnp.concatenate([total[:count] + part, total[count:]], axis=0)
    sides = [jnp.zeros_like(x[0])] + x[: slots - 1]
    total = total + jnp.dot(
        jnp.concatenate(sides, axis=0).astype(BF16), side_matrix(plan, 0),
        preferred_element_type=F32,
    )
    rest = jnp.concatenate(x[slots - 1 :], axis=0).astype(BF16)
    more = jnp.dot(rest, side_matrix(plan, 1), preferred_element_type=F32)
    count = more.shape[0]
    total = jnp.concatenate([total[:count] + more, total[count:]], axis=0)
    lane = lane_index(slots * rhs)
    one, two = plan.offset[2], plan.offset[3]
    scale = jnp.where(lane < two, SHRINK**2, jnp.where(lane < plan.spare, SHRINK**3, 1.0))
    total = total * jnp.where(lane < one, SHRINK, scale)
    own = total.reshape(slots, rhs, LANES)
    own_ref[...] = own
    lane = lane_index(rhs)
    down_ref[0] = x[-1]
    up_ref[0] = x[0]
    for k in range(2):
        three_own = own[h[3] + k]
        down_ref[1 + k] = jnp.where(
            lane < one, own[h[1] + k], jnp.where(lane < two, own[h[2] + k], three_own)
        )
        up_ref[1 + k] = own[k]


def merge_kernel(plan, own_ref, down_ref, up_ref, out_ref):
    r = lax.axis_index("px")
    rhs, h = plan.rhs, plan.h
    above = jnp.where(r > 0, 1.0, 0.0).astype(F32)
    below = jnp.where(r < plan.n - 1, 1.0, 0.0).astype(F32)
    lane = lane_index(rhs)
    one, two, end = plan.offset[2], plan.offset[3], plan.spare
    out_ref[...] = own_ref[...]
    wrapped = jnp.logical_and(lane >= two, lane < end)
    in_band = lane < end
    for k in range(2):
        piece = down_ref[1 + k]
        piece = jnp.where(wrapped, piece, jnp.where(in_band, piece * above, 0.0))
        out_ref[k] = out_ref[k] + piece
        piece = up_ref[1 + k]
        piece = jnp.where(wrapped, piece, jnp.where(in_band, piece * below, 0.0))
        for level, low, high in ((1, 0, one), (2, one, two), (3, two, end)):
            row = h[level] + k
            chosen = jnp.logical_and(lane >= low, lane < high)
            out_ref[row] = out_ref[row] + jnp.where(chosen, piece, 0.0)
    top = (down_ref[0] * above).astype(BF16)
    out_ref[0] = out_ref[0] + jnp.dot(top, side_matrix(plan, 0), preferred_element_type=F32)
    bottom = (up_ref[0] * below).astype(BF16)
    at = h[0] + 1 - plan.slots
    out_ref[at] = out_ref[at] + jnp.dot(bottom, side_matrix(plan, 1), preferred_element_type=F32)


def banded(bands, matrices):
    return product(jnp.concatenate(bands, axis=1), jnp.concatenate(matrices, axis=0))


def owners(plan):
    c = lax.axis_index("py")
    return [jnp.bitwise_xor(c, k) for k in range(plan.m)]


def gather_kernel(plan, blocks, block_ref, *refs):
    band_refs, out_ref = refs[:-1], refs[-1]
    rhs = plan.rhs
    values, matrices = [], []
    for band, owner in zip(band_refs, owners(plan)):
        for j in range(2):
            values.append(jnp.concatenate([band[j], band[2 + j]], axis=0))
            matrices.append(blocks.get(block_ref, "pairs", 2 * owner + j))
    total = banded(values, matrices)
    for half in range(2):
        out_ref[half] = total[half * rhs : (half + 1) * rhs]


def level_rows(plan, level, band_refs, blocks, block_ref):
    rhs, count = plan.rhs, plan.h[level] + 2
    values = [band[:count].reshape(count * rhs, LANES) for band in band_refs]
    matrices = [blocks.get(block_ref, f"place{level}", owner) for owner in owners(plan)]
    return banded(values, matrices)


def coarse_kernel(plan, blocks, block_ref, *refs):
    factors, bands, outs = refs[:3], refs[3 : 3 + plan.m], refs[3 + plan.m :]
    r, c = lax.axis_index("px"), lax.axis_index("py")
    rhs = plan.rhs
    above = jnp.where(r > 0, 1.0, 0.0).astype(F32)
    below = jnp.where(r < plan.n - 1, 1.0, 0.0).astype(F32)
    down_ref, up_ref = outs[3], outs[4]
    for level in (1, 2, 3):
        w, tiles = plan.tile[level], plan.tiles[level]
        whole = level_rows(plan, level, bands, blocks, block_ref)
        count = plan.h[level] + 2
        rows = [whole[i * rhs : (i + 1) * rhs] for i in range(count)]
        if level == 3:
            rows[0] = rows[0] * above
            rows[-1] = rows[-1] * below
        factor_ref, out_ref = factors[level - 1], outs[level - 1]
        solved = [[] for _ in range(tiles)]
        for b in range(plan.h[level] // 2):
            for t in range(tiles):
                pieces = []
                for k in range(4):
                    row = rows[2 * b + k]
                    lanes = range(t * w, t * w + w + 2, LANES)
                    pieces.append([row[:, lo : lo + LANES] for lo in lanes])
                solved[t].append(solve(assemble(pieces, w), factor_ref[b, t]))
        pairs = plan.h[level] // 2
        stacked = [jnp.concatenate(solved[t], axis=0) for t in range(tiles)]
        lifted = []
        name = f"lift{level}"
        for j in range(2):
            if w % LANES == 0:
                row = jnp.concatenate([v[:, j * w : (j + 1) * w] for v in stacked], axis=1)
                lifted.append(product(row, blocks.get(block_ref, name, c)))
            else:
                row = jnp.concatenate(stacked, axis=1)
                lifted.append(product(row, blocks.get(block_ref, name, 2 * c + j)))
        for b in range(pairs):
            for j in range(2):
                out_ref[2 * b + j] = lifted[j][b * rhs : (b + 1) * rhs]
        down_ref[level - 1] = lifted[1][(pairs - 1) * rhs :]
        up_ref[level - 1] = lifted[0][:rhs]


def fine_kernel(plan, blocks, block_ref, rows_ref, down_ref, up_ref, factor_ref, *refs):
    bands, out_ref = refs[: plan.m], refs[plan.m]
    r, c = lax.axis_index("px"), lax.axis_index("py")
    rhs, h0, w0, slots = plan.rhs, plan.h0, plan.w0, plan.slots
    above = jnp.where(r > 0, 1.0, 0.0).astype(F32)
    below = jnp.where(r < plan.n - 1, 1.0, 0.0).astype(F32)
    values, matrices = [], []
    left = blocks.get(block_ref, "halo", 0)
    right = blocks.get(block_ref, "halo", 1)
    for band, owner in zip(bands, owners(plan)):
        from_left = jnp.where(owner == c - 1, 1.0, 0.0).astype(BF16)
        from_right = jnp.where(owner == c + 1, 1.0, 0.0).astype(BF16)
        matrices.append(left * from_left + right * from_right)
        values.append(band[...].reshape(slots * rhs, LANES).astype(BF16))
    halo = jnp.dot(
        jnp.concatenate(values, axis=1), jnp.concatenate(matrices, axis=0),
        preferred_element_type=F32,
    )
    lane = lane_index(rhs)
    rows, sides = [], []
    for row in range(-1, h0 + 1):
        if row == -1:
            rows.append(down_ref[0] * above)
        elif row == h0:
            rows.append(up_ref[0] * below)
        else:
            rows.append(rows_ref[row])
        part, slot = divmod(row + 1, slots)
        sides.append(halo[slot * rhs : (slot + 1) * rhs, part * LANES : (part + 1) * LANES])
    for b in range(h0 // 2):
        tiles, before = [], None
        for k in range(5):
            if k < 4:
                row, side = rows[2 * b + k], sides[2 * b + k]
                rolled = pltpu.roll(row, 2 * k + 1, 1)
                value = jnp.where(lane == 2 * k, side, rolled)
            else:
                value = jnp.zeros((rhs, LANES), F32)
            if before is not None:
                old, old_side = before
                value = jnp.where(lane == 2 * k - 1, old_side, value)
                value = jnp.where(lane < 2 * k - 1, old, value)
            tiles.append(value)
            before = (rolled, side)
        lhs = jnp.concatenate(tiles, axis=1).astype(BF16)[:, : 4 * (w0 + 2)]
        solved = solve(lhs, factor_ref[b, 0])
        for j in range(2):
            out_ref[2 * b + j] = solved[:, j * w0 : (j + 1) * w0]


def whole_kernel(plan, group, blocks, block_ref, four_ref, inverse_ref, *refs):
    count = plan.n // 2
    gathered, out_ref, pair_ref, four_rows = refs[:count], refs[count], refs[-2], refs[-1]
    r, c = lax.axis_index("px"), lax.axis_index("py")
    rhs, n, ny3, ny4 = plan.rhs, plan.n, plan.ny[3], plan.ny[4]
    nx4, nx5 = plan.nx[4], plan.nx[5]
    odd = jnp.bitwise_and(c, 1)
    for k, block in enumerate(gathered):
        if k == 0 or (k == count - 1 and k % 2):
            partner = 2 * k
        elif k % 2:
            partner = 2 * (k + odd)
        else:
            partner = 2 * (k - odd)
        for half in range(2):
            at = lax.rem(jnp.bitwise_xor(r, partner) + half, n)
            pair_ref[at] = block[half]
    lane = lax.broadcasted_iota(jnp.int32, (rhs, 2 * ny3), 1)
    ring = pair_ref[0]
    pair_ref[0] = jnp.where(lane < ny3, 0.0, ring)
    pair_ref[n] = jnp.where(lane < ny3, ring, 0.0)
    low = pair_ref[0:n].reshape(n * rhs, 2 * ny3)
    high = pair_ref[1 : n + 1].reshape(n * rhs, 2 * ny3)
    both = jnp.concatenate([low, high], axis=1)
    four = product(both, blocks.get(block_ref, "shrink4")) * SHRINK
    zero = jnp.zeros((rhs, four.shape[1]), F32)
    rows = [zero] + [four[i * rhs : (i + 1) * rhs] for i in range(nx4)] + [zero]
    five = shrink_rows(rows, nx4, 1)[1:-1]
    flat = product(jnp.concatenate(five, axis=1), blocks.get(block_ref, "shrink5")) * SHRINK
    flat = flat[:, : inverse_ref.shape[0]]
    part_five = jnp.dot(flat.astype(BF16), inverse_ref[...], preferred_element_type=F32)
    spread = blocks.get(block_ref, "lift5")[: part_five.shape[1], : nx4 * ny4]
    lifted = product(part_five, spread) * SHRINK
    w, tiles = plan.tile[4], plan.tiles[4]
    parts = []
    for b in range(nx4 // 2):
        for t in range(tiles):
            pieces = []
            for k in range(4):
                lanes = range(t * w, t * w + w + 2, LANES)
                pieces.append([rows[2 * b + k][:, lo : lo + LANES] for lo in lanes])
            lhs = assemble(pieces, w)
            parts.append(
                lax.dot_general(
                    lhs, four_ref[b, t], (((1,), (1,)), ((), ())), preferred_element_type=F32
                )
            )
    correction = jnp.concatenate(parts, axis=1) + lifted
    width = group * 2 * w * tiles
    bands = nx4 // 2 // group
    stacked = jnp.concatenate(
        [correction[:, i * width : (i + 1) * width] for i in range(bands)], axis=0
    )
    four_rows[0] = jnp.zeros((rhs, LANES), F32)
    four_rows[nx4 + 1] = jnp.zeros((rhs, LANES), F32)
    for g in range(group):
        for j in range(2):
            value = product(stacked, blocks.get(block_ref, "lift4", (c * group + g) * 2 + j))
            for i in range(bands):
                four_rows[1 + 2 * (i * group + g) + j] = value[i * rhs : (i + 1) * rhs]
    for k in range(3):
        out_ref[k] = four_rows[r + k]


def final_kernel(plan, fine_ref, one_ref, two_ref, three_ref, four_ref, down_ref, up_ref, out_ref):
    r, rhs = lax.axis_index("px"), plan.rhs
    above = jnp.where(r > 0, 1.0, 0.0).astype(F32)
    below = jnp.where(r < plan.n - 1, 1.0, 0.0).astype(F32)
    rows = [four_ref[k] for k in range(3)]
    for level, own_ref in ((3, three_ref), (2, two_ref), (1, one_ref)):
        height = plan.h[level]
        lifted = lift_rows(rows, -1, height + 1)
        rows = [(lifted[0] + down_ref[level - 1]) * above]
        rows += [lifted[i + 1] + own_ref[i] for i in range(height)]
        rows += [(lifted[-1] + up_ref[level - 1]) * below]
    lifted = lift_rows(rows, 0, plan.h0)
    for row in range(plan.h0):
        out_ref[pl.ds(row, rhs, stride=plan.h0), :] = lifted[row] + fine_ref[row]


def per_device(mesh_shape, residual, factor_fine, factor_one, factor_two, factor_three,
               factor_four, coarse_inverse):
    factors = [factor_fine, factor_one, factor_two, factor_three, factor_four]
    plan = Plan(mesh_shape, residual.shape, [f.shape for f in factors])
    n, m, rhs, h, h0 = plan.n, plan.m, plan.rhs, plan.h, plan.h0
    x = residual.reshape(rhs * h0, plan.w0)

    def shift(value, by):
        return lax.ppermute(value, "px", [(i, (i + by) % n) for i in range(n)])

    def swap(value, bits):
        return lax.ppermute(value, "py", [(i, i ^ bits) for i in range(m)])

    width3 = 2 * plan.ny[3]
    blocks = Blocks()
    pairs = [plan.place(3, 0, width3, j * plan.ny[3]) for j in range(2)]
    blocks.add("pairs", np.stack(pairs, axis=1))
    for l in (1, 2, 3):
        blocks.add(f"place{l}", plan.place(l, 1, round_up(plan.ny[l] + 2)))
        if plan.tile[l] % LANES == 0:
            blocks.add(f"lift{l}", plan.lift_columns(l))
        else:
            lifted = plan.lift_rows_of(l)
            blocks.add(f"lift{l}", lifted.reshape(m, 2, -1, plan.w0))
    lifted, group = plan.level_four_lift()
    blocks.add("lift4", lifted)
    blocks.add("halo", plan.halo_lanes())
    blocks.add("shrink4", plan.coarse_shrink())
    blocks.add("shrink5", plan.coarsest_shrink())
    blocks.add("lift5", plan.coarsest_lift())
    matrices = blocks.array()

    own, down, up, rows = kernel_call(
        functools.partial(restrict_kernel, plan),
        (shape(plan.slots, rhs, LANES), shape(3, rhs, LANES), shape(3, rhs, LANES),
         shape(h0, rhs, plan.w0)),
    )(x)
    from_above, from_below = shift(down, 1), shift(up, -1)
    band = kernel_call(functools.partial(merge_kernel, plan), shape(plan.slots, rhs, LANES))(
        own, from_above, from_below
    )
    bands = {0: band}
    bit = m // 2
    while bit:
        bands.update({k ^ bit: swap(value, bit) for k, value in list(bands.items())})
        bit //= 2
    bands = [bands[k] for k in range(m)]

    pairs = kernel_call(
        functools.partial(gather_kernel, plan, blocks), shape(2, rhs, width3), cost_us=0.3
    )(matrices, *bands)
    order, gathered = list(range(1, n // 2)), [pairs]
    fetched = []
    for k in range(0, len(order), 2):
        even, odd = order[k], order[min(k + 1, len(order) - 1)]
        fetched.append(
            lax.ppermute(
                pairs, ("px", "py"),
                [(i * m + c, (i ^ (2 * (odd if c % 2 else even))) * m + c)
                 for i in range(n) for c in range(m)],
            )
        )
    bands, pairs = lax.optimization_barrier((bands, pairs))
    for k, value in enumerate(fetched):
        gathered.append(value)
        if 2 * k + 1 < len(order):
            gathered.append(swap(value, 1))

    one, two, three, down, up = kernel_call(
        functools.partial(coarse_kernel, plan, blocks),
        tuple(shape(h[l], rhs, LANES) for l in (1, 2, 3))
        + (shape(3, rhs, LANES), shape(3, rhs, LANES)),
        cost_us=2.5,
    )(matrices, factor_one, factor_two, factor_three, *bands)
    down, up = shift(down, 1), shift(up, -1)

    fine = kernel_call(
        functools.partial(fine_kernel, plan, blocks), shape(h0, rhs, plan.w0)
    )(matrices, rows, from_above, from_below, factor_fine, *bands)
    four = kernel_call(
        functools.partial(whole_kernel, plan, group, blocks),
        shape(3, rhs, LANES),
        scratch=(
            pltpu.VMEM((n + 1, rhs, width3), F32),
            pltpu.VMEM((plan.nx[4] + 2, rhs, LANES), F32),
        ),
    )(matrices, jnp.swapaxes(factor_four, 2, 3), coarse_inverse, *gathered)
    out = kernel_call(functools.partial(final_kernel, plan), shape(rhs * h0, plan.w0))(
        fine, one, two, three, four, down, up
    )
    return out.reshape(rhs, h0, plan.w0)


def solution(mesh):
    placed = (
        P(None, "px", "py"),
        P("px", "py", None, None),
        P("px", None, None, None),
        P("px", None, None, None),
        P("px", None, None, None),
        P(),
        P(),
    )
    return jax.shard_map(
        functools.partial(per_device, dict(mesh.shape)),
        mesh=mesh, in_specs=placed, out_specs=P(None, "px", "py"), check_vma=False,
    )
```

```python
import functools
import math

import jax
import jax.numpy as jnp
import numpy as np
from jax import lax
from jax.experimental import pallas as pl
from jax.experimental.pallas import tpu as pltpu
from jax.sharding import PartitionSpec as P

F32 = jnp.float32
BF16 = jnp.bfloat16
LANES = 128
SHRINK = 1.0 / 20.0
TAPS = (1, 3, 3, 1)
VMEM_BYTES = 24 * 1024 * 1024


def round_up(value, unit=LANES):
    return -(-value // unit) * unit


def global_prolong(coarse):
    out = np.zeros((coarse, 2 * coarse))
    for i in range(coarse):
        out[i, 2 * i] += 3
        out[i, 2 * i + 1] += 3
        if i > 0:
            out[i, 2 * i - 1] += 1
        if i + 1 < coarse:
            out[i, 2 * i + 2] += 1
    return out


def bf(array):
    return np.asarray(array, np.float32).astype(jnp.bfloat16)


class Plan:
    def __init__(self, mesh_shape, residual, factors):
        self.n, self.m = mesh_shape["px"], mesh_shape["py"]
        self.rhs, self.h0, self.w0 = residual
        self.h = [self.h0 >> l for l in range(5)]
        self.w = [self.w0 >> l for l in range(5)]
        self.ny = [self.w0 * self.m >> l for l in range(6)]
        self.nx = [self.h0 * self.n >> l for l in range(6)]
        self.tile = [f[3] // 2 for f in factors]
        self.tiles = [f[1] for f in factors]
        self.slots = self.h[1] + 2
        self.offset = [None, 0, self.w[1] + 2, self.w[1] + self.w[2] + 4]
        self.spare = self.w[1] + self.w[2] + self.w[3] + 6

    def place(self, level, lead, width, at=0):
        out = np.zeros((self.m, LANES, width))
        for c in range(self.m):
            for k in range(self.w[level] + 2):
                column = self.w[level] * c - 1 + k
                if -lead <= column < self.ny[level]:
                    out[c, self.offset[level] + k, at + column + lead] = 1
        return out

    def halo_lanes(self):
        out = np.zeros((2, LANES, 2 * LANES))
        for k in range(2):
            for position in range(4):
                out[0, self.spare + 2 * k + 1, LANES * k + 2 * position] = 1
                out[1, self.spare + 2 * k, LANES * k + 2 * position + 1] = 1
        return bf(out)

    def lift_columns(self, level):
        out = np.eye(self.ny[level])
        for l in range(level, 0, -1):
            out = out @ global_prolong(self.ny[l])
        return out.reshape(self.ny[level], self.m, self.w0).transpose(1, 0, 2)

    def lift_rows_of(self, level):
        w, tiles = self.tile[level], self.tiles[level]
        full = self.lift_columns(level).reshape(self.m, tiles, w, self.w0)
        out = np.zeros((self.m, 2, tiles, 2 * w, self.w0))
        for j in range(2):
            out[:, j, :, j * w : (j + 1) * w] = full
        return out

    def coarse_shrink(self):
        ny3, ny4 = self.ny[3], self.ny[4]
        columns = global_prolong(ny4).T
        width = round_up(ny4 + 2)
        out = np.zeros((2, 2, ny3, width))
        for side, taps in enumerate(((1, 3), (3, 1))):
            for j in range(2):
                out[side, j, :, 1 : 1 + ny4] = taps[j] * columns
        return bf(out.reshape(4 * ny3, width))

    def coarsest_shrink(self):
        nx5, ny5, ny4 = self.nx[5], self.ny[5], self.ny[4]
        columns = global_prolong(ny5).T
        width = round_up(ny4 + 2)
        out = np.zeros((nx5, width, nx5 * ny5))
        for i in range(nx5):
            out[i, 1 : 1 + ny4, i * ny5 : (i + 1) * ny5] = columns
        return bf(out.reshape(nx5 * width, nx5 * ny5))

    def coarsest_lift(self):
        rows, columns = global_prolong(self.nx[5]), global_prolong(self.ny[5])
        both = np.einsum("ia,jb->ijab", rows, columns)
        w, tiles = self.tile[4], self.tiles[4]
        both = both.reshape(self.nx[5] * self.ny[5], self.nx[4] // 2, 2, tiles, w)
        both = both.transpose(0, 1, 3, 2, 4)
        return bf(both.reshape(self.nx[5] * self.ny[5], self.nx[4] * self.ny[4]))

    def level_four_lift(self):
        pair = 2 * self.tile[4] * self.tiles[4]
        group = max(1, LANES // pair)
        width = group * pair
        rows = self.lift_rows_of(4).reshape(self.m, 2, pair, self.w0)
        out = np.zeros((self.m, group, 2, width, self.w0))
        for g in range(group):
            out[:, g, :, g * pair : (g + 1) * pair] = rows
        return bf(out), group


class Blocks:
    def __init__(self):
        self.parts, self.places, self.count = [], {}, 0

    def add(self, name, array):
        lead, (rows, columns) = array.shape[:-2], array.shape[-2:]
        high, wide = round_up(rows) // LANES, round_up(columns) // LANES
        out = np.zeros((math.prod(lead), high * LANES, wide * LANES), np.float32)
        out[:, :rows, :columns] = np.asarray(array, np.float32).reshape((-1, rows, columns))
        out = out.reshape(-1, high, LANES, wide, LANES).transpose(0, 1, 3, 2, 4)
        self.parts.append(out.reshape(-1, LANES, LANES))
        self.places[name] = (self.count, high, wide)
        self.count += len(self.parts[-1])

    def array(self):
        return jnp.asarray(bf(np.concatenate(self.parts, axis=0)))

    def get(self, ref, name, lead=0):
        base, high, wide = self.places[name]
        base = base + lead * (high * wide)
        rows = [
            jnp.concatenate([ref[base + i * wide + j] for j in range(wide)], axis=1)
            for i in range(high)
        ]
        return jnp.concatenate(rows, axis=0)


def split(value):
    high = value.astype(BF16)
    return high, (value - high.astype(F32)).astype(BF16)


def product(value, matrix):
    high, low = split(value)
    count = value.shape[0]
    both = jnp.dot(
        jnp.concatenate([high, low], axis=0), matrix, preferred_element_type=F32
    )
    return both[:count] + both[count:]


def shrink_rows(rows, count, halo):
    out = []
    for i in range(-1, count // 2 + 1):
        total = None
        for t, tap in enumerate(TAPS):
            j = 2 * i - 1 + t
            if -halo <= j < count + halo:
                term = rows[j + halo] * float(tap) if tap > 1 else rows[j + halo]
                total = term if total is None else total + term
        out.append(total)
    return out


def lift_rows(rows, first, last):
    out = []
    for f in range(first, last):
        i = f // 2
        other = i - 1 if f % 2 == 0 else i + 1
        out.append((rows[i + 1] * 3.0 + rows[other + 1]) * SHRINK)
    return out


def lane_index(rows):
    return lax.broadcasted_iota(jnp.int32, (rows, LANES), 1)


def assemble(pieces, width):
    total = 4 * (width + 2)
    tiles = [[] for _ in range(-(-total // LANES))]
    lane = lane_index(pieces[0][0].shape[0])
    for k, piece in enumerate(pieces):
        for q, value in enumerate(piece):
            start = k * (width + 2) + LANES * q
            count = min(LANES, width + 2 - LANES * q)
            shift, at = start % LANES, start // LANES
            rolled = pltpu.roll(value, shift, 1) if shift else value
            tiles[at].append((min(LANES, shift + count), rolled))
            if shift + count > LANES:
                tiles[at + 1].append((shift + count - LANES, rolled))
    out = []
    for segments in tiles:
        segments = sorted(segments, key=lambda s: -s[0])
        end, value = segments[0]
        if end < LANES:
            value = jnp.where(lane < end, value, 0.0)
        for end, part in segments[1:]:
            value = jnp.where(lane < end, part, value)
        out.append(value)
    return jnp.concatenate(out, axis=1).astype(BF16)[:, :total]


def solve(lhs, factor):
    return jnp.dot(lhs, factor, preferred_element_type=F32)


def kernel_call(body, out_shape, scratch=(), cost_us=1.0):
    whole = pl.BlockSpec(memory_space=pltpu.VMEM)

    def call(*operands):
        return pl.pallas_call(
            body,
            out_shape=out_shape,
            in_specs=[whole] * len(operands),
            out_specs=jax.tree.map(lambda _: whole, out_shape),
            scratch_shapes=list(scratch),
            compiler_params=pltpu.CompilerParams(vmem_limit_bytes=VMEM_BYTES),
            cost_estimate=pl.CostEstimate(
                flops=int(cost_us * 1e9), bytes_accessed=int(cost_us * 3e6), transcendentals=0
            ),
        )(*operands)

    return call


def shape(*dims):
    return jax.ShapeDtypeStruct(dims, F32)


def tap_matrix(row_lead, lane_lead, count, first, last):
    row = lax.broadcasted_iota(jnp.int32, (LANES, LANES), 0) - row_lead
    lane = lax.broadcasted_iota(jnp.int32, (LANES, LANES), 1) - lane_lead
    tap = row - 2 * lane + 3
    outer = jnp.logical_or(tap == 0, tap == 3)
    inner = jnp.logical_or(tap == 1, tap == 2)
    value = jnp.where(outer, 1.0, jnp.where(inner, 3.0, 0.0))
    value = jnp.where(jnp.logical_or(lane < first, lane > count + 1 - last), 0.0, value)
    return value.astype(BF16)


def side_matrix(plan, k):
    row = lax.broadcasted_iota(jnp.int32, (LANES, LANES), 0)
    lane = lax.broadcasted_iota(jnp.int32, (LANES, LANES), 1) - plan.spare - 2 * k
    left = jnp.logical_and(row == 0, lane == 0)
    right = jnp.logical_and(row == plan.w0 - 1, lane == 1)
    return jnp.where(jnp.logical_or(left, right), 1.0, 0.0).astype(BF16)


def write_halos(c, down, up, first_ref, second_ref):
    forward = jnp.bitwise_and(c, 2) == 0
    for k, (low, high) in enumerate(zip(down, up)):
        first_ref[k] = jnp.where(forward, low, high)
        second_ref[k] = jnp.where(forward, high, low)


def read_halos(plan, first_ref, second_ref):
    r, c = lax.axis_index("px"), lax.axis_index("py")
    forward = jnp.bitwise_and(c, 2) == 0
    above = jnp.where(r > 0, 1.0, 0.0).astype(F32)
    below = jnp.where(r < plan.n - 1, 1.0, 0.0).astype(F32)
    first, second = first_ref[...], second_ref[...]
    return jnp.where(forward, first, second) * above, jnp.where(forward, second, first) * below


def restrict_kernel(plan, x_ref, own_ref, first_ref, second_ref, rows_ref):
    r, c = lax.axis_index("px"), lax.axis_index("py")
    rhs, slots, h = plan.rhs, plan.slots, plan.h
    first = jnp.where(c == 0, 1, 0)
    last = jnp.where(c == plan.m - 1, 1, 0)
    shrink = None
    matrices = []
    for level in (1, 2, 3):
        lead = 0 if level == 1 else plan.offset[level - 1] + 1
        step = tap_matrix(lead, plan.offset[level], plan.w[level], first, last)
        if shrink is None:
            shrink = step
        else:
            shrink = jnp.dot(shrink, step, preferred_element_type=F32).astype(BF16)
        matrices.append(shrink)
    above = jnp.where(r > 0, 1.0, 0.0).astype(F32)
    below = jnp.where(r < plan.n - 1, 1.0, 0.0).astype(F32)
    x = [x_ref[pl.ds(row, rhs, stride=h[0]), :] for row in range(h[0])]
    for i, row in enumerate(x):
        rows_ref[i] = row
    rows, total = x, None
    for level in (1, 2, 3):
        rows = shrink_rows(rows, h[level - 1], 0 if level == 1 else 1)
        rows[0] = rows[0] * above
        rows[-1] = rows[-1] * below
        part = product(jnp.concatenate(rows, axis=0), matrices[level - 1])
        if total is None:
            total = part
        else:
            count = part.shape[0]
            total = jnp.concatenate([total[:count] + part, total[count:]], axis=0)
    sides = [jnp.zeros_like(x[0])] + x[: slots - 1]
    total = total + jnp.dot(
        jnp.concatenate(sides, axis=0).astype(BF16), side_matrix(plan, 0),
        preferred_element_type=F32,
    )
    rest = jnp.concatenate(x[slots - 1 :], axis=0).astype(BF16)
    more = jnp.dot(rest, side_matrix(plan, 1), preferred_element_type=F32)
    count = more.shape[0]
    total = jnp.concatenate([total[:count] + more, total[count:]], axis=0)
    lane = lane_index(slots * rhs)
    one, two = plan.offset[2], plan.offset[3]
    scale = jnp.where(lane < two, SHRINK**2, jnp.where(lane < plan.spare, SHRINK**3, 1.0))
    total = total * jnp.where(lane < one, SHRINK, scale)
    own = total.reshape(slots, rhs, LANES)
    own_ref[...] = own
    lane = lane_index(rhs)
    down, up = [x[-1]], [x[0]]
    for k in range(2):
        three_own = own[h[3] + k]
        down.append(
            jnp.where(lane < one, own[h[1] + k], jnp.where(lane < two, own[h[2] + k], three_own))
        )
        up.append(own[k])
    write_halos(c, down + [own[1]], up + [own[h[3]]], first_ref, second_ref)


def merge_kernel(plan, own_ref, first_ref, second_ref, out_ref):
    r = lax.axis_index("px")
    rhs, h = plan.rhs, plan.h
    lane = lane_index(rhs)
    above, below = read_halos(plan, first_ref, second_ref)
    one, two, end = plan.offset[2], plan.offset[3], plan.spare
    out_ref[...] = own_ref[...]
    for k in range(2):
        out_ref[k] = out_ref[k] + jnp.where(lane < end, above[1 + k], 0.0)
        for level, low, high in ((1, 0, one), (2, one, two), (3, two, end)):
            row = h[level] + k
            chosen = jnp.logical_and(lane >= low, lane < high)
            out_ref[row] = out_ref[row] + jnp.where(chosen, below[1 + k], 0.0)
    odd = lax.rem(r, 2) == 1
    row = jnp.where(odd, above[3], below[3])
    ends = jnp.where(r == jnp.where(odd, 1, plan.n - 2), 1.0, 0.0).astype(F32)
    chosen = jnp.logical_and(lane >= two, lane < end)
    at = h[3] + 2
    out_ref[at] = out_ref[at] + jnp.where(chosen, row * ends, 0.0)
    top = above[0].astype(BF16)
    out_ref[0] = out_ref[0] + jnp.dot(top, side_matrix(plan, 0), preferred_element_type=F32)
    bottom = below[0].astype(BF16)
    at = h[0] + 1 - plan.slots
    out_ref[at] = out_ref[at] + jnp.dot(bottom, side_matrix(plan, 1), preferred_element_type=F32)


def banded(bands, matrices):
    return product(jnp.concatenate(bands, axis=1), jnp.concatenate(matrices, axis=0))


def owners(plan):
    c = lax.axis_index("py")
    return [jnp.bitwise_xor(c, k) for k in range(plan.m)]


def gather_kernel(plan, blocks, block_ref, *refs):
    band_refs, out_ref = refs[:-1], refs[-1]
    rhs = plan.rhs
    values, matrices = [], []
    for band, owner in zip(band_refs, owners(plan)):
        for j in range(2):
            values.append(jnp.concatenate([band[j], band[2 + j], band[4]], axis=0))
            matrices.append(blocks.get(block_ref, "pairs", 2 * owner + j))
    total = banded(values, matrices)
    for half in range(3):
        out_ref[half] = total[half * rhs : (half + 1) * rhs]


def level_rows(plan, level, band_refs, blocks, block_ref):
    rhs, count = plan.rhs, plan.h[level] + 2
    values = [band[:count].reshape(count * rhs, LANES) for band in band_refs]
    matrices = [blocks.get(block_ref, f"place{level}", owner) for owner in owners(plan)]
    return banded(values, matrices)


def coarse_kernel(plan, blocks, block_ref, *refs):
    factors, bands, outs = refs[:3], refs[3 : 3 + plan.m], refs[3 + plan.m :]
    c, rhs = lax.axis_index("py"), plan.rhs
    down, up = [], []
    for level in (1, 2, 3):
        w, tiles = plan.tile[level], plan.tiles[level]
        whole = level_rows(plan, level, bands, blocks, block_ref)
        count = plan.h[level] + 2
        rows = [whole[i * rhs : (i + 1) * rhs] for i in range(count)]
        factor_ref, out_ref = factors[level - 1], outs[level - 1]
        solved = [[] for _ in range(tiles)]
        for b in range(plan.h[level] // 2):
            for t in range(tiles):
                pieces = []
                for k in range(4):
                    row = rows[2 * b + k]
                    lanes = range(t * w, t * w + w + 2, LANES)
                    pieces.append([row[:, lo : lo + LANES] for lo in lanes])
                solved[t].append(solve(assemble(pieces, w), factor_ref[b, t]))
        pairs = plan.h[level] // 2
        stacked = [jnp.concatenate(solved[t], axis=0) for t in range(tiles)]
        lifted = []
        name = f"lift{level}"
        for j in range(2):
            if w % LANES == 0:
                row = jnp.concatenate([v[:, j * w : (j + 1) * w] for v in stacked], axis=1)
                lifted.append(product(row, blocks.get(block_ref, name, c)))
            else:
                row = jnp.concatenate(stacked, axis=1)
                lifted.append(product(row, blocks.get(block_ref, name, 2 * c + j)))
        for b in range(pairs):
            for j in range(2):
                out_ref[2 * b + j] = lifted[j][b * rhs : (b + 1) * rhs]
        down.append(lifted[1][(pairs - 1) * rhs :])
        up.append(lifted[0][:rhs])
    write_halos(c, down, up, outs[3], outs[4])


def fine_kernel(plan, blocks, block_ref, rows_ref, first_ref, second_ref, factor_ref, *refs):
    bands, out_ref = refs[: plan.m], refs[plan.m]
    c = lax.axis_index("py")
    rhs, h0, w0, slots = plan.rhs, plan.h0, plan.w0, plan.slots
    above, below = read_halos(plan, first_ref, second_ref)
    values, matrices = [], []
    left = blocks.get(block_ref, "halo", 0)
    right = blocks.get(block_ref, "halo", 1)
    for band, owner in zip(bands, owners(plan)):
        from_left = jnp.where(owner == c - 1, 1.0, 0.0).astype(BF16)
        from_right = jnp.where(owner == c + 1, 1.0, 0.0).astype(BF16)
        matrices.append(left * from_left + right * from_right)
        values.append(band[...].reshape(slots * rhs, LANES).astype(BF16))
    halo = jnp.dot(
        jnp.concatenate(values, axis=1), jnp.concatenate(matrices, axis=0),
        preferred_element_type=F32,
    )
    lane = lane_index(rhs)
    rows, sides = [], []
    for row in range(-1, h0 + 1):
        if row == -1:
            rows.append(above[0])
        elif row == h0:
            rows.append(below[0])
        else:
            rows.append(rows_ref[row])
        part, slot = divmod(row + 1, slots)
        sides.append(halo[slot * rhs : (slot + 1) * rhs, part * LANES : (part + 1) * LANES])
    for b in range(h0 // 2):
        tiles, before = [], None
        for k in range(5):
            if k < 4:
                row, side = rows[2 * b + k], sides[2 * b + k]
                rolled = pltpu.roll(row, 2 * k + 1, 1)
                value = jnp.where(lane == 2 * k, side, rolled)
            else:
                value = jnp.zeros((rhs, LANES), F32)
            if before is not None:
                old, old_side = before
                value = jnp.where(lane == 2 * k - 1, old_side, value)
                value = jnp.where(lane < 2 * k - 1, old, value)
            tiles.append(value)
            before = (rolled, side)
        lhs = jnp.concatenate(tiles, axis=1).astype(BF16)[:, : 4 * (w0 + 2)]
        solved = solve(lhs, factor_ref[b, 0])
        for j in range(2):
            out_ref[2 * b + j] = solved[:, j * w0 : (j + 1) * w0]


def whole_kernel(plan, group, blocks, block_ref, four_ref, inverse_ref, *refs):
    count = plan.n // 2
    gathered, out_ref, pair_ref, four_rows = refs[:count], refs[count], refs[-2], refs[-1]
    r, c = lax.axis_index("px"), lax.axis_index("py")
    rhs, n, ny3, ny4 = plan.rhs, plan.n, plan.ny[3], plan.ny[4]
    nx4, nx5 = plan.nx[4], plan.nx[5]
    odd = jnp.bitwise_and(c, 1)
    even = lax.rem(r, 2) == 0
    lane = lax.broadcasted_iota(jnp.int32, (rhs, 2 * ny3), 1)
    for k, block in enumerate(gathered):
        if k == 0 or (k == count - 1 and k % 2):
            partner = 2 * k
        elif k % 2:
            partner = 2 * (k + odd)
        else:
            partner = 2 * (k - odd)
        row = jnp.bitwise_xor(r, partner)
        pair_ref[row] = block[0]
        pair_ref[row + 1] = block[1]
        at = jnp.where(even, jnp.where(row == n - 2, n, n + 1), jnp.where(row == 1, 0, n + 1))
        pair_ref[at] = jnp.where((lane < ny3) == even, block[2], 0.0)
    low = pair_ref[0:n].reshape(n * rhs, 2 * ny3)
    high = pair_ref[1 : n + 1].reshape(n * rhs, 2 * ny3)
    both = jnp.concatenate([low, high], axis=1)
    four = product(both, blocks.get(block_ref, "shrink4")) * SHRINK
    zero = jnp.zeros((rhs, four.shape[1]), F32)
    rows = [zero] + [four[i * rhs : (i + 1) * rhs] for i in range(nx4)] + [zero]
    five = shrink_rows(rows, nx4, 1)[1:-1]
    flat = product(jnp.concatenate(five, axis=1), blocks.get(block_ref, "shrink5")) * SHRINK
    flat = flat[:, : inverse_ref.shape[0]]
    part_five = jnp.dot(flat.astype(BF16), inverse_ref[...], preferred_element_type=F32)
    spread = blocks.get(block_ref, "lift5")[: part_five.shape[1], : nx4 * ny4]
    lifted = product(part_five, spread) * SHRINK
    w, tiles = plan.tile[4], plan.tiles[4]
    parts = []
    for b in range(nx4 // 2):
        for t in range(tiles):
            pieces = []
            for k in range(4):
                lanes = range(t * w, t * w + w + 2, LANES)
                pieces.append([rows[2 * b + k][:, lo : lo + LANES] for lo in lanes])
            lhs = assemble(pieces, w)
            parts.append(
                lax.dot_general(
                    lhs, four_ref[b, t], (((1,), (1,)), ((), ())), preferred_element_type=F32
                )
            )
    correction = jnp.concatenate(parts, axis=1) + lifted
    width = group * 2 * w * tiles
    bands = nx4 // 2 // group
    stacked = jnp.concatenate(
        [correction[:, i * width : (i + 1) * width] for i in range(bands)], axis=0
    )
    four_rows[0] = jnp.zeros((rhs, LANES), F32)
    four_rows[nx4 + 1] = jnp.zeros((rhs, LANES), F32)
    for g in range(group):
        for j in range(2):
            value = product(stacked, blocks.get(block_ref, "lift4", (c * group + g) * 2 + j))
            for i in range(bands):
                four_rows[1 + 2 * (i * group + g) + j] = value[i * rhs : (i + 1) * rhs]
    for k in range(3):
        out_ref[k] = four_rows[r + k]


def final_kernel(plan, fine_ref, one_ref, two_ref, three_ref, four_ref, first_ref, second_ref,
                 out_ref):
    r, rhs = lax.axis_index("px"), plan.rhs
    above = jnp.where(r > 0, 1.0, 0.0).astype(F32)
    below = jnp.where(r < plan.n - 1, 1.0, 0.0).astype(F32)
    from_above, from_below = read_halos(plan, first_ref, second_ref)
    rows = [four_ref[k] for k in range(3)]
    for level, own_ref in ((3, three_ref), (2, two_ref), (1, one_ref)):
        height = plan.h[level]
        lifted = lift_rows(rows, -1, height + 1)
        rows = [lifted[0] * above + from_above[level - 1]]
        rows += [lifted[i + 1] + own_ref[i] for i in range(height)]
        rows += [lifted[-1] * below + from_below[level - 1]]
    lifted = lift_rows(rows, 0, plan.h0)
    for row in range(plan.h0):
        out_ref[pl.ds(row, rhs, stride=plan.h0), :] = lifted[row] + fine_ref[row]


def per_device(mesh_shape, residual, factor_fine, factor_one, factor_two, factor_three,
               factor_four, coarse_inverse):
    factors = [factor_fine, factor_one, factor_two, factor_three, factor_four]
    plan = Plan(mesh_shape, residual.shape, [f.shape for f in factors])
    n, m, rhs, h, h0 = plan.n, plan.m, plan.rhs, plan.h, plan.h0
    x = residual.reshape(rhs * h0, plan.w0)

    def trade(first, second):
        def target(i, c):
            after = i - 1 if c & 2 else i + 1
            return (after, c) if 0 <= after < n else (i, c ^ 2)

        ring = []
        for i in range(n):
            for c in range(m):
                row, column = target(i, c)
                ring.append((i * m + c, row * m + column))
        back = [(b, a) for a, b in ring]
        return lax.ppermute(first, ("px", "py"), ring), lax.ppermute(second, ("px", "py"), back)

    def swap(value, bits):
        return lax.ppermute(value, "py", [(i, i ^ bits) for i in range(m)])

    width3 = 2 * plan.ny[3]
    blocks = Blocks()
    pairs = [plan.place(3, 0, width3, j * plan.ny[3]) for j in range(2)]
    blocks.add("pairs", np.stack(pairs, axis=1))
    for l in (1, 2, 3):
        blocks.add(f"place{l}", plan.place(l, 1, round_up(plan.ny[l] + 2)))
        if plan.tile[l] % LANES == 0:
            blocks.add(f"lift{l}", plan.lift_columns(l))
        else:
            lifted = plan.lift_rows_of(l)
            blocks.add(f"lift{l}", lifted.reshape(m, 2, -1, plan.w0))
    lifted, group = plan.level_four_lift()
    blocks.add("lift4", lifted)
    blocks.add("halo", plan.halo_lanes())
    blocks.add("shrink4", plan.coarse_shrink())
    blocks.add("shrink5", plan.coarsest_shrink())
    blocks.add("lift5", plan.coarsest_lift())
    matrices = blocks.array()

    own, first, second, rows = kernel_call(
        functools.partial(restrict_kernel, plan),
        (shape(plan.slots, rhs, LANES), shape(4, rhs, LANES), shape(4, rhs, LANES),
         shape(h0, rhs, plan.w0)),
    )(x)
    first, second = trade(first, second)
    band = kernel_call(functools.partial(merge_kernel, plan), shape(plan.slots, rhs, LANES))(
        own, first, second
    )
    bands = {0: band}
    bit = m // 2
    while bit:
        bands.update({k ^ bit: swap(value, bit) for k, value in list(bands.items())})
        bit //= 2
    bands = [bands[k] for k in range(m)]

    pairs = kernel_call(
        functools.partial(gather_kernel, plan, blocks), shape(3, rhs, width3), cost_us=0.3
    )(matrices, *bands)
    order, gathered = list(range(1, n // 2)), [pairs]
    fetched = []
    for k in range(0, len(order), 2):
        even, odd = order[k], order[min(k + 1, len(order) - 1)]
        fetched.append(
            lax.ppermute(
                pairs, ("px", "py"),
                [(i * m + c, (i ^ (2 * (odd if c % 2 else even))) * m + c)
                 for i in range(n) for c in range(m)],
            )
        )
    bands, pairs = lax.optimization_barrier((bands, pairs))
    for k, value in enumerate(fetched):
        gathered.append(value)
        if 2 * k + 1 < len(order):
            gathered.append(swap(value, 1))

    one, two, three, low, high = kernel_call(
        functools.partial(coarse_kernel, plan, blocks),
        tuple(shape(h[l], rhs, LANES) for l in (1, 2, 3))
        + (shape(3, rhs, LANES), shape(3, rhs, LANES)),
        cost_us=2.5,
    )(matrices, factor_one, factor_two, factor_three, *bands)
    low, high = trade(low, high)

    fine = kernel_call(
        functools.partial(fine_kernel, plan, blocks), shape(h0, rhs, plan.w0)
    )(matrices, rows, first, second, factor_fine, *bands)
    four = kernel_call(
        functools.partial(whole_kernel, plan, group, blocks),
        shape(3, rhs, LANES),
        scratch=(
            pltpu.VMEM((n + 2, rhs, width3), F32),
            pltpu.VMEM((plan.nx[4] + 2, rhs, LANES), F32),
        ),
    )(matrices, jnp.swapaxes(factor_four, 2, 3), coarse_inverse, *gathered)
    out = kernel_call(functools.partial(final_kernel, plan), shape(rhs * h0, plan.w0))(
        fine, one, two, three, four, low, high
    )
    return out.reshape(rhs, h0, plan.w0)


def solution(mesh):
    placed = (
        P(None, "px", "py"),
        P("px", "py", None, None),
        P("px", None, None, None),
        P("px", None, None, None),
        P("px", None, None, None),
        P(),
        P(),
    )
    return jax.shard_map(
        functools.partial(per_device, dict(mesh.shape)),
        mesh=mesh, in_specs=placed, out_specs=P(None, "px", "py"), check_vma=False,
    )
```

```python
import functools
import math

import jax
import jax.numpy as jnp
import numpy as np
from jax import lax
from jax.experimental import pallas as pl
from jax.experimental.pallas import tpu as pltpu
from jax.sharding import PartitionSpec as P

F32 = jnp.float32
BF16 = jnp.bfloat16
LANES = 128
SHRINK = 1.0 / 20.0
TAPS = (1, 3, 3, 1)
VMEM_BYTES = 24 * 1024 * 1024


def round_up(value, unit=LANES):
    return -(-value // unit) * unit


def global_prolong(coarse):
    out = np.zeros((coarse, 2 * coarse))
    for i in range(coarse):
        out[i, 2 * i] += 3
        out[i, 2 * i + 1] += 3
        if i > 0:
            out[i, 2 * i - 1] += 1
        if i + 1 < coarse:
            out[i, 2 * i + 2] += 1
    return out


def bf(array):
    return np.asarray(array, np.float32).astype(jnp.bfloat16)


class Plan:
    def __init__(self, mesh_shape, residual, factors):
        self.n, self.m = mesh_shape["px"], mesh_shape["py"]
        self.rhs, self.h0, self.w0 = residual
        self.h = [self.h0 >> l for l in range(5)]
        self.w = [self.w0 >> l for l in range(5)]
        self.ny = [self.w0 * self.m >> l for l in range(6)]
        self.nx = [self.h0 * self.n >> l for l in range(6)]
        self.tile = [f[3] // 2 for f in factors]
        self.tiles = [f[1] for f in factors]
        self.slots = self.h[1] + 2
        self.offset = [None, 0]
        for l in (2, 3, 4):
            self.offset.append(self.offset[-1] + self.w[l - 1] + 2)
        self.whole = self.h[2] + 2
        self.sent = self.whole + 2
        self.sides = (self.h0 + 2) // 2
        self.first = self.w[1] + 2
        self.rest = LANES - self.first

    def place(self, level, lead, width, at=0):
        out = np.zeros((self.m, LANES, width))
        for c in range(self.m):
            for k in range(self.w[level] + 2):
                column = self.w[level] * c - 1 + k
                if -lead <= column < self.ny[level]:
                    out[c, self.offset[level] + k, at + column + lead] = 1
        return out

    def place_tail(self):
        whole = self.place(1, 1, round_up(self.ny[1] + 2))
        out = np.zeros((self.m, 2) + whole.shape[1:])
        out[:, 0, self.first :] = whole[:, : self.rest]
        tail = self.first - self.rest
        out[:, 1, self.offset[4] : self.offset[4] + tail] = whole[:, self.rest : self.first]
        return out.reshape(self.m, 2 * LANES, -1)

    def place_four(self):
        rows = [self.place(4, 0, 4 * self.ny[4], j * self.ny[4]) for j in range(4)]
        return np.stack(rows, axis=1)

    def halo_lanes(self):
        out = np.zeros((2, LANES, self.sides, LANES))
        for j in range(self.sides):
            for position in range(4):
                out[0, self.offset[3] + 2 * j, j, 2 * position] = 1
                out[1, self.offset[3] + 2 * j + 1, j, 2 * position + 1] = 1
        return out.reshape(2, LANES, self.sides * LANES)

    def pick_band(self):
        out = []
        for l in (1, 2, 3):
            pick = np.zeros((self.m, round_up(self.ny[l]), LANES))
            one = self.place(l, 0, self.ny[l])
            pick[:, : self.ny[l]] = one.transpose(0, 2, 1)
            out.append(pick)
        return np.concatenate(out, axis=1)

    def lift_band(self):
        out = []
        for l in (1, 2, 3):
            one = self.place(l, 0, self.ny[l])
            out.append(np.einsum("cki,cif->ckf", one, self.lift_columns(l)))
        return np.concatenate(out, axis=2)

    def lift_columns(self, level):
        out = np.eye(self.ny[level])
        for l in range(level, 0, -1):
            out = out @ global_prolong(self.ny[l])
        return out.reshape(self.ny[level], self.m, self.w0).transpose(1, 0, 2)

    def lift_rows_of(self, level):
        w, tiles = self.tile[level], self.tiles[level]
        full = self.lift_columns(level).reshape(self.m, tiles, w, self.w0)
        out = np.zeros((self.m, 2, tiles, 2 * w, self.w0))
        for j in range(2):
            out[:, j, :, j * w : (j + 1) * w] = full
        return out

    def coarsest_shrink(self):
        nx5, ny5, ny4 = self.nx[5], self.ny[5], self.ny[4]
        columns = global_prolong(ny5).T
        width = round_up(ny4 + 2)
        out = np.zeros((nx5, width, nx5 * ny5))
        for i in range(nx5):
            out[i, 1 : 1 + ny4, i * ny5 : (i + 1) * ny5] = columns
        return bf(out.reshape(nx5 * width, nx5 * ny5))

    def coarsest_lift(self):
        rows, columns = global_prolong(self.nx[5]), global_prolong(self.ny[5])
        both = np.einsum("ia,jb->ijab", rows, columns)
        w, tiles = self.tile[4], self.tiles[4]
        both = both.reshape(self.nx[5] * self.ny[5], self.nx[4] // 2, 2, tiles, w)
        both = both.transpose(0, 1, 3, 2, 4)
        return bf(both.reshape(self.nx[5] * self.ny[5], self.nx[4] * self.ny[4]))

    def level_four_lift(self):
        pair = 2 * self.tile[4] * self.tiles[4]
        group = max(1, LANES // pair)
        width = group * pair
        rows = self.lift_rows_of(4).reshape(self.m, 2, pair, self.w0)
        out = np.zeros((self.m, group, 2, width, self.w0))
        for g in range(group):
            out[:, g, :, g * pair : (g + 1) * pair] = rows
        return bf(out), group


class Blocks:
    def __init__(self):
        self.parts, self.places, self.count = [], {}, 0

    def add(self, name, array):
        lead, (rows, columns) = array.shape[:-2], array.shape[-2:]
        high, wide = round_up(rows) // LANES, round_up(columns) // LANES
        out = np.zeros((math.prod(lead), high * LANES, wide * LANES), np.float32)
        out[:, :rows, :columns] = np.asarray(array, np.float32).reshape((-1, rows, columns))
        out = out.reshape(-1, high, LANES, wide, LANES).transpose(0, 1, 3, 2, 4)
        self.parts.append(out.reshape(-1, LANES, LANES))
        self.places[name] = (self.count, high, wide)
        self.count += len(self.parts[-1])

    def array(self):
        return jnp.asarray(bf(np.concatenate(self.parts, axis=0)))

    def get(self, ref, name, lead=0):
        base, high, wide = self.places[name]
        base = base + lead * (high * wide)
        rows = [
            jnp.concatenate([ref[base + i * wide + j] for j in range(wide)], axis=1)
            for i in range(high)
        ]
        return jnp.concatenate(rows, axis=0)


def split(value):
    high = value.astype(BF16)
    return high, (value - high.astype(F32)).astype(BF16)


def product(value, matrix):
    high, low = split(value)
    count = value.shape[0]
    both = jnp.dot(
        jnp.concatenate([high, low], axis=0), matrix, preferred_element_type=F32
    )
    return both[:count] + both[count:]


def shrink_rows(rows, count, halo):
    out = []
    for i in range(-1, count // 2 + 1):
        total = None
        for t, tap in enumerate(TAPS):
            j = 2 * i - 1 + t
            if -halo <= j < count + halo:
                term = rows[j + halo] * float(tap) if tap > 1 else rows[j + halo]
                total = term if total is None else total + term
        out.append(total)
    return out


def lift_rows(rows, first, last):
    out = []
    for f in range(first, last):
        i = f // 2
        other = i - 1 if f % 2 == 0 else i + 1
        out.append((rows[i + 1] * 3.0 + rows[other + 1]) * SHRINK)
    return out


def lane_index(rows):
    return lax.broadcasted_iota(jnp.int32, (rows, LANES), 1)


def assemble(pieces, width):
    total = 4 * (width + 2)
    tiles = [[] for _ in range(-(-total // LANES))]
    lane = lane_index(pieces[0][0].shape[0])
    for k, piece in enumerate(pieces):
        for q, value in enumerate(piece):
            start = k * (width + 2) + LANES * q
            count = min(LANES, width + 2 - LANES * q)
            shift, at = start % LANES, start // LANES
            rolled = pltpu.roll(value, shift, 1) if shift else value
            tiles[at].append((min(LANES, shift + count), rolled))
            if shift + count > LANES:
                tiles[at + 1].append((shift + count - LANES, rolled))
    out = []
    for segments in tiles:
        segments = sorted(segments, key=lambda s: -s[0])
        end, value = segments[0]
        if end < LANES:
            value = jnp.where(lane < end, value, 0.0)
        for end, part in segments[1:]:
            value = jnp.where(lane < end, part, value)
        out.append(value)
    return jnp.concatenate(out, axis=1).astype(BF16)[:, :total]


def solve(lhs, factor):
    return jnp.dot(lhs, factor, preferred_element_type=F32)


def kernel_call(body, out_shape, scratch=(), cost_us=1.0):
    whole = pl.BlockSpec(memory_space=pltpu.VMEM)

    def call(*operands):
        return pl.pallas_call(
            body,
            out_shape=out_shape,
            in_specs=[whole] * len(operands),
            out_specs=jax.tree.map(lambda _: whole, out_shape),
            scratch_shapes=list(scratch),
            compiler_params=pltpu.CompilerParams(vmem_limit_bytes=VMEM_BYTES),
            cost_estimate=pl.CostEstimate(
                flops=int(cost_us * 1e9), bytes_accessed=int(cost_us * 3e6), transcendentals=0
            ),
        )(*operands)

    return call


def shape(*dims):
    return jax.ShapeDtypeStruct(dims, F32)


def tap_matrix(row_lead, lane_lead, count, first, last):
    row = lax.broadcasted_iota(jnp.int32, (LANES, LANES), 0) - row_lead
    lane = lax.broadcasted_iota(jnp.int32, (LANES, LANES), 1) - lane_lead
    tap = row - 2 * lane + 3
    outer = jnp.logical_or(tap == 0, tap == 3)
    inner = jnp.logical_or(tap == 1, tap == 2)
    value = jnp.where(outer, 1.0, jnp.where(inner, 3.0, 0.0))
    value = jnp.where(jnp.logical_or(lane < first, lane > count + 1 - last), 0.0, value)
    return value.astype(BF16)


def place_sides(plan, slot_value, row, index):
    at = plan.offset[3] + 2 * (index % plan.sides)
    lane = lane_index(plan.rhs)
    chosen = jnp.logical_or(lane == at, lane == at + 1)
    return jnp.where(chosen, pltpu.roll(row, (at + 1) % LANES, 1), slot_value)


def column_ends(plan):
    c = lax.axis_index("py")
    return jnp.where(c == 0, 1, 0), jnp.where(c == plan.m - 1, 1, 0)


def write_halos(c, down, up, first_ref, second_ref):
    forward = jnp.bitwise_and(c, 2) == 0
    for k, (low, high) in enumerate(zip(down, up)):
        first_ref[k] = jnp.where(forward, low, high)
        second_ref[k] = jnp.where(forward, high, low)


def read_halos(plan, first_ref, second_ref):
    r, c = lax.axis_index("px"), lax.axis_index("py")
    forward = jnp.bitwise_and(c, 2) == 0
    above = jnp.where(r > 0, 1.0, 0.0).astype(F32)
    below = jnp.where(r < plan.n - 1, 1.0, 0.0).astype(F32)
    first, second = first_ref[...], second_ref[...]
    return jnp.where(forward, first, second) * above, jnp.where(forward, second, first) * below


def restrict_kernel(plan, x_ref, own_ref, first_ref, second_ref, rows_ref):
    r, c = lax.axis_index("px"), lax.axis_index("py")
    rhs, slots, h = plan.rhs, plan.slots, plan.h
    first, last = column_ends(plan)
    shrink = None
    matrices = []
    for level in (1, 2, 3, 4):
        lead = 0 if level == 1 else plan.offset[level - 1] + 1
        step = tap_matrix(lead, plan.offset[level], plan.w[level], first, last)
        if shrink is None:
            shrink = step
        else:
            shrink = jnp.dot(shrink, step, preferred_element_type=F32).astype(BF16)
        matrices.append(shrink)
    above = jnp.where(r > 0, 1.0, 0.0).astype(F32)
    below = jnp.where(r < plan.n - 1, 1.0, 0.0).astype(F32)
    x = [x_ref[pl.ds(row, rhs, stride=h[0]), :] for row in range(h[0])]
    for i, row in enumerate(x):
        rows_ref[i] = row
    rows, total = x, None
    for level in (1, 2, 3, 4):
        rows = shrink_rows(rows, h[level - 1], 0 if level == 1 else 1)
        rows[0] = rows[0] * above
        rows[-1] = rows[-1] * below
        part = product(jnp.concatenate(rows, axis=0), matrices[level - 1])
        if total is None:
            total = part
        else:
            count = part.shape[0]
            total = jnp.concatenate([total[:count] + part, total[count:]], axis=0)
    lane = lane_index(slots * rhs)
    scale = jnp.where(lane < plan.offset[2], SHRINK, SHRINK**2)
    scale = jnp.where(lane < plan.offset[3], scale, SHRINK**3)
    total = total * jnp.where(lane < plan.offset[4], scale, SHRINK**4)
    own = [total[i * rhs : (i + 1) * rhs] for i in range(slots)]
    for i, row in enumerate(x):
        slot = plan.h[2] + (i + 1) // plan.sides
        own[slot] = place_sides(plan, own[slot], row, i + 1)
    for i, value in enumerate(own):
        own_ref[i] = value
    lane = lane_index(rhs)
    one, two, three = plan.offset[2:]
    third = pltpu.roll(own[2], LANES - three, 1)
    down = [x[-1]]
    for k in range(2):
        value = jnp.where(lane < three, own[h[3] + k], own[k])
        value = jnp.where(lane < two, own[h[2] + k], value)
        down.append(jnp.where(lane < one, third if k else own[h[1]], value))
    up = [x[0], jnp.where(lane < one, third, own[0]), own[1]]
    write_halos(c, down, up, first_ref, second_ref)


def merge_kernel(plan, own_ref, first_ref, second_ref, out_ref):
    r, h, rhs = lax.axis_index("px"), plan.h, plan.rhs
    lane = lane_index(rhs)
    above, below = read_halos(plan, first_ref, second_ref)
    one, two, three = plan.offset[2:]
    slot = [own_ref[i] for i in range(plan.slots)]
    matrix = tap_matrix(0, 0, plan.w[1], *column_ends(plan))
    outer = product(jnp.concatenate([above[0], below[0]], axis=0), matrix) * SHRINK
    from_above, from_below = outer[:rhs], outer[rhs:]
    slot[0] = slot[0] + jnp.where(lane < three, above[1], 0.0)
    value = jnp.where(lane < one, from_above, above[2])
    slot[1] = slot[1] + jnp.where(lane < three, value, 0.0)
    for k in range(2):
        value = from_below if k == 0 else below[2]
        pieces = ((1, 0, one, value), (2, one, two, below[1 + k]), (3, two, three, below[1 + k]))
        for level, low, high, piece in pieces:
            chosen = jnp.logical_and(lane >= low, lane < high)
            row = h[level] + k
            slot[row] = slot[row] + jnp.where(chosen, piece, 0.0)
    even = lax.rem(r, 2) == 0
    own = [own_ref[k] for k in range(3)]
    partner = [jnp.where(even, below[k], above[k]) for k in (1, 2)]
    third = jnp.where(even, below[1], above[2])
    partner.append(pltpu.roll(third, three, 1))
    low = [jnp.where(even, a, b) for a, b in zip(own, partner)]
    high = [jnp.where(even, b, a) for a, b in zip(own, partner)]
    sums = [low[0], low[1] + high[0], low[2] + high[1], high[2]]
    for k in range(4):
        slot[k] = jnp.where(lane < three, slot[k], sums[k])
    sides = plan.h[2]
    slot[sides] = place_sides(plan, slot[sides], above[0], 0)
    slot[sides + 1] = place_sides(plan, slot[sides + 1], below[0], plan.h0 + 1)
    tail = plan.first - plan.rest
    for k in range(2):
        even_row, odd_row = slot[plan.whole + 2 * k], slot[plan.whole + 2 * k + 1]
        chosen = jnp.logical_and(lane >= three, lane < three + tail)
        moved = pltpu.roll(odd_row, (three - plan.rest) % LANES, 1)
        slot[sides + k] = jnp.where(chosen, moved, slot[sides + k])
        moved = pltpu.roll(odd_row, plan.first, 1)
        out_ref[plan.whole + k] = jnp.where(lane < plan.first, even_row, moved)
    for k in range(plan.whole):
        out_ref[k] = slot[k]


def banded(bands, matrices):
    return product(jnp.concatenate(bands, axis=1), jnp.concatenate(matrices, axis=0))


def owners(plan):
    c = lax.axis_index("py")
    return [jnp.bitwise_xor(c, k) for k in range(plan.m)]


def gather_kernel(plan, blocks, block_ref, *refs):
    band_refs, out_ref = refs[:-1], refs[-1]
    values, matrices = [], []
    for band, owner in zip(band_refs, owners(plan)):
        for j in range(4):
            values.append(band[j])
            matrices.append(blocks.get(block_ref, "four", 4 * owner + j))
    out_ref[...] = banded(values, matrices)


def level_rows(plan, level, band_refs, blocks, block_ref):
    rhs = plan.rhs
    count = plan.sent if level == 1 else plan.h[level] + 2
    values = [band[:count].reshape(count * rhs, LANES) for band in band_refs]
    matrices = [blocks.get(block_ref, f"place{level}", owner) for owner in owners(plan)]
    whole = banded(values, matrices)
    rows = [whole[i * rhs : (i + 1) * rhs] for i in range(count)]
    if level > 1:
        return rows
    values, at = [], plan.whole
    for band in band_refs:
        pair = [band[at : at + 2], band[at - 2 : at]]
        values.append(jnp.concatenate([v.reshape(2 * rhs, LANES) for v in pair], axis=1))
    matrices = [blocks.get(block_ref, "tail", owner) for owner in owners(plan)]
    odd = banded(values, matrices)
    return rows[:at] + [rows[at], odd[:rhs], rows[at + 1], odd[rhs:]]


def coarse_kernel(plan, blocks, block_ref, *refs):
    factors, bands, outs = refs[:3], refs[3 : 3 + plan.m], refs[3 + plan.m :]
    c, rhs = lax.axis_index("py"), plan.rhs
    down, up = [], []
    for level in (1, 2, 3):
        w, tiles = plan.tile[level], plan.tiles[level]
        rows = level_rows(plan, level, bands, blocks, block_ref)
        factor_ref, out_ref = factors[level - 1], outs[level - 1]
        solved = [[] for _ in range(tiles)]
        for b in range(plan.h[level] // 2):
            for t in range(tiles):
                pieces = []
                for k in range(4):
                    row = rows[2 * b + k]
                    lanes = range(t * w, t * w + w + 2, LANES)
                    pieces.append([row[:, lo : lo + LANES] for lo in lanes])
                solved[t].append(solve(assemble(pieces, w), factor_ref[b, t]))
        pairs = plan.h[level] // 2
        stacked = [jnp.concatenate(solved[t], axis=0) for t in range(tiles)]
        lifted = []
        name = f"lift{level}"
        for j in range(2):
            if w % LANES == 0:
                row = jnp.concatenate([v[:, j * w : (j + 1) * w] for v in stacked], axis=1)
                lifted.append(product(row, blocks.get(block_ref, name, c)))
            else:
                row = jnp.concatenate(stacked, axis=1)
                lifted.append(product(row, blocks.get(block_ref, name, 2 * c + j)))
        for b in range(pairs):
            for j in range(2):
                out_ref[2 * b + j] = lifted[j][b * rhs : (b + 1) * rhs]
        for j, (edge, at) in enumerate(((up, 0), (down, pairs - 1))):
            for value in solved:
                if w % LANES == 0:
                    edge.append(value[at][:, j * w : (j + 1) * w])
                else:
                    edge.append(pltpu.roll(value[at], LANES - w, 1) if j else value[at])
    edges = [jnp.concatenate(edge, axis=1) for edge in (down, up)]
    picked = product(jnp.concatenate(edges, axis=0), blocks.get(block_ref, "pick", c))
    write_halos(c, [picked[:rhs]], [picked[rhs:]], outs[3], outs[4])


def fine_kernel(plan, blocks, block_ref, rows_ref, first_ref, second_ref, factor_ref, *refs):
    bands, out_ref = refs[: plan.m], refs[plan.m]
    c = lax.axis_index("py")
    rhs, h0, w0 = plan.rhs, plan.h0, plan.w0
    above, below = read_halos(plan, first_ref, second_ref)
    values, matrices = [], []
    left = blocks.get(block_ref, "halo", 0)
    right = blocks.get(block_ref, "halo", 1)
    at = plan.h[2]
    for band, owner in zip(bands, owners(plan)):
        from_left = jnp.where(owner == c - 1, 1.0, 0.0).astype(BF16)
        from_right = jnp.where(owner == c + 1, 1.0, 0.0).astype(BF16)
        matrices.append(left * from_left + right * from_right)
        values.append(band[at : at + 2].reshape(2 * rhs, LANES).astype(BF16))
    halo = jnp.dot(
        jnp.concatenate(values, axis=1), jnp.concatenate(matrices, axis=0),
        preferred_element_type=F32,
    )
    lane = lane_index(rhs)
    rows, sides = [], []
    for row in range(-1, h0 + 1):
        if row == -1:
            rows.append(above[0])
        elif row == h0:
            rows.append(below[0])
        else:
            rows.append(rows_ref[row])
        slot, part = divmod(row + 1, plan.sides)
        sides.append(halo[slot * rhs : (slot + 1) * rhs, part * LANES : (part + 1) * LANES])
    for b in range(h0 // 2):
        tiles, before = [], None
        for k in range(5):
            if k < 4:
                row, side = rows[2 * b + k], sides[2 * b + k]
                rolled = pltpu.roll(row, 2 * k + 1, 1)
                value = jnp.where(lane == 2 * k, side, rolled)
            else:
                value = jnp.zeros((rhs, LANES), F32)
            if before is not None:
                old, old_side = before
                value = jnp.where(lane == 2 * k - 1, old_side, value)
                value = jnp.where(lane < 2 * k - 1, old, value)
            tiles.append(value)
            before = (rolled, side)
        lhs = jnp.concatenate(tiles, axis=1).astype(BF16)[:, : 4 * (w0 + 2)]
        solved = solve(lhs, factor_ref[b, 0])
        for j in range(2):
            out_ref[2 * b + j] = solved[:, j * w0 : (j + 1) * w0]


def whole_kernel(plan, group, blocks, block_ref, four_ref, inverse_ref, *refs):
    count = plan.n // 2
    gathered, out_ref, pair_ref, four_rows = refs[:count], refs[count], refs[-2], refs[-1]
    r, c = lax.axis_index("px"), lax.axis_index("py")
    rhs, ny4 = plan.rhs, plan.ny[4]
    nx4, nx5 = plan.nx[4], plan.nx[5]
    odd = jnp.bitwise_and(c, 1)
    for k, block in enumerate(gathered):
        if k == 0 or (k == count - 1 and k % 2):
            partner = 2 * k
        elif k % 2:
            partner = 2 * (k + odd)
        else:
            partner = 2 * (k - odd)
        pair_ref[jnp.bitwise_xor(r, partner) // 2] = block[...]
    lane = lane_index(rhs)
    inside = jnp.logical_and(lane >= 1, lane <= ny4)

    def part_row(pair, j):
        tile, start = divmod(j * ny4, LANES)
        value = pair_ref[pair, :, tile * LANES : (tile + 1) * LANES]
        return jnp.where(inside, pltpu.roll(value, (1 - start) % LANES, 1), 0.0)

    zero = jnp.zeros((rhs, LANES), F32)
    rows = [zero]
    for i in range(nx4):
        value = part_row(i // 2, 1 + i % 2)
        if i % 2 == 0 and i > 0:
            value = value + part_row(i // 2 - 1, 3)
        if i % 2 == 1 and i < nx4 - 1:
            value = value + part_row(i // 2 + 1, 0)
        rows.append(value)
    rows.append(zero)
    five = shrink_rows(rows, nx4, 1)[1:-1]
    flat = product(jnp.concatenate(five, axis=1), blocks.get(block_ref, "shrink5")) * SHRINK
    flat = flat[:, : inverse_ref.shape[0]]
    part_five = jnp.dot(flat.astype(BF16), inverse_ref[...], preferred_element_type=F32)
    spread = blocks.get(block_ref, "lift5")[: part_five.shape[1], : nx4 * ny4]
    lifted = product(part_five, spread) * SHRINK
    w, tiles = plan.tile[4], plan.tiles[4]
    parts = []
    for b in range(nx4 // 2):
        for t in range(tiles):
            pieces = []
            for k in range(4):
                lanes = range(t * w, t * w + w + 2, LANES)
                pieces.append([rows[2 * b + k][:, lo : lo + LANES] for lo in lanes])
            lhs = assemble(pieces, w)
            parts.append(
                lax.dot_general(
                    lhs, four_ref[b, t], (((1,), (1,)), ((), ())), preferred_element_type=F32
                )
            )
    correction = jnp.concatenate(parts, axis=1) + lifted
    width = group * 2 * w * tiles
    bands = nx4 // 2 // group
    stacked = jnp.concatenate(
        [correction[:, i * width : (i + 1) * width] for i in range(bands)], axis=0
    )
    four_rows[0] = jnp.zeros((rhs, LANES), F32)
    four_rows[nx4 + 1] = jnp.zeros((rhs, LANES), F32)
    for g in range(group):
        for j in range(2):
            value = product(stacked, blocks.get(block_ref, "lift4", (c * group + g) * 2 + j))
            for i in range(bands):
                four_rows[1 + 2 * (i * group + g) + j] = value[i * rhs : (i + 1) * rhs]
    for k in range(3):
        out_ref[k] = four_rows[r + k]


def final_kernel(plan, blocks, block_ref, fine_ref, one_ref, two_ref, three_ref, four_ref,
                 first_ref, second_ref, out_ref):
    r, rhs = lax.axis_index("px"), plan.rhs
    above = jnp.where(r > 0, 1.0, 0.0).astype(F32)
    below = jnp.where(r < plan.n - 1, 1.0, 0.0).astype(F32)
    halos = read_halos(plan, first_ref, second_ref)
    halo = product(
        jnp.concatenate([halos[0][0], halos[1][0]], axis=0),
        blocks.get(block_ref, "band", lax.axis_index("py")),
    )
    from_above, from_below = [
        [halo[k * rhs : (k + 1) * rhs, l * plan.w0 : (l + 1) * plan.w0] for l in range(3)]
        for k in range(2)
    ]
    rows = [four_ref[k] for k in range(3)]
    for level, own_ref in ((3, three_ref), (2, two_ref), (1, one_ref)):
        height = plan.h[level]
        lifted = lift_rows(rows, -1, height + 1)
        rows = [lifted[0] * above + from_above[level - 1]]
        rows += [lifted[i + 1] + own_ref[i] for i in range(height)]
        rows += [lifted[-1] * below + from_below[level - 1]]
    lifted = lift_rows(rows, 0, plan.h0)
    for row in range(plan.h0):
        out_ref[pl.ds(row, rhs, stride=plan.h0), :] = lifted[row] + fine_ref[row]


def per_device(mesh_shape, residual, factor_fine, factor_one, factor_two, factor_three,
               factor_four, coarse_inverse):
    factors = [factor_fine, factor_one, factor_two, factor_three, factor_four]
    plan = Plan(mesh_shape, residual.shape, [f.shape for f in factors])
    n, m, rhs, h, h0 = plan.n, plan.m, plan.rhs, plan.h, plan.h0
    x = residual.reshape(rhs * h0, plan.w0)

    def trade(first, second):
        def target(i, c):
            after = i - 1 if c & 2 else i + 1
            return (after, c) if 0 <= after < n else (i, c ^ 2)

        ring = []
        for i in range(n):
            for c in range(m):
                row, column = target(i, c)
                ring.append((i * m + c, row * m + column))
        back = [(b, a) for a, b in ring]
        return lax.ppermute(first, ("px", "py"), ring), lax.ppermute(second, ("px", "py"), back)

    def swap(value, bits):
        return lax.ppermute(value, "py", [(i, i ^ bits) for i in range(m)])

    blocks = Blocks()
    blocks.add("four", plan.place_four())
    blocks.add("tail", plan.place_tail())
    blocks.add("pick", plan.pick_band())
    blocks.add("band", plan.lift_band())
    for l in (1, 2, 3):
        blocks.add(f"place{l}", plan.place(l, 1, round_up(plan.ny[l] + 2)))
        if plan.tile[l] % LANES == 0:
            blocks.add(f"lift{l}", plan.lift_columns(l))
        else:
            lifted = plan.lift_rows_of(l)
            blocks.add(f"lift{l}", lifted.reshape(m, 2, -1, plan.w0))
    lifted, group = plan.level_four_lift()
    blocks.add("lift4", lifted)
    blocks.add("halo", plan.halo_lanes())
    blocks.add("shrink5", plan.coarsest_shrink())
    blocks.add("lift5", plan.coarsest_lift())
    matrices = blocks.array()

    own, first, second, rows = kernel_call(
        functools.partial(restrict_kernel, plan),
        (shape(plan.slots, rhs, LANES), shape(3, rhs, LANES), shape(3, rhs, LANES),
         shape(h0, rhs, plan.w0)),
    )(x)
    first, second = trade(first, second)
    band = kernel_call(functools.partial(merge_kernel, plan), shape(plan.sent, rhs, LANES))(
        own, first, second
    )
    bands = {0: band}
    bit = m // 2
    while bit:
        bands.update({k ^ bit: swap(value, bit) for k, value in list(bands.items())})
        bit //= 2
    bands = [bands[k] for k in range(m)]

    pairs = kernel_call(
        functools.partial(gather_kernel, plan, blocks), shape(rhs, 4 * plan.ny[4]), cost_us=0.3
    )(matrices, *bands)
    order, gathered = list(range(1, n // 2)), [pairs]
    fetched = []
    for k in range(0, len(order), 2):
        even, odd = order[k], order[min(k + 1, len(order) - 1)]
        fetched.append(
            lax.ppermute(
                pairs, ("px", "py"),
                [(i * m + c, (i ^ (2 * (odd if c % 2 else even))) * m + c)
                 for i in range(n) for c in range(m)],
            )
        )
    bands, pairs = lax.optimization_barrier((bands, pairs))
    for k, value in enumerate(fetched):
        gathered.append(value)
        if 2 * k + 1 < len(order):
            gathered.append(swap(value, 1))

    one, two, three, low, high = kernel_call(
        functools.partial(coarse_kernel, plan, blocks),
        tuple(shape(h[l], rhs, LANES) for l in (1, 2, 3))
        + (shape(1, rhs, LANES), shape(1, rhs, LANES)),
        cost_us=2.5,
    )(matrices, factor_one, factor_two, factor_three, *bands)
    low, high = trade(low, high)

    fine = kernel_call(
        functools.partial(fine_kernel, plan, blocks), shape(h0, rhs, plan.w0)
    )(matrices, rows, first, second, factor_fine, *bands)
    four = kernel_call(
        functools.partial(whole_kernel, plan, group, blocks),
        shape(3, rhs, LANES),
        scratch=(
            pltpu.VMEM((n // 2, rhs, 4 * plan.ny[4]), F32),
            pltpu.VMEM((plan.nx[4] + 2, rhs, LANES), F32),
        ),
    )(matrices, jnp.swapaxes(factor_four, 2, 3), coarse_inverse, *gathered)
    out = kernel_call(functools.partial(final_kernel, plan, blocks), shape(rhs * h0, plan.w0))(
        matrices, fine, one, two, three, four, low, high
    )
    return out.reshape(rhs, h0, plan.w0)


def solution(mesh):
    placed = (
        P(None, "px", "py"),
        P("px", "py", None, None),
        P("px", None, None, None),
        P("px", None, None, None),
        P("px", None, None, None),
        P(),
        P(),
    )
    return jax.shard_map(
        functools.partial(per_device, dict(mesh.shape)),
        mesh=mesh, in_specs=placed, out_specs=P(None, "px", "py"), check_vma=False,
    )
```

```python
import functools
import math

import jax
import jax.numpy as jnp
import numpy as np
from jax import lax
from jax.experimental import pallas as pl
from jax.experimental.pallas import tpu as pltpu
from jax.sharding import PartitionSpec as P

F32 = jnp.float32
BF16 = jnp.bfloat16
LANES = 128
SHRINK = 1.0 / 20.0
TAPS = (1, 3, 3, 1)
VMEM_BYTES = 24 * 1024 * 1024


def round_up(value, unit=LANES):
    return -(-value // unit) * unit


def global_prolong(coarse):
    out = np.zeros((coarse, 2 * coarse))
    for i in range(coarse):
        out[i, 2 * i] += 3
        out[i, 2 * i + 1] += 3
        if i > 0:
            out[i, 2 * i - 1] += 1
        if i + 1 < coarse:
            out[i, 2 * i + 2] += 1
    return out


def bf(array):
    return np.asarray(array, np.float32).astype(jnp.bfloat16)


class Plan:
    def __init__(self, mesh_shape, residual, factors):
        self.n, self.m = mesh_shape["px"], mesh_shape["py"]
        self.rhs, self.h0, self.w0 = residual
        self.h = [self.h0 >> l for l in range(5)]
        self.w = [self.w0 >> l for l in range(5)]
        self.ny = [self.w0 * self.m >> l for l in range(6)]
        self.nx = [self.h0 * self.n >> l for l in range(6)]
        self.tile = [f[3] // 2 for f in factors]
        self.tiles = [f[1] for f in factors]
        self.slots = self.h[1] + 2
        self.offset = [None, 0]
        for l in (2, 3, 4):
            self.offset.append(self.offset[-1] + self.w[l - 1] + 2)
        self.sides = self.h0 // 2 + 1
        self.first = self.w[1] + 2
        self.rest = LANES - self.first
        self.tail = self.offset[3] + 2 * self.sides

    def place(self, level, lead, width, at=0):
        out = np.zeros((self.m, LANES, width))
        for c in range(self.m):
            for k in range(self.w[level] + 2):
                column = self.w[level] * c - 1 + k
                if -lead <= column < self.ny[level]:
                    out[c, self.offset[level] + k, at + column + lead] = 1
        return out

    def place_whole(self, level):
        if self.tile[level] == LANES:
            return self.place(level, 0, self.ny[level])
        return self.place(level, 1, round_up(self.ny[level] + 2))

    def place_four(self):
        rows = [self.place(4, 0, 4 * self.ny[4], j * self.ny[4]) for j in range(4)]
        return np.stack(rows, axis=1)

    def halo_lanes(self):
        out = np.zeros((2, LANES, self.sides, LANES))
        for j in range(self.sides):
            for position in range(4):
                out[0, self.offset[3] + 2 * j, j, 2 * position] = 1
                out[1, self.offset[3] + 2 * j + 1, j, 2 * position + 1] = 1
        return out.reshape(2, LANES, self.sides * LANES)

    def pick_band(self):
        out = []
        for l in (1, 2, 3):
            pick = np.zeros((self.m, round_up(self.ny[l]), LANES))
            one = self.place(l, 0, self.ny[l])
            pick[:, : self.ny[l]] = one.transpose(0, 2, 1)
            out.append(pick)
        return np.concatenate(out, axis=1)

    def lift_band(self):
        out = []
        for l in (1, 2, 3):
            one = self.place(l, 0, self.ny[l])
            out.append(np.einsum("cki,cif->ckf", one, self.lift_columns(l)))
        return np.concatenate(out, axis=2)

    def lift_columns(self, level):
        out = np.eye(self.ny[level])
        for l in range(level, 0, -1):
            out = out @ global_prolong(self.ny[l])
        return out.reshape(self.ny[level], self.m, self.w0).transpose(1, 0, 2)

    def lift_rows_of(self, level):
        w, tiles = self.tile[level], self.tiles[level]
        full = self.lift_columns(level).reshape(self.m, tiles, w, self.w0)
        out = np.zeros((self.m, 2, tiles, 2 * w, self.w0))
        for j in range(2):
            out[:, j, :, j * w : (j + 1) * w] = full
        return out

    def coarsest_shrink(self):
        nx5, ny5, ny4 = self.nx[5], self.ny[5], self.ny[4]
        columns = global_prolong(ny5).T
        width = round_up(ny4 + 2)
        out = np.zeros((nx5, width, nx5 * ny5))
        for i in range(nx5):
            out[i, 1 : 1 + ny4, i * ny5 : (i + 1) * ny5] = columns
        return bf(out.reshape(nx5 * width, nx5 * ny5))

    def coarsest_lift(self):
        rows, columns = global_prolong(self.nx[5]), global_prolong(self.ny[5])
        both = np.einsum("ia,jb->ijab", rows, columns)
        w, tiles = self.tile[4], self.tiles[4]
        both = both.reshape(self.nx[5] * self.ny[5], self.nx[4] // 2, 2, tiles, w)
        both = both.transpose(0, 1, 3, 2, 4)
        return bf(both.reshape(self.nx[5] * self.ny[5], self.nx[4] * self.ny[4]))

    def level_four_lift(self):
        pair = 2 * self.tile[4] * self.tiles[4]
        group = max(1, LANES // pair)
        width = group * pair
        rows = self.lift_rows_of(4).reshape(self.m, 2, pair, self.w0)
        out = np.zeros((self.m, group, 2, width, self.w0))
        for g in range(group):
            out[:, g, :, g * pair : (g + 1) * pair] = rows
        return bf(out), group


class Blocks:
    def __init__(self):
        self.parts, self.places, self.count = [], {}, 0

    def add(self, name, array):
        lead, (rows, columns) = array.shape[:-2], array.shape[-2:]
        high, wide = round_up(rows) // LANES, round_up(columns) // LANES
        out = np.zeros((math.prod(lead), high * LANES, wide * LANES), np.float32)
        out[:, :rows, :columns] = np.asarray(array, np.float32).reshape((-1, rows, columns))
        out = out.reshape(-1, high, LANES, wide, LANES).transpose(0, 1, 3, 2, 4)
        self.parts.append(out.reshape(-1, LANES, LANES))
        self.places[name] = (self.count, high, wide)
        self.count += len(self.parts[-1])

    def array(self):
        return jnp.asarray(bf(np.concatenate(self.parts, axis=0)))

    def get(self, ref, name, lead=0):
        base, high, wide = self.places[name]
        base = base + lead * (high * wide)
        rows = [
            jnp.concatenate([ref[base + i * wide + j] for j in range(wide)], axis=1)
            for i in range(high)
        ]
        return jnp.concatenate(rows, axis=0)


def split(value):
    high = value.astype(BF16)
    return high, (value - high.astype(F32)).astype(BF16)


def product(value, matrix):
    high, low = split(value)
    count = value.shape[0]
    both = jnp.dot(
        jnp.concatenate([high, low], axis=0), matrix, preferred_element_type=F32
    )
    return both[:count] + both[count:]


def shrink_rows(rows, count, halo):
    out = []
    for i in range(-1, count // 2 + 1):
        total = None
        for t, tap in enumerate(TAPS):
            j = 2 * i - 1 + t
            if -halo <= j < count + halo:
                term = rows[j + halo] * float(tap) if tap > 1 else rows[j + halo]
                total = term if total is None else total + term
        out.append(total)
    return out


def lift_rows(rows, first, last):
    out = []
    for f in range(first, last):
        i = f // 2
        other = i - 1 if f % 2 == 0 else i + 1
        out.append((rows[i + 1] * 3.0 + rows[other + 1]) * SHRINK)
    return out


def lane_index(rows):
    return lax.broadcasted_iota(jnp.int32, (rows, LANES), 1)


def assemble(pieces, width):
    total = 4 * (width + 2)
    tiles = [[] for _ in range(-(-total // LANES))]
    lane = lane_index(pieces[0][0].shape[0])
    for k, piece in enumerate(pieces):
        for q, value in enumerate(piece):
            start = k * (width + 2) + LANES * q
            count = min(LANES, width + 2 - LANES * q)
            shift, at = start % LANES, start // LANES
            rolled = pltpu.roll(value, shift, 1) if shift else value
            tiles[at].append((min(LANES, shift + count), rolled))
            if shift + count > LANES:
                tiles[at + 1].append((shift + count - LANES, rolled))
    out = []
    for segments in tiles:
        segments = sorted(segments, key=lambda s: -s[0])
        end, value = segments[0]
        if end < LANES:
            value = jnp.where(lane < end, value, 0.0)
        for end, part in segments[1:]:
            value = jnp.where(lane < end, part, value)
        out.append(value)
    return jnp.concatenate(out, axis=1).astype(BF16)[:, :total]


def solve(lhs, factor):
    return jnp.dot(lhs, factor, preferred_element_type=F32)


def kernel_call(body, out_shape, scratch=(), cost_us=1.0, out_space=pltpu.VMEM):
    whole = pl.BlockSpec(memory_space=pltpu.VMEM)
    result = pl.BlockSpec(memory_space=out_space)

    def call(*operands):
        return pl.pallas_call(
            body,
            out_shape=out_shape,
            in_specs=[whole] * len(operands),
            out_specs=jax.tree.map(lambda _: result, out_shape),
            scratch_shapes=list(scratch),
            compiler_params=pltpu.CompilerParams(vmem_limit_bytes=VMEM_BYTES),
            cost_estimate=pl.CostEstimate(
                flops=int(cost_us * 1e9), bytes_accessed=int(cost_us * 3e6), transcendentals=0
            ),
        )(*operands)

    return call


def shape(*dims):
    return jax.ShapeDtypeStruct(dims, F32)


def tap_matrix(row_lead, lane_lead, count, first, last):
    row = lax.broadcasted_iota(jnp.int32, (LANES, LANES), 0) - row_lead
    lane = lax.broadcasted_iota(jnp.int32, (LANES, LANES), 1) - lane_lead
    tap = row - 2 * lane + 3
    outer = jnp.logical_or(tap == 0, tap == 3)
    inner = jnp.logical_or(tap == 1, tap == 2)
    value = jnp.where(outer, 1.0, jnp.where(inner, 3.0, 0.0))
    value = jnp.where(jnp.logical_or(lane < first, lane > count + 1 - last), 0.0, value)
    return value.astype(BF16)


def place_sides(plan, slot_value, row, at):
    lane = lane_index(plan.rhs)
    chosen = jnp.logical_or(lane == at, lane == at + 1)
    return jnp.where(chosen, pltpu.roll(row, (at + 1) % LANES, 1), slot_value)


def column_ends(plan):
    c = lax.axis_index("py")
    return jnp.where(c == 0, 1, 0), jnp.where(c == plan.m - 1, 1, 0)


def write_halos(c, down, up, first_ref, second_ref):
    forward = jnp.bitwise_and(c, 2) == 0
    for k, (low, high) in enumerate(zip(down, up)):
        first_ref[k] = jnp.where(forward, low, high)
        second_ref[k] = jnp.where(forward, high, low)


def read_halos(plan, first_ref, second_ref):
    r, c = lax.axis_index("px"), lax.axis_index("py")
    forward = jnp.bitwise_and(c, 2) == 0
    above = jnp.where(r > 0, 1.0, 0.0).astype(F32)
    below = jnp.where(r < plan.n - 1, 1.0, 0.0).astype(F32)
    first, second = first_ref[...], second_ref[...]
    return jnp.where(forward, first, second) * above, jnp.where(forward, second, first) * below


def shrink_kernel(plan, out_ref):
    first, last = column_ends(plan)
    shrink = None
    for level in (1, 2, 3, 4):
        lead = 0 if level == 1 else plan.offset[level - 1] + 1
        step = tap_matrix(lead, plan.offset[level], plan.w[level], first, last)
        if shrink is None:
            shrink = step
        else:
            shrink = jnp.dot(shrink, step, preferred_element_type=F32).astype(BF16)
        out_ref[level - 1] = shrink


def restrict_kernel(plan, x_ref, shrink_ref, early_ref, outer_ref, first_ref, second_ref, rows_ref):
    r, c = lax.axis_index("px"), lax.axis_index("py")
    rhs, slots, h = plan.rhs, plan.slots, plan.h
    above = jnp.where(r > 0, 1.0, 0.0).astype(F32)
    below = jnp.where(r < plan.n - 1, 1.0, 0.0).astype(F32)
    x = [x_ref[pl.ds(row, rhs, stride=h[0]), :] for row in range(h[0])]
    rows, total = x, None
    for level in (1, 2, 3, 4):
        rows = shrink_rows(rows, h[level - 1], 0 if level == 1 else 1)
        rows[0] = rows[0] * above
        rows[-1] = rows[-1] * below
        part = product(jnp.concatenate(rows, axis=0), shrink_ref[level - 1])
        if total is None:
            total = part
        else:
            count = part.shape[0]
            total = jnp.concatenate([total[:count] + part, total[count:]], axis=0)
    lane = lane_index(slots * rhs)
    scale = jnp.where(lane < plan.offset[2], SHRINK, SHRINK**2)
    scale = jnp.where(lane < plan.offset[3], scale, SHRINK**3)
    total = total * jnp.where(lane < plan.offset[4], scale, SHRINK**4)
    own = [total[i * rhs : (i + 1) * rhs] for i in range(slots)]
    lane = lane_index(rhs)
    one, two, three = plan.offset[2:]
    inner = [own[2], own[3], own[4], own[5]]
    for k in range(2):
        value = inner[k]
        value = jnp.where(lane < two, value, 0.0)
        for j in range(h[0] // 2):
            value = place_sides(plan, value, x[k * (h[0] // 2) + j], two + 2 * j)
        odd_row, end = own[6 + k], plan.tail + plan.first - plan.rest
        moved = pltpu.roll(odd_row, (plan.tail - plan.rest) % LANES, 1)
        chosen = jnp.logical_and(lane >= plan.tail, lane < end)
        early_ref[k] = jnp.where(chosen, moved, value)
        moved = pltpu.roll(odd_row, plan.first, 1)
        early_ref[2 + k] = jnp.where(lane < plan.first, inner[2 + k], moved)
    outer = [own[0], own[1]]
    for k in range(2):
        value = jnp.where(lane < two, own[h[2] + k], own[h[3] + k])
        outer.append(jnp.where(lane < one, own[h[1] + k], value))
    for k in range(4):
        outer_ref[k] = outer[k]
    third = pltpu.roll(own[2], LANES - three, 1)
    down = [x[-1], jnp.where(lane < three, outer[2], own[0])]
    down.append(jnp.where(lane < one, third, jnp.where(lane < three, outer[3], own[1])))
    up = [x[0], jnp.where(lane < one, third, own[0]), own[1]]
    write_halos(c, down, up, first_ref, second_ref)
    for i, row in enumerate(x):
        rows_ref[i] = row


def merge_kernel(plan, outer_ref, shrink_ref, first_ref, second_ref, out_ref):
    r, rhs = lax.axis_index("px"), plan.rhs
    lane = lane_index(rhs)
    above, below = read_halos(plan, first_ref, second_ref)
    one, two, three = plan.offset[2:]
    edge = product(jnp.concatenate([above[0], below[0]], axis=0), shrink_ref[0]) * SHRINK
    added = [
        above[1],
        jnp.where(lane < one, edge[:rhs], above[2]),
        jnp.where(lane < one, edge[rhs:], below[1]),
        below[2],
    ]
    even = lax.rem(r, 2) == 0
    own = [outer_ref[k] for k in range(3)]
    partner = [jnp.where(even, below[k], above[k]) for k in (1, 2)]
    third = jnp.where(even, below[1], above[2])
    partner.append(pltpu.roll(third, three, 1))
    low = [jnp.where(even, a, b) for a, b in zip(own, partner)]
    high = [jnp.where(even, b, a) for a, b in zip(own, partner)]
    sums = [low[0], low[1] + high[0], low[2] + high[1], high[2]]
    for k in range(4):
        value = jnp.where(lane < three, outer_ref[k] + added[k], sums[k])
        out_ref[k * rhs : (k + 1) * rhs] = value
    sides = place_sides(plan, jnp.zeros((rhs, LANES), F32), above[0], 0)
    sides = place_sides(plan, sides, below[0], 2)
    total = None
    for k in range(rhs // 8):
        part = sides[8 * k : 8 * (k + 1)]
        part = pltpu.roll(part, 4 * k, 1) if k else part
        total = part if total is None else total + part
    out_ref[4 * rhs :] = total


def banded(bands, matrices):
    return product(jnp.concatenate(bands, axis=1), jnp.concatenate(matrices, axis=0))


def owners(plan):
    c = lax.axis_index("py")
    return [jnp.bitwise_xor(c, k) for k in range(plan.m)]


def gather_kernel(plan, blocks, block_ref, *refs):
    band_refs, out_ref = refs[:-1], refs[-1]
    values, matrices = [], []
    for band, owner in zip(band_refs, owners(plan)):
        for j in range(4):
            values.append(band[j * plan.rhs : (j + 1) * plan.rhs])
            matrices.append(blocks.get(block_ref, "four", 4 * owner + j))
    out_ref[...] = banded(values, matrices)


def level_rows(plan, level, early_refs, late_refs, blocks, block_ref):
    rhs, values = plan.rhs, []
    lane = lane_index(rhs)
    for early, late in zip(early_refs, late_refs):
        outer = [late[i * rhs : (i + 1) * rhs] for i in range(4)]
        inner = []
        if level == 1:
            inner = [early[k] for k in range(4)]
            for k in range(2):
                begin = pltpu.roll(early[2 + k], plan.rest, 1)
                end = pltpu.roll(early[k], (plan.rest - plan.tail) % LANES, 1)
                inner.append(jnp.where(lane < plan.rest, begin, end))
        elif level == 2:
            inner = [early[k] for k in range(2)]
        values.append(jnp.concatenate(outer[:2] + inner + outer[2:], axis=0))
    matrices = [blocks.get(block_ref, f"place{level}", owner) for owner in owners(plan)]
    whole = jnp.dot(
        jnp.concatenate(values, axis=1).astype(BF16), jnp.concatenate(matrices, axis=0),
        preferred_element_type=F32,
    )
    return [whole[i * rhs : (i + 1) * rhs] for i in range(plan.h[level] + 2)]


def assemble_tiles(rows, t):
    rhs, count = rows[0].shape[0], rows[0].shape[1] // LANES
    lane = lane_index(rhs)

    def rolled(k, tile):
        if not 0 <= tile < count:
            return jnp.zeros((rhs, LANES), F32)
        return pltpu.roll(rows[k][:, tile * LANES : (tile + 1) * LANES], 2 * k + 1, 1)

    out = []
    for k in range(5):
        if k < 4:
            value = jnp.where(lane == 2 * k, rolled(k, t - 1), rolled(k, t))
        else:
            value = jnp.zeros((rhs, LANES), F32)
        if k > 0:
            value = jnp.where(lane == 2 * k - 1, rolled(k - 1, t + 1), value)
            value = jnp.where(lane < 2 * k - 1, rolled(k - 1, t), value)
        out.append(value)
    return jnp.concatenate(out, axis=1).astype(BF16)[:, : 4 * (LANES + 2)]


def coarse_kernel(plan, blocks, block_ref, *refs):
    factors, outs = refs[:3], refs[3 + 2 * plan.m :]
    early, late = refs[3 : 3 + plan.m], refs[3 + plan.m : 3 + 2 * plan.m]
    c, rhs = lax.axis_index("py"), plan.rhs
    down, up = [], []
    for level in (1, 2, 3):
        w, tiles = plan.tile[level], plan.tiles[level]
        rows = level_rows(plan, level, early, late, blocks, block_ref)
        factor_ref, out_ref = factors[level - 1], outs[level - 1]
        solved = [[] for _ in range(tiles)]
        for b in range(plan.h[level] // 2):
            for t in range(tiles):
                window = rows[2 * b : 2 * b + 4]
                if w == LANES:
                    lhs = assemble_tiles(window, t)
                else:
                    lhs = assemble([[row] for row in window], w)
                solved[t].append(solve(lhs, factor_ref[b, t]))
        pairs = plan.h[level] // 2
        stacked = [jnp.concatenate(solved[t], axis=0) for t in range(tiles)]
        lifted = []
        name = f"lift{level}"
        if w % LANES == 0:
            both = [
                jnp.concatenate([v[:, j * w : (j + 1) * w] for v in stacked], axis=1)
                for j in range(2)
            ]
            both = product(jnp.concatenate(both, axis=0), blocks.get(block_ref, name, c))
            lifted = [both[: pairs * rhs], both[pairs * rhs :]]
        else:
            row = jnp.concatenate(stacked, axis=1)
            lifted = [product(row, blocks.get(block_ref, name, 2 * c + j)) for j in range(2)]
        for b in range(pairs):
            for j in range(2):
                out_ref[2 * b + j] = lifted[j][b * rhs : (b + 1) * rhs]
        for j, (edge, at) in enumerate(((up, 0), (down, pairs - 1))):
            for value in solved:
                if w % LANES == 0:
                    edge.append(value[at][:, j * w : (j + 1) * w])
                else:
                    edge.append(pltpu.roll(value[at], LANES - w, 1) if j else value[at])
    edges = [jnp.concatenate(edge, axis=1) for edge in (down, up)]
    picked = product(jnp.concatenate(edges, axis=0), blocks.get(block_ref, "pick", c))
    write_halos(c, [picked[:rhs]], [picked[rhs:]], outs[3], outs[4])


def fine_kernel(plan, blocks, block_ref, rows_ref, first_ref, second_ref, factor_ref, *refs):
    early, late, out_ref = refs[: plan.m], refs[plan.m : 2 * plan.m], refs[2 * plan.m]
    c = lax.axis_index("py")
    rhs, h0, w0 = plan.rhs, plan.h0, plan.w0
    above, below = read_halos(plan, first_ref, second_ref)
    values, matrices = [], []
    left = blocks.get(block_ref, "halo", 0)
    right = blocks.get(block_ref, "halo", 1)
    lane = lane_index(rhs)
    spot = plan.offset[3] + plan.h0
    for inner, outer, owner in zip(early, late, owners(plan)):
        from_left = jnp.where(owner == c - 1, 1.0, 0.0).astype(BF16)
        from_right = jnp.where(owner == c + 1, 1.0, 0.0).astype(BF16)
        matrices.append(left * from_left + right * from_right)
        packed = outer[4 * rhs :]
        sides = [pltpu.roll(packed, (spot - 4 * k) % LANES, 1) for k in range(rhs // 8)]
        sides = jnp.concatenate(sides, axis=0)
        pair = []
        for k in range(2):
            moved = pltpu.roll(sides, LANES - 2 * k, 1) if k else sides
            chosen = jnp.logical_or(lane == spot, lane == spot + 1)
            pair.append(jnp.where(chosen, moved, inner[k]))
        values.append(jnp.concatenate(pair, axis=0).astype(BF16))
    halo = jnp.dot(
        jnp.concatenate(values, axis=1), jnp.concatenate(matrices, axis=0),
        preferred_element_type=F32,
    )
    lane = lane_index(rhs)
    rows, sides = [], []
    for row in range(-1, h0 + 1):
        if row == -1:
            rows.append(above[0])
        elif row == h0:
            rows.append(below[0])
        else:
            rows.append(rows_ref[row])
        if row < 0 or row == h0:
            slot, part = (0 if row < 0 else 1), plan.sides - 1
        else:
            slot, part = divmod(row, h0 // 2)
        sides.append(halo[slot * rhs : (slot + 1) * rhs, part * LANES : (part + 1) * LANES])
    for b in range(h0 // 2):
        tiles, before = [], None
        for k in range(5):
            if k < 4:
                row, side = rows[2 * b + k], sides[2 * b + k]
                rolled = pltpu.roll(row, 2 * k + 1, 1)
                value = jnp.where(lane == 2 * k, side, rolled)
            else:
                value = jnp.zeros((rhs, LANES), F32)
            if before is not None:
                old, old_side = before
                value = jnp.where(lane == 2 * k - 1, old_side, value)
                value = jnp.where(lane < 2 * k - 1, old, value)
            tiles.append(value)
            before = (rolled, side)
        lhs = jnp.concatenate(tiles, axis=1).astype(BF16)[:, : 4 * (w0 + 2)]
        solved = solve(lhs, factor_ref[b, 0])
        for j in range(2):
            out_ref[2 * b + j] = solved[:, j * w0 : (j + 1) * w0]


def whole_kernel(plan, group, blocks, block_ref, four_ref, inverse_ref, *refs):
    count = plan.n // 2
    gathered, out_ref, pair_ref, four_rows = refs[:count], refs[count], refs[-2], refs[-1]
    r, c = lax.axis_index("px"), lax.axis_index("py")
    rhs, ny4 = plan.rhs, plan.ny[4]
    nx4, nx5 = plan.nx[4], plan.nx[5]
    odd = jnp.bitwise_and(c, 1)
    for k, block in enumerate(gathered):
        if k == 0 or (k == count - 1 and k % 2):
            partner = 2 * k
        elif k % 2:
            partner = 2 * (k + odd)
        else:
            partner = 2 * (k - odd)
        pair_ref[jnp.bitwise_xor(r, partner) // 2] = block[...]
    lane = lane_index(rhs)
    inside = jnp.logical_and(lane >= 1, lane <= ny4)

    def part_row(pair, j):
        tile, start = divmod(j * ny4, LANES)
        value = pair_ref[pair, :, tile * LANES : (tile + 1) * LANES]
        return jnp.where(inside, pltpu.roll(value, (1 - start) % LANES, 1), 0.0)

    zero = jnp.zeros((rhs, LANES), F32)
    rows = [zero]
    for i in range(nx4):
        value = part_row(i // 2, 1 + i % 2)
        if i % 2 == 0 and i > 0:
            value = value + part_row(i // 2 - 1, 3)
        if i % 2 == 1 and i < nx4 - 1:
            value = value + part_row(i // 2 + 1, 0)
        rows.append(value)
    rows.append(zero)
    five = shrink_rows(rows, nx4, 1)[1:-1]
    flat = product(jnp.concatenate(five, axis=1), blocks.get(block_ref, "shrink5")) * SHRINK
    flat = flat[:, : inverse_ref.shape[0]]
    part_five = jnp.dot(flat.astype(BF16), inverse_ref[...], preferred_element_type=F32)
    spread = blocks.get(block_ref, "lift5")[: part_five.shape[1], : nx4 * ny4]
    lifted = product(part_five, spread) * SHRINK
    w, tiles = plan.tile[4], plan.tiles[4]
    parts = []
    for b in range(nx4 // 2):
        for t in range(tiles):
            pieces = []
            for k in range(4):
                lanes = range(t * w, t * w + w + 2, LANES)
                pieces.append([rows[2 * b + k][:, lo : lo + LANES] for lo in lanes])
            lhs = assemble(pieces, w)
            parts.append(
                lax.dot_general(
                    lhs, four_ref[b, t], (((1,), (1,)), ((), ())), preferred_element_type=F32
                )
            )
    correction = jnp.concatenate(parts, axis=1) + lifted
    width = group * 2 * w * tiles
    bands = nx4 // 2 // group
    stacked = jnp.concatenate(
        [correction[:, i * width : (i + 1) * width] for i in range(bands)], axis=0
    )
    four_rows[0] = jnp.zeros((rhs, LANES), F32)
    four_rows[nx4 + 1] = jnp.zeros((rhs, LANES), F32)
    for g in range(group):
        for j in range(2):
            value = product(stacked, blocks.get(block_ref, "lift4", (c * group + g) * 2 + j))
            for i in range(bands):
                four_rows[1 + 2 * (i * group + g) + j] = value[i * rhs : (i + 1) * rhs]
    for k in range(3):
        out_ref[k] = four_rows[r + k]


def final_kernel(plan, blocks, block_ref, fine_ref, one_ref, two_ref, three_ref, four_ref,
                 first_ref, second_ref, out_ref, whole_ref, semaphores):
    r, rhs = lax.axis_index("px"), plan.rhs
    above = jnp.where(r > 0, 1.0, 0.0).astype(F32)
    below = jnp.where(r < plan.n - 1, 1.0, 0.0).astype(F32)
    halos = read_halos(plan, first_ref, second_ref)
    halo = product(
        jnp.concatenate([halos[0][0], halos[1][0]], axis=0),
        blocks.get(block_ref, "band", lax.axis_index("py")),
    )
    from_above, from_below = [
        [halo[k * rhs : (k + 1) * rhs, l * plan.w0 : (l + 1) * plan.w0] for l in range(3)]
        for k in range(2)
    ]
    copies = []
    for part in range(rhs // 8):
        own = slice(8 * part, 8 * (part + 1))
        rows = [four_ref[k, own] for k in range(3)]
        for level, own_ref in ((3, three_ref), (2, two_ref), (1, one_ref)):
            height = plan.h[level]
            lifted = lift_rows(rows, -1, height + 1)
            rows = [lifted[0] * above + from_above[level - 1][own]]
            rows += [lifted[i + 1] + own_ref[i, own] for i in range(height)]
            rows += [lifted[-1] * below + from_below[level - 1][own]]
        lifted = lift_rows(rows, 0, plan.h0)
        start, count = 8 * part * plan.h0, 8 * plan.h0
        for row in range(plan.h0):
            value = lifted[row] + fine_ref[row, own]
            whole_ref[pl.ds(start + row, 8, stride=plan.h0), :] = value
        span = pl.ds(start, count)
        copies.append(
            pltpu.make_async_copy(whole_ref.at[span], out_ref.at[span], semaphores.at[part])
        )
        copies[-1].start()
    for copy in copies:
        copy.wait()


def per_device(mesh_shape, residual, factor_fine, factor_one, factor_two, factor_three,
               factor_four, coarse_inverse):
    factors = [factor_fine, factor_one, factor_two, factor_three, factor_four]
    plan = Plan(mesh_shape, residual.shape, [f.shape for f in factors])
    n, m, rhs, h, h0 = plan.n, plan.m, plan.rhs, plan.h, plan.h0
    x = residual.reshape(rhs * h0, plan.w0)

    def trade(first, second):
        def target(i, c):
            after = i - 1 if c & 2 else i + 1
            return (after, c) if 0 <= after < n else (i, c ^ 2)

        ring = []
        for i in range(n):
            for c in range(m):
                row, column = target(i, c)
                ring.append((i * m + c, row * m + column))
        back = [(b, a) for a, b in ring]
        return lax.ppermute(first, ("px", "py"), ring), lax.ppermute(second, ("px", "py"), back)

    def swap(value, bits):
        return lax.ppermute(value, "py", [(i, i ^ bits) for i in range(m)])

    blocks = Blocks()
    blocks.add("four", plan.place_four())
    blocks.add("pick", plan.pick_band())
    blocks.add("band", plan.lift_band())
    for l in (1, 2, 3):
        blocks.add(f"place{l}", plan.place_whole(l))
        if plan.tile[l] % LANES == 0:
            blocks.add(f"lift{l}", plan.lift_columns(l))
        else:
            lifted = plan.lift_rows_of(l)
            blocks.add(f"lift{l}", lifted.reshape(m, 2, -1, plan.w0))
    lifted, group = plan.level_four_lift()
    blocks.add("lift4", lifted)
    blocks.add("halo", plan.halo_lanes())
    blocks.add("shrink5", plan.coarsest_shrink())
    blocks.add("lift5", plan.coarsest_lift())
    matrices = blocks.array()

    shrink = kernel_call(
        functools.partial(shrink_kernel, plan),
        jax.ShapeDtypeStruct((4, LANES, LANES), BF16), cost_us=4.0,
    )()
    early, outer, first, second, rows = kernel_call(
        functools.partial(restrict_kernel, plan),
        (shape(4, rhs, LANES), shape(4, rhs, LANES), shape(3, rhs, LANES), shape(3, rhs, LANES),
         shape(h0, rhs, plan.w0)),
    )(x, shrink)
    first, second = trade(first, second)
    late = kernel_call(functools.partial(merge_kernel, plan), shape(4 * rhs + 8, LANES))(
        outer, shrink, first, second
    )

    def spread(value):
        bands = {0: value}
        bit = m // 2
        while bit:
            bands.update({k ^ bit: swap(band, bit) for k, band in list(bands.items())})
            bit //= 2
        return [bands[k] for k in range(m)]

    early, late = spread(early), spread(late)

    pairs = kernel_call(
        functools.partial(gather_kernel, plan, blocks), shape(rhs, 4 * plan.ny[4]), cost_us=0.3
    )(matrices, *late)
    order, gathered = list(range(1, n // 2)), [pairs]
    fetched = []
    for k in range(0, len(order), 2):
        even, odd = order[k], order[min(k + 1, len(order) - 1)]
        fetched.append(
            lax.ppermute(
                pairs, ("px", "py"),
                [(i * m + c, (i ^ (2 * (odd if c % 2 else even))) * m + c)
                 for i in range(n) for c in range(m)],
            )
        )
    late, pairs = lax.optimization_barrier((late, pairs))
    for k, value in enumerate(fetched):
        gathered.append(value)
        if 2 * k + 1 < len(order):
            gathered.append(swap(value, 1))

    one, two, three, low, high = kernel_call(
        functools.partial(coarse_kernel, plan, blocks),
        tuple(shape(h[l], rhs, LANES) for l in (1, 2, 3))
        + (shape(1, rhs, LANES), shape(1, rhs, LANES)),
        cost_us=2.5,
    )(matrices, factor_one, factor_two, factor_three, *early, *late)
    low, high = trade(low, high)

    fine = kernel_call(
        functools.partial(fine_kernel, plan, blocks), shape(h0, rhs, plan.w0)
    )(matrices, rows, first, second, factor_fine, *early, *late)
    four = kernel_call(
        functools.partial(whole_kernel, plan, group, blocks),
        shape(3, rhs, LANES),
        scratch=(
            pltpu.VMEM((n // 2, rhs, 4 * plan.ny[4]), F32),
            pltpu.VMEM((plan.nx[4] + 2, rhs, LANES), F32),
        ),
    )(matrices, jnp.swapaxes(factor_four, 2, 3), coarse_inverse, *gathered)
    out = kernel_call(
        functools.partial(final_kernel, plan, blocks), shape(rhs * h0, plan.w0),
        scratch=(pltpu.VMEM((rhs * h0, plan.w0), F32), pltpu.SemaphoreType.DMA((rhs // 8,))),
        out_space=pl.ANY,
    )(
        matrices, fine, one, two, three, four, low, high
    )
    return out.reshape(rhs, h0, plan.w0)


def solution(mesh):
    placed = (
        P(None, "px", "py"),
        P("px", "py", None, None),
        P("px", None, None, None),
        P("px", None, None, None),
        P("px", None, None, None),
        P(),
        P(),
    )
    return jax.shard_map(
        functools.partial(per_device, dict(mesh.shape)),
        mesh=mesh, in_specs=placed, out_specs=P(None, "px", "py"), check_vma=False,
    )
```

```python
import functools
import math

import jax
import jax.numpy as jnp
import numpy as np
from jax import lax
from jax.experimental import pallas as pl
from jax.experimental.pallas import tpu as pltpu
from jax.sharding import PartitionSpec as P

F32 = jnp.float32
BF16 = jnp.bfloat16
LANES = 128
SHRINK = 1.0 / 20.0
TAPS = (1, 3, 3, 1)
VMEM_BYTES = 24 * 1024 * 1024


def round_up(value, unit=LANES):
    return -(-value // unit) * unit


def global_prolong(coarse):
    out = np.zeros((coarse, 2 * coarse))
    for i in range(coarse):
        out[i, 2 * i] += 3
        out[i, 2 * i + 1] += 3
        if i > 0:
            out[i, 2 * i - 1] += 1
        if i + 1 < coarse:
            out[i, 2 * i + 2] += 1
    return out


def bf(array):
    return np.asarray(array, np.float32).astype(jnp.bfloat16)


class Plan:
    def __init__(self, mesh_shape, residual, factors):
        self.n, self.m = mesh_shape["px"], mesh_shape["py"]
        self.rhs, self.h0, self.w0 = residual
        self.h = [self.h0 >> l for l in range(5)]
        self.w = [self.w0 >> l for l in range(5)]
        self.ny = [self.w0 * self.m >> l for l in range(6)]
        self.nx = [self.h0 * self.n >> l for l in range(6)]
        self.tile = [f[3] // 2 for f in factors]
        self.tiles = [f[1] for f in factors]
        self.slots = self.h[1] + 2
        self.offset = [None, 0]
        for l in (2, 3, 4):
            self.offset.append(self.offset[-1] + self.w[l - 1] + 2)
        self.sides = self.h0 // 2 + 1
        self.first = self.w[1] + 2
        self.rest = LANES - self.first
        self.tail = self.offset[3] + 2 * self.sides

    def place(self, level, lead, width, at=0):
        out = np.zeros((self.m, LANES, width))
        for c in range(self.m):
            for k in range(self.w[level] + 2):
                column = self.w[level] * c - 1 + k
                if -lead <= column < self.ny[level]:
                    out[c, self.offset[level] + k, at + column + lead] = 1
        return out

    def place_whole(self, level):
        if self.tile[level] == LANES:
            return self.place(level, 0, self.ny[level])
        return self.place(level, 1, round_up(self.ny[level] + 2))

    def place_four(self):
        rows = [self.place(4, 0, 4 * self.ny[4], j * self.ny[4]) for j in range(4)]
        return np.stack(rows, axis=1)

    def halo_lanes(self):
        out = np.zeros((2, LANES, self.sides, LANES))
        for j in range(self.sides):
            for position in range(4):
                out[0, self.offset[3] + 2 * j, j, 2 * position] = 1
                out[1, self.offset[3] + 2 * j + 1, j, 2 * position + 1] = 1
        return out.reshape(2, LANES, self.sides * LANES)

    def pick_band(self):
        out = []
        for l in (1, 2, 3):
            pick = np.zeros((self.m, round_up(self.ny[l]), LANES))
            one = self.place(l, 0, self.ny[l])
            pick[:, : self.ny[l]] = one.transpose(0, 2, 1)
            out.append(pick)
        return np.concatenate(out, axis=1)

    def lift_band(self):
        out = []
        for l in (1, 2, 3):
            one = self.place(l, 0, self.ny[l])
            out.append(np.einsum("cki,cif->ckf", one, self.lift_columns(l)))
        return np.concatenate(out, axis=2)

    def lift_columns(self, level):
        out = np.eye(self.ny[level])
        for l in range(level, 0, -1):
            out = out @ global_prolong(self.ny[l])
        return out.reshape(self.ny[level], self.m, self.w0).transpose(1, 0, 2)

    def lift_rows_of(self, level):
        w, tiles = self.tile[level], self.tiles[level]
        full = self.lift_columns(level).reshape(self.m, tiles, w, self.w0)
        out = np.zeros((self.m, 2, tiles, 2 * w, self.w0))
        for j in range(2):
            out[:, j, :, j * w : (j + 1) * w] = full
        return out

    def coarsest_shrink(self):
        nx5, ny5, ny4 = self.nx[5], self.ny[5], self.ny[4]
        columns = global_prolong(ny5).T
        width = round_up(ny4 + 2)
        out = np.zeros((nx5, width, nx5 * ny5))
        for i in range(nx5):
            out[i, 1 : 1 + ny4, i * ny5 : (i + 1) * ny5] = columns
        return bf(out.reshape(nx5 * width, nx5 * ny5))

    def coarsest_lift(self):
        rows, columns = global_prolong(self.nx[5]), global_prolong(self.ny[5])
        both = np.einsum("ia,jb->ijab", rows, columns)
        w, tiles = self.tile[4], self.tiles[4]
        both = both.reshape(self.nx[5] * self.ny[5], self.nx[4] // 2, 2, tiles, w)
        both = both.transpose(0, 1, 3, 2, 4)
        return bf(both.reshape(self.nx[5] * self.ny[5], self.nx[4] * self.ny[4]))

    def level_four_lift(self):
        pair = 2 * self.tile[4] * self.tiles[4]
        group = max(1, LANES // pair)
        width = group * pair
        rows = self.lift_rows_of(4).reshape(self.m, 2, pair, self.w0)
        out = np.zeros((self.m, group, 2, width, self.w0))
        for g in range(group):
            out[:, g, :, g * pair : (g + 1) * pair] = rows
        return bf(out), group


class Blocks:
    def __init__(self):
        self.parts, self.places, self.count = [], {}, 0

    def add(self, name, array):
        lead, (rows, columns) = array.shape[:-2], array.shape[-2:]
        high, wide = round_up(rows) // LANES, round_up(columns) // LANES
        out = np.zeros((math.prod(lead), high * LANES, wide * LANES), np.float32)
        out[:, :rows, :columns] = np.asarray(array, np.float32).reshape((-1, rows, columns))
        out = out.reshape(-1, high, LANES, wide, LANES).transpose(0, 1, 3, 2, 4)
        self.parts.append(out.reshape(-1, LANES, LANES))
        self.places[name] = (self.count, high, wide)
        self.count += len(self.parts[-1])

    def array(self):
        return jnp.asarray(bf(np.concatenate(self.parts, axis=0)))

    def get(self, ref, name, lead=0):
        base, high, wide = self.places[name]
        base = base + lead * (high * wide)
        rows = [
            jnp.concatenate([ref[base + i * wide + j] for j in range(wide)], axis=1)
            for i in range(high)
        ]
        return jnp.concatenate(rows, axis=0)


def split(value):
    high = value.astype(BF16)
    return high, (value - high.astype(F32)).astype(BF16)


def product(value, matrix):
    high, low = split(value)
    count = value.shape[0]
    both = jnp.dot(
        jnp.concatenate([high, low], axis=0), matrix, preferred_element_type=F32
    )
    return both[:count] + both[count:]


def shrink_rows(rows, count, halo):
    out = []
    for i in range(-1, count // 2 + 1):
        total = None
        for t, tap in enumerate(TAPS):
            j = 2 * i - 1 + t
            if -halo <= j < count + halo:
                term = rows[j + halo] * float(tap) if tap > 1 else rows[j + halo]
                total = term if total is None else total + term
        out.append(total)
    return out


def lift_rows(rows, first, last):
    out = []
    for f in range(first, last):
        i = f // 2
        other = i - 1 if f % 2 == 0 else i + 1
        out.append((rows[i + 1] * 3.0 + rows[other + 1]) * SHRINK)
    return out


def lane_index(rows):
    return lax.broadcasted_iota(jnp.int32, (rows, LANES), 1)


def assemble(pieces, width):
    total = 4 * (width + 2)
    tiles = [[] for _ in range(-(-total // LANES))]
    lane = lane_index(pieces[0][0].shape[0])
    for k, piece in enumerate(pieces):
        for q, value in enumerate(piece):
            start = k * (width + 2) + LANES * q
            count = min(LANES, width + 2 - LANES * q)
            shift, at = start % LANES, start // LANES
            rolled = pltpu.roll(value, shift, 1) if shift else value
            tiles[at].append((min(LANES, shift + count), rolled))
            if shift + count > LANES:
                tiles[at + 1].append((shift + count - LANES, rolled))
    out = []
    for segments in tiles:
        segments = sorted(segments, key=lambda s: -s[0])
        end, value = segments[0]
        if end < LANES:
            value = jnp.where(lane < end, value, 0.0)
        for end, part in segments[1:]:
            value = jnp.where(lane < end, part, value)
        out.append(value)
    return jnp.concatenate(out, axis=1).astype(BF16)[:, :total]


def solve(lhs, factor):
    return jnp.dot(lhs, factor, preferred_element_type=F32)


def kernel_call(body, out_shape, scratch=(), cost_us=1.0, out_space=pltpu.VMEM):
    whole = pl.BlockSpec(memory_space=pltpu.VMEM)
    result = pl.BlockSpec(memory_space=out_space)

    def call(*operands):
        return pl.pallas_call(
            body,
            out_shape=out_shape,
            in_specs=[whole] * len(operands),
            out_specs=jax.tree.map(lambda _: result, out_shape),
            scratch_shapes=list(scratch),
            compiler_params=pltpu.CompilerParams(vmem_limit_bytes=VMEM_BYTES),
            cost_estimate=pl.CostEstimate(
                flops=int(cost_us * 1e9), bytes_accessed=int(cost_us * 3e6), transcendentals=0
            ),
        )(*operands)

    return call


def shape(*dims):
    return jax.ShapeDtypeStruct(dims, F32)


def tap_matrix(row_lead, lane_lead, count, first, last):
    row = lax.broadcasted_iota(jnp.int32, (LANES, LANES), 0) - row_lead
    lane = lax.broadcasted_iota(jnp.int32, (LANES, LANES), 1) - lane_lead
    tap = row - 2 * lane + 3
    outer = jnp.logical_or(tap == 0, tap == 3)
    inner = jnp.logical_or(tap == 1, tap == 2)
    value = jnp.where(outer, 1.0, jnp.where(inner, 3.0, 0.0))
    value = jnp.where(jnp.logical_or(lane < first, lane > count + 1 - last), 0.0, value)
    return value.astype(BF16)


def place_sides(plan, slot_value, row, at):
    lane = lane_index(plan.rhs)
    chosen = jnp.logical_or(lane == at, lane == at + 1)
    return jnp.where(chosen, pltpu.roll(row, (at + 1) % LANES, 1), slot_value)


def column_ends(plan):
    c = lax.axis_index("py")
    return jnp.where(c == 0, 1, 0), jnp.where(c == plan.m - 1, 1, 0)


def write_halos(c, down, up, first_ref, second_ref):
    forward = jnp.bitwise_and(c, 2) != 0
    for k, (low, high) in enumerate(zip(down, up)):
        first_ref[k] = jnp.where(forward, low, high)
        second_ref[k] = jnp.where(forward, high, low)


def read_halos(plan, first_ref, second_ref):
    r, c = lax.axis_index("px"), lax.axis_index("py")
    forward = jnp.bitwise_and(c, 2) != 0
    above = jnp.where(r > 0, 1.0, 0.0).astype(F32)
    below = jnp.where(r < plan.n - 1, 1.0, 0.0).astype(F32)
    first, second = first_ref[...], second_ref[...]
    return jnp.where(forward, first, second) * above, jnp.where(forward, second, first) * below


def shrink_kernel(plan, out_ref):
    first, last = column_ends(plan)
    shrink = None
    for level in (1, 2, 3, 4):
        lead = 0 if level == 1 else plan.offset[level - 1] + 1
        step = tap_matrix(lead, plan.offset[level], plan.w[level], first, last)
        if shrink is None:
            shrink = step
        else:
            shrink = jnp.dot(shrink, step, preferred_element_type=F32).astype(BF16)
        out_ref[level - 1] = shrink


def restrict_kernel(plan, x_ref, shrink_ref, early_ref, outer_ref, first_ref, second_ref, rows_ref):
    r, c = lax.axis_index("px"), lax.axis_index("py")
    rhs, slots, h = plan.rhs, plan.slots, plan.h
    above = jnp.where(r > 0, 1.0, 0.0).astype(F32)
    below = jnp.where(r < plan.n - 1, 1.0, 0.0).astype(F32)
    x = [x_ref[pl.ds(row, rhs, stride=h[0]), :] for row in range(h[0])]
    rows, total = x, None
    for level in (1, 2, 3, 4):
        rows = shrink_rows(rows, h[level - 1], 0 if level == 1 else 1)
        rows[0] = rows[0] * above
        rows[-1] = rows[-1] * below
        part = product(jnp.concatenate(rows, axis=0), shrink_ref[level - 1])
        if total is None:
            total = part
        else:
            count = part.shape[0]
            total = jnp.concatenate([total[:count] + part, total[count:]], axis=0)
    lane = lane_index(slots * rhs)
    scale = jnp.where(lane < plan.offset[2], SHRINK, SHRINK**2)
    scale = jnp.where(lane < plan.offset[3], scale, SHRINK**3)
    total = total * jnp.where(lane < plan.offset[4], scale, SHRINK**4)
    own = [total[i * rhs : (i + 1) * rhs] for i in range(slots)]
    lane = lane_index(rhs)
    one, two, three = plan.offset[2:]
    inner = [own[2], own[3], own[4], own[5]]
    for k in range(2):
        value = inner[k]
        value = jnp.where(lane < two, value, 0.0)
        for j in range(h[0] // 2):
            value = place_sides(plan, value, x[k * (h[0] // 2) + j], two + 2 * j)
        odd_row, end = own[6 + k], plan.tail + plan.first - plan.rest
        moved = pltpu.roll(odd_row, (plan.tail - plan.rest) % LANES, 1)
        chosen = jnp.logical_and(lane >= plan.tail, lane < end)
        early_ref[k] = jnp.where(chosen, moved, value)
        moved = pltpu.roll(odd_row, plan.first, 1)
        early_ref[2 + k] = jnp.where(lane < plan.first, inner[2 + k], moved)
    outer = [own[0], own[1]]
    for k in range(2):
        value = jnp.where(lane < two, own[h[2] + k], own[h[3] + k])
        outer.append(jnp.where(lane < one, own[h[1] + k], value))
    for k in range(4):
        outer_ref[k] = outer[k]
    third = pltpu.roll(own[2], LANES - three, 1)
    down = [x[-1], jnp.where(lane < three, outer[2], own[0])]
    down.append(jnp.where(lane < one, third, jnp.where(lane < three, outer[3], own[1])))
    up = [x[0], jnp.where(lane < one, third, own[0]), own[1]]
    write_halos(c, down, up, first_ref, second_ref)
    for i, row in enumerate(x):
        rows_ref[i] = row


def merge_kernel(plan, outer_ref, shrink_ref, first_ref, second_ref, out_ref):
    r, rhs = lax.axis_index("px"), plan.rhs
    lane = lane_index(rhs)
    above, below = read_halos(plan, first_ref, second_ref)
    one, two, three = plan.offset[2:]
    edge = product(jnp.concatenate([above[0], below[0]], axis=0), shrink_ref[0]) * SHRINK
    added = [
        above[1],
        jnp.where(lane < one, edge[:rhs], above[2]),
        jnp.where(lane < one, edge[rhs:], below[1]),
        below[2],
    ]
    even = lax.rem(r, 2) == 0
    own = [outer_ref[k] for k in range(3)]
    partner = [jnp.where(even, below[k], above[k]) for k in (1, 2)]
    third = jnp.where(even, below[1], above[2])
    partner.append(pltpu.roll(third, three, 1))
    low = [jnp.where(even, a, b) for a, b in zip(own, partner)]
    high = [jnp.where(even, b, a) for a, b in zip(own, partner)]
    sums = [low[0], low[1] + high[0], low[2] + high[1], high[2]]
    for k in range(4):
        value = jnp.where(lane < three, outer_ref[k] + added[k], sums[k])
        out_ref[k * rhs : (k + 1) * rhs] = value
    sides = place_sides(plan, jnp.zeros((rhs, LANES), F32), above[0], 0)
    sides = place_sides(plan, sides, below[0], 2)
    total = None
    for k in range(rhs // 8):
        part = sides[8 * k : 8 * (k + 1)]
        part = pltpu.roll(part, 4 * k, 1) if k else part
        total = part if total is None else total + part
    out_ref[4 * rhs :] = total


def banded(bands, matrices):
    return product(jnp.concatenate(bands, axis=1), jnp.concatenate(matrices, axis=0))


def owners(plan):
    c = lax.axis_index("py")
    return [jnp.bitwise_xor(c, k) for k in range(plan.m)]


def gather_kernel(plan, blocks, block_ref, *refs):
    band_refs, out_ref = refs[:-1], refs[-1]
    values, matrices = [], []
    for band, owner in zip(band_refs, owners(plan)):
        for j in range(4):
            values.append(band[j * plan.rhs : (j + 1) * plan.rhs])
            matrices.append(blocks.get(block_ref, "four", 4 * owner + j))
    out_ref[...] = banded(values, matrices)


def level_rows(plan, level, early_refs, late_refs, blocks, block_ref):
    rhs, values = plan.rhs, []
    lane = lane_index(rhs)
    for early, late in zip(early_refs, late_refs):
        outer = [late[i * rhs : (i + 1) * rhs] for i in range(4)]
        inner = []
        if level == 1:
            inner = [early[k] for k in range(4)]
            for k in range(2):
                begin = pltpu.roll(early[2 + k], plan.rest, 1)
                end = pltpu.roll(early[k], (plan.rest - plan.tail) % LANES, 1)
                inner.append(jnp.where(lane < plan.rest, begin, end))
        elif level == 2:
            inner = [early[k] for k in range(2)]
        values.append(jnp.concatenate(outer[:2] + inner + outer[2:], axis=0))
    matrices = [blocks.get(block_ref, f"place{level}", owner) for owner in owners(plan)]
    whole = jnp.dot(
        jnp.concatenate(values, axis=1).astype(BF16), jnp.concatenate(matrices, axis=0),
        preferred_element_type=F32,
    )
    return [whole[i * rhs : (i + 1) * rhs] for i in range(plan.h[level] + 2)]


def assemble_tiles(rows, t):
    rhs, count = rows[0].shape[0], rows[0].shape[1] // LANES
    lane = lane_index(rhs)

    def rolled(k, tile):
        if not 0 <= tile < count:
            return jnp.zeros((rhs, LANES), F32)
        return pltpu.roll(rows[k][:, tile * LANES : (tile + 1) * LANES], 2 * k + 1, 1)

    out = []
    for k in range(5):
        if k < 4:
            value = jnp.where(lane == 2 * k, rolled(k, t - 1), rolled(k, t))
        else:
            value = jnp.zeros((rhs, LANES), F32)
        if k > 0:
            value = jnp.where(lane == 2 * k - 1, rolled(k - 1, t + 1), value)
            value = jnp.where(lane < 2 * k - 1, rolled(k - 1, t), value)
        out.append(value)
    return jnp.concatenate(out, axis=1).astype(BF16)[:, : 4 * (LANES + 2)]


def solve_pairs(plan, level, rows, pairs, factor_ref):
    w, solved = plan.tile[level], []
    for t in range(plan.tiles[level]):
        solved.append([])
        for at, b in pairs:
            window = rows[at : at + 4]
            if w == LANES:
                lhs = assemble_tiles(window, t)
            else:
                lhs = assemble([[row] for row in window], w)
            solved[t].append(solve(lhs, factor_ref[b, t]))
    return solved


def lift_pairs(plan, level, solved, blocks, block_ref):
    c, w = lax.axis_index("py"), plan.tile[level]
    name, count = f"lift{level}", len(solved[0]) * plan.rhs
    stacked = [jnp.concatenate(values, axis=0) for values in solved]
    if w % LANES == 0:
        both = [
            jnp.concatenate([v[:, j * w : (j + 1) * w] for v in stacked], axis=1)
            for j in range(2)
        ]
        both = product(jnp.concatenate(both, axis=0), blocks.get(block_ref, name, c))
        return [both[:count], both[count:]]
    row = jnp.concatenate(stacked, axis=1)
    return [product(row, blocks.get(block_ref, name, 2 * c + j)) for j in range(2)]


def coarse_kernel(plan, blocks, block_ref, *refs):
    factors, outs = refs[:3], refs[3 + 2 * plan.m :]
    early, late = refs[3 : 3 + plan.m], refs[3 + plan.m : 3 + 2 * plan.m]
    c, rhs = lax.axis_index("py"), plan.rhs
    down, up = [], []
    for level in (1, 2, 3):
        rows = level_rows(plan, level, early, late, blocks, block_ref)
        w, count = plan.tile[level], plan.h[level] // 2
        pairs = [(2 * b, b) for b in sorted({0, count - 1})]
        if level == 1:
            for i, row in enumerate(rows[2:-2]):
                outs[3][i] = row
        else:
            pairs = [(2 * b, b) for b in range(count)]
        solved = solve_pairs(plan, level, rows, pairs, factors[level - 1])
        lifted = lift_pairs(plan, level, solved, blocks, block_ref)
        for b in range(len(pairs)):
            for j in range(2):
                outs[level - 1][2 * b + j] = lifted[j][b * rhs : (b + 1) * rhs]
        for j, (edge, at) in enumerate(((up, 0), (down, -1))):
            for value in solved:
                if w % LANES == 0:
                    edge.append(value[at][:, j * w : (j + 1) * w])
                else:
                    edge.append(pltpu.roll(value[at], LANES - w, 1) if j else value[at])
    edges = [jnp.concatenate(edge, axis=1) for edge in (down, up)]
    picked = product(jnp.concatenate(edges, axis=0), blocks.get(block_ref, "pick", c))
    write_halos(c, [picked[:rhs]], [picked[rhs:]], outs[4], outs[5])


def inner_kernel(plan, blocks, block_ref, factor_ref, rows_ref, out_ref):
    rhs, count = plan.rhs, plan.h[1] // 2
    rows = [rows_ref[i] for i in range(rows_ref.shape[0])]
    pairs = [(2 * (b - 1), b) for b in range(1, count - 1)]
    solved = solve_pairs(plan, 1, rows, pairs, factor_ref)
    lifted = lift_pairs(plan, 1, solved, blocks, block_ref)
    for b in range(len(pairs)):
        for j in range(2):
            out_ref[2 * b + j] = lifted[j][b * rhs : (b + 1) * rhs]


def fine_kernel(plan, blocks, block_ref, rows_ref, first_ref, second_ref, factor_ref, *refs):
    early, late, out_ref = refs[: plan.m], refs[plan.m : 2 * plan.m], refs[2 * plan.m]
    c = lax.axis_index("py")
    rhs, h0, w0 = plan.rhs, plan.h0, plan.w0
    above, below = read_halos(plan, first_ref, second_ref)
    values, matrices = [], []
    left = blocks.get(block_ref, "halo", 0)
    right = blocks.get(block_ref, "halo", 1)
    lane = lane_index(rhs)
    spot = plan.offset[3] + plan.h0
    for inner, outer, owner in zip(early, late, owners(plan)):
        from_left = jnp.where(owner == c - 1, 1.0, 0.0).astype(BF16)
        from_right = jnp.where(owner == c + 1, 1.0, 0.0).astype(BF16)
        matrices.append(left * from_left + right * from_right)
        packed = outer[4 * rhs :]
        sides = [pltpu.roll(packed, (spot - 4 * k) % LANES, 1) for k in range(rhs // 8)]
        sides = jnp.concatenate(sides, axis=0)
        pair = []
        for k in range(2):
            moved = pltpu.roll(sides, LANES - 2 * k, 1) if k else sides
            chosen = jnp.logical_or(lane == spot, lane == spot + 1)
            pair.append(jnp.where(chosen, moved, inner[k]))
        values.append(jnp.concatenate(pair, axis=0).astype(BF16))
    halo = jnp.dot(
        jnp.concatenate(values, axis=1), jnp.concatenate(matrices, axis=0),
        preferred_element_type=F32,
    )
    lane = lane_index(rhs)
    rows, sides = [], []
    for row in range(-1, h0 + 1):
        if row == -1:
            rows.append(above[0])
        elif row == h0:
            rows.append(below[0])
        else:
            rows.append(rows_ref[row])
        if row < 0 or row == h0:
            slot, part = (0 if row < 0 else 1), plan.sides - 1
        else:
            slot, part = divmod(row, h0 // 2)
        sides.append(halo[slot * rhs : (slot + 1) * rhs, part * LANES : (part + 1) * LANES])
    for b in range(h0 // 2):
        tiles, before = [], None
        for k in range(5):
            if k < 4:
                row, side = rows[2 * b + k], sides[2 * b + k]
                rolled = pltpu.roll(row, 2 * k + 1, 1)
                value = jnp.where(lane == 2 * k, side, rolled)
            else:
                value = jnp.zeros((rhs, LANES), F32)
            if before is not None:
                old, old_side = before
                value = jnp.where(lane == 2 * k - 1, old_side, value)
                value = jnp.where(lane < 2 * k - 1, old, value)
            tiles.append(value)
            before = (rolled, side)
        lhs = jnp.concatenate(tiles, axis=1).astype(BF16)[:, : 4 * (w0 + 2)]
        solved = solve(lhs, factor_ref[b, 0])
        for j in range(2):
            out_ref[2 * b + j] = solved[:, j * w0 : (j + 1) * w0]


def whole_kernel(plan, group, blocks, block_ref, four_ref, inverse_ref, *refs):
    count = plan.n // 2
    gathered, out_ref, pair_ref, four_rows = refs[:count], refs[count], refs[-2], refs[-1]
    r, c = lax.axis_index("px"), lax.axis_index("py")
    rhs, ny4 = plan.rhs, plan.ny[4]
    nx4, nx5 = plan.nx[4], plan.nx[5]
    odd = jnp.bitwise_and(c, 1)
    for k, block in enumerate(gathered):
        if k == 0 or (k == count - 1 and k % 2):
            partner = 2 * k
        elif k % 2:
            partner = 2 * (k + odd)
        else:
            partner = 2 * (k - odd)
        pair_ref[jnp.bitwise_xor(r, partner) // 2] = block[...]
    lane = lane_index(rhs)
    inside = jnp.logical_and(lane >= 1, lane <= ny4)

    def part_row(pair, j):
        tile, start = divmod(j * ny4, LANES)
        value = pair_ref[pair, :, tile * LANES : (tile + 1) * LANES]
        return jnp.where(inside, pltpu.roll(value, (1 - start) % LANES, 1), 0.0)

    zero = jnp.zeros((rhs, LANES), F32)
    rows = [zero]
    for i in range(nx4):
        value = part_row(i // 2, 1 + i % 2)
        if i % 2 == 0 and i > 0:
            value = value + part_row(i // 2 - 1, 3)
        if i % 2 == 1 and i < nx4 - 1:
            value = value + part_row(i // 2 + 1, 0)
        rows.append(value)
    rows.append(zero)
    five = shrink_rows(rows, nx4, 1)[1:-1]
    flat = product(jnp.concatenate(five, axis=1), blocks.get(block_ref, "shrink5")) * SHRINK
    flat = flat[:, : inverse_ref.shape[0]]
    part_five = jnp.dot(flat.astype(BF16), inverse_ref[...], preferred_element_type=F32)
    spread = blocks.get(block_ref, "lift5")[: part_five.shape[1], : nx4 * ny4]
    lifted = product(part_five, spread) * SHRINK
    w, tiles = plan.tile[4], plan.tiles[4]
    parts = []
    for b in range(nx4 // 2):
        for t in range(tiles):
            pieces = []
            for k in range(4):
                lanes = range(t * w, t * w + w + 2, LANES)
                pieces.append([rows[2 * b + k][:, lo : lo + LANES] for lo in lanes])
            lhs = assemble(pieces, w)
            parts.append(
                lax.dot_general(
                    lhs, four_ref[b, t], (((1,), (1,)), ((), ())), preferred_element_type=F32
                )
            )
    correction = jnp.concatenate(parts, axis=1) + lifted
    width = group * 2 * w * tiles
    bands = nx4 // 2 // group
    stacked = jnp.concatenate(
        [correction[:, i * width : (i + 1) * width] for i in range(bands)], axis=0
    )
    four_rows[0] = jnp.zeros((rhs, LANES), F32)
    four_rows[nx4 + 1] = jnp.zeros((rhs, LANES), F32)
    for g in range(group):
        for j in range(2):
            value = product(stacked, blocks.get(block_ref, "lift4", (c * group + g) * 2 + j))
            for i in range(bands):
                four_rows[1 + 2 * (i * group + g) + j] = value[i * rhs : (i + 1) * rhs]
    for k in range(3):
        out_ref[k] = four_rows[r + k]


def final_kernel(plan, blocks, block_ref, fine_ref, one_ref, inner_ref, two_ref, three_ref,
                 four_ref, first_ref, second_ref, out_ref, whole_ref, semaphores):
    r, rhs = lax.axis_index("px"), plan.rhs
    above = jnp.where(r > 0, 1.0, 0.0).astype(F32)
    below = jnp.where(r < plan.n - 1, 1.0, 0.0).astype(F32)
    halos = read_halos(plan, first_ref, second_ref)
    halo = product(
        jnp.concatenate([halos[0][0], halos[1][0]], axis=0),
        blocks.get(block_ref, "band", lax.axis_index("py")),
    )
    from_above, from_below = [
        [halo[k * rhs : (k + 1) * rhs, l * plan.w0 : (l + 1) * plan.w0] for l in range(3)]
        for k in range(2)
    ]
    copies = []
    for part in range(rhs // 8):
        own = slice(8 * part, 8 * (part + 1))
        rows = [four_ref[k, own] for k in range(3)]
        for level, own_ref in ((3, three_ref), (2, two_ref), (1, one_ref)):
            height = plan.h[level]
            lifted = lift_rows(rows, -1, height + 1)
            rows = [lifted[0] * above + from_above[level - 1][own]]
            parts = [own_ref[i, own] for i in range(own_ref.shape[0])]
            if level == 1:
                parts[2:2] = [inner_ref[i, own] for i in range(inner_ref.shape[0])]
            rows += [lifted[i + 1] + parts[i] for i in range(height)]
            rows += [lifted[-1] * below + from_below[level - 1][own]]
        lifted = lift_rows(rows, 0, plan.h0)
        start, count = 8 * part * plan.h0, 8 * plan.h0
        for row in range(plan.h0):
            value = lifted[row] + fine_ref[row, own]
            whole_ref[pl.ds(start + row, 8, stride=plan.h0), :] = value
        span = pl.ds(start, count)
        copies.append(
            pltpu.make_async_copy(whole_ref.at[span], out_ref.at[span], semaphores.at[part])
        )
        copies[-1].start()
    for copy in copies:
        copy.wait()


def per_device(mesh_shape, residual, factor_fine, factor_one, factor_two, factor_three,
               factor_four, coarse_inverse):
    factors = [factor_fine, factor_one, factor_two, factor_three, factor_four]
    plan = Plan(mesh_shape, residual.shape, [f.shape for f in factors])
    n, m, rhs, h, h0 = plan.n, plan.m, plan.rhs, plan.h, plan.h0
    x = residual.reshape(rhs * h0, plan.w0)

    def trade(first, second):
        def target(i, c):
            after = i + 1 if c & 2 else i - 1
            return (after, c) if 0 <= after < n else (i, c ^ 2)

        ring = []
        for i in range(n):
            for c in range(m):
                row, column = target(i, c)
                ring.append((i * m + c, row * m + column))
        back = [(b, a) for a, b in ring]
        return lax.ppermute(first, ("px", "py"), ring), lax.ppermute(second, ("px", "py"), back)

    def swap(value, bits):
        return lax.ppermute(value, "py", [(i, i ^ bits) for i in range(m)])

    blocks = Blocks()
    blocks.add("four", plan.place_four())
    blocks.add("pick", plan.pick_band())
    blocks.add("band", plan.lift_band())
    for l in (1, 2, 3):
        blocks.add(f"place{l}", plan.place_whole(l))
        if plan.tile[l] % LANES == 0:
            blocks.add(f"lift{l}", plan.lift_columns(l))
        else:
            lifted = plan.lift_rows_of(l)
            blocks.add(f"lift{l}", lifted.reshape(m, 2, -1, plan.w0))
    lifted, group = plan.level_four_lift()
    blocks.add("lift4", lifted)
    blocks.add("halo", plan.halo_lanes())
    blocks.add("shrink5", plan.coarsest_shrink())
    blocks.add("lift5", plan.coarsest_lift())
    matrices = blocks.array()

    shrink = kernel_call(
        functools.partial(shrink_kernel, plan),
        jax.ShapeDtypeStruct((4, LANES, LANES), BF16), cost_us=4.0,
    )()
    early, outer, first, second, rows = kernel_call(
        functools.partial(restrict_kernel, plan),
        (shape(4, rhs, LANES), shape(4, rhs, LANES), shape(3, rhs, LANES), shape(3, rhs, LANES),
         shape(h0, rhs, plan.w0)),
    )(x, shrink)
    first, second = trade(first, second)
    late = kernel_call(functools.partial(merge_kernel, plan), shape(4 * rhs + 8, LANES))(
        outer, shrink, first, second
    )

    def spread(value):
        bands = {0: value}
        bit = m // 2
        while bit:
            bands.update({k ^ bit: swap(band, bit) for k, band in list(bands.items())})
            bit //= 2
        return [bands[k] for k in range(m)]

    early, late = spread(early), spread(late)

    pairs = kernel_call(
        functools.partial(gather_kernel, plan, blocks), shape(rhs, 4 * plan.ny[4]), cost_us=0.3
    )(matrices, *late)
    order, gathered = list(range(1, n // 2)), [pairs]
    fetched = []
    for k in range(0, len(order), 2):
        even, odd = order[k], order[min(k + 1, len(order) - 1)]
        fetched.append(
            lax.ppermute(
                pairs, ("px", "py"),
                [(i * m + c, (i ^ (2 * (odd if c % 2 else even))) * m + c)
                 for i in range(n) for c in range(m)],
            )
        )
    late, pairs = lax.optimization_barrier((late, pairs))
    for k, value in enumerate(fetched):
        gathered.append(value)
        if 2 * k + 1 < len(order):
            gathered.append(swap(value, 1))

    one, two, three, inner, low, high = kernel_call(
        functools.partial(coarse_kernel, plan, blocks),
        (shape(4, rhs, LANES), shape(h[2], rhs, LANES), shape(h[3], rhs, LANES),
         shape(h[1] - 2, rhs, plan.ny[1]))
        + (shape(1, rhs, LANES), shape(1, rhs, LANES)),
        cost_us=2.5,
    )(matrices, factor_one, factor_two, factor_three, *early, *late)
    low, high = trade(low, high)
    inner = kernel_call(
        functools.partial(inner_kernel, plan, blocks), shape(h[1] - 4, rhs, LANES), cost_us=0.6
    )(matrices, factor_one, inner)

    fine = kernel_call(
        functools.partial(fine_kernel, plan, blocks), shape(h0, rhs, plan.w0)
    )(matrices, rows, first, second, factor_fine, *early, *late)
    four = kernel_call(
        functools.partial(whole_kernel, plan, group, blocks),
        shape(3, rhs, LANES),
        scratch=(
            pltpu.VMEM((n // 2, rhs, 4 * plan.ny[4]), F32),
            pltpu.VMEM((plan.nx[4] + 2, rhs, LANES), F32),
        ),
    )(matrices, jnp.swapaxes(factor_four, 2, 3), coarse_inverse, *gathered)
    out = kernel_call(
        functools.partial(final_kernel, plan, blocks), shape(rhs * h0, plan.w0),
        scratch=(pltpu.VMEM((rhs * h0, plan.w0), F32), pltpu.SemaphoreType.DMA((rhs // 8,))),
        out_space=pl.ANY,
    )(
        matrices, fine, one, inner, two, three, four, low, high
    )
    return out.reshape(rhs, h0, plan.w0)


def solution(mesh):
    placed = (
        P(None, "px", "py"),
        P("px", "py", None, None),
        P("px", None, None, None),
        P("px", None, None, None),
        P("px", None, None, None),
        P(),
        P(),
    )
    return jax.shard_map(
        functools.partial(per_device, dict(mesh.shape)),
        mesh=mesh, in_specs=placed, out_specs=P(None, "px", "py"), check_vma=False,
    )
```

```python
import functools
import math

import jax
import jax.numpy as jnp
import numpy as np
from jax import lax
from jax.experimental import pallas as pl
from jax.experimental.pallas import tpu as pltpu
from jax.sharding import PartitionSpec as P

F32 = jnp.float32
BF16 = jnp.bfloat16
LANES = 128
SHRINK = 1.0 / 20.0
TAPS = (1, 3, 3, 1)
VMEM_BYTES = 24 * 1024 * 1024


def round_up(value, unit=LANES):
    return -(-value // unit) * unit


def global_prolong(coarse):
    out = np.zeros((coarse, 2 * coarse))
    for i in range(coarse):
        out[i, 2 * i] += 3
        out[i, 2 * i + 1] += 3
        if i > 0:
            out[i, 2 * i - 1] += 1
        if i + 1 < coarse:
            out[i, 2 * i + 2] += 1
    return out


def bf(array):
    return np.asarray(array, np.float32).astype(jnp.bfloat16)


class Plan:
    def __init__(self, mesh_shape, residual, factors):
        self.n, self.m = mesh_shape["px"], mesh_shape["py"]
        self.rhs, self.h0, self.w0 = residual
        self.h = [self.h0 >> l for l in range(5)]
        self.w = [self.w0 >> l for l in range(5)]
        self.ny = [self.w0 * self.m >> l for l in range(6)]
        self.nx = [self.h0 * self.n >> l for l in range(6)]
        self.tile = [f[3] // 2 for f in factors]
        self.tiles = [f[1] for f in factors]
        self.slots = self.h[1] + 2
        self.offset = [None, 0]
        for l in (2, 3, 4):
            self.offset.append(self.offset[-1] + self.w[l - 1] + 2)
        self.sides = self.h0 // 2 + 1
        self.first = self.w[1] + 2
        self.rest = LANES - self.first
        self.tail = self.offset[3] + 2 * self.sides

    def place(self, level, lead, width, at=0):
        out = np.zeros((self.m, LANES, width))
        for c in range(self.m):
            for k in range(self.w[level] + 2):
                column = self.w[level] * c - 1 + k
                if -lead <= column < self.ny[level]:
                    out[c, self.offset[level] + k, at + column + lead] = 1
        return out

    def place_whole(self, level):
        if self.tile[level] == LANES:
            return self.place(level, 0, self.ny[level])
        return self.place(level, 1, round_up(self.ny[level] + 2))

    def place_four(self):
        rows = [self.place(4, 0, 4 * self.ny[4], j * self.ny[4]) for j in range(4)]
        return np.stack(rows, axis=1)

    def pick_band(self):
        out = []
        for l in (1, 2, 3):
            pick = np.zeros((self.m, round_up(self.ny[l]), LANES))
            one = self.place(l, 0, self.ny[l])
            pick[:, : self.ny[l]] = one.transpose(0, 2, 1)
            out.append(pick)
        return np.concatenate(out, axis=1)

    def lift_band(self):
        out = []
        for l in (1, 2, 3):
            one = self.place(l, 0, self.ny[l])
            out.append(np.einsum("cki,cif->ckf", one, self.lift_columns(l)))
        return np.concatenate(out, axis=2)

    def lift_columns(self, level):
        out = np.eye(self.ny[level])
        for l in range(level, 0, -1):
            out = out @ global_prolong(self.ny[l])
        return out.reshape(self.ny[level], self.m, self.w0).transpose(1, 0, 2)

    def lift_rows_of(self, level):
        w, tiles = self.tile[level], self.tiles[level]
        full = self.lift_columns(level).reshape(self.m, tiles, w, self.w0)
        out = np.zeros((self.m, 2, tiles, 2 * w, self.w0))
        for j in range(2):
            out[:, j, :, j * w : (j + 1) * w] = full
        return out

    def coarsest_shrink(self):
        nx5, ny5, ny4 = self.nx[5], self.ny[5], self.ny[4]
        columns = global_prolong(ny5).T
        width = round_up(ny4 + 2)
        out = np.zeros((nx5, width, nx5 * ny5))
        for i in range(nx5):
            out[i, 1 : 1 + ny4, i * ny5 : (i + 1) * ny5] = columns
        return bf(out.reshape(nx5 * width, nx5 * ny5))

    def coarsest_lift(self):
        rows, columns = global_prolong(self.nx[5]), global_prolong(self.ny[5])
        both = np.einsum("ia,jb->ijab", rows, columns)
        w, tiles = self.tile[4], self.tiles[4]
        both = both.reshape(self.nx[5] * self.ny[5], self.nx[4] // 2, 2, tiles, w)
        both = both.transpose(0, 1, 3, 2, 4)
        return bf(both.reshape(self.nx[5] * self.ny[5], self.nx[4] * self.ny[4]))

    def level_four_lift(self):
        pair = 2 * self.tile[4] * self.tiles[4]
        group = max(1, LANES // pair)
        width = group * pair
        rows = self.lift_rows_of(4).reshape(self.m, 2, pair, self.w0)
        out = np.zeros((self.m, group, 2, width, self.w0))
        for g in range(group):
            out[:, g, :, g * pair : (g + 1) * pair] = rows
        return bf(out), group


class Blocks:
    def __init__(self):
        self.parts, self.places, self.count = [], {}, 0

    def add(self, name, array):
        lead, (rows, columns) = array.shape[:-2], array.shape[-2:]
        high, wide = round_up(rows) // LANES, round_up(columns) // LANES
        out = np.zeros((math.prod(lead), high * LANES, wide * LANES), np.float32)
        out[:, :rows, :columns] = np.asarray(array, np.float32).reshape((-1, rows, columns))
        out = out.reshape(-1, high, LANES, wide, LANES).transpose(0, 1, 3, 2, 4)
        self.parts.append(out.reshape(-1, LANES, LANES))
        self.places[name] = (self.count, high, wide)
        self.count += len(self.parts[-1])

    def array(self):
        return jnp.asarray(bf(np.concatenate(self.parts, axis=0)))

    def get(self, ref, name, lead=0):
        base, high, wide = self.places[name]
        base = base + lead * (high * wide)
        rows = [
            jnp.concatenate([ref[base + i * wide + j] for j in range(wide)], axis=1)
            for i in range(high)
        ]
        return jnp.concatenate(rows, axis=0)


def split(value):
    high = value.astype(BF16)
    return high, (value - high.astype(F32)).astype(BF16)


def product(value, matrix):
    high, low = split(value)
    count = value.shape[0]
    both = jnp.dot(
        jnp.concatenate([high, low], axis=0), matrix, preferred_element_type=F32
    )
    return both[:count] + both[count:]


def shrink_rows(rows, count, halo):
    out = []
    for i in range(-1, count // 2 + 1):
        total = None
        for t, tap in enumerate(TAPS):
            j = 2 * i - 1 + t
            if -halo <= j < count + halo:
                term = rows[j + halo] * float(tap) if tap > 1 else rows[j + halo]
                total = term if total is None else total + term
        out.append(total)
    return out


def lift_rows(rows, first, last):
    out = []
    for f in range(first, last):
        i = f // 2
        other = i - 1 if f % 2 == 0 else i + 1
        out.append((rows[i + 1] * 3.0 + rows[other + 1]) * SHRINK)
    return out


def lane_index(rows):
    return lax.broadcasted_iota(jnp.int32, (rows, LANES), 1)


def assemble(pieces, width):
    total = 4 * (width + 2)
    tiles = [[] for _ in range(-(-total // LANES))]
    lane = lane_index(pieces[0][0].shape[0])
    for k, piece in enumerate(pieces):
        for q, value in enumerate(piece):
            start = k * (width + 2) + LANES * q
            count = min(LANES, width + 2 - LANES * q)
            shift, at = start % LANES, start // LANES
            rolled = pltpu.roll(value, shift, 1) if shift else value
            tiles[at].append((min(LANES, shift + count), rolled))
            if shift + count > LANES:
                tiles[at + 1].append((shift + count - LANES, rolled))
    out = []
    for segments in tiles:
        segments = sorted(segments, key=lambda s: -s[0])
        end, value = segments[0]
        if end < LANES:
            value = jnp.where(lane < end, value, 0.0)
        for end, part in segments[1:]:
            value = jnp.where(lane < end, part, value)
        out.append(value)
    return jnp.concatenate(out, axis=1).astype(BF16)[:, :total]


def solve(lhs, factor):
    return jnp.dot(lhs, factor, preferred_element_type=F32)


def kernel_call(body, out_shape, scratch=(), cost_us=1.0, out_space=pltpu.VMEM):
    whole = pl.BlockSpec(memory_space=pltpu.VMEM)
    result = pl.BlockSpec(memory_space=out_space)

    def call(*operands):
        return pl.pallas_call(
            body,
            out_shape=out_shape,
            in_specs=[whole] * len(operands),
            out_specs=jax.tree.map(lambda _: result, out_shape),
            scratch_shapes=list(scratch),
            compiler_params=pltpu.CompilerParams(vmem_limit_bytes=VMEM_BYTES),
            cost_estimate=pl.CostEstimate(
                flops=int(cost_us * 1e9), bytes_accessed=int(cost_us * 3e6), transcendentals=0
            ),
        )(*operands)

    return call


def shape(*dims):
    return jax.ShapeDtypeStruct(dims, F32)


def tap_matrix(row_lead, lane_lead, count, first, last):
    row = lax.broadcasted_iota(jnp.int32, (LANES, LANES), 0) - row_lead
    lane = lax.broadcasted_iota(jnp.int32, (LANES, LANES), 1) - lane_lead
    tap = row - 2 * lane + 3
    outer = jnp.logical_or(tap == 0, tap == 3)
    inner = jnp.logical_or(tap == 1, tap == 2)
    value = jnp.where(outer, 1.0, jnp.where(inner, 3.0, 0.0))
    value = jnp.where(jnp.logical_or(lane < first, lane > count + 1 - last), 0.0, value)
    return value.astype(BF16)


def place_sides(plan, slot_value, row, at):
    lane = lane_index(plan.rhs)
    chosen = jnp.logical_or(lane == at, lane == at + 1)
    return jnp.where(chosen, pltpu.roll(row, (at + 1) % LANES, 1), slot_value)


def column_ends(plan):
    c = lax.axis_index("py")
    return jnp.where(c == 0, 1, 0), jnp.where(c == plan.m - 1, 1, 0)


def write_halos(c, down, up, first_ref, second_ref):
    forward = jnp.bitwise_and(c, 2) != 0
    for k, (low, high) in enumerate(zip(down, up)):
        first_ref[k] = jnp.where(forward, low, high)
        second_ref[k] = jnp.where(forward, high, low)


def read_halos(plan, first_ref, second_ref):
    r, c = lax.axis_index("px"), lax.axis_index("py")
    forward = jnp.bitwise_and(c, 2) != 0
    above = jnp.where(r > 0, 1.0, 0.0).astype(F32)
    below = jnp.where(r < plan.n - 1, 1.0, 0.0).astype(F32)
    first, second = first_ref[...], second_ref[...]
    return jnp.where(forward, first, second) * above, jnp.where(forward, second, first) * below


def shrink_kernel(plan, out_ref):
    first, last = column_ends(plan)
    shrink = None
    for level in (1, 2, 3, 4):
        lead = 0 if level == 1 else plan.offset[level - 1] + 1
        step = tap_matrix(lead, plan.offset[level], plan.w[level], first, last)
        if shrink is None:
            shrink = step
        else:
            shrink = jnp.dot(shrink, step, preferred_element_type=F32).astype(BF16)
        out_ref[level - 1] = shrink


def restrict_kernel(plan, x_ref, shrink_ref, early_ref, outer_ref, first_ref, second_ref, rows_ref):
    r, c = lax.axis_index("px"), lax.axis_index("py")
    rhs, slots, h = plan.rhs, plan.slots, plan.h
    above = jnp.where(r > 0, 1.0, 0.0).astype(F32)
    below = jnp.where(r < plan.n - 1, 1.0, 0.0).astype(F32)
    x = [x_ref[pl.ds(row, rhs, stride=h[0]), :] for row in range(h[0])]
    rows, total = x, None
    for level in (1, 2, 3, 4):
        rows = shrink_rows(rows, h[level - 1], 0 if level == 1 else 1)
        rows[0] = rows[0] * above
        rows[-1] = rows[-1] * below
        part = product(jnp.concatenate(rows, axis=0), shrink_ref[level - 1])
        if total is None:
            total = part
        else:
            count = part.shape[0]
            total = jnp.concatenate([total[:count] + part, total[count:]], axis=0)
    lane = lane_index(slots * rhs)
    scale = jnp.where(lane < plan.offset[2], SHRINK, SHRINK**2)
    scale = jnp.where(lane < plan.offset[3], scale, SHRINK**3)
    total = total * jnp.where(lane < plan.offset[4], scale, SHRINK**4)
    own = [total[i * rhs : (i + 1) * rhs] for i in range(slots)]
    lane = lane_index(rhs)
    one, two, three = plan.offset[2:]
    inner = [own[2], own[3], own[4], own[5]]
    for k in range(2):
        value = inner[k]
        value = jnp.where(lane < two, value, 0.0)
        for j in range(h[0] // 2):
            value = place_sides(plan, value, x[k * (h[0] // 2) + j], two + 2 * j)
        odd_row, end = own[6 + k], plan.tail + plan.first - plan.rest
        moved = pltpu.roll(odd_row, (plan.tail - plan.rest) % LANES, 1)
        chosen = jnp.logical_and(lane >= plan.tail, lane < end)
        early_ref[k] = jnp.where(chosen, moved, value)
        moved = pltpu.roll(odd_row, plan.first, 1)
        early_ref[2 + k] = jnp.where(lane < plan.first, inner[2 + k], moved)
    outer = [own[0], own[1]]
    for k in range(2):
        value = jnp.where(lane < two, own[h[2] + k], own[h[3] + k])
        outer.append(jnp.where(lane < one, own[h[1] + k], value))
    for k in range(4):
        outer_ref[k] = outer[k]
    third = pltpu.roll(own[2], LANES - three, 1)
    down = [x[-1], jnp.where(lane < three, outer[2], own[0])]
    down.append(jnp.where(lane < one, third, jnp.where(lane < three, outer[3], own[1])))
    up = [x[0], jnp.where(lane < one, third, own[0]), own[1]]
    write_halos(c, down, up, first_ref, second_ref)
    for i, row in enumerate(x):
        rows_ref[i] = row


def merge_kernel(plan, outer_ref, shrink_ref, first_ref, second_ref, out_ref):
    r, rhs = lax.axis_index("px"), plan.rhs
    lane = lane_index(rhs)
    above, below = read_halos(plan, first_ref, second_ref)
    one, two, three = plan.offset[2:]
    edge = product(jnp.concatenate([above[0], below[0]], axis=0), shrink_ref[0]) * SHRINK
    added = [
        above[1],
        jnp.where(lane < one, edge[:rhs], above[2]),
        jnp.where(lane < one, edge[rhs:], below[1]),
        below[2],
    ]
    even = lax.rem(r, 2) == 0
    own = [outer_ref[k] for k in range(3)]
    partner = [jnp.where(even, below[k], above[k]) for k in (1, 2)]
    third = jnp.where(even, below[1], above[2])
    partner.append(pltpu.roll(third, three, 1))
    low = [jnp.where(even, a, b) for a, b in zip(own, partner)]
    high = [jnp.where(even, b, a) for a, b in zip(own, partner)]
    sums = [low[0], low[1] + high[0], low[2] + high[1], high[2]]
    for k in range(4):
        value = jnp.where(lane < three, outer_ref[k] + added[k], sums[k])
        out_ref[k * rhs : (k + 1) * rhs] = value
    sides = place_sides(plan, jnp.zeros((rhs, LANES), F32), above[0], 0)
    sides = place_sides(plan, sides, below[0], 2)
    total = None
    for k in range(rhs // 8):
        part = sides[8 * k : 8 * (k + 1)]
        part = pltpu.roll(part, 4 * k, 1) if k else part
        total = part if total is None else total + part
    out_ref[4 * rhs :] = total


def banded(bands, matrices):
    return product(jnp.concatenate(bands, axis=1), jnp.concatenate(matrices, axis=0))


def owners(plan):
    c = lax.axis_index("py")
    return [jnp.bitwise_xor(c, k) for k in range(plan.m)]


def gather_kernel(plan, blocks, block_ref, *refs):
    band_refs, out_ref = refs[:-1], refs[-1]
    values, matrices = [], []
    for band, owner in zip(band_refs, owners(plan)):
        for j in range(4):
            values.append(band[j * plan.rhs : (j + 1) * plan.rhs])
            matrices.append(blocks.get(block_ref, "four", 4 * owner + j))
    out_ref[...] = banded(values, matrices)


def level_rows(plan, level, early_refs, late_refs, blocks, block_ref):
    rhs, values = plan.rhs, []
    lane = lane_index(rhs)
    for early, late in zip(early_refs, late_refs):
        outer = [late[i * rhs : (i + 1) * rhs] for i in range(4)]
        inner = []
        if level == 1:
            inner = [early[k] for k in range(4)]
            for k in range(2):
                begin = pltpu.roll(early[2 + k], plan.rest, 1)
                end = pltpu.roll(early[k], (plan.rest - plan.tail) % LANES, 1)
                inner.append(jnp.where(lane < plan.rest, begin, end))
        elif level == 2:
            inner = [early[k] for k in range(2)]
        values.append(jnp.concatenate(outer[:2] + inner + outer[2:], axis=0))
    matrices = [blocks.get(block_ref, f"place{level}", owner) for owner in owners(plan)]
    whole = jnp.dot(
        jnp.concatenate(values, axis=1).astype(BF16), jnp.concatenate(matrices, axis=0),
        preferred_element_type=F32,
    )
    return [whole[i * rhs : (i + 1) * rhs] for i in range(plan.h[level] + 2)]


def assemble_tiles(rows, t):
    rhs, count = rows[0].shape[0], rows[0].shape[1] // LANES
    lane = lane_index(rhs)

    def rolled(k, tile):
        if not 0 <= tile < count:
            return jnp.zeros((rhs, LANES), F32)
        return pltpu.roll(rows[k][:, tile * LANES : (tile + 1) * LANES], 2 * k + 1, 1)

    out = []
    for k in range(5):
        if k < 4:
            value = jnp.where(lane == 2 * k, rolled(k, t - 1), rolled(k, t))
        else:
            value = jnp.zeros((rhs, LANES), F32)
        if k > 0:
            value = jnp.where(lane == 2 * k - 1, rolled(k - 1, t + 1), value)
            value = jnp.where(lane < 2 * k - 1, rolled(k - 1, t), value)
        out.append(value)
    return jnp.concatenate(out, axis=1).astype(BF16)[:, : 4 * (LANES + 2)]


def solve_pairs(plan, level, rows, pairs, factor_ref):
    w, solved = plan.tile[level], []
    for t in range(plan.tiles[level]):
        solved.append([])
        for at, b in pairs:
            window = rows[at : at + 4]
            if w == LANES:
                lhs = assemble_tiles(window, t)
            else:
                lhs = assemble([[row] for row in window], w)
            solved[t].append(solve(lhs, factor_ref[b, t]))
    return solved


def lift_pairs(plan, level, solved, blocks, block_ref):
    c, w = lax.axis_index("py"), plan.tile[level]
    name, count = f"lift{level}", len(solved[0]) * plan.rhs
    stacked = [jnp.concatenate(values, axis=0) for values in solved]
    if w % LANES == 0:
        both = [
            jnp.concatenate([v[:, j * w : (j + 1) * w] for v in stacked], axis=1)
            for j in range(2)
        ]
        both = product(jnp.concatenate(both, axis=0), blocks.get(block_ref, name, c))
        return [both[:count], both[count:]]
    row = jnp.concatenate(stacked, axis=1)
    return [product(row, blocks.get(block_ref, name, 2 * c + j)) for j in range(2)]


def coarse_kernel(plan, blocks, block_ref, *refs):
    factors, outs = refs[:3], refs[3 + 2 * plan.m :]
    early, late = refs[3 : 3 + plan.m], refs[3 + plan.m : 3 + 2 * plan.m]
    c, rhs = lax.axis_index("py"), plan.rhs
    down, up = [], []
    for level in (1, 2, 3):
        rows = level_rows(plan, level, early, late, blocks, block_ref)
        w, count = plan.tile[level], plan.h[level] // 2
        pairs = [(2 * b, b) for b in sorted({0, count - 1})]
        if level == 1:
            for i, row in enumerate(rows[2:-2]):
                outs[3][i] = row
        else:
            pairs = [(2 * b, b) for b in range(count)]
        solved = solve_pairs(plan, level, rows, pairs, factors[level - 1])
        for t, values in enumerate(solved):
            for k, value in enumerate(values):
                outs[level - 1][t, k] = value
        for j, (edge, at) in enumerate(((up, 0), (down, -1))):
            for value in solved:
                if w % LANES == 0:
                    edge.append(value[at][:, j * w : (j + 1) * w])
                else:
                    edge.append(pltpu.roll(value[at], LANES - w, 1) if j else value[at])
    edges = [jnp.concatenate(edge, axis=1) for edge in (down, up)]
    picked = product(jnp.concatenate(edges, axis=0), blocks.get(block_ref, "pick", c))
    write_halos(c, [picked[:rhs]], [picked[rhs:]], outs[4], outs[5])


def inner_kernel(plan, blocks, block_ref, factor_ref, rows_ref, one_ref, two_ref, three_ref,
                 main_ref, picked_ref, *refs):
    early, late = refs[: plan.m], refs[plan.m : 2 * plan.m]
    outs, fine_ref = refs[2 * plan.m : -1], refs[-1]
    rhs, count = plan.rhs, plan.h[1] // 2
    rows = [rows_ref[i] for i in range(rows_ref.shape[0])]
    pairs = [(2 * (b - 1), b) for b in range(1, count - 1)]
    inner = solve_pairs(plan, 1, rows, pairs, factor_ref)
    for level, ref in ((1, one_ref), (2, two_ref), (3, three_ref)):
        solved = []
        for t in range(ref.shape[0]):
            values = [ref[t, k] for k in range(ref.shape[1])]
            if level == 1:
                values[1:1] = inner[t]
            solved.append(values)
        lifted = lift_pairs(plan, level, solved, blocks, block_ref)
        for b in range(plan.h[level] // 2):
            for j in range(2):
                outs[level - 1][2 * b + j] = lifted[j][b * rhs : (b + 1) * rhs]
    sides, w0 = side_columns(plan, early, late), plan.w0
    lane = lane_index(rhs)
    for b in range(plan.h0 // 2):
        value = pltpu.roll(sides, (LANES - 4 * b) % LANES, 1) if b else sides
        value = jnp.where(lane < 8, value, 0.0)[:, :16].astype(BF16)
        added = jnp.dot(value, picked_ref[b], preferred_element_type=F32)
        for j in range(2):
            fine_ref[2 * b + j] = main_ref[2 * b + j] + added[:, j * w0 : (j + 1) * w0]


def fine_kernel(plan, rows_ref, first_ref, second_ref, factor_ref, out_ref, picked_ref):
    rhs, h0, w0 = plan.rhs, plan.h0, plan.w0
    above, below = read_halos(plan, first_ref, second_ref)
    lane = lane_index(rhs)
    rows = [above[0]] + [rows_ref[row] for row in range(h0)] + [below[0]]
    length = 4 * (w0 + 2)
    side = lax.broadcasted_iota(jnp.int32, (16, length), 0)
    at = lax.broadcasted_iota(jnp.int32, (16, length), 1)
    wanted = (side // 2) * (w0 + 2) + (side % 2) * (w0 + 1)
    pick = jnp.where(at == wanted, 1.0, 0.0).astype(BF16)
    for b in range(h0 // 2):
        tiles, before = [], None
        for k in range(5):
            if k < 4:
                rolled = pltpu.roll(rows[2 * b + k], 2 * k + 1, 1)
                value = jnp.where(lane > 2 * k, rolled, 0.0)
            else:
                value = jnp.zeros((rhs, LANES), F32)
            if before is not None:
                value = jnp.where(lane < 2 * k - 1, before, value)
            tiles.append(value)
            before = rolled
        lhs = jnp.concatenate(tiles, axis=1).astype(BF16)[:, :length]
        solved = solve(jnp.concatenate([lhs, pick], axis=0), factor_ref[b, 0])
        for j in range(2):
            out_ref[2 * b + j] = solved[:rhs, j * w0 : (j + 1) * w0]
        picked_ref[b] = solved[rhs:].astype(BF16)


def side_columns(plan, early_refs, late_refs):
    c, rhs, h0 = lax.axis_index("py"), plan.rhs, plan.h0
    found = []
    for offset in (-1, 1):
        total = None
        for early, late, owner in zip(early_refs, late_refs, owners(plan)):
            chosen = jnp.where(owner == c + offset, 1.0, 0.0).astype(F32)
            parts = [early[0] * chosen, early[1] * chosen, late[4 * rhs :] * chosen]
            total = parts if total is None else [a + b for a, b in zip(total, parts)]
        found.append(total)
    slots = []
    for left, right in zip(*found):
        even = lane_index(left.shape[0]) % 2 == 0
        slots.append(jnp.where(even, left, right))
    packed = slots.pop()
    outer = [pltpu.roll(packed, LANES - 4 * k, 1) if k else packed for k in range(rhs // 8)]
    outer = jnp.concatenate(outer, axis=0)
    lane, start = lane_index(rhs), plan.offset[3]
    inner = [
        pltpu.roll(slot, (2 + k * h0 - start) % LANES, 1) for k, slot in enumerate(slots)
    ]
    value = jnp.where(lane < 2 * h0 + 4, pltpu.roll(outer, 2 * h0, 1), 0.0)
    value = jnp.where(lane < 2 * h0 + 2, inner[1], value)
    value = jnp.where(lane < h0 + 2, inner[0], value)
    return jnp.where(lane < 2, outer, value)


def whole_kernel(plan, group, partners, blocks, block_ref, four_ref, inverse_ref, *refs):
    count = plan.n // 2
    gathered, out_ref, pair_ref, four_rows = refs[:count], refs[count], refs[-2], refs[-1]
    r, c = lax.axis_index("px"), lax.axis_index("py")
    rhs, ny4 = plan.rhs, plan.ny[4]
    nx4, nx5 = plan.nx[4], plan.nx[5]
    odd = jnp.bitwise_and(c, 1)
    for block, (left, right) in zip(gathered, partners):
        partner = jnp.where(odd == 1, right, left)
        pair_ref[jnp.bitwise_xor(r, partner) // 2] = block[...]
    lane = lane_index(rhs)
    inside = jnp.logical_and(lane >= 1, lane <= ny4)

    def part_row(pair, j):
        tile, start = divmod(j * ny4, LANES)
        value = pair_ref[pair, :, tile * LANES : (tile + 1) * LANES]
        return jnp.where(inside, pltpu.roll(value, (1 - start) % LANES, 1), 0.0)

    zero = jnp.zeros((rhs, LANES), F32)
    rows = [zero]
    for i in range(nx4):
        value = part_row(i // 2, 1 + i % 2)
        if i % 2 == 0 and i > 0:
            value = value + part_row(i // 2 - 1, 3)
        if i % 2 == 1 and i < nx4 - 1:
            value = value + part_row(i // 2 + 1, 0)
        rows.append(value)
    rows.append(zero)
    five = shrink_rows(rows, nx4, 1)[1:-1]
    flat = product(jnp.concatenate(five, axis=1), blocks.get(block_ref, "shrink5")) * SHRINK
    flat = flat[:, : inverse_ref.shape[0]]
    part_five = jnp.dot(flat.astype(BF16), inverse_ref[...], preferred_element_type=F32)
    spread = blocks.get(block_ref, "lift5")[: part_five.shape[1], : nx4 * ny4]
    lifted = product(part_five, spread) * SHRINK
    w, tiles = plan.tile[4], plan.tiles[4]
    parts = []
    for b in range(nx4 // 2):
        for t in range(tiles):
            pieces = []
            for k in range(4):
                lanes = range(t * w, t * w + w + 2, LANES)
                pieces.append([rows[2 * b + k][:, lo : lo + LANES] for lo in lanes])
            lhs = assemble(pieces, w)
            parts.append(
                lax.dot_general(
                    lhs, four_ref[b, t], (((1,), (1,)), ((), ())), preferred_element_type=F32
                )
            )
    correction = jnp.concatenate(parts, axis=1) + lifted
    width = group * 2 * w * tiles
    bands = nx4 // 2 // group
    stacked = jnp.concatenate(
        [correction[:, i * width : (i + 1) * width] for i in range(bands)], axis=0
    )
    four_rows[0] = jnp.zeros((rhs, LANES), F32)
    four_rows[nx4 + 1] = jnp.zeros((rhs, LANES), F32)
    for g in range(group):
        for j in range(2):
            value = product(stacked, blocks.get(block_ref, "lift4", (c * group + g) * 2 + j))
            for i in range(bands):
                four_rows[1 + 2 * (i * group + g) + j] = value[i * rhs : (i + 1) * rhs]
    for k in range(3):
        out_ref[k] = four_rows[r + k]


def final_kernel(plan, blocks, block_ref, fine_ref, one_ref, two_ref, three_ref, four_ref,
                 first_ref, second_ref, out_ref, whole_ref, semaphores):
    r, rhs = lax.axis_index("px"), plan.rhs
    above = jnp.where(r > 0, 1.0, 0.0).astype(F32)
    below = jnp.where(r < plan.n - 1, 1.0, 0.0).astype(F32)
    halos = read_halos(plan, first_ref, second_ref)
    halo = product(
        jnp.concatenate([halos[0][0], halos[1][0]], axis=0),
        blocks.get(block_ref, "band", lax.axis_index("py")),
    )
    from_above, from_below = [
        [halo[k * rhs : (k + 1) * rhs, l * plan.w0 : (l + 1) * plan.w0] for l in range(3)]
        for k in range(2)
    ]
    copies = []
    for part in range(rhs // 8):
        own = slice(8 * part, 8 * (part + 1))
        rows = [four_ref[k, own] for k in range(3)]
        for level, own_ref in ((3, three_ref), (2, two_ref), (1, one_ref)):
            height = plan.h[level]
            lifted = lift_rows(rows, -1, height + 1)
            rows = [lifted[0] * above + from_above[level - 1][own]]
            rows += [lifted[i + 1] + own_ref[i, own] for i in range(height)]
            rows += [lifted[-1] * below + from_below[level - 1][own]]
        lifted = lift_rows(rows, 0, plan.h0)
        start, count = 8 * part * plan.h0, 8 * plan.h0
        for row in range(plan.h0):
            value = lifted[row] + fine_ref[row, own]
            whole_ref[pl.ds(start + row, 8, stride=plan.h0), :] = value
        span = pl.ds(start, count)
        copies.append(
            pltpu.make_async_copy(whole_ref.at[span], out_ref.at[span], semaphores.at[part])
        )
        copies[-1].start()
    for copy in copies:
        copy.wait()


def per_device(mesh_shape, residual, factor_fine, factor_one, factor_two, factor_three,
               factor_four, coarse_inverse):
    factors = [factor_fine, factor_one, factor_two, factor_three, factor_four]
    plan = Plan(mesh_shape, residual.shape, [f.shape for f in factors])
    n, m, rhs, h, h0 = plan.n, plan.m, plan.rhs, plan.h, plan.h0
    x = residual.reshape(rhs * h0, plan.w0)

    def trade(first, second):
        def target(i, c):
            after = i + 1 if c & 2 else i - 1
            return (after, c) if 0 <= after < n else (i, c ^ 2)

        ring = []
        for i in range(n):
            for c in range(m):
                row, column = target(i, c)
                ring.append((i * m + c, row * m + column))
        back = [(b, a) for a, b in ring]
        return lax.ppermute(first, ("px", "py"), ring), lax.ppermute(second, ("px", "py"), back)

    def swap(value, bits):
        return lax.ppermute(value, "py", [(i, i ^ bits) for i in range(m)])

    blocks = Blocks()
    blocks.add("four", plan.place_four())
    blocks.add("pick", plan.pick_band())
    blocks.add("band", plan.lift_band())
    for l in (1, 2, 3):
        blocks.add(f"place{l}", plan.place_whole(l))
        if plan.tile[l] % LANES == 0:
            blocks.add(f"lift{l}", plan.lift_columns(l))
        else:
            lifted = plan.lift_rows_of(l)
            blocks.add(f"lift{l}", lifted.reshape(m, 2, -1, plan.w0))
    lifted, group = plan.level_four_lift()
    blocks.add("lift4", lifted)
    blocks.add("shrink5", plan.coarsest_shrink())
    blocks.add("lift5", plan.coarsest_lift())
    matrices = blocks.array()

    shrink = kernel_call(
        functools.partial(shrink_kernel, plan),
        jax.ShapeDtypeStruct((4, LANES, LANES), BF16), cost_us=4.0,
    )()
    early, outer, first, second, rows = kernel_call(
        functools.partial(restrict_kernel, plan),
        (shape(4, rhs, LANES), shape(4, rhs, LANES), shape(3, rhs, LANES), shape(3, rhs, LANES),
         shape(h0, rhs, plan.w0)),
    )(x, shrink)
    first, second = trade(first, second)
    late = kernel_call(functools.partial(merge_kernel, plan), shape(4 * rhs + 8, LANES))(
        outer, shrink, first, second
    )

    main, picked = kernel_call(
        functools.partial(fine_kernel, plan),
        (shape(h0, rhs, plan.w0), jax.ShapeDtypeStruct((h0 // 2, 16, 2 * plan.w0), BF16)),
        cost_us=0.7,
    )(rows, first, second, factor_fine)
    def spread(bands, bits):
        for bit in bits:
            bands.update({k ^ bit: swap(band, bit) for k, band in list(bands.items())})
        return bands

    bits = [1 << k for k in reversed(range(m.bit_length() - 1))]
    late = spread({0: late}, bits[:1])
    late, main, picked = lax.optimization_barrier((late, main, picked))
    early, late = spread({0: early}, bits), spread(late, bits[1:])
    early, late = [early[k] for k in range(m)], [late[k] for k in range(m)]

    pairs = kernel_call(
        functools.partial(gather_kernel, plan, blocks), shape(rhs, 4 * plan.ny[4]), cost_us=0.3
    )(matrices, *late)
    order, fetched, gathered, partners = list(range(n // 2 - 1, 0, -1)), [], [pairs], [(0, 0)]
    for k in range(0, len(order), 2):
        even, odd = order[k], order[min(k + 1, len(order) - 1)]
        routes = [
            (i * m + c, (i ^ (2 * (odd if c % 2 else even))) * m + c)
            for i in range(n) for c in range(m)
        ]
        fetched.append((lax.ppermute(pairs, ("px", "py"), routes), even, odd))
    late, pairs = lax.optimization_barrier((late, pairs))
    for value, even, odd in fetched:
        gathered.append(value)
        partners.append((2 * even, 2 * odd))
        if even != odd:
            gathered.append(swap(value, 1))
            partners.append((2 * odd, 2 * even))


    one, two, three, inner, low, high = kernel_call(
        functools.partial(coarse_kernel, plan, blocks),
        tuple(
            shape(plan.tiles[l], count, rhs, 2 * plan.tile[l])
            for l, count in ((1, 2), (2, h[2] // 2), (3, h[3] // 2))
        )
        + (shape(h[1] - 2, rhs, plan.ny[1]),)
        + (shape(1, rhs, LANES), shape(1, rhs, LANES)),
        cost_us=2.5,
    )(matrices, factor_one, factor_two, factor_three, *early, *late)
    low, high = trade(low, high)
    one, two, three, fine = kernel_call(
        functools.partial(inner_kernel, plan, blocks),
        tuple(shape(h[l], rhs, LANES) for l in (1, 2, 3)) + (shape(h0, rhs, plan.w0),),
        cost_us=1.2,
    )(matrices, factor_one, inner, one, two, three, main, picked, *early, *late)
    four = kernel_call(
        functools.partial(whole_kernel, plan, group, partners, blocks),
        shape(3, rhs, LANES),
        scratch=(
            pltpu.VMEM((n // 2, rhs, 4 * plan.ny[4]), F32),
            pltpu.VMEM((plan.nx[4] + 2, rhs, LANES), F32),
        ),
    )(matrices, jnp.swapaxes(factor_four, 2, 3), coarse_inverse, *gathered)
    out = kernel_call(
        functools.partial(final_kernel, plan, blocks), shape(rhs * h0, plan.w0),
        scratch=(pltpu.VMEM((rhs * h0, plan.w0), F32), pltpu.SemaphoreType.DMA((rhs // 8,))),
        out_space=pl.ANY,
    )(
        matrices, fine, one, two, three, four, low, high
    )
    return out.reshape(rhs, h0, plan.w0)


def solution(mesh):
    placed = (
        P(None, "px", "py"),
        P("px", "py", None, None),
        P("px", None, None, None),
        P("px", None, None, None),
        P("px", None, None, None),
        P(),
        P(),
    )
    return jax.shard_map(
        functools.partial(per_device, dict(mesh.shape)),
        mesh=mesh, in_specs=placed, out_specs=P(None, "px", "py"), check_vma=False,
    )
```

```python
import functools
import math

import jax
import jax.numpy as jnp
import numpy as np
from jax import lax
from jax.experimental import pallas as pl
from jax.experimental.pallas import tpu as pltpu
from jax.sharding import PartitionSpec as P

F32 = jnp.float32
BF16 = jnp.bfloat16
LANES = 128
SHRINK = 1.0 / 20.0
TAPS = (1, 3, 3, 1)
VMEM_BYTES = 24 * 1024 * 1024


def round_up(value, unit=LANES):
    return -(-value // unit) * unit


def global_prolong(coarse):
    out = np.zeros((coarse, 2 * coarse))
    for i in range(coarse):
        out[i, 2 * i] += 3
        out[i, 2 * i + 1] += 3
        if i > 0:
            out[i, 2 * i - 1] += 1
        if i + 1 < coarse:
            out[i, 2 * i + 2] += 1
    return out


def bf(array):
    return np.asarray(array, np.float32).astype(jnp.bfloat16)


class Plan:
    def __init__(self, mesh_shape, residual, factors):
        self.n, self.m = mesh_shape["px"], mesh_shape["py"]
        self.rhs, self.h0, self.w0 = residual
        self.h = [self.h0 >> l for l in range(5)]
        self.w = [self.w0 >> l for l in range(5)]
        self.ny = [self.w0 * self.m >> l for l in range(6)]
        self.nx = [self.h0 * self.n >> l for l in range(6)]
        self.tile = [f[3] // 2 for f in factors]
        self.tiles = [f[1] for f in factors]
        self.slots = self.h[1] + 2
        self.offset = [None, 0]
        for l in (2, 3, 4):
            self.offset.append(self.offset[-1] + self.w[l - 1] + 2)
        self.sides = self.h0 // 2 + 1
        self.first = self.w[1] + 2
        self.rest = LANES - self.first
        self.tail = self.offset[3] + 2 * self.sides

    def place(self, level, lead, width, at=0):
        out = np.zeros((self.m, LANES, width))
        for c in range(self.m):
            for k in range(self.w[level] + 2):
                column = self.w[level] * c - 1 + k
                if -lead <= column < self.ny[level]:
                    out[c, self.offset[level] + k, at + column + lead] = 1
        return out

    def place_whole(self, level):
        if self.tile[level] == LANES:
            return self.place(level, 0, self.ny[level])
        return self.place(level, 1, round_up(self.ny[level] + 2))

    def place_four(self):
        rows = [self.place(4, 0, 4 * self.ny[4], j * self.ny[4]) for j in range(4)]
        return np.stack(rows, axis=1)

    def pick_band(self):
        out = []
        for l in (1, 2, 3):
            pick = np.zeros((self.m, round_up(self.ny[l]), LANES))
            one = self.place(l, 0, self.ny[l])
            pick[:, : self.ny[l]] = one.transpose(0, 2, 1)
            out.append(pick)
        return np.concatenate(out, axis=1)

    def lift_band(self):
        out = []
        for l in (1, 2, 3):
            one = self.place(l, 0, self.ny[l])
            out.append(np.einsum("cki,cif->ckf", one, self.lift_columns(l)))
        return np.concatenate(out, axis=2)

    def lift_columns(self, level):
        out = np.eye(self.ny[level])
        for l in range(level, 0, -1):
            out = out @ global_prolong(self.ny[l])
        return out.reshape(self.ny[level], self.m, self.w0).transpose(1, 0, 2)

    def lift_rows_of(self, level):
        w, tiles = self.tile[level], self.tiles[level]
        full = self.lift_columns(level).reshape(self.m, tiles, w, self.w0)
        out = np.zeros((self.m, 2, tiles, 2 * w, self.w0))
        for j in range(2):
            out[:, j, :, j * w : (j + 1) * w] = full
        return out

    def coarsest_shrink(self):
        nx5, ny5, ny4 = self.nx[5], self.ny[5], self.ny[4]
        columns = global_prolong(ny5).T
        width = round_up(ny4 + 2)
        out = np.zeros((nx5, width, nx5 * ny5))
        for i in range(nx5):
            out[i, 1 : 1 + ny4, i * ny5 : (i + 1) * ny5] = columns
        return bf(out.reshape(nx5 * width, nx5 * ny5))

    def coarsest_lift(self):
        rows, columns = global_prolong(self.nx[5]), global_prolong(self.ny[5])
        both = np.einsum("ia,jb->ijab", rows, columns)
        w, tiles = self.tile[4], self.tiles[4]
        both = both.reshape(self.nx[5] * self.ny[5], self.nx[4] // 2, 2, tiles, w)
        both = both.transpose(0, 1, 3, 2, 4)
        return bf(both.reshape(self.nx[5] * self.ny[5], self.nx[4] * self.ny[4]))

    def level_four_lift(self):
        pair = 2 * self.tile[4] * self.tiles[4]
        group = max(1, LANES // pair)
        width = group * pair
        rows = self.lift_rows_of(4).reshape(self.m, 2, pair, self.w0)
        out = np.zeros((self.m, group, 2, width, self.w0))
        for g in range(group):
            out[:, g, :, g * pair : (g + 1) * pair] = rows
        return bf(out), group


class Blocks:
    def __init__(self):
        self.parts, self.places, self.count = [], {}, 0

    def add(self, name, array):
        lead, (rows, columns) = array.shape[:-2], array.shape[-2:]
        high, wide = round_up(rows) // LANES, round_up(columns) // LANES
        out = np.zeros((math.prod(lead), high * LANES, wide * LANES), np.float32)
        out[:, :rows, :columns] = np.asarray(array, np.float32).reshape((-1, rows, columns))
        out = out.reshape(-1, high, LANES, wide, LANES).transpose(0, 1, 3, 2, 4)
        self.parts.append(out.reshape(-1, LANES, LANES))
        self.places[name] = (self.count, high, wide)
        self.count += len(self.parts[-1])

    def array(self):
        return jnp.asarray(bf(np.concatenate(self.parts, axis=0)))

    def get(self, ref, name, lead=0):
        base, high, wide = self.places[name]
        base = base + lead * (high * wide)
        rows = [
            jnp.concatenate([ref[base + i * wide + j] for j in range(wide)], axis=1)
            for i in range(high)
        ]
        return jnp.concatenate(rows, axis=0)


def split(value):
    high = value.astype(BF16)
    return high, (value - high.astype(F32)).astype(BF16)


def product(value, matrix):
    high, low = split(value)
    count = value.shape[0]
    both = jnp.dot(
        jnp.concatenate([high, low], axis=0), matrix, preferred_element_type=F32
    )
    return both[:count] + both[count:]


def shrink_rows(rows, count, halo):
    out = []
    for i in range(-1, count // 2 + 1):
        total = None
        for t, tap in enumerate(TAPS):
            j = 2 * i - 1 + t
            if -halo <= j < count + halo:
                term = rows[j + halo] * float(tap) if tap > 1 else rows[j + halo]
                total = term if total is None else total + term
        out.append(total)
    return out


def lift_rows(rows, first, last):
    out = []
    for f in range(first, last):
        i = f // 2
        other = i - 1 if f % 2 == 0 else i + 1
        out.append((rows[i + 1] * 3.0 + rows[other + 1]) * SHRINK)
    return out


def lane_index(rows):
    return lax.broadcasted_iota(jnp.int32, (rows, LANES), 1)


def assemble(pieces, width):
    total = 4 * (width + 2)
    tiles = [[] for _ in range(-(-total // LANES))]
    lane = lane_index(pieces[0][0].shape[0])
    for k, piece in enumerate(pieces):
        for q, value in enumerate(piece):
            start = k * (width + 2) + LANES * q
            count = min(LANES, width + 2 - LANES * q)
            shift, at = start % LANES, start // LANES
            rolled = pltpu.roll(value, shift, 1) if shift else value
            tiles[at].append((min(LANES, shift + count), rolled))
            if shift + count > LANES:
                tiles[at + 1].append((shift + count - LANES, rolled))
    out = []
    for segments in tiles:
        segments = sorted(segments, key=lambda s: -s[0])
        end, value = segments[0]
        if end < LANES:
            value = jnp.where(lane < end, value, 0.0)
        for end, part in segments[1:]:
            value = jnp.where(lane < end, part, value)
        out.append(value)
    return jnp.concatenate(out, axis=1).astype(BF16)[:, :total]


def solve(lhs, factor):
    return jnp.dot(lhs, factor, preferred_element_type=F32)


def kernel_call(body, out_shape, scratch=(), cost_us=1.0, out_space=pltpu.VMEM):
    whole = pl.BlockSpec(memory_space=pltpu.VMEM)
    result = pl.BlockSpec(memory_space=out_space)

    def call(*operands):
        return pl.pallas_call(
            body,
            out_shape=out_shape,
            in_specs=[whole] * len(operands),
            out_specs=jax.tree.map(lambda _: result, out_shape),
            scratch_shapes=list(scratch),
            compiler_params=pltpu.CompilerParams(vmem_limit_bytes=VMEM_BYTES),
            cost_estimate=pl.CostEstimate(
                flops=int(cost_us * 1e9), bytes_accessed=int(cost_us * 3e6), transcendentals=0
            ),
        )(*operands)

    return call


def shape(*dims):
    return jax.ShapeDtypeStruct(dims, F32)


def tap_matrix(row_lead, lane_lead, count, first, last):
    row = lax.broadcasted_iota(jnp.int32, (LANES, LANES), 0) - row_lead
    lane = lax.broadcasted_iota(jnp.int32, (LANES, LANES), 1) - lane_lead
    tap = row - 2 * lane + 3
    outer = jnp.logical_or(tap == 0, tap == 3)
    inner = jnp.logical_or(tap == 1, tap == 2)
    value = jnp.where(outer, 1.0, jnp.where(inner, 3.0, 0.0))
    value = jnp.where(jnp.logical_or(lane < first, lane > count + 1 - last), 0.0, value)
    return value.astype(BF16)


def place_sides(plan, slot_value, row, at):
    lane = lane_index(plan.rhs)
    chosen = jnp.logical_or(lane == at, lane == at + 1)
    return jnp.where(chosen, pltpu.roll(row, (at + 1) % LANES, 1), slot_value)


def column_ends(plan):
    c = lax.axis_index("py")
    return jnp.where(c == 0, 1, 0), jnp.where(c == plan.m - 1, 1, 0)


def write_halos(c, down, up, first_ref, second_ref):
    forward = jnp.bitwise_and(c, 2) != 0
    for k, (low, high) in enumerate(zip(down, up)):
        first_ref[k] = jnp.where(forward, low, high)
        second_ref[k] = jnp.where(forward, high, low)


def read_halos(plan, first_ref, second_ref):
    r, c = lax.axis_index("px"), lax.axis_index("py")
    forward = jnp.bitwise_and(c, 2) != 0
    above = jnp.where(r > 0, 1.0, 0.0).astype(F32)
    below = jnp.where(r < plan.n - 1, 1.0, 0.0).astype(F32)
    first, second = first_ref[...], second_ref[...]
    return jnp.where(forward, first, second) * above, jnp.where(forward, second, first) * below


def shrink_kernel(plan, out_ref):
    first, last = column_ends(plan)
    shrink = None
    for level in (1, 2, 3, 4):
        lead = 0 if level == 1 else plan.offset[level - 1] + 1
        step = tap_matrix(lead, plan.offset[level], plan.w[level], first, last)
        if shrink is None:
            shrink = step
        else:
            shrink = jnp.dot(shrink, step, preferred_element_type=F32).astype(BF16)
        out_ref[level - 1] = shrink


def restrict_kernel(plan, x_ref, shrink_ref, early_ref, outer_ref, first_ref, second_ref, rows_ref):
    r, c = lax.axis_index("px"), lax.axis_index("py")
    rhs, slots, h = plan.rhs, plan.slots, plan.h
    above = jnp.where(r > 0, 1.0, 0.0).astype(F32)
    below = jnp.where(r < plan.n - 1, 1.0, 0.0).astype(F32)
    x = [x_ref[pl.ds(row, rhs, stride=h[0]), :] for row in range(h[0])]
    rows, total = x, None
    for level in (1, 2, 3, 4):
        rows = shrink_rows(rows, h[level - 1], 0 if level == 1 else 1)
        rows[0] = rows[0] * above
        rows[-1] = rows[-1] * below
        part = product(jnp.concatenate(rows, axis=0), shrink_ref[level - 1])
        if total is None:
            total = part
        else:
            count = part.shape[0]
            total = jnp.concatenate([total[:count] + part, total[count:]], axis=0)
    lane = lane_index(slots * rhs)
    scale = jnp.where(lane < plan.offset[2], SHRINK, SHRINK**2)
    scale = jnp.where(lane < plan.offset[3], scale, SHRINK**3)
    total = total * jnp.where(lane < plan.offset[4], scale, SHRINK**4)
    own = [total[i * rhs : (i + 1) * rhs] for i in range(slots)]
    lane = lane_index(rhs)
    one, two, three = plan.offset[2:]
    for k in range(6):
        early_ref[k] = own[2 + k]
    outer = [own[0], own[1]]
    for k in range(2):
        value = jnp.where(lane < two, own[h[2] + k], own[h[3] + k])
        outer.append(jnp.where(lane < one, own[h[1] + k], value))
    for k in range(4):
        outer_ref[k] = outer[k]
    third = pltpu.roll(own[2], LANES - three, 1)
    down = [x[-1], jnp.where(lane < three, outer[2], own[0])]
    down.append(jnp.where(lane < one, third, jnp.where(lane < three, outer[3], own[1])))
    up = [x[0], jnp.where(lane < one, third, own[0]), own[1]]
    write_halos(c, down, up, first_ref, second_ref)
    for i, row in enumerate(x):
        rows_ref[i] = row


def inner_rows_kernel(plan, own_ref, rows_ref, early_ref):
    h, rhs = plan.h, plan.rhs
    lane = lane_index(rhs)
    two = plan.offset[3]
    own = [None, None] + [own_ref[k] for k in range(6)]
    x = [rows_ref[k] for k in range(h[0])]
    inner = [own[2], own[3], own[4], own[5]]
    for k in range(2):
        value = inner[k]
        value = jnp.where(lane < two, value, 0.0)
        for j in range(h[0] // 2):
            value = place_sides(plan, value, x[k * (h[0] // 2) + j], two + 2 * j)
        odd_row, end = own[6 + k], plan.tail + plan.first - plan.rest
        moved = pltpu.roll(odd_row, (plan.tail - plan.rest) % LANES, 1)
        chosen = jnp.logical_and(lane >= plan.tail, lane < end)
        early_ref[k] = jnp.where(chosen, moved, value)
        moved = pltpu.roll(odd_row, plan.first, 1)
        early_ref[2 + k] = jnp.where(lane < plan.first, inner[2 + k], moved)


def merge_kernel(plan, outer_ref, shrink_ref, first_ref, second_ref, out_ref):
    r, rhs = lax.axis_index("px"), plan.rhs
    lane = lane_index(rhs)
    above, below = read_halos(plan, first_ref, second_ref)
    one, two, three = plan.offset[2:]
    edge = product(jnp.concatenate([above[0], below[0]], axis=0), shrink_ref[0]) * SHRINK
    added = [
        above[1],
        jnp.where(lane < one, edge[:rhs], above[2]),
        jnp.where(lane < one, edge[rhs:], below[1]),
        below[2],
    ]
    even = lax.rem(r, 2) == 0
    own = [outer_ref[k] for k in range(3)]
    partner = [jnp.where(even, below[k], above[k]) for k in (1, 2)]
    third = jnp.where(even, below[1], above[2])
    partner.append(pltpu.roll(third, three, 1))
    low = [jnp.where(even, a, b) for a, b in zip(own, partner)]
    high = [jnp.where(even, b, a) for a, b in zip(own, partner)]
    sums = [low[0], low[1] + high[0], low[2] + high[1], high[2]]
    for k in range(4):
        value = jnp.where(lane < three, outer_ref[k] + added[k], sums[k])
        out_ref[k * rhs : (k + 1) * rhs] = value
    sides = place_sides(plan, jnp.zeros((rhs, LANES), F32), above[0], 0)
    sides = place_sides(plan, sides, below[0], 2)
    total = None
    for k in range(rhs // 8):
        part = sides[8 * k : 8 * (k + 1)]
        part = pltpu.roll(part, 4 * k, 1) if k else part
        total = part if total is None else total + part
    out_ref[4 * rhs :] = total


def banded(bands, matrices):
    return product(jnp.concatenate(bands, axis=1), jnp.concatenate(matrices, axis=0))


def owners(plan):
    c = lax.axis_index("py")
    return [jnp.bitwise_xor(c, k) for k in range(plan.m)]


def gather_kernel(plan, blocks, block_ref, *refs):
    band_refs, out_ref = refs[:-1], refs[-1]
    values, matrices = [], []
    for band, owner in zip(band_refs, owners(plan)):
        for j in range(4):
            values.append(band[j * plan.rhs : (j + 1) * plan.rhs])
            matrices.append(blocks.get(block_ref, "four", 4 * owner + j))
    out_ref[...] = banded(values, matrices)


def level_rows(plan, level, early_refs, late_refs, blocks, block_ref):
    rhs, values = plan.rhs, []
    lane = lane_index(rhs)
    for early, late in zip(early_refs, late_refs):
        outer = [late[i * rhs : (i + 1) * rhs] for i in range(4)]
        inner = []
        if level == 1:
            inner = [early[k] for k in range(4)]
            for k in range(2):
                begin = pltpu.roll(early[2 + k], plan.rest, 1)
                end = pltpu.roll(early[k], (plan.rest - plan.tail) % LANES, 1)
                inner.append(jnp.where(lane < plan.rest, begin, end))
        elif level == 2:
            inner = [early[k] for k in range(2)]
        values.append(jnp.concatenate(outer[:2] + inner + outer[2:], axis=0))
    matrices = [blocks.get(block_ref, f"place{level}", owner) for owner in owners(plan)]
    whole = jnp.dot(
        jnp.concatenate(values, axis=1).astype(BF16), jnp.concatenate(matrices, axis=0),
        preferred_element_type=F32,
    )
    return [whole[i * rhs : (i + 1) * rhs] for i in range(plan.h[level] + 2)]


def assemble_tiles(rows, t):
    rhs, count = rows[0].shape[0], rows[0].shape[1] // LANES
    lane = lane_index(rhs)

    def rolled(k, tile):
        if not 0 <= tile < count:
            return jnp.zeros((rhs, LANES), F32)
        return pltpu.roll(rows[k][:, tile * LANES : (tile + 1) * LANES], 2 * k + 1, 1)

    out = []
    for k in range(5):
        if k < 4:
            value = jnp.where(lane == 2 * k, rolled(k, t - 1), rolled(k, t))
        else:
            value = jnp.zeros((rhs, LANES), F32)
        if k > 0:
            value = jnp.where(lane == 2 * k - 1, rolled(k - 1, t + 1), value)
            value = jnp.where(lane < 2 * k - 1, rolled(k - 1, t), value)
        out.append(value)
    return jnp.concatenate(out, axis=1).astype(BF16)[:, : 4 * (LANES + 2)]


def solve_pairs(plan, level, rows, pairs, factor_ref):
    w, solved = plan.tile[level], []
    for t in range(plan.tiles[level]):
        solved.append([])
        for at, b in pairs:
            window = rows[at : at + 4]
            if w == LANES:
                lhs = assemble_tiles(window, t)
            else:
                lhs = assemble([[row] for row in window], w)
            solved[t].append(solve(lhs, factor_ref[b, t]))
    return solved


def lift_pairs(plan, level, solved, blocks, block_ref):
    c, w = lax.axis_index("py"), plan.tile[level]
    name, count = f"lift{level}", len(solved[0]) * plan.rhs
    stacked = [jnp.concatenate(values, axis=0) for values in solved]
    if w % LANES == 0:
        both = [
            jnp.concatenate([v[:, j * w : (j + 1) * w] for v in stacked], axis=1)
            for j in range(2)
        ]
        both = product(jnp.concatenate(both, axis=0), blocks.get(block_ref, name, c))
        return [both[:count], both[count:]]
    row = jnp.concatenate(stacked, axis=1)
    return [product(row, blocks.get(block_ref, name, 2 * c + j)) for j in range(2)]


def coarse_kernel(plan, blocks, block_ref, *refs):
    factors, outs = refs[:3], refs[3 + 2 * plan.m :]
    early, late = refs[3 : 3 + plan.m], refs[3 + plan.m : 3 + 2 * plan.m]
    c, rhs = lax.axis_index("py"), plan.rhs
    down, up = [], []
    rows = {
        level: level_rows(plan, level, early, late, blocks, block_ref) for level in (1, 2, 3)
    }
    solved = {}
    for level in (1, 2, 3):
        count = plan.h[level] // 2
        pairs = range(count) if level > 1 else sorted({0, count - 1})
        solved[level] = solve_pairs(
            plan, level, rows[level], [(2 * b, b) for b in pairs], factors[level - 1]
        )
    for level in (1, 2, 3):
        w = plan.tile[level]
        for j, (edge, at) in enumerate(((up, 0), (down, -1))):
            for value in solved[level]:
                if w % LANES == 0:
                    edge.append(value[at][:, j * w : (j + 1) * w])
                else:
                    edge.append(pltpu.roll(value[at], LANES - w, 1) if j else value[at])
    edges = [jnp.concatenate(edge, axis=1) for edge in (down, up)]
    picked = product(jnp.concatenate(edges, axis=0), blocks.get(block_ref, "pick", c))
    write_halos(c, [picked[:rhs]], [picked[rhs:]], outs[4], outs[5])
    for level in (1, 2, 3):
        for t, values in enumerate(solved[level]):
            for k, value in enumerate(values):
                outs[level - 1][t, k] = value
    for i, row in enumerate(rows[1][2:-2]):
        outs[3][i] = row


def inner_kernel(plan, blocks, block_ref, factor_ref, rows_ref, one_ref, two_ref, three_ref,
                 main_ref, picked_ref, *refs):
    early, late = refs[: plan.m], refs[plan.m : 2 * plan.m]
    outs, fine_ref = refs[2 * plan.m : -1], refs[-1]
    rhs, count = plan.rhs, plan.h[1] // 2
    rows = [rows_ref[i] for i in range(rows_ref.shape[0])]
    pairs = [(2 * (b - 1), b) for b in range(1, count - 1)]
    inner = solve_pairs(plan, 1, rows, pairs, factor_ref)
    for level, ref in ((1, one_ref), (2, two_ref), (3, three_ref)):
        solved = []
        for t in range(ref.shape[0]):
            values = [ref[t, k] for k in range(ref.shape[1])]
            if level == 1:
                values[1:1] = inner[t]
            solved.append(values)
        lifted = lift_pairs(plan, level, solved, blocks, block_ref)
        for b in range(plan.h[level] // 2):
            for j in range(2):
                outs[level - 1][2 * b + j] = lifted[j][b * rhs : (b + 1) * rhs]
    sides, w0 = side_columns(plan, early, late), plan.w0
    lane = lane_index(rhs)
    for b in range(plan.h0 // 2):
        value = pltpu.roll(sides, (LANES - 4 * b) % LANES, 1) if b else sides
        value = jnp.where(lane < 8, value, 0.0)[:, :16].astype(BF16)
        added = jnp.dot(value, picked_ref[b], preferred_element_type=F32)
        for j in range(2):
            fine_ref[2 * b + j] = main_ref[2 * b + j] + added[:, j * w0 : (j + 1) * w0]


def fine_kernel(plan, rows_ref, first_ref, second_ref, factor_ref, out_ref, picked_ref):
    rhs, h0, w0 = plan.rhs, plan.h0, plan.w0
    above, below = read_halos(plan, first_ref, second_ref)
    lane = lane_index(rhs)
    rows = [above[0]] + [rows_ref[row] for row in range(h0)] + [below[0]]
    length = 4 * (w0 + 2)
    side = lax.broadcasted_iota(jnp.int32, (16, length), 0)
    at = lax.broadcasted_iota(jnp.int32, (16, length), 1)
    wanted = (side // 2) * (w0 + 2) + (side % 2) * (w0 + 1)
    pick = jnp.where(at == wanted, 1.0, 0.0).astype(BF16)
    for b in range(h0 // 2):
        tiles, before = [], None
        for k in range(5):
            if k < 4:
                rolled = pltpu.roll(rows[2 * b + k], 2 * k + 1, 1)
                value = jnp.where(lane > 2 * k, rolled, 0.0)
            else:
                value = jnp.zeros((rhs, LANES), F32)
            if before is not None:
                value = jnp.where(lane < 2 * k - 1, before, value)
            tiles.append(value)
            before = rolled
        lhs = jnp.concatenate(tiles, axis=1).astype(BF16)[:, :length]
        solved = solve(jnp.concatenate([lhs, pick], axis=0), factor_ref[b, 0])
        for j in range(2):
            out_ref[2 * b + j] = solved[:rhs, j * w0 : (j + 1) * w0]
        picked_ref[b] = solved[rhs:].astype(BF16)


def side_columns(plan, early_refs, late_refs):
    c, rhs, h0 = lax.axis_index("py"), plan.rhs, plan.h0
    found = []
    for offset in (-1, 1):
        total = None
        for early, late, owner in zip(early_refs, late_refs, owners(plan)):
            chosen = jnp.where(owner == c + offset, 1.0, 0.0).astype(F32)
            parts = [early[0] * chosen, early[1] * chosen, late[4 * rhs :] * chosen]
            total = parts if total is None else [a + b for a, b in zip(total, parts)]
        found.append(total)
    slots = []
    for left, right in zip(*found):
        even = lane_index(left.shape[0]) % 2 == 0
        slots.append(jnp.where(even, left, right))
    packed = slots.pop()
    outer = [pltpu.roll(packed, LANES - 4 * k, 1) if k else packed for k in range(rhs // 8)]
    outer = jnp.concatenate(outer, axis=0)
    lane, start = lane_index(rhs), plan.offset[3]
    inner = [
        pltpu.roll(slot, (2 + k * h0 - start) % LANES, 1) for k, slot in enumerate(slots)
    ]
    value = jnp.where(lane < 2 * h0 + 4, pltpu.roll(outer, 2 * h0, 1), 0.0)
    value = jnp.where(lane < 2 * h0 + 2, inner[1], value)
    value = jnp.where(lane < h0 + 2, inner[0], value)
    return jnp.where(lane < 2, outer, value)


def whole_kernel(plan, group, partners, blocks, block_ref, four_ref, inverse_ref, *refs):
    count = plan.n // 2
    gathered, out_ref, pair_ref, four_rows = refs[:count], refs[count], refs[-2], refs[-1]
    r, c = lax.axis_index("px"), lax.axis_index("py")
    rhs, ny4 = plan.rhs, plan.ny[4]
    nx4, nx5 = plan.nx[4], plan.nx[5]
    odd = jnp.bitwise_and(c, 1)
    for block, (left, right) in zip(gathered, partners):
        partner = jnp.where(odd == 1, right, left)
        pair_ref[jnp.bitwise_xor(r, partner) // 2] = block[...]
    lane = lane_index(rhs)
    inside = jnp.logical_and(lane >= 1, lane <= ny4)

    def part_row(pair, j):
        tile, start = divmod(j * ny4, LANES)
        value = pair_ref[pair, :, tile * LANES : (tile + 1) * LANES]
        return jnp.where(inside, pltpu.roll(value, (1 - start) % LANES, 1), 0.0)

    zero = jnp.zeros((rhs, LANES), F32)
    rows = [zero]
    for i in range(nx4):
        value = part_row(i // 2, 1 + i % 2)
        if i % 2 == 0 and i > 0:
            value = value + part_row(i // 2 - 1, 3)
        if i % 2 == 1 and i < nx4 - 1:
            value = value + part_row(i // 2 + 1, 0)
        rows.append(value)
    rows.append(zero)
    five = shrink_rows(rows, nx4, 1)[1:-1]
    flat = product(jnp.concatenate(five, axis=1), blocks.get(block_ref, "shrink5")) * SHRINK
    flat = flat[:, : inverse_ref.shape[0]]
    part_five = jnp.dot(flat.astype(BF16), inverse_ref[...], preferred_element_type=F32)
    spread = blocks.get(block_ref, "lift5")[: part_five.shape[1], : nx4 * ny4]
    lifted = product(part_five, spread) * SHRINK
    w, tiles = plan.tile[4], plan.tiles[4]
    parts = []
    for b in range(nx4 // 2):
        for t in range(tiles):
            pieces = []
            for k in range(4):
                lanes = range(t * w, t * w + w + 2, LANES)
                pieces.append([rows[2 * b + k][:, lo : lo + LANES] for lo in lanes])
            lhs = assemble(pieces, w)
            parts.append(
                lax.dot_general(
                    lhs, four_ref[b, t], (((1,), (1,)), ((), ())), preferred_element_type=F32
                )
            )
    correction = jnp.concatenate(parts, axis=1) + lifted
    width = group * 2 * w * tiles
    bands = nx4 // 2 // group
    stacked = jnp.concatenate(
        [correction[:, i * width : (i + 1) * width] for i in range(bands)], axis=0
    )
    four_rows[0] = jnp.zeros((rhs, LANES), F32)
    four_rows[nx4 + 1] = jnp.zeros((rhs, LANES), F32)
    for g in range(group):
        for j in range(2):
            value = product(stacked, blocks.get(block_ref, "lift4", (c * group + g) * 2 + j))
            for i in range(bands):
                four_rows[1 + 2 * (i * group + g) + j] = value[i * rhs : (i + 1) * rhs]
    for k in range(3):
        out_ref[k] = four_rows[r + k]


def final_kernel(plan, blocks, block_ref, fine_ref, one_ref, two_ref, three_ref, four_ref,
                 first_ref, second_ref, out_ref, whole_ref, semaphores):
    r, rhs = lax.axis_index("px"), plan.rhs
    above = jnp.where(r > 0, 1.0, 0.0).astype(F32)
    below = jnp.where(r < plan.n - 1, 1.0, 0.0).astype(F32)
    halos = read_halos(plan, first_ref, second_ref)
    halo = product(
        jnp.concatenate([halos[0][0], halos[1][0]], axis=0),
        blocks.get(block_ref, "band", lax.axis_index("py")),
    )
    from_above, from_below = [
        [halo[k * rhs : (k + 1) * rhs, l * plan.w0 : (l + 1) * plan.w0] for l in range(3)]
        for k in range(2)
    ]
    copies = []
    for part in range(rhs // 8):
        own = slice(8 * part, 8 * (part + 1))
        rows = [four_ref[k, own] for k in range(3)]
        for level, own_ref in ((3, three_ref), (2, two_ref), (1, one_ref)):
            height = plan.h[level]
            lifted = lift_rows(rows, -1, height + 1)
            rows = [lifted[0] * above + from_above[level - 1][own]]
            rows += [lifted[i + 1] + own_ref[i, own] for i in range(height)]
            rows += [lifted[-1] * below + from_below[level - 1][own]]
        lifted = lift_rows(rows, 0, plan.h0)
        start, count = 8 * part * plan.h0, 8 * plan.h0
        for row in range(plan.h0):
            value = lifted[row] + fine_ref[row, own]
            whole_ref[pl.ds(start + row, 8, stride=plan.h0), :] = value
        span = pl.ds(start, count)
        copies.append(
            pltpu.make_async_copy(whole_ref.at[span], out_ref.at[span], semaphores.at[part])
        )
        copies[-1].start()
    for copy in copies:
        copy.wait()


def per_device(mesh_shape, residual, factor_fine, factor_one, factor_two, factor_three,
               factor_four, coarse_inverse):
    factors = [factor_fine, factor_one, factor_two, factor_three, factor_four]
    plan = Plan(mesh_shape, residual.shape, [f.shape for f in factors])
    n, m, rhs, h, h0 = plan.n, plan.m, plan.rhs, plan.h, plan.h0
    x = residual.reshape(rhs * h0, plan.w0)

    def trade(first, second):
        def target(i, c):
            after = i + 1 if c & 2 else i - 1
            return (after, c) if 0 <= after < n else (i, c ^ 2)

        ring = []
        for i in range(n):
            for c in range(m):
                row, column = target(i, c)
                ring.append((i * m + c, row * m + column))
        back = [(b, a) for a, b in ring]
        return lax.ppermute(first, ("px", "py"), ring), lax.ppermute(second, ("px", "py"), back)

    def swap(value, bits):
        return lax.ppermute(value, "py", [(i, i ^ bits) for i in range(m)])

    blocks = Blocks()
    blocks.add("four", plan.place_four())
    blocks.add("pick", plan.pick_band())
    blocks.add("band", plan.lift_band())
    for l in (1, 2, 3):
        blocks.add(f"place{l}", plan.place_whole(l))
        if plan.tile[l] % LANES == 0:
            blocks.add(f"lift{l}", plan.lift_columns(l))
        else:
            lifted = plan.lift_rows_of(l)
            blocks.add(f"lift{l}", lifted.reshape(m, 2, -1, plan.w0))
    lifted, group = plan.level_four_lift()
    blocks.add("lift4", lifted)
    blocks.add("shrink5", plan.coarsest_shrink())
    blocks.add("lift5", plan.coarsest_lift())
    matrices = blocks.array()

    shrink = kernel_call(
        functools.partial(shrink_kernel, plan),
        jax.ShapeDtypeStruct((4, LANES, LANES), BF16), cost_us=4.0,
    )()
    early, outer, first, second, rows = kernel_call(
        functools.partial(restrict_kernel, plan),
        (shape(6, rhs, LANES), shape(4, rhs, LANES), shape(3, rhs, LANES), shape(3, rhs, LANES),
         shape(h0, rhs, plan.w0)),
    )(x, shrink)
    first, second = trade(first, second)
    early = kernel_call(
        functools.partial(inner_rows_kernel, plan), shape(4, rhs, LANES), cost_us=0.3
    )(early, rows)

    def spread(bands, bits):
        for bit in bits:
            bands.update({k ^ bit: swap(band, bit) for k, band in list(bands.items())})
        return bands

    bits = [1 << k for k in reversed(range(m.bit_length() - 1))]
    early, first, second = lax.optimization_barrier((early, first, second))
    early = spread({0: early}, bits[:1])
    late = kernel_call(functools.partial(merge_kernel, plan), shape(4 * rhs + 8, LANES))(
        outer, shrink, first, second
    )

    main, picked = kernel_call(
        functools.partial(fine_kernel, plan),
        (shape(h0, rhs, plan.w0), jax.ShapeDtypeStruct((h0 // 2, 16, 2 * plan.w0), BF16)),
        cost_us=0.7,
    )(rows, first, second, factor_fine)
    late = spread({0: late}, bits[:1])
    late, main, picked = lax.optimization_barrier((late, main, picked))
    early, late = spread(early, bits[1:]), spread(late, bits[1:])
    early, late = [early[k] for k in range(m)], [late[k] for k in range(m)]

    pairs = kernel_call(
        functools.partial(gather_kernel, plan, blocks), shape(rhs, 4 * plan.ny[4]), cost_us=0.3
    )(matrices, *late)
    order, fetched, gathered, partners = list(range(n // 2 - 1, 0, -1)), [], [pairs], [(0, 0)]
    for k in range(0, len(order), 2):
        even, odd = order[k], order[min(k + 1, len(order) - 1)]
        routes = [
            (i * m + c, (i ^ (2 * (odd if c % 2 else even))) * m + c)
            for i in range(n) for c in range(m)
        ]
        fetched.append((lax.ppermute(pairs, ("px", "py"), routes), even, odd))
    late, pairs = lax.optimization_barrier((late, pairs))
    for value, even, odd in fetched:
        gathered.append(value)
        partners.append((2 * even, 2 * odd))
        if even != odd:
            gathered.append(swap(value, 1))
            partners.append((2 * odd, 2 * even))


    one, two, three, inner, low, high = kernel_call(
        functools.partial(coarse_kernel, plan, blocks),
        tuple(
            shape(plan.tiles[l], count, rhs, 2 * plan.tile[l])
            for l, count in ((1, 2), (2, h[2] // 2), (3, h[3] // 2))
        )
        + (shape(h[1] - 2, rhs, plan.ny[1]),)
        + (shape(1, rhs, LANES), shape(1, rhs, LANES)),
        cost_us=2.5,
    )(matrices, factor_one, factor_two, factor_three, *early, *late)
    low, high = trade(low, high)
    one, two, three, fine = kernel_call(
        functools.partial(inner_kernel, plan, blocks),
        tuple(shape(h[l], rhs, LANES) for l in (1, 2, 3)) + (shape(h0, rhs, plan.w0),),
        cost_us=1.2,
    )(matrices, factor_one, inner, one, two, three, main, picked, *early, *late)
    four = kernel_call(
        functools.partial(whole_kernel, plan, group, partners, blocks),
        shape(3, rhs, LANES),
        scratch=(
            pltpu.VMEM((n // 2, rhs, 4 * plan.ny[4]), F32),
            pltpu.VMEM((plan.nx[4] + 2, rhs, LANES), F32),
        ),
    )(matrices, jnp.swapaxes(factor_four, 2, 3), coarse_inverse, *gathered)
    out = kernel_call(
        functools.partial(final_kernel, plan, blocks), shape(rhs * h0, plan.w0),
        scratch=(pltpu.VMEM((rhs * h0, plan.w0), F32), pltpu.SemaphoreType.DMA((rhs // 8,))),
        out_space=pl.ANY,
    )(
        matrices, fine, one, two, three, four, low, high
    )
    return out.reshape(rhs, h0, plan.w0)


def solution(mesh):
    placed = (
        P(None, "px", "py"),
        P("px", "py", None, None),
        P("px", None, None, None),
        P("px", None, None, None),
        P("px", None, None, None),
        P(),
        P(),
    )
    return jax.shard_map(
        functools.partial(per_device, dict(mesh.shape)),
        mesh=mesh, in_specs=placed, out_specs=P(None, "px", "py"), check_vma=False,
    )
```

```python
import functools
import math

import jax
import jax.numpy as jnp
import numpy as np
from jax import lax
from jax.experimental import pallas as pl
from jax.experimental.pallas import tpu as pltpu
from jax.sharding import PartitionSpec as P

F32 = jnp.float32
BF16 = jnp.bfloat16
LANES = 128
SHRINK = 1.0 / 20.0
TAPS = (1, 3, 3, 1)
VMEM_BYTES = 24 * 1024 * 1024


def round_up(value, unit=LANES):
    return -(-value // unit) * unit


def global_prolong(coarse):
    out = np.zeros((coarse, 2 * coarse))
    for i in range(coarse):
        out[i, 2 * i] += 3
        out[i, 2 * i + 1] += 3
        if i > 0:
            out[i, 2 * i - 1] += 1
        if i + 1 < coarse:
            out[i, 2 * i + 2] += 1
    return out


def bf(array):
    return np.asarray(array, np.float32).astype(jnp.bfloat16)


class Plan:
    def __init__(self, mesh_shape, residual, factors):
        self.n, self.m = mesh_shape["px"], mesh_shape["py"]
        self.rhs, self.h0, self.w0 = residual
        self.h = [self.h0 >> l for l in range(5)]
        self.w = [self.w0 >> l for l in range(5)]
        self.ny = [self.w0 * self.m >> l for l in range(6)]
        self.nx = [self.h0 * self.n >> l for l in range(6)]
        self.tile = [f[3] // 2 for f in factors]
        self.tiles = [f[1] for f in factors]
        self.slots = self.h[1] + 2
        self.offset = [None, 0]
        for l in (2, 3, 4):
            self.offset.append(self.offset[-1] + self.w[l - 1] + 2)
        self.sides = self.h0 // 2 + 1
        self.first = self.w[1] + 2
        self.rest = LANES - self.first
        self.tail = self.offset[3] + 2 * self.sides

    def place(self, level, lead, width, at=0):
        out = np.zeros((self.m, LANES, width))
        for c in range(self.m):
            for k in range(self.w[level] + 2):
                column = self.w[level] * c - 1 + k
                if -lead <= column < self.ny[level]:
                    out[c, self.offset[level] + k, at + column + lead] = 1
        return out

    def place_whole(self, level):
        if self.tile[level] == LANES:
            return self.place(level, 0, self.ny[level])
        return self.place(level, 1, round_up(self.ny[level] + 2))

    def place_four(self):
        rows = [self.place(4, 0, 4 * self.ny[4], j * self.ny[4]) for j in range(4)]
        return np.stack(rows, axis=1)

    def pick_band(self):
        out = []
        for l in (1, 2, 3):
            pick = np.zeros((self.m, round_up(self.ny[l]), LANES))
            one = self.place(l, 0, self.ny[l])
            pick[:, : self.ny[l]] = one.transpose(0, 2, 1)
            out.append(pick)
        return np.concatenate(out, axis=1)

    def lift_band(self):
        out = []
        for l in (1, 2, 3):
            one = self.place(l, 0, self.ny[l])
            out.append(np.einsum("cki,cif->ckf", one, self.lift_columns(l)))
        return np.concatenate(out, axis=2)

    def lift_columns(self, level):
        out = np.eye(self.ny[level])
        for l in range(level, 0, -1):
            out = out @ global_prolong(self.ny[l])
        return out.reshape(self.ny[level], self.m, self.w0).transpose(1, 0, 2)

    def lift_rows_of(self, level):
        w, tiles = self.tile[level], self.tiles[level]
        full = self.lift_columns(level).reshape(self.m, tiles, w, self.w0)
        out = np.zeros((self.m, 2, tiles, 2 * w, self.w0))
        for j in range(2):
            out[:, j, :, j * w : (j + 1) * w] = full
        return out

    def coarsest_shrink(self):
        nx5, ny5, ny4 = self.nx[5], self.ny[5], self.ny[4]
        columns = global_prolong(ny5).T
        width = round_up(ny4 + 2)
        out = np.zeros((nx5, width, nx5 * ny5))
        for i in range(nx5):
            out[i, 1 : 1 + ny4, i * ny5 : (i + 1) * ny5] = columns
        return bf(out.reshape(nx5 * width, nx5 * ny5))

    def coarsest_lift(self):
        rows, columns = global_prolong(self.nx[5]), global_prolong(self.ny[5])
        both = np.einsum("ia,jb->ijab", rows, columns)
        w, tiles = self.tile[4], self.tiles[4]
        both = both.reshape(self.nx[5] * self.ny[5], self.nx[4] // 2, 2, tiles, w)
        both = both.transpose(0, 1, 3, 2, 4)
        return bf(both.reshape(self.nx[5] * self.ny[5], self.nx[4] * self.ny[4]))

    def level_four_lift(self):
        pair = 2 * self.tile[4] * self.tiles[4]
        group = max(1, LANES // pair)
        width = group * pair
        rows = self.lift_rows_of(4).reshape(self.m, 2, pair, self.w0)
        out = np.zeros((self.m, group, 2, width, self.w0))
        for g in range(group):
            out[:, g, :, g * pair : (g + 1) * pair] = rows
        return bf(out), group


class Blocks:
    def __init__(self):
        self.parts, self.places, self.count = [], {}, 0

    def add(self, name, array):
        lead, (rows, columns) = array.shape[:-2], array.shape[-2:]
        high, wide = round_up(rows) // LANES, round_up(columns) // LANES
        out = np.zeros((math.prod(lead), high * LANES, wide * LANES), np.float32)
        out[:, :rows, :columns] = np.asarray(array, np.float32).reshape((-1, rows, columns))
        out = out.reshape(-1, high, LANES, wide, LANES).transpose(0, 1, 3, 2, 4)
        self.parts.append(out.reshape(-1, LANES, LANES))
        self.places[name] = (self.count, high, wide)
        self.count += len(self.parts[-1])

    def array(self):
        return jnp.asarray(bf(np.concatenate(self.parts, axis=0)))

    def get(self, ref, name, lead=0):
        base, high, wide = self.places[name]
        base = base + lead * (high * wide)
        rows = [
            jnp.concatenate([ref[base + i * wide + j] for j in range(wide)], axis=1)
            for i in range(high)
        ]
        return jnp.concatenate(rows, axis=0)


def split(value):
    high = value.astype(BF16)
    return high, (value - high.astype(F32)).astype(BF16)


def product(value, matrix):
    high, low = split(value)
    count = value.shape[0]
    both = jnp.dot(
        jnp.concatenate([high, low], axis=0), matrix, preferred_element_type=F32
    )
    return both[:count] + both[count:]


def shrink_rows(rows, count, halo):
    out = []
    for i in range(-1, count // 2 + 1):
        total = None
        for t, tap in enumerate(TAPS):
            j = 2 * i - 1 + t
            if -halo <= j < count + halo:
                term = rows[j + halo] * float(tap) if tap > 1 else rows[j + halo]
                total = term if total is None else total + term
        out.append(total)
    return out


def lift_rows(rows, first, last):
    out = []
    for f in range(first, last):
        i = f // 2
        other = i - 1 if f % 2 == 0 else i + 1
        out.append((rows[i + 1] * 3.0 + rows[other + 1]) * SHRINK)
    return out


def lane_index(rows):
    return lax.broadcasted_iota(jnp.int32, (rows, LANES), 1)


def assemble(pieces, width):
    total = 4 * (width + 2)
    tiles = [[] for _ in range(-(-total // LANES))]
    lane = lane_index(pieces[0][0].shape[0])
    for k, piece in enumerate(pieces):
        for q, value in enumerate(piece):
            start = k * (width + 2) + LANES * q
            count = min(LANES, width + 2 - LANES * q)
            shift, at = start % LANES, start // LANES
            rolled = pltpu.roll(value, shift, 1) if shift else value
            tiles[at].append((min(LANES, shift + count), rolled))
            if shift + count > LANES:
                tiles[at + 1].append((shift + count - LANES, rolled))
    out = []
    for segments in tiles:
        segments = sorted(segments, key=lambda s: -s[0])
        end, value = segments[0]
        if end < LANES:
            value = jnp.where(lane < end, value, 0.0)
        for end, part in segments[1:]:
            value = jnp.where(lane < end, part, value)
        out.append(value)
    return jnp.concatenate(out, axis=1).astype(BF16)[:, :total]


def solve(lhs, factor):
    return jnp.dot(lhs, factor, preferred_element_type=F32)


def kernel_call(body, out_shape, scratch=(), cost_us=1.0, out_space=pltpu.VMEM):
    whole = pl.BlockSpec(memory_space=pltpu.VMEM)
    result = pl.BlockSpec(memory_space=out_space)

    def call(*operands):
        return pl.pallas_call(
            body,
            out_shape=out_shape,
            in_specs=[whole] * len(operands),
            out_specs=jax.tree.map(lambda _: result, out_shape),
            scratch_shapes=list(scratch),
            compiler_params=pltpu.CompilerParams(vmem_limit_bytes=VMEM_BYTES),
            cost_estimate=pl.CostEstimate(
                flops=int(cost_us * 1e9), bytes_accessed=int(cost_us * 3e6), transcendentals=0
            ),
        )(*operands)

    return call


def shape(*dims):
    return jax.ShapeDtypeStruct(dims, F32)


def tap_matrix(row_lead, lane_lead, count, first, last):
    row = lax.broadcasted_iota(jnp.int32, (LANES, LANES), 0) - row_lead
    lane = lax.broadcasted_iota(jnp.int32, (LANES, LANES), 1) - lane_lead
    tap = row - 2 * lane + 3
    outer = jnp.logical_or(tap == 0, tap == 3)
    inner = jnp.logical_or(tap == 1, tap == 2)
    value = jnp.where(outer, 1.0, jnp.where(inner, 3.0, 0.0))
    value = jnp.where(jnp.logical_or(lane < first, lane > count + 1 - last), 0.0, value)
    return value.astype(BF16)


def place_sides(plan, slot_value, row, at):
    lane = lane_index(plan.rhs)
    chosen = jnp.logical_or(lane == at, lane == at + 1)
    return jnp.where(chosen, pltpu.roll(row, (at + 1) % LANES, 1), slot_value)


def column_ends(plan):
    c = lax.axis_index("py")
    return jnp.where(c == 0, 1, 0), jnp.where(c == plan.m - 1, 1, 0)


def write_halos(c, down, up, first_ref, second_ref, pairs=False):
    forward = jnp.bitwise_and(c, 2) != 0
    if pairs:
        forward = lax.rem(lax.axis_index("px"), 2) == 1
    for k, (low, high) in enumerate(zip(down, up)):
        first_ref[k] = jnp.where(forward, low, high)
        second_ref[k] = jnp.where(forward, high, low)


def read_halos(plan, first_ref, second_ref, pairs=False):
    r, c = lax.axis_index("px"), lax.axis_index("py")
    forward = jnp.bitwise_and(c, 2) != 0
    if pairs:
        forward = lax.rem(r, 2) == 0
    above = jnp.where(r > 0, 1.0, 0.0).astype(F32)
    below = jnp.where(r < plan.n - 1, 1.0, 0.0).astype(F32)
    first, second = first_ref[...], second_ref[...]
    return jnp.where(forward, first, second) * above, jnp.where(forward, second, first) * below


def shrink_kernel(plan, out_ref):
    first, last = column_ends(plan)
    shrink = None
    for level in (1, 2, 3, 4):
        lead = 0 if level == 1 else plan.offset[level - 1] + 1
        step = tap_matrix(lead, plan.offset[level], plan.w[level], first, last)
        if shrink is None:
            shrink = step
        else:
            shrink = jnp.dot(shrink, step, preferred_element_type=F32).astype(BF16)
        out_ref[level - 1] = shrink


def restrict_kernel(plan, x_ref, shrink_ref, early_ref, outer_ref, first_ref, second_ref, rows_ref):
    r, c = lax.axis_index("px"), lax.axis_index("py")
    rhs, slots, h = plan.rhs, plan.slots, plan.h
    above = jnp.where(r > 0, 1.0, 0.0).astype(F32)
    below = jnp.where(r < plan.n - 1, 1.0, 0.0).astype(F32)
    x = [x_ref[pl.ds(row, rhs, stride=h[0]), :] for row in range(h[0])]
    rows, total = x, None
    for level in (1, 2, 3, 4):
        rows = shrink_rows(rows, h[level - 1], 0 if level == 1 else 1)
        rows[0] = rows[0] * above
        rows[-1] = rows[-1] * below
        part = product(jnp.concatenate(rows, axis=0), shrink_ref[level - 1])
        if total is None:
            total = part
        else:
            count = part.shape[0]
            total = jnp.concatenate([total[:count] + part, total[count:]], axis=0)
    lane = lane_index(slots * rhs)
    scale = jnp.where(lane < plan.offset[2], SHRINK, SHRINK**2)
    scale = jnp.where(lane < plan.offset[3], scale, SHRINK**3)
    total = total * jnp.where(lane < plan.offset[4], scale, SHRINK**4)
    own = [total[i * rhs : (i + 1) * rhs] for i in range(slots)]
    lane = lane_index(rhs)
    one, two, three = plan.offset[2:]
    for k in range(6):
        early_ref[k] = own[2 + k]
    outer = [own[0], own[1]]
    for k in range(2):
        value = jnp.where(lane < two, own[h[2] + k], own[h[3] + k])
        outer.append(jnp.where(lane < one, own[h[1] + k], value))
    for k in range(4):
        outer_ref[k] = outer[k]
    third = pltpu.roll(own[2], LANES - three, 1)
    down = [x[-1], jnp.where(lane < three, outer[2], own[0])]
    down.append(jnp.where(lane < one, third, jnp.where(lane < three, outer[3], own[1])))
    up = [x[0], jnp.where(lane < one, third, own[0]), own[1]]
    write_halos(c, down, up, first_ref, second_ref, True)
    for i, row in enumerate(x):
        rows_ref[i] = row


def inner_rows_kernel(plan, own_ref, rows_ref, early_ref):
    h, rhs = plan.h, plan.rhs
    lane = lane_index(rhs)
    two = plan.offset[3]
    own = [None, None] + [own_ref[k] for k in range(6)]
    x = [rows_ref[k] for k in range(h[0])]
    inner = [own[2], own[3], own[4], own[5]]
    for k in range(2):
        value = inner[k]
        value = jnp.where(lane < two, value, 0.0)
        for j in range(h[0] // 2):
            value = place_sides(plan, value, x[k * (h[0] // 2) + j], two + 2 * j)
        odd_row, end = own[6 + k], plan.tail + plan.first - plan.rest
        moved = pltpu.roll(odd_row, (plan.tail - plan.rest) % LANES, 1)
        chosen = jnp.logical_and(lane >= plan.tail, lane < end)
        early_ref[k] = jnp.where(chosen, moved, value)
        moved = pltpu.roll(odd_row, plan.first, 1)
        early_ref[2 + k] = jnp.where(lane < plan.first, inner[2 + k], moved)


def merge_kernel(plan, outer_ref, shrink_ref, first_ref, second_ref, out_ref):
    r, rhs = lax.axis_index("px"), plan.rhs
    lane = lane_index(rhs)
    above, below = read_halos(plan, first_ref, second_ref, True)
    one, two, three = plan.offset[2:]
    edge = product(jnp.concatenate([above[0], below[0]], axis=0), shrink_ref[0]) * SHRINK
    added = [
        above[1],
        jnp.where(lane < one, edge[:rhs], above[2]),
        jnp.where(lane < one, edge[rhs:], below[1]),
        below[2],
    ]
    even = lax.rem(r, 2) == 0
    own = [outer_ref[k] for k in range(3)]
    partner = [jnp.where(even, below[k], above[k]) for k in (1, 2)]
    third = jnp.where(even, below[1], above[2])
    partner.append(pltpu.roll(third, three, 1))
    low = [jnp.where(even, a, b) for a, b in zip(own, partner)]
    high = [jnp.where(even, b, a) for a, b in zip(own, partner)]
    sums = [low[0], low[1] + high[0], low[2] + high[1], high[2]]
    for k in range(4):
        value = jnp.where(lane < three, outer_ref[k] + added[k], sums[k])
        out_ref[k * rhs : (k + 1) * rhs] = value
    sides = place_sides(plan, jnp.zeros((rhs, LANES), F32), above[0], 0)
    sides = place_sides(plan, sides, below[0], 2)
    total = None
    for k in range(rhs // 8):
        part = sides[8 * k : 8 * (k + 1)]
        part = pltpu.roll(part, 4 * k, 1) if k else part
        total = part if total is None else total + part
    out_ref[4 * rhs :] = total


def banded(bands, matrices):
    return product(jnp.concatenate(bands, axis=1), jnp.concatenate(matrices, axis=0))


def owners(plan):
    c = lax.axis_index("py")
    return [jnp.bitwise_xor(c, k) for k in range(plan.m)]


def gather_kernel(plan, blocks, block_ref, *refs):
    band_refs, out_ref = refs[:-1], refs[-1]
    values, matrices = [], []
    for band, owner in zip(band_refs, owners(plan)):
        for j in range(4):
            values.append(band[j * plan.rhs : (j + 1) * plan.rhs])
            matrices.append(blocks.get(block_ref, "four", 4 * owner + j))
    out_ref[...] = banded(values, matrices)


def level_rows(plan, level, early_refs, late_refs, blocks, block_ref):
    rhs, values = plan.rhs, []
    lane = lane_index(rhs)
    for early, late in zip(early_refs, late_refs):
        outer = [late[i * rhs : (i + 1) * rhs] for i in range(4)]
        inner = []
        if level == 1:
            inner = [early[k] for k in range(4)]
            for k in range(2):
                begin = pltpu.roll(early[2 + k], plan.rest, 1)
                end = pltpu.roll(early[k], (plan.rest - plan.tail) % LANES, 1)
                inner.append(jnp.where(lane < plan.rest, begin, end))
        elif level == 2:
            inner = [early[k] for k in range(2)]
        values.append(jnp.concatenate(outer[:2] + inner + outer[2:], axis=0))
    matrices = [blocks.get(block_ref, f"place{level}", owner) for owner in owners(plan)]
    whole = jnp.dot(
        jnp.concatenate(values, axis=1).astype(BF16), jnp.concatenate(matrices, axis=0),
        preferred_element_type=F32,
    )
    return [whole[i * rhs : (i + 1) * rhs] for i in range(plan.h[level] + 2)]


def assemble_tiles(rows, t):
    rhs, count = rows[0].shape[0], rows[0].shape[1] // LANES
    lane = lane_index(rhs)

    def rolled(k, tile):
        if not 0 <= tile < count:
            return jnp.zeros((rhs, LANES), F32)
        return pltpu.roll(rows[k][:, tile * LANES : (tile + 1) * LANES], 2 * k + 1, 1)

    out = []
    for k in range(5):
        if k < 4:
            value = jnp.where(lane == 2 * k, rolled(k, t - 1), rolled(k, t))
        else:
            value = jnp.zeros((rhs, LANES), F32)
        if k > 0:
            value = jnp.where(lane == 2 * k - 1, rolled(k - 1, t + 1), value)
            value = jnp.where(lane < 2 * k - 1, rolled(k - 1, t), value)
        out.append(value)
    return jnp.concatenate(out, axis=1).astype(BF16)[:, : 4 * (LANES + 2)]


def solve_pairs(plan, level, rows, pairs, factor_ref):
    w, solved = plan.tile[level], []
    for t in range(plan.tiles[level]):
        solved.append([])
        for at, b in pairs:
            window = rows[at : at + 4]
            if w == LANES:
                lhs = assemble_tiles(window, t)
            else:
                lhs = assemble([[row] for row in window], w)
            solved[t].append(solve(lhs, factor_ref[b, t]))
    return solved


def lift_pairs(plan, level, solved, blocks, block_ref):
    c, w = lax.axis_index("py"), plan.tile[level]
    name, count = f"lift{level}", len(solved[0]) * plan.rhs
    stacked = [jnp.concatenate(values, axis=0) for values in solved]
    if w % LANES == 0:
        both = [
            jnp.concatenate([v[:, j * w : (j + 1) * w] for v in stacked], axis=1)
            for j in range(2)
        ]
        both = product(jnp.concatenate(both, axis=0), blocks.get(block_ref, name, c))
        return [both[:count], both[count:]]
    row = jnp.concatenate(stacked, axis=1)
    return [product(row, blocks.get(block_ref, name, 2 * c + j)) for j in range(2)]


def coarse_kernel(plan, blocks, block_ref, *refs):
    factors, outs = refs[:3], refs[3 + 2 * plan.m :]
    early, late = refs[3 : 3 + plan.m], refs[3 + plan.m : 3 + 2 * plan.m]
    c, rhs = lax.axis_index("py"), plan.rhs
    down, up = [], []
    rows = {
        level: level_rows(plan, level, early, late, blocks, block_ref) for level in (1, 2, 3)
    }
    solved = {}
    for level in (1, 2, 3):
        count = plan.h[level] // 2
        pairs = range(count) if level > 1 else sorted({0, count - 1})
        solved[level] = solve_pairs(
            plan, level, rows[level], [(2 * b, b) for b in pairs], factors[level - 1]
        )
    for level in (1, 2, 3):
        w = plan.tile[level]
        for j, (edge, at) in enumerate(((up, 0), (down, -1))):
            for value in solved[level]:
                if w % LANES == 0:
                    edge.append(value[at][:, j * w : (j + 1) * w])
                else:
                    edge.append(pltpu.roll(value[at], LANES - w, 1) if j else value[at])
    edges = [jnp.concatenate(edge, axis=1) for edge in (down, up)]
    picked = product(jnp.concatenate(edges, axis=0), blocks.get(block_ref, "pick", c))
    write_halos(c, [picked[:rhs]], [picked[rhs:]], outs[4], outs[5], False)
    for level in (1, 2, 3):
        for t, values in enumerate(solved[level]):
            for k, value in enumerate(values):
                outs[level - 1][t, k] = value
    for i, row in enumerate(rows[1][2:-2]):
        outs[3][i] = row


def inner_kernel(plan, blocks, block_ref, factor_ref, rows_ref, one_ref, two_ref, three_ref,
                 main_ref, picked_ref, *refs):
    early, late = refs[: plan.m], refs[plan.m : 2 * plan.m]
    outs, fine_ref = refs[2 * plan.m : -1], refs[-1]
    rhs, count = plan.rhs, plan.h[1] // 2
    rows = [rows_ref[i] for i in range(rows_ref.shape[0])]
    pairs = [(2 * (b - 1), b) for b in range(1, count - 1)]
    inner = solve_pairs(plan, 1, rows, pairs, factor_ref)
    for level, ref in ((1, one_ref), (2, two_ref), (3, three_ref)):
        solved = []
        for t in range(ref.shape[0]):
            values = [ref[t, k] for k in range(ref.shape[1])]
            if level == 1:
                values[1:1] = inner[t]
            solved.append(values)
        lifted = lift_pairs(plan, level, solved, blocks, block_ref)
        for b in range(plan.h[level] // 2):
            for j in range(2):
                outs[level - 1][2 * b + j] = lifted[j][b * rhs : (b + 1) * rhs]
    sides, w0 = side_columns(plan, early, late), plan.w0
    lane = lane_index(rhs)
    for b in range(plan.h0 // 2):
        value = pltpu.roll(sides, (LANES - 4 * b) % LANES, 1) if b else sides
        value = jnp.where(lane < 8, value, 0.0)[:, :16].astype(BF16)
        added = jnp.dot(value, picked_ref[b], preferred_element_type=F32)
        for j in range(2):
            fine_ref[2 * b + j] = main_ref[2 * b + j] + added[:, j * w0 : (j + 1) * w0]


def fine_kernel(plan, rows_ref, first_ref, second_ref, factor_ref, out_ref, picked_ref):
    rhs, h0, w0 = plan.rhs, plan.h0, plan.w0
    above, below = read_halos(plan, first_ref, second_ref, True)
    lane = lane_index(rhs)
    rows = [above[0]] + [rows_ref[row] for row in range(h0)] + [below[0]]
    length = 4 * (w0 + 2)
    side = lax.broadcasted_iota(jnp.int32, (16, length), 0)
    at = lax.broadcasted_iota(jnp.int32, (16, length), 1)
    wanted = (side // 2) * (w0 + 2) + (side % 2) * (w0 + 1)
    pick = jnp.where(at == wanted, 1.0, 0.0).astype(BF16)
    for b in range(h0 // 2):
        tiles, before = [], None
        for k in range(5):
            if k < 4:
                rolled = pltpu.roll(rows[2 * b + k], 2 * k + 1, 1)
                value = jnp.where(lane > 2 * k, rolled, 0.0)
            else:
                value = jnp.zeros((rhs, LANES), F32)
            if before is not None:
                value = jnp.where(lane < 2 * k - 1, before, value)
            tiles.append(value)
            before = rolled
        lhs = jnp.concatenate(tiles, axis=1).astype(BF16)[:, :length]
        solved = solve(jnp.concatenate([lhs, pick], axis=0), factor_ref[b, 0])
        for j in range(2):
            out_ref[2 * b + j] = solved[:rhs, j * w0 : (j + 1) * w0]
        picked_ref[b] = solved[rhs:].astype(BF16)


def side_columns(plan, early_refs, late_refs):
    c, rhs, h0 = lax.axis_index("py"), plan.rhs, plan.h0
    found = []
    for offset in (-1, 1):
        total = None
        for early, late, owner in zip(early_refs, late_refs, owners(plan)):
            chosen = jnp.where(owner == c + offset, 1.0, 0.0).astype(F32)
            parts = [early[0] * chosen, early[1] * chosen, late[4 * rhs :] * chosen]
            total = parts if total is None else [a + b for a, b in zip(total, parts)]
        found.append(total)
    slots = []
    for left, right in zip(*found):
        even = lane_index(left.shape[0]) % 2 == 0
        slots.append(jnp.where(even, left, right))
    packed = slots.pop()
    outer = [pltpu.roll(packed, LANES - 4 * k, 1) if k else packed for k in range(rhs // 8)]
    outer = jnp.concatenate(outer, axis=0)
    lane, start = lane_index(rhs), plan.offset[3]
    inner = [
        pltpu.roll(slot, (2 + k * h0 - start) % LANES, 1) for k, slot in enumerate(slots)
    ]
    value = jnp.where(lane < 2 * h0 + 4, pltpu.roll(outer, 2 * h0, 1), 0.0)
    value = jnp.where(lane < 2 * h0 + 2, inner[1], value)
    value = jnp.where(lane < h0 + 2, inner[0], value)
    return jnp.where(lane < 2, outer, value)


def whole_kernel(plan, group, partners, blocks, block_ref, four_ref, inverse_ref, *refs):
    count = plan.n // 2
    gathered, out_ref, pair_ref, four_rows = refs[:count], refs[count], refs[-2], refs[-1]
    r, c = lax.axis_index("px"), lax.axis_index("py")
    rhs, ny4 = plan.rhs, plan.ny[4]
    nx4, nx5 = plan.nx[4], plan.nx[5]
    odd = jnp.bitwise_and(c, 1)
    for block, (left, right) in zip(gathered, partners):
        partner = jnp.where(odd == 1, right, left)
        pair_ref[jnp.bitwise_xor(r, partner) // 2] = block[...]
    lane = lane_index(rhs)
    inside = jnp.logical_and(lane >= 1, lane <= ny4)

    def part_row(pair, j):
        tile, start = divmod(j * ny4, LANES)
        value = pair_ref[pair, :, tile * LANES : (tile + 1) * LANES]
        return jnp.where(inside, pltpu.roll(value, (1 - start) % LANES, 1), 0.0)

    zero = jnp.zeros((rhs, LANES), F32)
    rows = [zero]
    for i in range(nx4):
        value = part_row(i // 2, 1 + i % 2)
        if i % 2 == 0 and i > 0:
            value = value + part_row(i // 2 - 1, 3)
        if i % 2 == 1 and i < nx4 - 1:
            value = value + part_row(i // 2 + 1, 0)
        rows.append(value)
    rows.append(zero)
    five = shrink_rows(rows, nx4, 1)[1:-1]
    flat = product(jnp.concatenate(five, axis=1), blocks.get(block_ref, "shrink5")) * SHRINK
    flat = flat[:, : inverse_ref.shape[0]]
    part_five = jnp.dot(flat.astype(BF16), inverse_ref[...], preferred_element_type=F32)
    spread = blocks.get(block_ref, "lift5")[: part_five.shape[1], : nx4 * ny4]
    lifted = product(part_five, spread) * SHRINK
    w, tiles = plan.tile[4], plan.tiles[4]
    parts = []
    for b in range(nx4 // 2):
        for t in range(tiles):
            pieces = []
            for k in range(4):
                lanes = range(t * w, t * w + w + 2, LANES)
                pieces.append([rows[2 * b + k][:, lo : lo + LANES] for lo in lanes])
            lhs = assemble(pieces, w)
            parts.append(
                lax.dot_general(
                    lhs, four_ref[b, t], (((1,), (1,)), ((), ())), preferred_element_type=F32
                )
            )
    correction = jnp.concatenate(parts, axis=1) + lifted
    width = group * 2 * w * tiles
    bands = nx4 // 2 // group
    stacked = jnp.concatenate(
        [correction[:, i * width : (i + 1) * width] for i in range(bands)], axis=0
    )
    four_rows[0] = jnp.zeros((rhs, LANES), F32)
    four_rows[nx4 + 1] = jnp.zeros((rhs, LANES), F32)
    for g in range(group):
        for j in range(2):
            value = product(stacked, blocks.get(block_ref, "lift4", (c * group + g) * 2 + j))
            for i in range(bands):
                four_rows[1 + 2 * (i * group + g) + j] = value[i * rhs : (i + 1) * rhs]
    for k in range(3):
        out_ref[k] = four_rows[r + k]


def final_kernel(plan, blocks, block_ref, fine_ref, one_ref, two_ref, three_ref, four_ref,
                 first_ref, second_ref, out_ref, whole_ref, semaphores):
    r, rhs = lax.axis_index("px"), plan.rhs
    above = jnp.where(r > 0, 1.0, 0.0).astype(F32)
    below = jnp.where(r < plan.n - 1, 1.0, 0.0).astype(F32)
    halos = read_halos(plan, first_ref, second_ref, False)
    halo = product(
        jnp.concatenate([halos[0][0], halos[1][0]], axis=0),
        blocks.get(block_ref, "band", lax.axis_index("py")),
    )
    from_above, from_below = [
        [halo[k * rhs : (k + 1) * rhs, l * plan.w0 : (l + 1) * plan.w0] for l in range(3)]
        for k in range(2)
    ]
    copies = []
    for part in range(rhs // 8):
        own = slice(8 * part, 8 * (part + 1))
        rows = [four_ref[k, own] for k in range(3)]
        for level, own_ref in ((3, three_ref), (2, two_ref), (1, one_ref)):
            height = plan.h[level]
            lifted = lift_rows(rows, -1, height + 1)
            rows = [lifted[0] * above + from_above[level - 1][own]]
            rows += [lifted[i + 1] + own_ref[i, own] for i in range(height)]
            rows += [lifted[-1] * below + from_below[level - 1][own]]
        lifted = lift_rows(rows, 0, plan.h0)
        start, count = 8 * part * plan.h0, 8 * plan.h0
        for row in range(plan.h0):
            value = lifted[row] + fine_ref[row, own]
            whole_ref[pl.ds(start + row, 8, stride=plan.h0), :] = value
        span = pl.ds(start, count)
        copies.append(
            pltpu.make_async_copy(whole_ref.at[span], out_ref.at[span], semaphores.at[part])
        )
        copies[-1].start()
    for copy in copies:
        copy.wait()


def per_device(mesh_shape, residual, factor_fine, factor_one, factor_two, factor_three,
               factor_four, coarse_inverse):
    factors = [factor_fine, factor_one, factor_two, factor_three, factor_four]
    plan = Plan(mesh_shape, residual.shape, [f.shape for f in factors])
    n, m, rhs, h, h0 = plan.n, plan.m, plan.rhs, plan.h, plan.h0
    x = residual.reshape(rhs * h0, plan.w0)

    def trade(first, second):
        def target(i, c):
            after = i + 1 if c & 2 else i - 1
            return (after, c) if 0 <= after < n else (i, c ^ 2)

        ring = []
        for i in range(n):
            for c in range(m):
                row, column = target(i, c)
                ring.append((i * m + c, row * m + column))
        back = [(b, a) for a, b in ring]
        return lax.ppermute(first, ("px", "py"), ring), lax.ppermute(second, ("px", "py"), back)

    def trade_pairs(first, second):
        far = []
        for i in range(n):
            for c in range(m):
                j = ((i + 1) ^ 1) - 1
                at = j * m + c if 0 <= j < n else i * m + (c ^ 2)
                far.append((i * m + c, at))
        near = [(i, i ^ 1) for i in range(n)]
        return lax.ppermute(first, ("px", "py"), far), lax.ppermute(second, "px", near)

    def swap(value, bits):
        return lax.ppermute(value, "py", [(i, i ^ bits) for i in range(m)])

    blocks = Blocks()
    blocks.add("four", plan.place_four())
    blocks.add("pick", plan.pick_band())
    blocks.add("band", plan.lift_band())
    for l in (1, 2, 3):
        blocks.add(f"place{l}", plan.place_whole(l))
        if plan.tile[l] % LANES == 0:
            blocks.add(f"lift{l}", plan.lift_columns(l))
        else:
            lifted = plan.lift_rows_of(l)
            blocks.add(f"lift{l}", lifted.reshape(m, 2, -1, plan.w0))
    lifted, group = plan.level_four_lift()
    blocks.add("lift4", lifted)
    blocks.add("shrink5", plan.coarsest_shrink())
    blocks.add("lift5", plan.coarsest_lift())
    matrices = blocks.array()

    shrink = kernel_call(
        functools.partial(shrink_kernel, plan),
        jax.ShapeDtypeStruct((4, LANES, LANES), BF16), cost_us=4.0,
    )()
    early, outer, first, second, rows = kernel_call(
        functools.partial(restrict_kernel, plan),
        (shape(6, rhs, LANES), shape(4, rhs, LANES), shape(3, rhs, LANES), shape(3, rhs, LANES),
         shape(h0, rhs, plan.w0)),
    )(x, shrink)
    first, second = trade_pairs(first, second)
    early = kernel_call(
        functools.partial(inner_rows_kernel, plan), shape(4, rhs, LANES), cost_us=0.3
    )(early, rows)

    def spread(bands, bits):
        for bit in bits:
            bands.update({k ^ bit: swap(band, bit) for k, band in list(bands.items())})
        return bands

    bits = [1 << k for k in reversed(range(m.bit_length() - 1))]
    early, first, second = lax.optimization_barrier((early, first, second))
    early = spread({0: early}, bits[:1])
    late = kernel_call(functools.partial(merge_kernel, plan), shape(4 * rhs + 8, LANES))(
        outer, shrink, first, second
    )

    main, picked = kernel_call(
        functools.partial(fine_kernel, plan),
        (shape(h0, rhs, plan.w0), jax.ShapeDtypeStruct((h0 // 2, 16, 2 * plan.w0), BF16)),
        cost_us=0.7,
    )(rows, first, second, factor_fine)
    late = spread({0: late}, bits[:1])
    late, main, picked = lax.optimization_barrier((late, main, picked))
    early, late = spread(early, bits[1:]), spread(late, bits[1:])
    early, late = [early[k] for k in range(m)], [late[k] for k in range(m)]

    pairs = kernel_call(
        functools.partial(gather_kernel, plan, blocks), shape(rhs, 4 * plan.ny[4]), cost_us=0.3
    )(matrices, *late)
    order, fetched, gathered, partners = list(range(n // 2 - 1, 0, -1)), [], [pairs], [(0, 0)]
    for k in range(0, len(order), 2):
        even, odd = order[k], order[min(k + 1, len(order) - 1)]
        routes = [
            (i * m + c, (i ^ (2 * (odd if c % 2 else even))) * m + c)
            for i in range(n) for c in range(m)
        ]
        fetched.append((lax.ppermute(pairs, ("px", "py"), routes), even, odd))
    late, pairs = lax.optimization_barrier((late, pairs))
    for value, even, odd in fetched:
        gathered.append(value)
        partners.append((2 * even, 2 * odd))
        if even != odd:
            gathered.append(swap(value, 1))
            partners.append((2 * odd, 2 * even))


    one, two, three, inner, low, high = kernel_call(
        functools.partial(coarse_kernel, plan, blocks),
        tuple(
            shape(plan.tiles[l], count, rhs, 2 * plan.tile[l])
            for l, count in ((1, 2), (2, h[2] // 2), (3, h[3] // 2))
        )
        + (shape(h[1] - 2, rhs, plan.ny[1]),)
        + (shape(1, rhs, LANES), shape(1, rhs, LANES)),
        cost_us=2.5,
    )(matrices, factor_one, factor_two, factor_three, *early, *late)
    low, high = trade(low, high)
    one, two, three, fine = kernel_call(
        functools.partial(inner_kernel, plan, blocks),
        tuple(shape(h[l], rhs, LANES) for l in (1, 2, 3)) + (shape(h0, rhs, plan.w0),),
        cost_us=1.2,
    )(matrices, factor_one, inner, one, two, three, main, picked, *early, *late)
    four = kernel_call(
        functools.partial(whole_kernel, plan, group, partners, blocks),
        shape(3, rhs, LANES),
        scratch=(
            pltpu.VMEM((n // 2, rhs, 4 * plan.ny[4]), F32),
            pltpu.VMEM((plan.nx[4] + 2, rhs, LANES), F32),
        ),
    )(matrices, jnp.swapaxes(factor_four, 2, 3), coarse_inverse, *gathered)
    out = kernel_call(
        functools.partial(final_kernel, plan, blocks), shape(rhs * h0, plan.w0),
        scratch=(pltpu.VMEM((rhs * h0, plan.w0), F32), pltpu.SemaphoreType.DMA((rhs // 8,))),
        out_space=pl.ANY,
    )(
        matrices, fine, one, two, three, four, low, high
    )
    return out.reshape(rhs, h0, plan.w0)


def solution(mesh):
    placed = (
        P(None, "px", "py"),
        P("px", "py", None, None),
        P("px", None, None, None),
        P("px", None, None, None),
        P("px", None, None, None),
        P(),
        P(),
    )
    return jax.shard_map(
        functools.partial(per_device, dict(mesh.shape)),
        mesh=mesh, in_specs=placed, out_specs=P(None, "px", "py"), check_vma=False,
    )
```

```python
import functools
import math

import jax
import jax.numpy as jnp
import numpy as np
from jax import lax
from jax.experimental import pallas as pl
from jax.experimental.pallas import tpu as pltpu
from jax.sharding import PartitionSpec as P

F32 = jnp.float32
BF16 = jnp.bfloat16
LANES = 128
SHRINK = 1.0 / 20.0
TAPS = (1, 3, 3, 1)
VMEM_BYTES = 24 * 1024 * 1024


def round_up(value, unit=LANES):
    return -(-value // unit) * unit


def global_prolong(coarse):
    out = np.zeros((coarse, 2 * coarse))
    for i in range(coarse):
        out[i, 2 * i] += 3
        out[i, 2 * i + 1] += 3
        if i > 0:
            out[i, 2 * i - 1] += 1
        if i + 1 < coarse:
            out[i, 2 * i + 2] += 1
    return out


def bf(array):
    return np.asarray(array, np.float32).astype(jnp.bfloat16)


class Plan:
    def __init__(self, mesh_shape, residual, factors):
        self.n, self.m = mesh_shape["px"], mesh_shape["py"]
        self.rhs, self.h0, self.w0 = residual
        self.h = [self.h0 >> l for l in range(5)]
        self.w = [self.w0 >> l for l in range(5)]
        self.ny = [self.w0 * self.m >> l for l in range(6)]
        self.nx = [self.h0 * self.n >> l for l in range(6)]
        self.tile = [f[3] // 2 for f in factors]
        self.tiles = [f[1] for f in factors]
        self.slots = self.h[1] + 2
        self.offset = [None, 0]
        for l in (2, 3, 4):
            self.offset.append(self.offset[-1] + self.w[l - 1] + 2)
        self.sides = self.h0 // 2 + 1
        self.first = self.w[1] + 2
        self.rest = LANES - self.first
        self.tail = self.offset[3] + 2 * self.sides

    def place(self, level, lead, width, at=0):
        out = np.zeros((self.m, LANES, width))
        for c in range(self.m):
            for k in range(self.w[level] + 2):
                column = self.w[level] * c - 1 + k
                if -lead <= column < self.ny[level]:
                    out[c, self.offset[level] + k, at + column + lead] = 1
        return out

    def place_whole(self, level):
        if self.tile[level] == LANES:
            return self.place(level, 0, self.ny[level])
        return self.place(level, 1, round_up(self.ny[level] + 2))

    def place_four(self):
        rows = [self.place(4, 0, 4 * self.ny[4], j * self.ny[4]) for j in range(4)]
        return np.stack(rows, axis=1)

    def pick_band(self):
        out = []
        for l in (1, 2, 3):
            pick = np.zeros((self.m, round_up(self.ny[l]), LANES))
            one = self.place(l, 0, self.ny[l])
            pick[:, : self.ny[l]] = one.transpose(0, 2, 1)
            out.append(pick)
        return np.concatenate(out, axis=1)

    def lift_band(self):
        out = []
        for l in (1, 2, 3):
            one = self.place(l, 0, self.ny[l])
            out.append(np.einsum("cki,cif->ckf", one, self.lift_columns(l)))
        return np.concatenate(out, axis=2)

    def lift_columns(self, level):
        out = np.eye(self.ny[level])
        for l in range(level, 0, -1):
            out = out @ global_prolong(self.ny[l])
        return out.reshape(self.ny[level], self.m, self.w0).transpose(1, 0, 2)

    def lift_rows_of(self, level):
        w, tiles = self.tile[level], self.tiles[level]
        full = self.lift_columns(level).reshape(self.m, tiles, w, self.w0)
        out = np.zeros((self.m, 2, tiles, 2 * w, self.w0))
        for j in range(2):
            out[:, j, :, j * w : (j + 1) * w] = full
        return out

    def coarsest_shrink(self):
        nx5, ny5, ny4 = self.nx[5], self.ny[5], self.ny[4]
        columns = global_prolong(ny5).T
        width = round_up(ny4 + 2)
        out = np.zeros((nx5, width, nx5 * ny5))
        for i in range(nx5):
            out[i, 1 : 1 + ny4, i * ny5 : (i + 1) * ny5] = columns
        return bf(out.reshape(nx5 * width, nx5 * ny5))

    def coarsest_lift(self):
        rows, columns = global_prolong(self.nx[5]), global_prolong(self.ny[5])
        both = np.einsum("ia,jb->ijab", rows, columns)
        w, tiles = self.tile[4], self.tiles[4]
        both = both.reshape(self.nx[5] * self.ny[5], self.nx[4] // 2, 2, tiles, w)
        both = both.transpose(0, 1, 3, 2, 4)
        return bf(both.reshape(self.nx[5] * self.ny[5], self.nx[4] * self.ny[4]))

    def level_four_lift(self):
        pair = 2 * self.tile[4] * self.tiles[4]
        group = max(1, LANES // pair)
        width = group * pair
        rows = self.lift_rows_of(4).reshape(self.m, 2, pair, self.w0)
        out = np.zeros((self.m, group, 2, width, self.w0))
        for g in range(group):
            out[:, g, :, g * pair : (g + 1) * pair] = rows
        return bf(out), group


class Blocks:
    def __init__(self):
        self.parts, self.places, self.count = [], {}, 0

    def add(self, name, array):
        lead, (rows, columns) = array.shape[:-2], array.shape[-2:]
        high, wide = round_up(rows) // LANES, round_up(columns) // LANES
        out = np.zeros((math.prod(lead), high * LANES, wide * LANES), np.float32)
        out[:, :rows, :columns] = np.asarray(array, np.float32).reshape((-1, rows, columns))
        out = out.reshape(-1, high, LANES, wide, LANES).transpose(0, 1, 3, 2, 4)
        self.parts.append(out.reshape(-1, LANES, LANES))
        self.places[name] = (self.count, high, wide)
        self.count += len(self.parts[-1])

    def array(self):
        return jnp.asarray(bf(np.concatenate(self.parts, axis=0)))

    def get(self, ref, name, lead=0):
        base, high, wide = self.places[name]
        base = base + lead * (high * wide)
        rows = [
            jnp.concatenate([ref[base + i * wide + j] for j in range(wide)], axis=1)
            for i in range(high)
        ]
        return jnp.concatenate(rows, axis=0)


def split(value):
    high = value.astype(BF16)
    return high, (value - high.astype(F32)).astype(BF16)


def product(value, matrix):
    high, low = split(value)
    count = value.shape[0]
    both = jnp.dot(
        jnp.concatenate([high, low], axis=0), matrix, preferred_element_type=F32
    )
    return both[:count] + both[count:]


def shrink_rows(rows, count, halo):
    out = []
    for i in range(-1, count // 2 + 1):
        total = None
        for t, tap in enumerate(TAPS):
            j = 2 * i - 1 + t
            if -halo <= j < count + halo:
                term = rows[j + halo] * float(tap) if tap > 1 else rows[j + halo]
                total = term if total is None else total + term
        out.append(total)
    return out


def lift_rows(rows, first, last):
    out = []
    for f in range(first, last):
        i = f // 2
        other = i - 1 if f % 2 == 0 else i + 1
        out.append((rows[i + 1] * 3.0 + rows[other + 1]) * SHRINK)
    return out


def lane_index(rows):
    return lax.broadcasted_iota(jnp.int32, (rows, LANES), 1)


def assemble(pieces, width):
    total = 4 * (width + 2)
    tiles = [[] for _ in range(-(-total // LANES))]
    lane = lane_index(pieces[0][0].shape[0])
    for k, piece in enumerate(pieces):
        for q, value in enumerate(piece):
            start = k * (width + 2) + LANES * q
            count = min(LANES, width + 2 - LANES * q)
            shift, at = start % LANES, start // LANES
            rolled = pltpu.roll(value, shift, 1) if shift else value
            tiles[at].append((min(LANES, shift + count), rolled))
            if shift + count > LANES:
                tiles[at + 1].append((shift + count - LANES, rolled))
    out = []
    for segments in tiles:
        segments = sorted(segments, key=lambda s: -s[0])
        end, value = segments[0]
        if end < LANES:
            value = jnp.where(lane < end, value, 0.0)
        for end, part in segments[1:]:
            value = jnp.where(lane < end, part, value)
        out.append(value)
    return jnp.concatenate(out, axis=1).astype(BF16)[:, :total]


def solve(lhs, factor):
    return jnp.dot(lhs, factor, preferred_element_type=F32)


def kernel_call(body, out_shape, scratch=(), cost_us=1.0, out_space=pltpu.VMEM):
    whole = pl.BlockSpec(memory_space=pltpu.VMEM)
    result = pl.BlockSpec(memory_space=out_space)

    def call(*operands):
        return pl.pallas_call(
            body,
            out_shape=out_shape,
            in_specs=[whole] * len(operands),
            out_specs=jax.tree.map(lambda _: result, out_shape),
            scratch_shapes=list(scratch),
            compiler_params=pltpu.CompilerParams(vmem_limit_bytes=VMEM_BYTES),
            cost_estimate=pl.CostEstimate(
                flops=int(cost_us * 1e9), bytes_accessed=int(cost_us * 3e6), transcendentals=0
            ),
        )(*operands)

    return call


def shape(*dims):
    return jax.ShapeDtypeStruct(dims, F32)


def tap_matrix(row_lead, lane_lead, count, first, last):
    row = lax.broadcasted_iota(jnp.int32, (LANES, LANES), 0) - row_lead
    lane = lax.broadcasted_iota(jnp.int32, (LANES, LANES), 1) - lane_lead
    tap = row - 2 * lane + 3
    outer = jnp.logical_or(tap == 0, tap == 3)
    inner = jnp.logical_or(tap == 1, tap == 2)
    value = jnp.where(outer, 1.0, jnp.where(inner, 3.0, 0.0))
    value = jnp.where(jnp.logical_or(lane < first, lane > count + 1 - last), 0.0, value)
    return value.astype(BF16)


def place_sides(plan, slot_value, row, at):
    lane = lane_index(plan.rhs)
    chosen = jnp.logical_or(lane == at, lane == at + 1)
    return jnp.where(chosen, pltpu.roll(row, (at + 1) % LANES, 1), slot_value)


def column_ends(plan):
    c = lax.axis_index("py")
    return jnp.where(c == 0, 1, 0), jnp.where(c == plan.m - 1, 1, 0)


def write_halos(c, down, up, first_ref, second_ref, pairs=False):
    forward = jnp.bitwise_and(c, 1) != 0
    if pairs:
        forward = lax.rem(lax.axis_index("px"), 2) == 1
    for k, (low, high) in enumerate(zip(down, up)):
        first_ref[k] = jnp.where(forward, low, high)
        second_ref[k] = jnp.where(forward, high, low)


def read_halos(plan, first_ref, second_ref, pairs=False):
    r, c = lax.axis_index("px"), lax.axis_index("py")
    forward = jnp.bitwise_and(c, 1) != 0
    if pairs:
        forward = lax.rem(r, 2) == 0
    above = jnp.where(r > 0, 1.0, 0.0).astype(F32)
    below = jnp.where(r < plan.n - 1, 1.0, 0.0).astype(F32)
    first, second = first_ref[...], second_ref[...]
    return jnp.where(forward, first, second) * above, jnp.where(forward, second, first) * below


def shrink_kernel(plan, out_ref):
    first, last = column_ends(plan)
    shrink = None
    for level in (1, 2, 3, 4):
        lead = 0 if level == 1 else plan.offset[level - 1] + 1
        step = tap_matrix(lead, plan.offset[level], plan.w[level], first, last)
        if shrink is None:
            shrink = step
        else:
            shrink = jnp.dot(shrink, step, preferred_element_type=F32).astype(BF16)
        out_ref[level - 1] = shrink


def restrict_kernel(plan, x_ref, shrink_ref, early_ref, outer_ref, first_ref, second_ref, rows_ref):
    r, c = lax.axis_index("px"), lax.axis_index("py")
    rhs, slots, h = plan.rhs, plan.slots, plan.h
    above = jnp.where(r > 0, 1.0, 0.0).astype(F32)
    below = jnp.where(r < plan.n - 1, 1.0, 0.0).astype(F32)
    x = [x_ref[pl.ds(row, rhs, stride=h[0]), :] for row in range(h[0])]
    rows, total = x, None
    for level in (1, 2, 3, 4):
        rows = shrink_rows(rows, h[level - 1], 0 if level == 1 else 1)
        rows[0] = rows[0] * above
        rows[-1] = rows[-1] * below
        part = product(jnp.concatenate(rows, axis=0), shrink_ref[level - 1])
        if total is None:
            total = part
        else:
            count = part.shape[0]
            total = jnp.concatenate([total[:count] + part, total[count:]], axis=0)
    lane = lane_index(slots * rhs)
    scale = jnp.where(lane < plan.offset[2], SHRINK, SHRINK**2)
    scale = jnp.where(lane < plan.offset[3], scale, SHRINK**3)
    total = total * jnp.where(lane < plan.offset[4], scale, SHRINK**4)
    own = [total[i * rhs : (i + 1) * rhs] for i in range(slots)]
    lane = lane_index(rhs)
    one, two, three = plan.offset[2:]
    for k in range(6):
        early_ref[k] = own[2 + k]
    outer = [own[0], own[1]]
    for k in range(2):
        value = jnp.where(lane < two, own[h[2] + k], own[h[3] + k])
        outer.append(jnp.where(lane < one, own[h[1] + k], value))
    for k in range(4):
        outer_ref[k] = outer[k]
    third = pltpu.roll(own[2], LANES - three, 1)
    down = [x[-1], jnp.where(lane < three, outer[2], own[0])]
    down.append(jnp.where(lane < one, third, jnp.where(lane < three, outer[3], own[1])))
    up = [x[0], jnp.where(lane < one, third, own[0]), own[1]]
    write_halos(c, down, up, first_ref, second_ref, True)
    for i, row in enumerate(x):
        rows_ref[i] = row


def inner_rows_kernel(plan, own_ref, rows_ref, early_ref):
    h, rhs = plan.h, plan.rhs
    lane = lane_index(rhs)
    two = plan.offset[3]
    own = [None, None] + [own_ref[k] for k in range(6)]
    x = [rows_ref[k] for k in range(h[0])]
    inner = [own[2], own[3], own[4], own[5]]
    for k in range(2):
        value = inner[k]
        value = jnp.where(lane < two, value, 0.0)
        for j in range(h[0] // 2):
            value = place_sides(plan, value, x[k * (h[0] // 2) + j], two + 2 * j)
        odd_row, end = own[6 + k], plan.tail + plan.first - plan.rest
        moved = pltpu.roll(odd_row, (plan.tail - plan.rest) % LANES, 1)
        chosen = jnp.logical_and(lane >= plan.tail, lane < end)
        early_ref[k] = jnp.where(chosen, moved, value)
        moved = pltpu.roll(odd_row, plan.first, 1)
        early_ref[2 + k] = jnp.where(lane < plan.first, inner[2 + k], moved)


def merge_kernel(plan, outer_ref, shrink_ref, first_ref, second_ref, out_ref):
    r, rhs = lax.axis_index("px"), plan.rhs
    lane = lane_index(rhs)
    above, below = read_halos(plan, first_ref, second_ref, True)
    one, two, three = plan.offset[2:]
    edge = product(jnp.concatenate([above[0], below[0]], axis=0), shrink_ref[0]) * SHRINK
    added = [
        above[1],
        jnp.where(lane < one, edge[:rhs], above[2]),
        jnp.where(lane < one, edge[rhs:], below[1]),
        below[2],
    ]
    even = lax.rem(r, 2) == 0
    own = [outer_ref[k] for k in range(3)]
    partner = [jnp.where(even, below[k], above[k]) for k in (1, 2)]
    third = jnp.where(even, below[1], above[2])
    partner.append(pltpu.roll(third, three, 1))
    low = [jnp.where(even, a, b) for a, b in zip(own, partner)]
    high = [jnp.where(even, b, a) for a, b in zip(own, partner)]
    sums = [low[0], low[1] + high[0], low[2] + high[1], high[2]]
    for k in range(4):
        value = jnp.where(lane < three, outer_ref[k] + added[k], sums[k])
        out_ref[k * rhs : (k + 1) * rhs] = value
    sides = place_sides(plan, jnp.zeros((rhs, LANES), F32), above[0], 0)
    sides = place_sides(plan, sides, below[0], 2)
    total = None
    for k in range(rhs // 8):
        part = sides[8 * k : 8 * (k + 1)]
        part = pltpu.roll(part, 4 * k, 1) if k else part
        total = part if total is None else total + part
    out_ref[4 * rhs :] = total


def banded(bands, matrices):
    return product(jnp.concatenate(bands, axis=1), jnp.concatenate(matrices, axis=0))


def owners(plan):
    c = lax.axis_index("py")
    return [jnp.bitwise_xor(c, k) for k in range(plan.m)]


def gather_kernel(plan, blocks, block_ref, *refs):
    band_refs, out_ref = refs[:-1], refs[-1]
    values, matrices = [], []
    for band, owner in zip(band_refs, owners(plan)):
        for j in range(4):
            values.append(band[j * plan.rhs : (j + 1) * plan.rhs])
            matrices.append(blocks.get(block_ref, "four", 4 * owner + j))
    out_ref[...] = banded(values, matrices)


def level_rows(plan, level, early_refs, late_refs, blocks, block_ref):
    rhs, values = plan.rhs, []
    lane = lane_index(rhs)
    for early, late in zip(early_refs, late_refs):
        outer = [late[i * rhs : (i + 1) * rhs] for i in range(4)]
        inner = []
        if level == 1:
            inner = [early[k] for k in range(4)]
            for k in range(2):
                begin = pltpu.roll(early[2 + k], plan.rest, 1)
                end = pltpu.roll(early[k], (plan.rest - plan.tail) % LANES, 1)
                inner.append(jnp.where(lane < plan.rest, begin, end))
        elif level == 2:
            inner = [early[k] for k in range(2)]
        values.append(jnp.concatenate(outer[:2] + inner + outer[2:], axis=0))
    matrices = [blocks.get(block_ref, f"place{level}", owner) for owner in owners(plan)]
    whole = jnp.dot(
        jnp.concatenate(values, axis=1).astype(BF16), jnp.concatenate(matrices, axis=0),
        preferred_element_type=F32,
    )
    return [whole[i * rhs : (i + 1) * rhs] for i in range(plan.h[level] + 2)]


def assemble_tiles(rows, t):
    rhs, count = rows[0].shape[0], rows[0].shape[1] // LANES
    lane = lane_index(rhs)

    def rolled(k, tile):
        if not 0 <= tile < count:
            return jnp.zeros((rhs, LANES), F32)
        return pltpu.roll(rows[k][:, tile * LANES : (tile + 1) * LANES], 2 * k + 1, 1)

    out = []
    for k in range(5):
        if k < 4:
            value = jnp.where(lane == 2 * k, rolled(k, t - 1), rolled(k, t))
        else:
            value = jnp.zeros((rhs, LANES), F32)
        if k > 0:
            value = jnp.where(lane == 2 * k - 1, rolled(k - 1, t + 1), value)
            value = jnp.where(lane < 2 * k - 1, rolled(k - 1, t), value)
        out.append(value)
    return jnp.concatenate(out, axis=1).astype(BF16)[:, : 4 * (LANES + 2)]


def solve_pairs(plan, level, rows, pairs, factor_ref):
    w, solved = plan.tile[level], []
    for t in range(plan.tiles[level]):
        solved.append([])
        for at, b in pairs:
            window = rows[at : at + 4]
            if w == LANES:
                lhs = assemble_tiles(window, t)
            else:
                lhs = assemble([[row] for row in window], w)
            solved[t].append(solve(lhs, factor_ref[b, t]))
    return solved


def lift_pairs(plan, level, solved, blocks, block_ref):
    c, w = lax.axis_index("py"), plan.tile[level]
    name, count = f"lift{level}", len(solved[0]) * plan.rhs
    stacked = [jnp.concatenate(values, axis=0) for values in solved]
    if w % LANES == 0:
        both = [
            jnp.concatenate([v[:, j * w : (j + 1) * w] for v in stacked], axis=1)
            for j in range(2)
        ]
        both = product(jnp.concatenate(both, axis=0), blocks.get(block_ref, name, c))
        return [both[:count], both[count:]]
    row = jnp.concatenate(stacked, axis=1)
    return [product(row, blocks.get(block_ref, name, 2 * c + j)) for j in range(2)]


def coarse_kernel(plan, blocks, block_ref, *refs):
    factors, outs = refs[:3], refs[3 + 2 * plan.m :]
    early, late = refs[3 : 3 + plan.m], refs[3 + plan.m : 3 + 2 * plan.m]
    c, rhs = lax.axis_index("py"), plan.rhs
    down, up = [], []
    rows = {
        level: level_rows(plan, level, early, late, blocks, block_ref) for level in (1, 2, 3)
    }
    solved = {}
    for level in (1, 2, 3):
        count = plan.h[level] // 2
        pairs = range(count) if level > 1 else sorted({0, count - 1})
        solved[level] = solve_pairs(
            plan, level, rows[level], [(2 * b, b) for b in pairs], factors[level - 1]
        )
    for level in (1, 2, 3):
        w = plan.tile[level]
        for j, (edge, at) in enumerate(((up, 0), (down, -1))):
            for value in solved[level]:
                if w % LANES == 0:
                    edge.append(value[at][:, j * w : (j + 1) * w])
                else:
                    edge.append(pltpu.roll(value[at], LANES - w, 1) if j else value[at])
    edges = [jnp.concatenate(edge, axis=1) for edge in (down, up)]
    picked = product(jnp.concatenate(edges, axis=0), blocks.get(block_ref, "pick", c))
    write_halos(c, [picked[:rhs]], [picked[rhs:]], outs[4], outs[5], False)
    for level in (1, 2, 3):
        for t, values in enumerate(solved[level]):
            for k, value in enumerate(values):
                outs[level - 1][t, k] = value
    for i, row in enumerate(rows[1][2:-2]):
        outs[3][i] = row


def inner_kernel(plan, blocks, block_ref, factor_ref, rows_ref, one_ref, two_ref, three_ref,
                 main_ref, picked_ref, *refs):
    early, late = refs[: plan.m], refs[plan.m : 2 * plan.m]
    outs, fine_ref = refs[2 * plan.m : -1], refs[-1]
    rhs, count = plan.rhs, plan.h[1] // 2
    rows = [rows_ref[i] for i in range(rows_ref.shape[0])]
    pairs = [(2 * (b - 1), b) for b in range(1, count - 1)]
    inner = solve_pairs(plan, 1, rows, pairs, factor_ref)
    for level, ref in ((1, one_ref), (2, two_ref), (3, three_ref)):
        solved = []
        for t in range(ref.shape[0]):
            values = [ref[t, k] for k in range(ref.shape[1])]
            if level == 1:
                values[1:1] = inner[t]
            solved.append(values)
        lifted = lift_pairs(plan, level, solved, blocks, block_ref)
        for b in range(plan.h[level] // 2):
            for j in range(2):
                outs[level - 1][2 * b + j] = lifted[j][b * rhs : (b + 1) * rhs]
    sides, w0 = side_columns(plan, early, late), plan.w0
    lane = lane_index(rhs)
    for b in range(plan.h0 // 2):
        value = pltpu.roll(sides, (LANES - 4 * b) % LANES, 1) if b else sides
        value = jnp.where(lane < 8, value, 0.0)[:, :16].astype(BF16)
        added = jnp.dot(value, picked_ref[b], preferred_element_type=F32)
        for j in range(2):
            fine_ref[2 * b + j] = main_ref[2 * b + j] + added[:, j * w0 : (j + 1) * w0]


def fine_kernel(plan, rows_ref, first_ref, second_ref, factor_ref, out_ref, picked_ref):
    rhs, h0, w0 = plan.rhs, plan.h0, plan.w0
    above, below = read_halos(plan, first_ref, second_ref, True)
    lane = lane_index(rhs)
    rows = [above[0]] + [rows_ref[row] for row in range(h0)] + [below[0]]
    length = 4 * (w0 + 2)
    side = lax.broadcasted_iota(jnp.int32, (16, length), 0)
    at = lax.broadcasted_iota(jnp.int32, (16, length), 1)
    wanted = (side // 2) * (w0 + 2) + (side % 2) * (w0 + 1)
    pick = jnp.where(at == wanted, 1.0, 0.0).astype(BF16)
    for b in range(h0 // 2):
        tiles, before = [], None
        for k in range(5):
            if k < 4:
                rolled = pltpu.roll(rows[2 * b + k], 2 * k + 1, 1)
                value = jnp.where(lane > 2 * k, rolled, 0.0)
            else:
                value = jnp.zeros((rhs, LANES), F32)
            if before is not None:
                value = jnp.where(lane < 2 * k - 1, before, value)
            tiles.append(value)
            before = rolled
        lhs = jnp.concatenate(tiles, axis=1).astype(BF16)[:, :length]
        solved = solve(jnp.concatenate([lhs, pick], axis=0), factor_ref[b, 0])
        for j in range(2):
            out_ref[2 * b + j] = solved[:rhs, j * w0 : (j + 1) * w0]
        picked_ref[b] = solved[rhs:].astype(BF16)


def side_columns(plan, early_refs, late_refs):
    c, rhs, h0 = lax.axis_index("py"), plan.rhs, plan.h0
    found = []
    for offset in (-1, 1):
        total = None
        for early, late, owner in zip(early_refs, late_refs, owners(plan)):
            chosen = jnp.where(owner == c + offset, 1.0, 0.0).astype(F32)
            parts = [early[0] * chosen, early[1] * chosen, late[4 * rhs :] * chosen]
            total = parts if total is None else [a + b for a, b in zip(total, parts)]
        found.append(total)
    slots = []
    for left, right in zip(*found):
        even = lane_index(left.shape[0]) % 2 == 0
        slots.append(jnp.where(even, left, right))
    packed = slots.pop()
    outer = [pltpu.roll(packed, LANES - 4 * k, 1) if k else packed for k in range(rhs // 8)]
    outer = jnp.concatenate(outer, axis=0)
    lane, start = lane_index(rhs), plan.offset[3]
    inner = [
        pltpu.roll(slot, (2 + k * h0 - start) % LANES, 1) for k, slot in enumerate(slots)
    ]
    value = jnp.where(lane < 2 * h0 + 4, pltpu.roll(outer, 2 * h0, 1), 0.0)
    value = jnp.where(lane < 2 * h0 + 2, inner[1], value)
    value = jnp.where(lane < h0 + 2, inner[0], value)
    return jnp.where(lane < 2, outer, value)


def whole_kernel(plan, group, partners, blocks, block_ref, four_ref, inverse_ref, *refs):
    count = plan.n // 2
    gathered, out_ref, pair_ref, four_rows = refs[:count], refs[count], refs[-2], refs[-1]
    r, c = lax.axis_index("px"), lax.axis_index("py")
    rhs, ny4 = plan.rhs, plan.ny[4]
    nx4, nx5 = plan.nx[4], plan.nx[5]
    odd = jnp.bitwise_and(c, 1)
    for block, (left, right) in zip(gathered, partners):
        partner = jnp.where(odd == 1, right, left)
        pair_ref[jnp.bitwise_xor(r, partner) // 2] = block[...]
    lane = lane_index(rhs)
    inside = jnp.logical_and(lane >= 1, lane <= ny4)

    def part_row(pair, j):
        tile, start = divmod(j * ny4, LANES)
        value = pair_ref[pair, :, tile * LANES : (tile + 1) * LANES]
        return jnp.where(inside, pltpu.roll(value, (1 - start) % LANES, 1), 0.0)

    zero = jnp.zeros((rhs, LANES), F32)
    rows = [zero]
    for i in range(nx4):
        value = part_row(i // 2, 1 + i % 2)
        if i % 2 == 0 and i > 0:
            value = value + part_row(i // 2 - 1, 3)
        if i % 2 == 1 and i < nx4 - 1:
            value = value + part_row(i // 2 + 1, 0)
        rows.append(value)
    rows.append(zero)
    five = shrink_rows(rows, nx4, 1)[1:-1]
    flat = product(jnp.concatenate(five, axis=1), blocks.get(block_ref, "shrink5")) * SHRINK
    flat = flat[:, : inverse_ref.shape[0]]
    part_five = jnp.dot(flat.astype(BF16), inverse_ref[...], preferred_element_type=F32)
    spread = blocks.get(block_ref, "lift5")[: part_five.shape[1], : nx4 * ny4]
    lifted = product(part_five, spread) * SHRINK
    w, tiles = plan.tile[4], plan.tiles[4]
    parts = []
    for b in range(nx4 // 2):
        for t in range(tiles):
            pieces = []
            for k in range(4):
                lanes = range(t * w, t * w + w + 2, LANES)
                pieces.append([rows[2 * b + k][:, lo : lo + LANES] for lo in lanes])
            lhs = assemble(pieces, w)
            parts.append(
                lax.dot_general(
                    lhs, four_ref[b, t], (((1,), (1,)), ((), ())), preferred_element_type=F32
                )
            )
    correction = jnp.concatenate(parts, axis=1) + lifted
    width = group * 2 * w * tiles
    bands = nx4 // 2 // group
    stacked = jnp.concatenate(
        [correction[:, i * width : (i + 1) * width] for i in range(bands)], axis=0
    )
    four_rows[0] = jnp.zeros((rhs, LANES), F32)
    four_rows[nx4 + 1] = jnp.zeros((rhs, LANES), F32)
    for g in range(group):
        for j in range(2):
            value = product(stacked, blocks.get(block_ref, "lift4", (c * group + g) * 2 + j))
            for i in range(bands):
                four_rows[1 + 2 * (i * group + g) + j] = value[i * rhs : (i + 1) * rhs]
    for k in range(3):
        out_ref[k] = four_rows[r + k]


def final_kernel(plan, blocks, block_ref, fine_ref, one_ref, two_ref, three_ref, four_ref,
                 first_ref, second_ref, out_ref, whole_ref, semaphores):
    r, rhs = lax.axis_index("px"), plan.rhs
    above = jnp.where(r > 0, 1.0, 0.0).astype(F32)
    below = jnp.where(r < plan.n - 1, 1.0, 0.0).astype(F32)
    halos = read_halos(plan, first_ref, second_ref, False)
    halo = product(
        jnp.concatenate([halos[0][0], halos[1][0]], axis=0),
        blocks.get(block_ref, "band", lax.axis_index("py")),
    )
    from_above, from_below = [
        [halo[k * rhs : (k + 1) * rhs, l * plan.w0 : (l + 1) * plan.w0] for l in range(3)]
        for k in range(2)
    ]
    copies = []
    for part in range(rhs // 8):
        own = slice(8 * part, 8 * (part + 1))
        rows = [four_ref[k, own] for k in range(3)]
        for level, own_ref in ((3, three_ref), (2, two_ref), (1, one_ref)):
            height = plan.h[level]
            lifted = lift_rows(rows, -1, height + 1)
            rows = [lifted[0] * above + from_above[level - 1][own]]
            rows += [lifted[i + 1] + own_ref[i, own] for i in range(height)]
            rows += [lifted[-1] * below + from_below[level - 1][own]]
        lifted = lift_rows(rows, 0, plan.h0)
        start, count = 8 * part * plan.h0, 8 * plan.h0
        for row in range(plan.h0):
            value = lifted[row] + fine_ref[row, own]
            whole_ref[pl.ds(start + row, 8, stride=plan.h0), :] = value
        span = pl.ds(start, count)
        copies.append(
            pltpu.make_async_copy(whole_ref.at[span], out_ref.at[span], semaphores.at[part])
        )
        copies[-1].start()
    for copy in copies:
        copy.wait()


def per_device(mesh_shape, residual, factor_fine, factor_one, factor_two, factor_three,
               factor_four, coarse_inverse):
    factors = [factor_fine, factor_one, factor_two, factor_three, factor_four]
    plan = Plan(mesh_shape, residual.shape, [f.shape for f in factors])
    n, m, rhs, h, h0 = plan.n, plan.m, plan.rhs, plan.h, plan.h0
    x = residual.reshape(rhs * h0, plan.w0)

    def trade(first, second):
        def target(i, c):
            after = i + 1 if c & 1 else i - 1
            return (after, c) if 0 <= after < n else (i, c ^ 1)

        ring = []
        for i in range(n):
            for c in range(m):
                row, column = target(i, c)
                ring.append((i * m + c, row * m + column))
        back = [(b, a) for a, b in ring]
        return lax.ppermute(first, ("px", "py"), ring), lax.ppermute(second, ("px", "py"), back)

    def trade_pairs(first, second):
        far = []
        for i in range(n):
            for c in range(m):
                j = ((i + 1) ^ 1) - 1
                at = j * m + c if 0 <= j < n else i * m + (c ^ 1)
                far.append((i * m + c, at))
        near = [(i, i ^ 1) for i in range(n)]
        return lax.ppermute(first, ("px", "py"), far), lax.ppermute(second, "px", near)

    def swap(value, bits):
        return lax.ppermute(value, "py", [(i, i ^ bits) for i in range(m)])

    blocks = Blocks()
    blocks.add("four", plan.place_four())
    blocks.add("pick", plan.pick_band())
    blocks.add("band", plan.lift_band())
    for l in (1, 2, 3):
        blocks.add(f"place{l}", plan.place_whole(l))
        if plan.tile[l] % LANES == 0:
            blocks.add(f"lift{l}", plan.lift_columns(l))
        else:
            lifted = plan.lift_rows_of(l)
            blocks.add(f"lift{l}", lifted.reshape(m, 2, -1, plan.w0))
    lifted, group = plan.level_four_lift()
    blocks.add("lift4", lifted)
    blocks.add("shrink5", plan.coarsest_shrink())
    blocks.add("lift5", plan.coarsest_lift())
    matrices = blocks.array()

    shrink = kernel_call(
        functools.partial(shrink_kernel, plan),
        jax.ShapeDtypeStruct((4, LANES, LANES), BF16), cost_us=4.0,
    )()
    early, outer, first, second, rows = kernel_call(
        functools.partial(restrict_kernel, plan),
        (shape(6, rhs, LANES), shape(4, rhs, LANES), shape(3, rhs, LANES), shape(3, rhs, LANES),
         shape(h0, rhs, plan.w0)),
    )(x, shrink)
    first, second = trade_pairs(first, second)
    early = kernel_call(
        functools.partial(inner_rows_kernel, plan), shape(4, rhs, LANES), cost_us=0.3
    )(early, rows)

    def spread(bands, bits):
        for bit in bits:
            bands.update({k ^ bit: swap(band, bit) for k, band in list(bands.items())})
        return bands

    bits = [1 << k for k in reversed(range(m.bit_length() - 1))]
    early, first, second = lax.optimization_barrier((early, first, second))
    early = spread({0: early}, bits[:1])
    late = kernel_call(functools.partial(merge_kernel, plan), shape(4 * rhs + 8, LANES))(
        outer, shrink, first, second
    )

    main, picked = kernel_call(
        functools.partial(fine_kernel, plan),
        (shape(h0, rhs, plan.w0), jax.ShapeDtypeStruct((h0 // 2, 16, 2 * plan.w0), BF16)),
        cost_us=0.7,
    )(rows, first, second, factor_fine)
    late = spread({0: late}, bits[:1])
    late, main, picked = lax.optimization_barrier((late, main, picked))
    early, late = spread(early, bits[1:]), spread(late, bits[1:])
    early, late = [early[k] for k in range(m)], [late[k] for k in range(m)]

    pairs = kernel_call(
        functools.partial(gather_kernel, plan, blocks), shape(rhs, 4 * plan.ny[4]), cost_us=0.3
    )(matrices, *late)
    order, fetched, gathered, partners = list(range(n // 2 - 1, 0, -1)), [], [pairs], [(0, 0)]
    for k in range(0, len(order), 2):
        even, odd = order[k], order[min(k + 1, len(order) - 1)]
        routes = [
            (i * m + c, (i ^ (2 * (odd if c % 2 else even))) * m + c)
            for i in range(n) for c in range(m)
        ]
        fetched.append((lax.ppermute(pairs, ("px", "py"), routes), even, odd))
    late, pairs = lax.optimization_barrier((late, pairs))
    for value, even, odd in fetched:
        gathered.append(value)
        partners.append((2 * even, 2 * odd))
        if even != odd:
            gathered.append(swap(value, 1))
            partners.append((2 * odd, 2 * even))


    one, two, three, inner, low, high = kernel_call(
        functools.partial(coarse_kernel, plan, blocks),
        tuple(
            shape(plan.tiles[l], count, rhs, 2 * plan.tile[l])
            for l, count in ((1, 2), (2, h[2] // 2), (3, h[3] // 2))
        )
        + (shape(h[1] - 2, rhs, plan.ny[1]),)
        + (shape(1, rhs, LANES), shape(1, rhs, LANES)),
        cost_us=2.5,
    )(matrices, factor_one, factor_two, factor_three, *early, *late)
    low, high = trade(low, high)
    one, two, three, fine = kernel_call(
        functools.partial(inner_kernel, plan, blocks),
        tuple(shape(h[l], rhs, LANES) for l in (1, 2, 3)) + (shape(h0, rhs, plan.w0),),
        cost_us=1.2,
    )(matrices, factor_one, inner, one, two, three, main, picked, *early, *late)
    four = kernel_call(
        functools.partial(whole_kernel, plan, group, partners, blocks),
        shape(3, rhs, LANES),
        scratch=(
            pltpu.VMEM((n // 2, rhs, 4 * plan.ny[4]), F32),
            pltpu.VMEM((plan.nx[4] + 2, rhs, LANES), F32),
        ),
    )(matrices, jnp.swapaxes(factor_four, 2, 3), coarse_inverse, *gathered)
    out = kernel_call(
        functools.partial(final_kernel, plan, blocks), shape(rhs * h0, plan.w0),
        scratch=(pltpu.VMEM((rhs * h0, plan.w0), F32), pltpu.SemaphoreType.DMA((rhs // 8,))),
        out_space=pl.ANY,
    )(
        matrices, fine, one, two, three, four, low, high
    )
    return out.reshape(rhs, h0, plan.w0)


def solution(mesh):
    placed = (
        P(None, "px", "py"),
        P("px", "py", None, None),
        P("px", None, None, None),
        P("px", None, None, None),
        P("px", None, None, None),
        P(),
        P(),
    )
    return jax.shard_map(
        functools.partial(per_device, dict(mesh.shape)),
        mesh=mesh, in_specs=placed, out_specs=P(None, "px", "py"), check_vma=False,
    )
```

```python
import functools
import math

import jax
import jax.numpy as jnp
import numpy as np
from jax import lax
from jax.experimental import pallas as pl
from jax.experimental.pallas import tpu as pltpu
from jax.sharding import PartitionSpec as P

F32 = jnp.float32
BF16 = jnp.bfloat16
LANES = 128
SHRINK = 1.0 / 20.0
TAPS = (1, 3, 3, 1)
VMEM_BYTES = 24 * 1024 * 1024


def round_up(value, unit=LANES):
    return -(-value // unit) * unit


def global_prolong(coarse):
    out = np.zeros((coarse, 2 * coarse))
    for i in range(coarse):
        out[i, 2 * i] += 3
        out[i, 2 * i + 1] += 3
        if i > 0:
            out[i, 2 * i - 1] += 1
        if i + 1 < coarse:
            out[i, 2 * i + 2] += 1
    return out


def bf(array):
    return np.asarray(array, np.float32).astype(jnp.bfloat16)


class Plan:
    def __init__(self, mesh_shape, residual, factors):
        self.n, self.m = mesh_shape["px"], mesh_shape["py"]
        self.rhs, self.h0, self.w0 = residual
        self.h = [self.h0 >> l for l in range(5)]
        self.w = [self.w0 >> l for l in range(5)]
        self.ny = [self.w0 * self.m >> l for l in range(6)]
        self.nx = [self.h0 * self.n >> l for l in range(6)]
        self.tile = [f[3] // 2 for f in factors]
        self.tiles = [f[1] for f in factors]
        self.slots = self.h[1] + 2
        self.offset = [None, 0]
        for l in (2, 3, 4):
            self.offset.append(self.offset[-1] + self.w[l - 1] + 2)
        self.sides = self.h0 // 2 + 1
        self.first = self.w[1] + 2
        self.rest = LANES - self.first
        self.tail = self.offset[3] + 2 * self.sides

    def place(self, level, lead, width, at=0):
        out = np.zeros((self.m, LANES, width))
        for c in range(self.m):
            for k in range(self.w[level] + 2):
                column = self.w[level] * c - 1 + k
                if -lead <= column < self.ny[level]:
                    out[c, self.offset[level] + k, at + column + lead] = 1
        return out

    def place_whole(self, level):
        if self.tile[level] == LANES:
            return self.place(level, 0, self.ny[level])
        return self.place(level, 1, round_up(self.ny[level] + 2))

    def place_four(self):
        rows = [self.place(4, 0, 4 * self.ny[4], j * self.ny[4]) for j in range(4)]
        return np.stack(rows, axis=1)

    def pick_band(self):
        out = []
        for l in (1, 2, 3):
            pick = np.zeros((self.m, round_up(self.ny[l]), LANES))
            one = self.place(l, 0, self.ny[l])
            pick[:, : self.ny[l]] = one.transpose(0, 2, 1)
            out.append(pick)
        return np.concatenate(out, axis=1)

    def lift_band(self):
        out = []
        for l in (1, 2, 3):
            one = self.place(l, 0, self.ny[l])
            out.append(np.einsum("cki,cif->ckf", one, self.lift_columns(l)))
        return np.concatenate(out, axis=2)

    def lift_columns(self, level):
        out = np.eye(self.ny[level])
        for l in range(level, 0, -1):
            out = out @ global_prolong(self.ny[l])
        return out.reshape(self.ny[level], self.m, self.w0).transpose(1, 0, 2)

    def lift_rows_of(self, level):
        w, tiles = self.tile[level], self.tiles[level]
        full = self.lift_columns(level).reshape(self.m, tiles, w, self.w0)
        out = np.zeros((self.m, 2, tiles, 2 * w, self.w0))
        for j in range(2):
            out[:, j, :, j * w : (j + 1) * w] = full
        return out

    def coarsest_shrink(self):
        nx5, ny5, ny4 = self.nx[5], self.ny[5], self.ny[4]
        columns = global_prolong(ny5).T
        width = round_up(ny4 + 2)
        out = np.zeros((nx5, width, nx5 * ny5))
        for i in range(nx5):
            out[i, 1 : 1 + ny4, i * ny5 : (i + 1) * ny5] = columns
        return bf(out.reshape(nx5 * width, nx5 * ny5))

    def coarsest_lift(self):
        rows, columns = global_prolong(self.nx[5]), global_prolong(self.ny[5])
        both = np.einsum("ia,jb->ijab", rows, columns)
        w, tiles = self.tile[4], self.tiles[4]
        both = both.reshape(self.nx[5] * self.ny[5], self.nx[4] // 2, 2, tiles, w)
        both = both.transpose(0, 1, 3, 2, 4)
        return bf(both.reshape(self.nx[5] * self.ny[5], self.nx[4] * self.ny[4]))

    def level_four_lift(self):
        pair = 2 * self.tile[4] * self.tiles[4]
        group = max(1, LANES // pair)
        width = group * pair
        rows = self.lift_rows_of(4).reshape(self.m, 2, pair, self.w0)
        out = np.zeros((self.m, group, 2, width, self.w0))
        for g in range(group):
            out[:, g, :, g * pair : (g + 1) * pair] = rows
        return bf(out), group


class Blocks:
    def __init__(self):
        self.parts, self.places, self.count = [], {}, 0

    def add(self, name, array):
        lead, (rows, columns) = array.shape[:-2], array.shape[-2:]
        high, wide = round_up(rows) // LANES, round_up(columns) // LANES
        out = np.zeros((math.prod(lead), high * LANES, wide * LANES), np.float32)
        out[:, :rows, :columns] = np.asarray(array, np.float32).reshape((-1, rows, columns))
        out = out.reshape(-1, high, LANES, wide, LANES).transpose(0, 1, 3, 2, 4)
        self.parts.append(out.reshape(-1, LANES, LANES))
        self.places[name] = (self.count, high, wide)
        self.count += len(self.parts[-1])

    def array(self):
        return jnp.asarray(bf(np.concatenate(self.parts, axis=0)))

    def get(self, ref, name, lead=0):
        base, high, wide = self.places[name]
        base = base + lead * (high * wide)
        rows = [
            jnp.concatenate([ref[base + i * wide + j] for j in range(wide)], axis=1)
            for i in range(high)
        ]
        return jnp.concatenate(rows, axis=0)


def split(value):
    high = value.astype(BF16)
    return high, (value - high.astype(F32)).astype(BF16)


def product(value, matrix):
    high, low = split(value)
    count = value.shape[0]
    if matrix.shape[0] == LANES:
        return jnp.dot(
            jnp.concatenate([high, low], axis=1), jnp.concatenate([matrix, matrix], axis=0),
            preferred_element_type=F32,
        )
    both = jnp.dot(
        jnp.concatenate([high, low], axis=0), matrix, preferred_element_type=F32
    )
    return both[:count] + both[count:]


def shrink_rows(rows, count, halo):
    out = []
    for i in range(-1, count // 2 + 1):
        total = None
        for t, tap in enumerate(TAPS):
            j = 2 * i - 1 + t
            if -halo <= j < count + halo:
                term = rows[j + halo] * float(tap) if tap > 1 else rows[j + halo]
                total = term if total is None else total + term
        out.append(total)
    return out


def lift_rows(rows, first, last):
    out = []
    for f in range(first, last):
        i = f // 2
        other = i - 1 if f % 2 == 0 else i + 1
        out.append((rows[i + 1] * 3.0 + rows[other + 1]) * SHRINK)
    return out


def lane_index(rows):
    return lax.broadcasted_iota(jnp.int32, (rows, LANES), 1)


def assemble(pieces, width):
    total = 4 * (width + 2)
    tiles = [[] for _ in range(-(-total // LANES))]
    lane = lane_index(pieces[0][0].shape[0])
    for k, piece in enumerate(pieces):
        for q, value in enumerate(piece):
            start = k * (width + 2) + LANES * q
            count = min(LANES, width + 2 - LANES * q)
            shift, at = start % LANES, start // LANES
            rolled = pltpu.roll(value, shift, 1) if shift else value
            tiles[at].append((min(LANES, shift + count), rolled))
            if shift + count > LANES:
                tiles[at + 1].append((shift + count - LANES, rolled))
    out = []
    for segments in tiles:
        segments = sorted(segments, key=lambda s: -s[0])
        end, value = segments[0]
        if end < LANES:
            value = jnp.where(lane < end, value, 0.0)
        for end, part in segments[1:]:
            value = jnp.where(lane < end, part, value)
        out.append(value)
    return jnp.concatenate(out, axis=1).astype(BF16)[:, :total]


def solve(lhs, factor):
    return jnp.dot(lhs, factor, preferred_element_type=F32)


def kernel_call(body, out_shape, scratch=(), cost_us=1.0, out_space=pltpu.VMEM):
    whole = pl.BlockSpec(memory_space=pltpu.VMEM)
    result = pl.BlockSpec(memory_space=out_space)

    def call(*operands):
        return pl.pallas_call(
            body,
            out_shape=out_shape,
            in_specs=[whole] * len(operands),
            out_specs=jax.tree.map(lambda _: result, out_shape),
            scratch_shapes=list(scratch),
            compiler_params=pltpu.CompilerParams(vmem_limit_bytes=VMEM_BYTES),
            cost_estimate=pl.CostEstimate(
                flops=int(cost_us * 1e9), bytes_accessed=int(cost_us * 3e6), transcendentals=0
            ),
        )(*operands)

    return call


def shape(*dims):
    return jax.ShapeDtypeStruct(dims, F32)


def tap_matrix(row_lead, lane_lead, count, first, last):
    row = lax.broadcasted_iota(jnp.int32, (LANES, LANES), 0) - row_lead
    lane = lax.broadcasted_iota(jnp.int32, (LANES, LANES), 1) - lane_lead
    tap = row - 2 * lane + 3
    outer = jnp.logical_or(tap == 0, tap == 3)
    inner = jnp.logical_or(tap == 1, tap == 2)
    value = jnp.where(outer, 1.0, jnp.where(inner, 3.0, 0.0))
    value = jnp.where(jnp.logical_or(lane < first, lane > count + 1 - last), 0.0, value)
    return value.astype(BF16)


def place_sides(plan, slot_value, row, at):
    lane = lane_index(plan.rhs)
    chosen = jnp.logical_or(lane == at, lane == at + 1)
    return jnp.where(chosen, pltpu.roll(row, (at + 1) % LANES, 1), slot_value)


def column_ends(plan):
    c = lax.axis_index("py")
    return jnp.where(c == 0, 1, 0), jnp.where(c == plan.m - 1, 1, 0)


def write_halos(c, down, up, first_ref, second_ref, pairs=False):
    forward = jnp.bitwise_and(c, 1) != 0
    if pairs:
        forward = lax.rem(lax.axis_index("px"), 2) == 1
    for k, (low, high) in enumerate(zip(down, up)):
        first_ref[k] = jnp.where(forward, low, high)
        second_ref[k] = jnp.where(forward, high, low)


def read_halos(plan, first_ref, second_ref, pairs=False):
    r, c = lax.axis_index("px"), lax.axis_index("py")
    forward = jnp.bitwise_and(c, 1) != 0
    if pairs:
        forward = lax.rem(r, 2) == 0
    above = jnp.where(r > 0, 1.0, 0.0).astype(F32)
    below = jnp.where(r < plan.n - 1, 1.0, 0.0).astype(F32)
    first, second = first_ref[...], second_ref[...]
    return jnp.where(forward, first, second) * above, jnp.where(forward, second, first) * below


def shrink_kernel(plan, out_ref):
    first, last = column_ends(plan)
    shrink = None
    for level in (1, 2, 3, 4):
        lead = 0 if level == 1 else plan.offset[level - 1] + 1
        step = tap_matrix(lead, plan.offset[level], plan.w[level], first, last)
        if shrink is None:
            shrink = step
        else:
            shrink = jnp.dot(shrink, step, preferred_element_type=F32).astype(BF16)
        out_ref[level - 1] = shrink


def restrict_kernel(plan, x_ref, shrink_ref, early_ref, outer_ref, first_ref, second_ref, rows_ref):
    r, c = lax.axis_index("px"), lax.axis_index("py")
    rhs, slots, h = plan.rhs, plan.slots, plan.h
    above = jnp.where(r > 0, 1.0, 0.0).astype(F32)
    below = jnp.where(r < plan.n - 1, 1.0, 0.0).astype(F32)
    x = [x_ref[pl.ds(row, rhs, stride=h[0]), :] for row in range(h[0])]
    rows, total = x, None
    for level in (1, 2, 3, 4):
        rows = shrink_rows(rows, h[level - 1], 0 if level == 1 else 1)
        rows[0] = rows[0] * above
        rows[-1] = rows[-1] * below
        part = product(jnp.concatenate(rows, axis=0), shrink_ref[level - 1])
        if total is None:
            total = part
        else:
            count = part.shape[0]
            total = jnp.concatenate([total[:count] + part, total[count:]], axis=0)
    lane = lane_index(slots * rhs)
    scale = jnp.where(lane < plan.offset[2], SHRINK, SHRINK**2)
    scale = jnp.where(lane < plan.offset[3], scale, SHRINK**3)
    total = total * jnp.where(lane < plan.offset[4], scale, SHRINK**4)
    own = [total[i * rhs : (i + 1) * rhs] for i in range(slots)]
    lane = lane_index(rhs)
    one, two, three = plan.offset[2:]
    for k in range(6):
        early_ref[k] = own[2 + k]
    outer = [own[0], own[1]]
    for k in range(2):
        value = jnp.where(lane < two, own[h[2] + k], own[h[3] + k])
        outer.append(jnp.where(lane < one, own[h[1] + k], value))
    for k in range(4):
        outer_ref[k] = outer[k]
    third = pltpu.roll(own[2], LANES - three, 1)
    down = [x[-1], jnp.where(lane < three, outer[2], own[0])]
    down.append(jnp.where(lane < one, third, jnp.where(lane < three, outer[3], own[1])))
    up = [x[0], jnp.where(lane < one, third, own[0]), own[1]]
    write_halos(c, down, up, first_ref, second_ref, True)
    for i, row in enumerate(x):
        rows_ref[i] = row


def inner_rows_kernel(plan, own_ref, rows_ref, early_ref):
    h, rhs = plan.h, plan.rhs
    lane = lane_index(rhs)
    two = plan.offset[3]
    own = [None, None] + [own_ref[k] for k in range(6)]
    x = [rows_ref[k] for k in range(h[0])]
    inner = [own[2], own[3], own[4], own[5]]
    for k in range(2):
        value = inner[k]
        value = jnp.where(lane < two, value, 0.0)
        for j in range(h[0] // 2):
            value = place_sides(plan, value, x[k * (h[0] // 2) + j], two + 2 * j)
        odd_row, end = own[6 + k], plan.tail + plan.first - plan.rest
        moved = pltpu.roll(odd_row, (plan.tail - plan.rest) % LANES, 1)
        chosen = jnp.logical_and(lane >= plan.tail, lane < end)
        early_ref[k] = jnp.where(chosen, moved, value)
        moved = pltpu.roll(odd_row, plan.first, 1)
        early_ref[2 + k] = jnp.where(lane < plan.first, inner[2 + k], moved)


def merge_kernel(plan, outer_ref, shrink_ref, first_ref, second_ref, out_ref):
    r, rhs = lax.axis_index("px"), plan.rhs
    lane = lane_index(rhs)
    above, below = read_halos(plan, first_ref, second_ref, True)
    one, two, three = plan.offset[2:]
    edge = product(jnp.concatenate([above[0], below[0]], axis=0), shrink_ref[0]) * SHRINK
    added = [
        above[1],
        jnp.where(lane < one, edge[:rhs], above[2]),
        jnp.where(lane < one, edge[rhs:], below[1]),
        below[2],
    ]
    even = lax.rem(r, 2) == 0
    own = [outer_ref[k] for k in range(3)]
    partner = [jnp.where(even, below[k], above[k]) for k in (1, 2)]
    third = jnp.where(even, below[1], above[2])
    partner.append(pltpu.roll(third, three, 1))
    low = [jnp.where(even, a, b) for a, b in zip(own, partner)]
    high = [jnp.where(even, b, a) for a, b in zip(own, partner)]
    sums = [low[0], low[1] + high[0], low[2] + high[1], high[2]]
    for k in range(4):
        value = jnp.where(lane < three, outer_ref[k] + added[k], sums[k])
        out_ref[k * rhs : (k + 1) * rhs] = value
    sides = place_sides(plan, jnp.zeros((rhs, LANES), F32), above[0], 0)
    sides = place_sides(plan, sides, below[0], 2)
    total = None
    for k in range(rhs // 8):
        part = sides[8 * k : 8 * (k + 1)]
        part = pltpu.roll(part, 4 * k, 1) if k else part
        total = part if total is None else total + part
    out_ref[4 * rhs :] = total


def banded(bands, matrices):
    return product(jnp.concatenate(bands, axis=1), jnp.concatenate(matrices, axis=0))


def owners(plan):
    c = lax.axis_index("py")
    return [jnp.bitwise_xor(c, k) for k in range(plan.m)]


def gather_kernel(plan, blocks, block_ref, *refs):
    band_refs, out_ref = refs[:-1], refs[-1]
    values, matrices = [], []
    for band, owner in zip(band_refs, owners(plan)):
        for j in range(4):
            values.append(band[j * plan.rhs : (j + 1) * plan.rhs])
            matrices.append(blocks.get(block_ref, "four", 4 * owner + j))
    out_ref[...] = banded(values, matrices)


def level_rows(plan, level, early_refs, late_refs, blocks, block_ref):
    rhs, values = plan.rhs, []
    lane = lane_index(rhs)
    for early, late in zip(early_refs, late_refs):
        outer = [late[i * rhs : (i + 1) * rhs] for i in range(4)]
        inner = []
        if level == 1:
            inner = [early[k] for k in range(4)]
            for k in range(2):
                begin = pltpu.roll(early[2 + k], plan.rest, 1)
                end = pltpu.roll(early[k], (plan.rest - plan.tail) % LANES, 1)
                inner.append(jnp.where(lane < plan.rest, begin, end))
        elif level == 2:
            inner = [early[k] for k in range(2)]
        values.append(jnp.concatenate(outer[:2] + inner + outer[2:], axis=0))
    matrices = [blocks.get(block_ref, f"place{level}", owner) for owner in owners(plan)]
    whole = jnp.dot(
        jnp.concatenate(values, axis=1).astype(BF16), jnp.concatenate(matrices, axis=0),
        preferred_element_type=F32,
    )
    return [whole[i * rhs : (i + 1) * rhs] for i in range(plan.h[level] + 2)]


def assemble_tiles(rows, t):
    rhs, count = rows[0].shape[0], rows[0].shape[1] // LANES
    lane = lane_index(rhs)

    def rolled(k, tile):
        if not 0 <= tile < count:
            return jnp.zeros((rhs, LANES), F32)
        return pltpu.roll(rows[k][:, tile * LANES : (tile + 1) * LANES], 2 * k + 1, 1)

    out = []
    for k in range(5):
        if k < 4:
            value = jnp.where(lane == 2 * k, rolled(k, t - 1), rolled(k, t))
        else:
            value = jnp.zeros((rhs, LANES), F32)
        if k > 0:
            value = jnp.where(lane == 2 * k - 1, rolled(k - 1, t + 1), value)
            value = jnp.where(lane < 2 * k - 1, rolled(k - 1, t), value)
        out.append(value)
    return jnp.concatenate(out, axis=1).astype(BF16)[:, : 4 * (LANES + 2)]


def solve_pairs(plan, level, rows, pairs, factor_ref):
    w, solved = plan.tile[level], []
    for t in range(plan.tiles[level]):
        solved.append([])
        for at, b in pairs:
            window = rows[at : at + 4]
            if w == LANES:
                lhs = assemble_tiles(window, t)
            else:
                lhs = assemble([[row] for row in window], w)
            solved[t].append(solve(lhs, factor_ref[b, t]))
    return solved


def lift_pairs(plan, level, solved, blocks, block_ref):
    c, w = lax.axis_index("py"), plan.tile[level]
    name, count = f"lift{level}", len(solved[0]) * plan.rhs
    stacked = [jnp.concatenate(values, axis=0) for values in solved]
    if w % LANES == 0:
        both = [
            jnp.concatenate([v[:, j * w : (j + 1) * w] for v in stacked], axis=1)
            for j in range(2)
        ]
        both = product(jnp.concatenate(both, axis=0), blocks.get(block_ref, name, c))
        return [both[:count], both[count:]]
    row = jnp.concatenate(stacked, axis=1)
    return [product(row, blocks.get(block_ref, name, 2 * c + j)) for j in range(2)]


def coarse_kernel(plan, blocks, block_ref, *refs):
    factors, outs = refs[:3], refs[3 + 2 * plan.m :]
    early, late = refs[3 : 3 + plan.m], refs[3 + plan.m : 3 + 2 * plan.m]
    c, rhs = lax.axis_index("py"), plan.rhs
    down, up = [], []
    rows = {
        level: level_rows(plan, level, early, late, blocks, block_ref) for level in (1, 2, 3)
    }
    solved = {}
    for level in (1, 2, 3):
        count = plan.h[level] // 2
        pairs = range(count) if level > 1 else sorted({0, count - 1})
        solved[level] = solve_pairs(
            plan, level, rows[level], [(2 * b, b) for b in pairs], factors[level - 1]
        )
    for level in (1, 2, 3):
        w = plan.tile[level]
        for j, (edge, at) in enumerate(((up, 0), (down, -1))):
            for value in solved[level]:
                if w % LANES == 0:
                    edge.append(value[at][:, j * w : (j + 1) * w])
                else:
                    edge.append(pltpu.roll(value[at], LANES - w, 1) if j else value[at])
    edges = [jnp.concatenate(edge, axis=1) for edge in (down, up)]
    picked = product(jnp.concatenate(edges, axis=0), blocks.get(block_ref, "pick", c))
    write_halos(c, [picked[:rhs]], [picked[rhs:]], outs[4], outs[5], False)
    for level in (1, 2, 3):
        for t, values in enumerate(solved[level]):
            for k, value in enumerate(values):
                outs[level - 1][t, k] = value
    for i, row in enumerate(rows[1][2:-2]):
        outs[3][i] = row


def inner_kernel(plan, blocks, block_ref, factor_ref, rows_ref, one_ref, two_ref, three_ref,
                 main_ref, picked_ref, *refs):
    early, late = refs[: plan.m], refs[plan.m : 2 * plan.m]
    outs, fine_ref = refs[2 * plan.m : -1], refs[-1]
    rhs, count = plan.rhs, plan.h[1] // 2
    rows = [rows_ref[i] for i in range(rows_ref.shape[0])]
    pairs = [(2 * (b - 1), b) for b in range(1, count - 1)]
    inner = solve_pairs(plan, 1, rows, pairs, factor_ref)
    for level, ref in ((1, one_ref), (2, two_ref), (3, three_ref)):
        solved = []
        for t in range(ref.shape[0]):
            values = [ref[t, k] for k in range(ref.shape[1])]
            if level == 1:
                values[1:1] = inner[t]
            solved.append(values)
        lifted = lift_pairs(plan, level, solved, blocks, block_ref)
        for b in range(plan.h[level] // 2):
            for j in range(2):
                outs[level - 1][2 * b + j] = lifted[j][b * rhs : (b + 1) * rhs]
    sides, w0 = side_columns(plan, early, late), plan.w0
    lane = lane_index(rhs)
    for b in range(plan.h0 // 2):
        value = pltpu.roll(sides, (LANES - 4 * b) % LANES, 1) if b else sides
        value = jnp.where(lane < 8, value, 0.0)[:, :16].astype(BF16)
        added = jnp.dot(value, picked_ref[b], preferred_element_type=F32)
        for j in range(2):
            fine_ref[2 * b + j] = main_ref[2 * b + j] + added[:, j * w0 : (j + 1) * w0]


def fine_kernel(plan, rows_ref, first_ref, second_ref, factor_ref, out_ref, picked_ref):
    rhs, h0, w0 = plan.rhs, plan.h0, plan.w0
    above, below = read_halos(plan, first_ref, second_ref, True)
    lane = lane_index(rhs)
    rows = [above[0]] + [rows_ref[row] for row in range(h0)] + [below[0]]
    length = 4 * (w0 + 2)
    side = lax.broadcasted_iota(jnp.int32, (16, length), 0)
    at = lax.broadcasted_iota(jnp.int32, (16, length), 1)
    wanted = (side // 2) * (w0 + 2) + (side % 2) * (w0 + 1)
    pick = jnp.where(at == wanted, 1.0, 0.0).astype(BF16)
    for b in range(h0 // 2):
        tiles, before = [], None
        for k in range(5):
            if k < 4:
                rolled = pltpu.roll(rows[2 * b + k], 2 * k + 1, 1)
                value = jnp.where(lane > 2 * k, rolled, 0.0)
            else:
                value = jnp.zeros((rhs, LANES), F32)
            if before is not None:
                value = jnp.where(lane < 2 * k - 1, before, value)
            tiles.append(value)
            before = rolled
        lhs = jnp.concatenate(tiles, axis=1).astype(BF16)[:, :length]
        solved = solve(jnp.concatenate([lhs, pick], axis=0), factor_ref[b, 0])
        for j in range(2):
            out_ref[2 * b + j] = solved[:rhs, j * w0 : (j + 1) * w0]
        picked_ref[b] = solved[rhs:].astype(BF16)


def side_columns(plan, early_refs, late_refs):
    c, rhs, h0 = lax.axis_index("py"), plan.rhs, plan.h0
    found = []
    for offset in (-1, 1):
        total = None
        for early, late, owner in zip(early_refs, late_refs, owners(plan)):
            chosen = jnp.where(owner == c + offset, 1.0, 0.0).astype(F32)
            parts = [early[0] * chosen, early[1] * chosen, late[4 * rhs :] * chosen]
            total = parts if total is None else [a + b for a, b in zip(total, parts)]
        found.append(total)
    slots = []
    for left, right in zip(*found):
        even = lane_index(left.shape[0]) % 2 == 0
        slots.append(jnp.where(even, left, right))
    packed = slots.pop()
    outer = [pltpu.roll(packed, LANES - 4 * k, 1) if k else packed for k in range(rhs // 8)]
    outer = jnp.concatenate(outer, axis=0)
    lane, start = lane_index(rhs), plan.offset[3]
    inner = [
        pltpu.roll(slot, (2 + k * h0 - start) % LANES, 1) for k, slot in enumerate(slots)
    ]
    value = jnp.where(lane < 2 * h0 + 4, pltpu.roll(outer, 2 * h0, 1), 0.0)
    value = jnp.where(lane < 2 * h0 + 2, inner[1], value)
    value = jnp.where(lane < h0 + 2, inner[0], value)
    return jnp.where(lane < 2, outer, value)


def whole_kernel(plan, group, partners, blocks, block_ref, four_ref, inverse_ref, *refs):
    count = plan.n // 2
    gathered, out_ref, pair_ref, four_rows = refs[:count], refs[count], refs[-2], refs[-1]
    r, c = lax.axis_index("px"), lax.axis_index("py")
    rhs, ny4 = plan.rhs, plan.ny[4]
    nx4, nx5 = plan.nx[4], plan.nx[5]
    odd = jnp.bitwise_and(c, 1)
    for block, (left, right) in zip(gathered, partners):
        partner = jnp.where(odd == 1, right, left)
        pair_ref[jnp.bitwise_xor(r, partner) // 2] = block[...]
    lane = lane_index(rhs)
    inside = jnp.logical_and(lane >= 1, lane <= ny4)

    def part_row(pair, j):
        tile, start = divmod(j * ny4, LANES)
        value = pair_ref[pair, :, tile * LANES : (tile + 1) * LANES]
        return jnp.where(inside, pltpu.roll(value, (1 - start) % LANES, 1), 0.0)

    zero = jnp.zeros((rhs, LANES), F32)
    rows = [zero]
    for i in range(nx4):
        value = part_row(i // 2, 1 + i % 2)
        if i % 2 == 0 and i > 0:
            value = value + part_row(i // 2 - 1, 3)
        if i % 2 == 1 and i < nx4 - 1:
            value = value + part_row(i // 2 + 1, 0)
        rows.append(value)
    rows.append(zero)
    five = shrink_rows(rows, nx4, 1)[1:-1]
    flat = product(jnp.concatenate(five, axis=1), blocks.get(block_ref, "shrink5")) * SHRINK
    flat = flat[:, : inverse_ref.shape[0]]
    part_five = jnp.dot(flat.astype(BF16), inverse_ref[...], preferred_element_type=F32)
    spread = blocks.get(block_ref, "lift5")[: part_five.shape[1], : nx4 * ny4]
    lifted = product(part_five, spread) * SHRINK
    w, tiles = plan.tile[4], plan.tiles[4]
    parts = []
    for b in range(nx4 // 2):
        for t in range(tiles):
            pieces = []
            for k in range(4):
                lanes = range(t * w, t * w + w + 2, LANES)
                pieces.append([rows[2 * b + k][:, lo : lo + LANES] for lo in lanes])
            lhs = assemble(pieces, w)
            parts.append(
                lax.dot_general(
                    lhs, four_ref[b, t], (((1,), (1,)), ((), ())), preferred_element_type=F32
                )
            )
    correction = jnp.concatenate(parts, axis=1) + lifted
    width = group * 2 * w * tiles
    bands = nx4 // 2 // group
    stacked = jnp.concatenate(
        [correction[:, i * width : (i + 1) * width] for i in range(bands)], axis=0
    )
    four_rows[0] = jnp.zeros((rhs, LANES), F32)
    four_rows[nx4 + 1] = jnp.zeros((rhs, LANES), F32)
    for g in range(group):
        for j in range(2):
            value = product(stacked, blocks.get(block_ref, "lift4", (c * group + g) * 2 + j))
            for i in range(bands):
                four_rows[1 + 2 * (i * group + g) + j] = value[i * rhs : (i + 1) * rhs]
    for k in range(3):
        out_ref[k] = four_rows[r + k]


def final_kernel(plan, blocks, block_ref, fine_ref, one_ref, two_ref, three_ref, four_ref,
                 first_ref, second_ref, out_ref, whole_ref, semaphores):
    r, rhs = lax.axis_index("px"), plan.rhs
    above = jnp.where(r > 0, 1.0, 0.0).astype(F32)
    below = jnp.where(r < plan.n - 1, 1.0, 0.0).astype(F32)
    halos = read_halos(plan, first_ref, second_ref, False)
    halo = product(
        jnp.concatenate([halos[0][0], halos[1][0]], axis=0),
        blocks.get(block_ref, "band", lax.axis_index("py")),
    )
    from_above, from_below = [
        [halo[k * rhs : (k + 1) * rhs, l * plan.w0 : (l + 1) * plan.w0] for l in range(3)]
        for k in range(2)
    ]
    copies = []
    for part in range(rhs // 8):
        own = slice(8 * part, 8 * (part + 1))
        rows = [four_ref[k, own] for k in range(3)]
        for level, own_ref in ((3, three_ref), (2, two_ref), (1, one_ref)):
            height = plan.h[level]
            lifted = lift_rows(rows, -1, height + 1)
            rows = [lifted[0] * above + from_above[level - 1][own]]
            rows += [lifted[i + 1] + own_ref[i, own] for i in range(height)]
            rows += [lifted[-1] * below + from_below[level - 1][own]]
        lifted = lift_rows(rows, 0, plan.h0)
        start, count = 8 * part * plan.h0, 8 * plan.h0
        for row in range(plan.h0):
            value = lifted[row] + fine_ref[row, own]
            whole_ref[pl.ds(start + row, 8, stride=plan.h0), :] = value
        span = pl.ds(start, count)
        copies.append(
            pltpu.make_async_copy(whole_ref.at[span], out_ref.at[span], semaphores.at[part])
        )
        copies[-1].start()
    for copy in copies:
        copy.wait()


def per_device(mesh_shape, residual, factor_fine, factor_one, factor_two, factor_three,
               factor_four, coarse_inverse):
    factors = [factor_fine, factor_one, factor_two, factor_three, factor_four]
    plan = Plan(mesh_shape, residual.shape, [f.shape for f in factors])
    n, m, rhs, h, h0 = plan.n, plan.m, plan.rhs, plan.h, plan.h0
    x = residual.reshape(rhs * h0, plan.w0)

    def trade(first, second):
        def target(i, c):
            after = i + 1 if c & 1 else i - 1
            return (after, c) if 0 <= after < n else (i, c ^ 1)

        ring = []
        for i in range(n):
            for c in range(m):
                row, column = target(i, c)
                ring.append((i * m + c, row * m + column))
        back = [(b, a) for a, b in ring]
        return lax.ppermute(first, ("px", "py"), ring), lax.ppermute(second, ("px", "py"), back)

    def trade_pairs(first, second):
        far = []
        for i in range(n):
            for c in range(m):
                j = ((i + 1) ^ 1) - 1
                at = j * m + c if 0 <= j < n else i * m + (c ^ 1)
                far.append((i * m + c, at))
        near = [(i, i ^ 1) for i in range(n)]
        return lax.ppermute(first, ("px", "py"), far), lax.ppermute(second, "px", near)

    def swap(value, bits):
        return lax.ppermute(value, "py", [(i, i ^ bits) for i in range(m)])

    blocks = Blocks()
    blocks.add("four", plan.place_four())
    blocks.add("pick", plan.pick_band())
    blocks.add("band", plan.lift_band())
    for l in (1, 2, 3):
        blocks.add(f"place{l}", plan.place_whole(l))
        if plan.tile[l] % LANES == 0:
            blocks.add(f"lift{l}", plan.lift_columns(l))
        else:
            lifted = plan.lift_rows_of(l)
            blocks.add(f"lift{l}", lifted.reshape(m, 2, -1, plan.w0))
    lifted, group = plan.level_four_lift()
    blocks.add("lift4", lifted)
    blocks.add("shrink5", plan.coarsest_shrink())
    blocks.add("lift5", plan.coarsest_lift())
    matrices = blocks.array()

    shrink = kernel_call(
        functools.partial(shrink_kernel, plan),
        jax.ShapeDtypeStruct((4, LANES, LANES), BF16), cost_us=4.0,
    )()
    early, outer, first, second, rows = kernel_call(
        functools.partial(restrict_kernel, plan),
        (shape(6, rhs, LANES), shape(4, rhs, LANES), shape(3, rhs, LANES), shape(3, rhs, LANES),
         shape(h0, rhs, plan.w0)),
    )(x, shrink)
    first, second = trade_pairs(first, second)
    early = kernel_call(
        functools.partial(inner_rows_kernel, plan), shape(4, rhs, LANES), cost_us=0.3
    )(early, rows)

    def spread(bands, bits):
        for bit in bits:
            bands.update({k ^ bit: swap(band, bit) for k, band in list(bands.items())})
        return bands

    bits = [1 << k for k in reversed(range(m.bit_length() - 1))]
    early, first, second = lax.optimization_barrier((early, first, second))
    early = spread({0: early}, bits[:1])
    late = kernel_call(functools.partial(merge_kernel, plan), shape(4 * rhs + 8, LANES))(
        outer, shrink, first, second
    )

    main, picked = kernel_call(
        functools.partial(fine_kernel, plan),
        (shape(h0, rhs, plan.w0), jax.ShapeDtypeStruct((h0 // 2, 16, 2 * plan.w0), BF16)),
        cost_us=0.7,
    )(rows, first, second, factor_fine)
    late = spread({0: late}, bits[:1])
    late, main, picked = lax.optimization_barrier((late, main, picked))
    early, late = spread(early, bits[1:]), spread(late, bits[1:])
    early, late = [early[k] for k in range(m)], [late[k] for k in range(m)]

    pairs = kernel_call(
        functools.partial(gather_kernel, plan, blocks), shape(rhs, 4 * plan.ny[4]), cost_us=0.3
    )(matrices, *late)
    order, fetched, gathered, partners = list(range(n // 2 - 1, 0, -1)), [], [pairs], [(0, 0)]
    for k in range(0, len(order), 2):
        even, odd = order[k], order[min(k + 1, len(order) - 1)]
        routes = [
            (i * m + c, (i ^ (2 * (odd if c % 2 else even))) * m + c)
            for i in range(n) for c in range(m)
        ]
        fetched.append((lax.ppermute(pairs, ("px", "py"), routes), even, odd))
    late, pairs = lax.optimization_barrier((late, pairs))
    for value, even, odd in fetched:
        gathered.append(value)
        partners.append((2 * even, 2 * odd))
        if even != odd:
            gathered.append(swap(value, 1))
            partners.append((2 * odd, 2 * even))


    one, two, three, inner, low, high = kernel_call(
        functools.partial(coarse_kernel, plan, blocks),
        tuple(
            shape(plan.tiles[l], count, rhs, 2 * plan.tile[l])
            for l, count in ((1, 2), (2, h[2] // 2), (3, h[3] // 2))
        )
        + (shape(h[1] - 2, rhs, plan.ny[1]),)
        + (shape(1, rhs, LANES), shape(1, rhs, LANES)),
        cost_us=2.5,
    )(matrices, factor_one, factor_two, factor_three, *early, *late)
    low, high = trade(low, high)
    one, two, three, fine = kernel_call(
        functools.partial(inner_kernel, plan, blocks),
        tuple(shape(h[l], rhs, LANES) for l in (1, 2, 3)) + (shape(h0, rhs, plan.w0),),
        cost_us=1.2,
    )(matrices, factor_one, inner, one, two, three, main, picked, *early, *late)
    four = kernel_call(
        functools.partial(whole_kernel, plan, group, partners, blocks),
        shape(3, rhs, LANES),
        scratch=(
            pltpu.VMEM((n // 2, rhs, 4 * plan.ny[4]), F32),
            pltpu.VMEM((plan.nx[4] + 2, rhs, LANES), F32),
        ),
    )(matrices, jnp.swapaxes(factor_four, 2, 3), coarse_inverse, *gathered)
    out = kernel_call(
        functools.partial(final_kernel, plan, blocks), shape(rhs * h0, plan.w0),
        scratch=(pltpu.VMEM((rhs * h0, plan.w0), F32), pltpu.SemaphoreType.DMA((rhs // 8,))),
        out_space=pl.ANY,
    )(
        matrices, fine, one, two, three, four, low, high
    )
    return out.reshape(rhs, h0, plan.w0)


def solution(mesh):
    placed = (
        P(None, "px", "py"),
        P("px", "py", None, None),
        P("px", None, None, None),
        P("px", None, None, None),
        P("px", None, None, None),
        P(),
        P(),
    )
    return jax.shard_map(
        functools.partial(per_device, dict(mesh.shape)),
        mesh=mesh, in_specs=placed, out_specs=P(None, "px", "py"), check_vma=False,
    )
```
